32 devices in a mesh: blk: 8 (over y, x, core), head: 4 (over z).
Axes of the slice: x: 2, y: 2, z: 4, core: 2. Of those that a mesh axis runs over, the one named last changes fastest.
Arguments:
- query_states: bfloat16 [8, 2, 64, 2048], P('blk', None, 'head'), may hold values from -24 to 24
- key_states: bfloat16 [8, 2, 64, 512], P('blk', None, None, 'head'), may hold values from -6 to 6
- value_states: bfloat16 [8, 2, 64, 512], P('blk', None, None, 'head'), may hold values from -6 to 6
- doc_lengths: int32 [3], replicated, may hold values from 1 to 768, 1024 in all
- page_slot: int32 [8, 2, 4], replicated, may hold values from 0 to 127, as said below
Outputs:
- attended: bfloat16 [8, 2, 64, 2048], P('blk', None, None, 'head')
- kv_cache: bfloat16 [128, 4, 16, 256], P('blk', 'head')
The draws below stay inside these ranges and needn't reach their ends.
Inputs may be any that keep to these rules, and one draw needn't show every extreme that they name: `page_slot`: all entries differ. The busiest owners hold 16 pages, the least busy 4.
All inputs are finite; a program needn't handle non-finite values.
Results may differ from the reference program's by a relative error of at most 0.007.
Values may be sent and summed in bfloat16 or wider, within the bound.
No kernel may reach another device: no remote copies, remote signals or barrier semaphores. Data moves between devices by JAX's collectives and lax.ppermute only.
A program may use at most 64 MiB of HBM per device.

```python
import math
import jax
import jax.numpy as jnp
import numpy as np
from jax import lax

HEADS = 16
KV_HEADS = 4
HEAD_DIM = 128
BLK_TOK = 64
PAGE = 16
DOCS = 3
PAGES_BLK = 4
TOKENS = 1024
LONGEST = 768
N_BLK = 8


def drawn_parts(key):
    query_key = jax.random.fold_in(key, 11)
    keys_key = jax.random.fold_in(key, 23)
    query_shape = (N_BLK, 2, BLK_TOK, HEADS * HEAD_DIM)
    key_shape = (N_BLK, 2, BLK_TOK, KV_HEADS * HEAD_DIM)
    query_final = jnp.clip(jax.random.normal(query_key, query_shape, jnp.float32), -6.0, 6.0)
    key_final = jnp.clip(jax.random.normal(keys_key, key_shape, jnp.float32), -6.0, 6.0)
    return (query_final, key_final)


def draw_query_states(key, part):
    return drawn_parts(key)[0].astype(jnp.bfloat16)


def draw_key_states(key, part):
    return drawn_parts(key)[1].astype(jnp.bfloat16)


def draw_page_slot(key, part):
    owner_key = jax.random.fold_in(key, 5)
    order_key = jax.random.fold_in(key, 7)
    slot_count = 4 * PAGES_BLK
    all_slots = N_BLK * slot_count
    pattern = jnp.array([4, 4, 2, 2, 1, 1, 1, 1], jnp.int32) * PAGES_BLK
    counts = jax.random.permutation(owner_key, jnp.tile(pattern, N_BLK // 8))
    slot_ids = jnp.arange(all_slots, dtype=jnp.int32)
    unused = (slot_ids % slot_count >= counts[slot_ids // slot_count]).astype(jnp.int32)
    ordering = jnp.argsort(unused * all_slots + slot_ids)
    used_slots = ordering[:N_BLK * 2 * PAGES_BLK].astype(jnp.int32)
    shuffled = jax.random.permutation(order_key, used_slots)
    return shuffled.reshape(N_BLK, 2, PAGES_BLK).astype(jnp.int32)


def shard_levels(rng, dims, cuts, smallest, top_value):
    loudness = 1.0
    for position, shards_of in cuts:
        steps = jax.random.uniform(jax.random.fold_in(jax.random.fold_in(rng, 6), position), (shards_of,), jnp.float32, smallest / len(cuts), top_value / len(cuts))
        loudness = loudness * jnp.repeat(jnp.exp(steps), dims[position] // shards_of).reshape((-1,) + (1,) * (len(dims) - 1 - position))
    return loudness


def length_profile(count, total, bound, slope):
    portions = [(1 << 20) // math.isqrt(standing ** slope) + 1 for standing in range(2, count + 1)]
    spare, given = total - bound - (count - 1), [1] * (count - 1)
    while spare > 0:
        free = [i for i in range(count - 1) if given[i] < bound]
        mass, budget = sum([portions[i] for i in free]), spare
        for i in free:
            addition = min(bound - given[i], max(1, budget * portions[i] // mass), spare)
            given[i] = given[i] + addition
            spare = spare - addition
    return np.array([bound] + given)


def ragged(stream_key, count, total, bound, slope):
    if count == 2:
        one = jax.random.randint(stream_key, (), max(1, total - bound), min(bound, total - 1) + 1)
        return jnp.stack([one, total - one])
    lengths = jnp.asarray(length_profile(count, total, bound, slope), jnp.int32)
    couples = (count - 1) // 2
    giver, receiver = lengths[1:1 + 2 * couples:2], lengths[2:2 + 2 * couples:2]
    slack = jnp.minimum(giver - 1, bound - receiver)
    moved = jax.random.randint(jax.random.fold_in(stream_key, 1), (couples,), 0, 1 << 20) % (slack + 1)
    lengths = lengths.at[1:1 + 2 * couples:2].set(giver - moved).at[2:2 + 2 * couples:2].set(receiver + moved)
    return lengths[jax.random.permutation(jax.random.fold_in(stream_key, 2), count)]


def gaussian(stream_key, shape, scale, reach, shards=(), kind=jnp.bfloat16):
    values = jax.random.normal(stream_key, shape, jnp.float32) * scale
    if len(shards) > 0:
        values = shard_levels(stream_key, shape, shards, -0.22, 0.18) * values
    return jnp.clip(values, min=-reach, max=reach).astype(kind)


def setup_inputs(seed: int = 0) -> dict:
    key_list = jax.random.split(jax.random.key(seed), 6)
    query_states = draw_query_states(jax.random.fold_in(key_list[5], 71), 0)
    key_states = draw_key_states(jax.random.fold_in(key_list[5], 71), 0)
    value_states = gaussian(key_list[2], (N_BLK, 2, BLK_TOK, KV_HEADS * HEAD_DIM), 1.0, 6.0, ((0, 8), (3, 4)))
    doc_lengths = ragged(key_list[3], DOCS, TOKENS, LONGEST, 2).astype(jnp.int32)
    page_slot = draw_page_slot(jax.random.fold_in(key_list[5], 71), 0)
    return {"query_states": query_states, "key_states": key_states, "value_states": value_states, "doc_lengths": doc_lengths, "page_slot": page_slot}


def to_sequence(array):
    first_half = array[:, 0]
    second = array[::-1, 1]
    joined = jnp.concatenate([first_half, second], axis=0)
    return joined.reshape(-1, array.shape[-1])


def from_sequence(matrix, blocks, block_tok):
    shaped = matrix.reshape(2 * blocks, block_tok, matrix.shape[-1])
    return jnp.stack([shaped[:blocks], shaped[blocks:][::-1]], axis=1)


def reference(query_states, key_states, value_states, doc_lengths, page_slot):
    blocks = query_states.shape[0]
    block_tok = query_states.shape[2]
    total_rows = 2 * blocks * block_tok
    group_size = HEADS // KV_HEADS
    seq_q = to_sequence(query_states).reshape(total_rows, KV_HEADS, group_size, HEAD_DIM)
    key_float = to_sequence(key_states).reshape(total_rows, KV_HEADS, HEAD_DIM).astype(jnp.float32)
    value_float = to_sequence(value_states).reshape(total_rows, KV_HEADS, HEAD_DIM).astype(jnp.float32)
    positions = jnp.arange(total_rows, dtype=jnp.int32)
    doc_bounds = jnp.cumsum(doc_lengths)[:-1]
    doc_ids = jnp.sum((positions[:, None] >= doc_bounds[None, :]).astype(jnp.int32), axis=1)
    rows_blk = 8 * block_tok
    block_count = total_rows // rows_blk
    score_scale = HEAD_DIM ** -0.5

    def one_block(block_index):
        first_row = block_index * rows_blk
        q_part = lax.dynamic_slice_in_dim(seq_q, first_row, rows_blk, 0).astype(jnp.float32)
        pos_part = first_row + jnp.arange(rows_blk, dtype=jnp.int32)
        doc_part = lax.dynamic_slice_in_dim(doc_ids, first_row, rows_blk, 0)
        allowed = (positions[None, :] <= pos_part[:, None]) & (doc_ids[None, :] == doc_part[:, None])

        def per_group(group_index):
            query_group = lax.dynamic_index_in_dim(q_part, group_index, 1, keepdims=False)
            key_group = lax.dynamic_index_in_dim(key_float, group_index, 1, keepdims=False)
            value_group = lax.dynamic_index_in_dim(value_float, group_index, 1, keepdims=False)
            scores = jnp.einsum("qhd,kd->qhk", query_group, key_group) * score_scale
            masked = jnp.where(allowed[:, None, :], scores, -1e30)
            running_max = jnp.max(masked, axis=2, keepdims=True)
            weights = jnp.where(allowed[:, None, :], jnp.exp(masked - running_max), 0.0)
            weight_sum = jnp.sum(weights, axis=2)
            rounded = lax.optimization_barrier(weights.astype(jnp.bfloat16)).astype(jnp.float32)
            output = jnp.einsum("qhk,kd->qhd", rounded, value_group) / weight_sum[..., None]
            return output.astype(jnp.bfloat16)

        outputs = lax.map(per_group, jnp.arange(KV_HEADS, dtype=jnp.int32))
        return jnp.moveaxis(outputs, 0, 1).reshape(rows_blk, HEADS * HEAD_DIM)

    pieces_out = lax.map(one_block, jnp.arange(block_count, dtype=jnp.int32))
    attended = from_sequence(pieces_out.reshape(total_rows, HEADS * HEAD_DIM), blocks, block_tok)

    page_count = block_tok // PAGE
    slot_count = 4 * page_count
    key_split = key_states.reshape(blocks, 2, block_tok, KV_HEADS, HEAD_DIM)
    value_split = value_states.reshape(blocks, 2, block_tok, KV_HEADS, HEAD_DIM)
    joined = jnp.concatenate([key_split, value_split], axis=-1)
    page_rows = joined.reshape(blocks, 2, page_count, PAGE, KV_HEADS, 2 * HEAD_DIM)
    page_rows = page_rows.transpose(0, 1, 2, 4, 3, 5).reshape(-1, KV_HEADS, PAGE, 2 * HEAD_DIM)
    kv_cache = jnp.zeros((blocks * slot_count, KV_HEADS, PAGE, 2 * HEAD_DIM), jnp.bfloat16)
    kv_cache = kv_cache.at[page_slot.reshape(-1)].set(page_rows)
    return attended, kv_cache
```

```python
import functools

import jax
import jax.numpy as jnp
from jax import lax
from jax.experimental import pallas as pl
from jax.experimental.pallas import tpu as pltpu
from jax.sharding import PartitionSpec as P

PAGE = 16
LOG2E = 1.4426950408889634


def attend_kernel(blk_count, head_count, meta, doc_lengths, page_slot, *refs):
    q_refs = refs[:head_count]
    kv_refs = refs[head_count : head_count + blk_count]
    attended, kv_cache, q_rows, kv_rows, inverse = refs[head_count + blk_count :]
    my_blk = meta[0]
    my_head = meta[1]
    block_tok = kv_refs[0].shape[2]
    head_dim = kv_refs[0].shape[3] // 2
    sub_tok = block_tok // head_count
    width = q_refs[1].shape[3]
    group = width // head_dim
    pages_blk = block_tok // PAGE
    slot_count = kv_cache.shape[0]
    page_total = blk_count * 2 * pages_blk
    half_rows = blk_count * block_tok
    scale = head_dim**-0.5 * LOG2E

    for slot in range(slot_count):
        inverse[slot] = -1
    first_slot = my_blk * slot_count
    for page in range(page_total):
        local = page_slot[page] - first_slot
        mine = (local >= 0) & (local < slot_count)
        inverse[jnp.where(mine, local, slot_count)] = page

    for d in range(blk_count):
        owner = my_blk ^ d
        for half in range(2):
            block = owner if half == 0 else 2 * blk_count - 1 - owner
            kv_rows[pl.ds(pl.multiple_of(block * block_tok, block_tok), block_tok), :] = kv_refs[d][0, half]
    for d in range(head_count):
        row = pl.multiple_of((my_head ^ d) * sub_tok, sub_tok)
        for half in range(2):
            for g in range(group):
                if d == 0:
                    lane = pl.multiple_of(my_head * width + g * head_dim, head_dim)
                    piece = q_refs[0][0, half, :, pl.ds(lane, head_dim)]
                else:
                    piece = q_refs[d][0, half, :, g * head_dim : (g + 1) * head_dim]
                q_rows[half, g, pl.ds(row, sub_tok), :] = piece

    for slot in range(slot_count):
        page = inverse[slot]
        used = page >= 0
        page = jnp.maximum(page, 0)
        pair = page // (2 * pages_blk)
        rest = page - pair * (2 * pages_blk)
        second = rest >= pages_blk
        block = jnp.where(second, 2 * blk_count - 1 - pair, pair)
        start = block * block_tok + jnp.where(second, rest - pages_blk, rest) * PAGE
        rows = kv_rows[pl.ds(pl.multiple_of(start, PAGE), PAGE), :]
        kv_cache[slot, 0] = jnp.where(used, rows, jnp.zeros_like(rows))

    bounds = []
    total = 0
    for k in range(doc_lengths.shape[0] - 1):
        total = total + doc_lengths[k]
        bounds.append(total)

    for half in range(2):
        cols = half_rows * (half + 1)
        block = my_blk if half == 0 else 2 * blk_count - 1 - my_blk
        q_pos = block * block_tok + lax.broadcasted_iota(jnp.int32, (block_tok, 1), 0)
        first = jnp.zeros_like(q_pos)
        for bound in bounds:
            first = jnp.where(q_pos >= bound, bound, first)
        k_pos = lax.broadcasted_iota(jnp.int32, (block_tok, cols), 1)
        bias = jnp.where((k_pos <= q_pos) & (k_pos >= first), 0.0, -1e30)
        queries = q_rows[half].reshape(group * block_tok, head_dim)
        scores = lax.dot_general(
            queries,
            kv_rows[:cols, :head_dim],
            (((1,), (1,)), ((), ())),
            preferred_element_type=jnp.float32,
        )
        scores = scores.reshape(group, block_tok, cols) * scale + bias[None]
        top = jnp.max(scores, axis=2, keepdims=True)
        weights = jnp.exp2(scores - top)
        weight_sum = jnp.sum(weights, axis=2, keepdims=True)
        out = jnp.dot(
            weights.astype(jnp.bfloat16).reshape(group * block_tok, cols),
            kv_rows[:cols, head_dim:],
            preferred_element_type=jnp.float32,
        ).reshape(group, block_tok, head_dim)
        out = (out / weight_sum).astype(jnp.bfloat16)
        for g in range(group):
            attended[0, half, :, g * head_dim : (g + 1) * head_dim] = out[g]


def per_device(query_states, key_states, value_states, doc_lengths, page_slot):
    blk_count = lax.axis_size("blk")
    head_count = lax.axis_size("head")
    my_blk = lax.axis_index("blk")
    my_head = lax.axis_index("head")
    block_tok, head_dim = key_states.shape[2:]
    width = query_states.shape[3] // head_count
    group = width // head_dim
    slot_count = 4 * (block_tok // PAGE)
    meta = jnp.stack([my_blk, my_head]).astype(jnp.int32)

    pair = jnp.concatenate([key_states, value_states], axis=3)
    kv_pieces = [pair] + [
        lax.ppermute(pair, "blk", [(i, i ^ d) for i in range(blk_count)]) for d in range(1, blk_count)
    ]
    q_pieces = [query_states]
    for d in range(1, head_count):
        part = lax.dynamic_slice_in_dim(query_states, (my_head ^ d) * width, width, axis=3)
        q_pieces.append(lax.ppermute(part, "head", [(i, i ^ d) for i in range(head_count)]))

    smem = pl.BlockSpec(memory_space=pltpu.SMEM)
    vmem = pl.BlockSpec(memory_space=pltpu.VMEM)
    return pl.pallas_call(
        functools.partial(attend_kernel, blk_count, head_count),
        out_shape=(
            jax.ShapeDtypeStruct((1, 2, block_tok, width), jnp.bfloat16),
            jax.ShapeDtypeStruct((slot_count, 1, PAGE, 2 * head_dim), jnp.bfloat16),
        ),
        in_specs=[smem] * 3 + [vmem] * (head_count + blk_count),
        out_specs=(vmem, vmem),
        scratch_shapes=[
            pltpu.VMEM((2, group, block_tok, head_dim), jnp.bfloat16),
            pltpu.VMEM((2 * blk_count * block_tok, 2 * head_dim), jnp.bfloat16),
            pltpu.SMEM((slot_count + 1,), jnp.int32),
        ],
        compiler_params=pltpu.CompilerParams(vmem_limit_bytes=32 * 1024 * 1024),
    )(meta, doc_lengths, page_slot.reshape(-1), *q_pieces, *kv_pieces)


def per_device_long(query_states, key_states, value_states, doc_lengths, page_slot):
    q_local = lax.all_to_all(query_states, "head", split_axis=3, concat_axis=2, tiled=True)
    axis_count = lax.axis_size("blk")
    my_index = lax.axis_index("blk")
    block_tok = q_local.shape[2]
    head_dim = key_states.shape[3]
    group_size = q_local.shape[3] // head_dim
    query_rows = q_local.reshape(2 * block_tok, group_size, head_dim)
    offsets = jnp.arange(block_tok, dtype=jnp.int32)
    doc_bounds = jnp.cumsum(doc_lengths)[:-1]
    page_count = block_tok // PAGE
    slot_count = 4 * page_count
    slot_range = jnp.arange(slot_count, dtype=jnp.int32)
    score_scale = head_dim ** (-0.5)

    def group_positions(owner_ids):
        block_starts = jnp.stack([owner_ids, 2 * axis_count - 1 - owner_ids], axis=1) * block_tok
        return (block_starts[:, :, None] + offsets[None, None, :]).reshape(-1)

    def doc_of(positions):
        return jnp.sum((positions[:, None] >= doc_bounds[None, :]).astype(jnp.int32), axis=1)

    q_pos = group_positions(my_index.reshape(1))
    q_doc = doc_of(q_pos)

    def attend_group(attn_state, key_rows, value_rows, allowed):
        running_max, weight_sum, accum = attn_state
        scores = (
            jnp.einsum("qhd,kd->qhk", query_rows, key_rows, preferred_element_type=jnp.float32)
            * score_scale
        )
        masked = jnp.where(allowed[:, None, :], scores, -1e30)
        new_max = jnp.maximum(running_max, jnp.max(masked, axis=2))
        weights = jnp.where(allowed[:, None, :], jnp.exp(masked - new_max[..., None]), 0.0)
        factor = jnp.exp(running_max - new_max)
        weight_sum = weight_sum * factor + jnp.sum(weights, axis=2)
        update = jnp.einsum(
            "qhk,kd->qhd",
            weights.astype(jnp.bfloat16),
            value_rows,
            preferred_element_type=jnp.float32,
        )
        accum = accum * factor[..., None] + update
        return (new_max, weight_sum, accum)

    def visit_group(attn_state, key_group, value_group, owner_ids):
        key_rows = key_group.reshape(-1, head_dim)
        value_rows = value_group.reshape(-1, head_dim)
        k_pos = group_positions(owner_ids)
        allowed = (k_pos[None, :] <= q_pos[:, None]) & (doc_of(k_pos)[None, :] == q_doc[:, None])
        return attend_group(attn_state, key_rows, value_rows, allowed)

    def place_pages(page_store, key_group, value_group, owner_ids):
        page_rows = jnp.concatenate([key_group, value_group], axis=-1).reshape(
            -1, PAGE * 2 * head_dim
        )
        slot_ids = jnp.take(page_slot, owner_ids, axis=0).reshape(-1) - my_index * slot_count
        selector = (slot_range[:, None] == slot_ids[None, :]).astype(jnp.bfloat16)
        return page_store + jnp.dot(selector, page_rows, preferred_element_type=jnp.float32)

    def fold_groups(step_fn, carried, kv_piece):
        key_piece, value_piece = kv_piece
        piece_len = key_piece.shape[0]
        width = 4
        owner_ids = jnp.arange(piece_len, dtype=jnp.int32).reshape(piece_len // width, width)
        key_groups = key_piece.reshape(piece_len // width, width, 2, block_tok, head_dim)
        value_groups = value_piece.reshape(piece_len // width, width, 2, block_tok, head_dim)

        def visit_one(inner_state, entry_tuple):
            key_group, value_group, owners = entry_tuple
            return (step_fn(inner_state, key_group, value_group, owners), None)

        return lax.scan(visit_one, carried, (key_groups, value_groups, owner_ids))[0]

    empty_store = jnp.zeros((slot_count, PAGE * 2 * head_dim), jnp.float32)
    start_state = (
        jnp.full((2 * block_tok, group_size), -1e30, jnp.float32),
        jnp.zeros((2 * block_tok, group_size), jnp.float32),
        jnp.zeros((2 * block_tok, group_size, head_dim), jnp.float32),
    )
    final_state = fold_groups(
        visit_group,
        start_state,
        (
            lax.all_gather(key_states, "blk", axis=0, tiled=True),
            lax.all_gather(value_states, "blk", axis=0, tiled=True),
        ),
    )
    page_store = fold_groups(
        place_pages,
        empty_store,
        (
            lax.all_gather(key_states, "blk", axis=0, tiled=True),
            lax.all_gather(value_states, "blk", axis=0, tiled=True),
        ),
    )
    running_max, weight_sum, accum = final_state
    attended = (
        (accum / weight_sum[..., None])
        .astype(jnp.bfloat16)
        .reshape(1, 2, block_tok, group_size * head_dim)
    )
    kv_cache = page_store.astype(jnp.bfloat16).reshape(slot_count, 1, PAGE, 2 * head_dim)
    return (attended, kv_cache)


def solution(mesh):
    return jax.shard_map(
        per_device if mesh.shape["blk"] <= 8 else per_device_long,
        mesh=mesh,
        in_specs=(
            P("blk", None, "head", None),
            P("blk", None, None, "head"),
            P("blk", None, None, "head"),
            P(),
            P(),
        ),
        out_specs=(P("blk", None, None, "head"), P("blk", "head", None, None)),
        check_vma=False,
    )
```

```python
import functools

import jax
import jax.numpy as jnp
from jax import lax
from jax.experimental import pallas as pl
from jax.experimental.pallas import tpu as pltpu
from jax.sharding import PartitionSpec as P

PAGE = 16
LOG2E = 1.4426950408889634


def attend_kernel(blk_count, head_count, meta, doc_lengths, page_slot, *refs):
    q_refs = refs[:head_count]
    kv_refs = refs[head_count : head_count + 2]
    attended, kv_cache, q_rows, kv_rows, inverse = refs[head_count + 2 :]
    my_blk = meta[0]
    my_head = meta[1]
    block_tok = kv_refs[0].shape[2]
    head_dim = kv_refs[0].shape[3] // 2
    sub_tok = block_tok // head_count
    width = q_refs[1].shape[3]
    group = width // head_dim
    pages_blk = block_tok // PAGE
    slot_count = kv_cache.shape[0]
    page_total = blk_count * 2 * pages_blk
    half_rows = blk_count * block_tok
    scale = head_dim**-0.5 * LOG2E

    for slot in range(slot_count):
        inverse[slot] = -1
    first_slot = my_blk * slot_count
    for page in range(page_total):
        local = page_slot[page] - first_slot
        mine = (local >= 0) & (local < slot_count)
        inverse[jnp.where(mine, local, slot_count)] = page

    for d in range(blk_count):
        owner = my_blk ^ d
        for half in range(2):
            block = owner if half == 0 else 2 * blk_count - 1 - owner
            kv_rows[pl.ds(pl.multiple_of(block * block_tok, block_tok), block_tok), :] = kv_refs[d % 2][d // 2, half]
    for d in range(head_count):
        row = pl.multiple_of((my_head ^ d) * sub_tok, sub_tok)
        for half in range(2):
            for g in range(group):
                if d == 0:
                    lane = pl.multiple_of(my_head * width + g * head_dim, head_dim)
                    piece = q_refs[0][0, half, :, pl.ds(lane, head_dim)]
                else:
                    piece = q_refs[d][0, half, :, g * head_dim : (g + 1) * head_dim]
                q_rows[half, g, pl.ds(row, sub_tok), :] = piece

    for slot in range(slot_count):
        page = inverse[slot]
        used = page >= 0
        page = jnp.maximum(page, 0)
        pair = page // (2 * pages_blk)
        rest = page - pair * (2 * pages_blk)
        second = rest >= pages_blk
        block = jnp.where(second, 2 * blk_count - 1 - pair, pair)
        start = block * block_tok + jnp.where(second, rest - pages_blk, rest) * PAGE
        rows = kv_rows[pl.ds(pl.multiple_of(start, PAGE), PAGE), :]
        kv_cache[slot, 0] = jnp.where(used, rows, jnp.zeros_like(rows))

    bounds = []
    total = 0
    for k in range(doc_lengths.shape[0] - 1):
        total = total + doc_lengths[k]
        bounds.append(total)

    for half in range(2):
        cols = half_rows * (half + 1)
        block = my_blk if half == 0 else 2 * blk_count - 1 - my_blk
        q_pos = block * block_tok + lax.broadcasted_iota(jnp.int32, (block_tok, 1), 0)
        first = jnp.zeros_like(q_pos)
        for bound in bounds:
            first = jnp.where(q_pos >= bound, bound, first)
        k_pos = lax.broadcasted_iota(jnp.int32, (block_tok, cols), 1)
        bias = jnp.where((k_pos <= q_pos) & (k_pos >= first), 0.0, -1e30)
        queries = q_rows[half].reshape(group * block_tok, head_dim)
        scores = lax.dot_general(
            queries,
            kv_rows[:cols, :head_dim],
            (((1,), (1,)), ((), ())),
            preferred_element_type=jnp.float32,
        )
        scores = scores.reshape(group, block_tok, cols) * scale + bias[None]
        top = jnp.max(scores, axis=2, keepdims=True)
        weights = jnp.exp2(scores - top)
        weight_sum = jnp.sum(weights, axis=2, keepdims=True)
        out = jnp.dot(
            weights.astype(jnp.bfloat16).reshape(group * block_tok, cols),
            kv_rows[:cols, head_dim:],
            preferred_element_type=jnp.float32,
        ).reshape(group, block_tok, head_dim)
        out = (out / weight_sum).astype(jnp.bfloat16)
        for g in range(group):
            attended[0, half, :, g * head_dim : (g + 1) * head_dim] = out[g]


def per_device(query_states, key_states, value_states, doc_lengths, page_slot):
    blk_count = lax.axis_size("blk")
    head_count = lax.axis_size("head")
    my_blk = lax.axis_index("blk")
    my_head = lax.axis_index("head")
    block_tok, head_dim = key_states.shape[2:]
    width = query_states.shape[3] // head_count
    group = width // head_dim
    slot_count = 4 * (block_tok // PAGE)
    meta = jnp.stack([my_blk, my_head]).astype(jnp.int32)

    pair = jnp.concatenate([key_states, value_states], axis=3)
    near = [pair] + [
        lax.ppermute(pair, "blk", [(i, i ^ d) for i in range(blk_count)]) for d in range(2, blk_count, 2)
    ]
    near = jnp.concatenate(near, axis=0)
    far = lax.ppermute(near, "blk", [(i, i ^ 1) for i in range(blk_count)])
    q_pieces = [query_states]
    for d in range(1, head_count):
        part = lax.dynamic_slice_in_dim(query_states, (my_head ^ d) * width, width, axis=3)
        q_pieces.append(lax.ppermute(part, "head", [(i, i ^ d) for i in range(head_count)]))

    smem = pl.BlockSpec(memory_space=pltpu.SMEM)
    vmem = pl.BlockSpec(memory_space=pltpu.VMEM)
    return pl.pallas_call(
        functools.partial(attend_kernel, blk_count, head_count),
        out_shape=(
            jax.ShapeDtypeStruct((1, 2, block_tok, width), jnp.bfloat16),
            jax.ShapeDtypeStruct((slot_count, 1, PAGE, 2 * head_dim), jnp.bfloat16),
        ),
        in_specs=[smem] * 3 + [vmem] * (head_count + 2),
        out_specs=(vmem, vmem),
        scratch_shapes=[
            pltpu.VMEM((2, group, block_tok, head_dim), jnp.bfloat16),
            pltpu.VMEM((2 * blk_count * block_tok, 2 * head_dim), jnp.bfloat16),
            pltpu.SMEM((slot_count + 1,), jnp.int32),
        ],
        compiler_params=pltpu.CompilerParams(vmem_limit_bytes=32 * 1024 * 1024),
    )(meta, doc_lengths, page_slot.reshape(-1), *q_pieces, near, far)


def per_device_long(query_states, key_states, value_states, doc_lengths, page_slot):
    q_local = lax.all_to_all(query_states, "head", split_axis=3, concat_axis=2, tiled=True)
    axis_count = lax.axis_size("blk")
    my_index = lax.axis_index("blk")
    block_tok = q_local.shape[2]
    head_dim = key_states.shape[3]
    group_size = q_local.shape[3] // head_dim
    query_rows = q_local.reshape(2 * block_tok, group_size, head_dim)
    offsets = jnp.arange(block_tok, dtype=jnp.int32)
    doc_bounds = jnp.cumsum(doc_lengths)[:-1]
    page_count = block_tok // PAGE
    slot_count = 4 * page_count
    slot_range = jnp.arange(slot_count, dtype=jnp.int32)
    score_scale = head_dim ** (-0.5)

    def group_positions(owner_ids):
        block_starts = jnp.stack([owner_ids, 2 * axis_count - 1 - owner_ids], axis=1) * block_tok
        return (block_starts[:, :, None] + offsets[None, None, :]).reshape(-1)

    def doc_of(positions):
        return jnp.sum((positions[:, None] >= doc_bounds[None, :]).astype(jnp.int32), axis=1)

    q_pos = group_positions(my_index.reshape(1))
    q_doc = doc_of(q_pos)

    def attend_group(attn_state, key_rows, value_rows, allowed):
        running_max, weight_sum, accum = attn_state
        scores = (
            jnp.einsum("qhd,kd->qhk", query_rows, key_rows, preferred_element_type=jnp.float32)
            * score_scale
        )
        masked = jnp.where(allowed[:, None, :], scores, -1e30)
        new_max = jnp.maximum(running_max, jnp.max(masked, axis=2))
        weights = jnp.where(allowed[:, None, :], jnp.exp(masked - new_max[..., None]), 0.0)
        factor = jnp.exp(running_max - new_max)
        weight_sum = weight_sum * factor + jnp.sum(weights, axis=2)
        update = jnp.einsum(
            "qhk,kd->qhd",
            weights.astype(jnp.bfloat16),
            value_rows,
            preferred_element_type=jnp.float32,
        )
        accum = accum * factor[..., None] + update
        return (new_max, weight_sum, accum)

    def visit_group(attn_state, key_group, value_group, owner_ids):
        key_rows = key_group.reshape(-1, head_dim)
        value_rows = value_group.reshape(-1, head_dim)
        k_pos = group_positions(owner_ids)
        allowed = (k_pos[None, :] <= q_pos[:, None]) & (doc_of(k_pos)[None, :] == q_doc[:, None])
        return attend_group(attn_state, key_rows, value_rows, allowed)

    def place_pages(page_store, key_group, value_group, owner_ids):
        page_rows = jnp.concatenate([key_group, value_group], axis=-1).reshape(
            -1, PAGE * 2 * head_dim
        )
        slot_ids = jnp.take(page_slot, owner_ids, axis=0).reshape(-1) - my_index * slot_count
        selector = (slot_range[:, None] == slot_ids[None, :]).astype(jnp.bfloat16)
        return page_store + jnp.dot(selector, page_rows, preferred_element_type=jnp.float32)

    def fold_groups(step_fn, carried, kv_piece):
        key_piece, value_piece = kv_piece
        piece_len = key_piece.shape[0]
        width = 4
        owner_ids = jnp.arange(piece_len, dtype=jnp.int32).reshape(piece_len // width, width)
        key_groups = key_piece.reshape(piece_len // width, width, 2, block_tok, head_dim)
        value_groups = value_piece.reshape(piece_len // width, width, 2, block_tok, head_dim)

        def visit_one(inner_state, entry_tuple):
            key_group, value_group, owners = entry_tuple
            return (step_fn(inner_state, key_group, value_group, owners), None)

        return lax.scan(visit_one, carried, (key_groups, value_groups, owner_ids))[0]

    empty_store = jnp.zeros((slot_count, PAGE * 2 * head_dim), jnp.float32)
    start_state = (
        jnp.full((2 * block_tok, group_size), -1e30, jnp.float32),
        jnp.zeros((2 * block_tok, group_size), jnp.float32),
        jnp.zeros((2 * block_tok, group_size, head_dim), jnp.float32),
    )
    final_state = fold_groups(
        visit_group,
        start_state,
        (
            lax.all_gather(key_states, "blk", axis=0, tiled=True),
            lax.all_gather(value_states, "blk", axis=0, tiled=True),
        ),
    )
    page_store = fold_groups(
        place_pages,
        empty_store,
        (
            lax.all_gather(key_states, "blk", axis=0, tiled=True),
            lax.all_gather(value_states, "blk", axis=0, tiled=True),
        ),
    )
    running_max, weight_sum, accum = final_state
    attended = (
        (accum / weight_sum[..., None])
        .astype(jnp.bfloat16)
        .reshape(1, 2, block_tok, group_size * head_dim)
    )
    kv_cache = page_store.astype(jnp.bfloat16).reshape(slot_count, 1, PAGE, 2 * head_dim)
    return (attended, kv_cache)


def solution(mesh):
    return jax.shard_map(
        per_device if mesh.shape["blk"] <= 8 else per_device_long,
        mesh=mesh,
        in_specs=(
            P("blk", None, "head", None),
            P("blk", None, None, "head"),
            P("blk", None, None, "head"),
            P(),
            P(),
        ),
        out_specs=(P("blk", None, None, "head"), P("blk", "head", None, None)),
        check_vma=False,
    )
```

```python
import functools

import jax
import jax.numpy as jnp
from jax import lax
from jax.experimental import pallas as pl
from jax.experimental.pallas import tpu as pltpu
from jax.sharding import PartitionSpec as P

PAGE = 16
LOG2E = 1.4426950408889634


def attend_kernel(blk_count, head_count, meta, doc_lengths, page_slot, *refs):
    q_refs = refs[:head_count]
    kv_refs = refs[head_count : head_count + 2]
    attended, kv_cache, q_rows, kv_rows, inverse = refs[head_count + 2 :]
    my_blk = meta[0]
    my_head = meta[1]
    block_tok = kv_refs[0].shape[2]
    head_dim = kv_refs[0].shape[3] // 2
    sub_tok = block_tok // head_count
    width = q_refs[1].shape[3]
    group = width // head_dim
    pages_blk = block_tok // PAGE
    slot_count = kv_cache.shape[0]
    page_total = blk_count * 2 * pages_blk
    half_rows = blk_count * block_tok
    scale = head_dim**-0.5 * LOG2E

    for slot in range(slot_count):
        inverse[slot] = -1
    first_slot = my_blk * slot_count
    for page in range(page_total):
        local = page_slot[page] - first_slot
        mine = (local >= 0) & (local < slot_count)
        inverse[jnp.where(mine, local, slot_count)] = page

    for d in range(blk_count):
        owner = my_blk ^ d
        for half in range(2):
            block = owner if half == 0 else 2 * blk_count - 1 - owner
            kv_rows[pl.ds(pl.multiple_of(block * block_tok, block_tok), block_tok), :] = kv_refs[d % 2][d // 2, half]
    for d in range(head_count):
        row = pl.multiple_of((my_head ^ d) * sub_tok, sub_tok)
        for half in range(2):
            for g in range(group):
                if d == 0:
                    lane = pl.multiple_of(my_head * width + g * head_dim, head_dim)
                    piece = q_refs[0][0, half, :, pl.ds(lane, head_dim)]
                else:
                    piece = q_refs[d][0, half, :, g * head_dim : (g + 1) * head_dim]
                q_rows[half, g, pl.ds(row, sub_tok), :] = piece

    for slot in range(slot_count):
        page = inverse[slot]
        used = page >= 0
        page = jnp.maximum(page, 0)
        pair = page // (2 * pages_blk)
        rest = page - pair * (2 * pages_blk)
        second = rest >= pages_blk
        block = jnp.where(second, 2 * blk_count - 1 - pair, pair)
        start = block * block_tok + jnp.where(second, rest - pages_blk, rest) * PAGE
        rows = kv_rows[pl.ds(pl.multiple_of(start, PAGE), PAGE), :]
        kv_cache[slot, 0] = jnp.where(used, rows, jnp.zeros_like(rows))

    bounds = []
    total = 0
    for k in range(doc_lengths.shape[0] - 1):
        total = total + doc_lengths[k]
        bounds.append(total)

    for half in range(2):
        cols = half_rows * (half + 1)
        block = my_blk if half == 0 else 2 * blk_count - 1 - my_blk
        q_pos = block * block_tok + lax.broadcasted_iota(jnp.int32, (block_tok, 1), 0)
        first = jnp.zeros_like(q_pos)
        for bound in bounds:
            first = jnp.where(q_pos >= bound, bound, first)
        k_pos = lax.broadcasted_iota(jnp.int32, (block_tok, cols), 1)
        bias = jnp.where((k_pos <= q_pos) & (k_pos >= first), 0.0, -1e30)
        queries = q_rows[half].reshape(group * block_tok, head_dim)
        scores = lax.dot_general(
            queries,
            kv_rows[:cols, :head_dim],
            (((1,), (1,)), ((), ())),
            preferred_element_type=jnp.float32,
        )
        scores = scores.reshape(group, block_tok, cols) * scale + bias[None]
        top = jnp.max(scores, axis=2, keepdims=True)
        weights = jnp.exp2(scores - top)
        weight_sum = jnp.sum(weights, axis=2, keepdims=True)
        out = jnp.dot(
            weights.astype(jnp.bfloat16).reshape(group * block_tok, cols),
            kv_rows[:cols, head_dim:],
            preferred_element_type=jnp.float32,
        ).reshape(group, block_tok, head_dim)
        out = (out / weight_sum).astype(jnp.bfloat16)
        for g in range(group):
            attended[0, half, :, g * head_dim : (g + 1) * head_dim] = out[g]


def per_device(query_states, key_states, value_states, doc_lengths, page_slot):
    blk_count = lax.axis_size("blk")
    head_count = lax.axis_size("head")
    my_blk = lax.axis_index("blk")
    my_head = lax.axis_index("head")
    block_tok, head_dim = key_states.shape[2:]
    width = query_states.shape[3] // head_count
    group = width // head_dim
    slot_count = 4 * (block_tok // PAGE)
    meta = jnp.stack([my_blk, my_head]).astype(jnp.int32)

    pair = jnp.concatenate([key_states, value_states], axis=3)
    near = [
        lax.ppermute(pair, "blk", [(i, i ^ d) for i in range(blk_count)]) for d in range(2, blk_count, 2)
    ]
    q_parts = []
    for d in range(1, head_count):
        part = lax.dynamic_slice_in_dim(query_states, (my_head ^ d) * width, width, axis=3)
        q_parts.append(lax.ppermute(part, "head", [(i, i ^ d) for i in range(head_count)]))
    near, q_parts = lax.optimization_barrier((near, q_parts))
    near = jnp.concatenate([pair] + near, axis=0)
    far = lax.ppermute(near, "blk", [(i, i ^ 1) for i in range(blk_count)])
    q_pieces = [query_states] + q_parts

    smem = pl.BlockSpec(memory_space=pltpu.SMEM)
    vmem = pl.BlockSpec(memory_space=pltpu.VMEM)
    return pl.pallas_call(
        functools.partial(attend_kernel, blk_count, head_count),
        out_shape=(
            jax.ShapeDtypeStruct((1, 2, block_tok, width), jnp.bfloat16),
            jax.ShapeDtypeStruct((slot_count, 1, PAGE, 2 * head_dim), jnp.bfloat16),
        ),
        in_specs=[smem] * 3 + [vmem] * (head_count + 2),
        out_specs=(vmem, vmem),
        scratch_shapes=[
            pltpu.VMEM((2, group, block_tok, head_dim), jnp.bfloat16),
            pltpu.VMEM((2 * blk_count * block_tok, 2 * head_dim), jnp.bfloat16),
            pltpu.SMEM((slot_count + 1,), jnp.int32),
        ],
        compiler_params=pltpu.CompilerParams(vmem_limit_bytes=32 * 1024 * 1024),
    )(meta, doc_lengths, page_slot.reshape(-1), *q_pieces, near, far)


def per_device_long(query_states, key_states, value_states, doc_lengths, page_slot):
    q_local = lax.all_to_all(query_states, "head", split_axis=3, concat_axis=2, tiled=True)
    axis_count = lax.axis_size("blk")
    my_index = lax.axis_index("blk")
    block_tok = q_local.shape[2]
    head_dim = key_states.shape[3]
    group_size = q_local.shape[3] // head_dim
    query_rows = q_local.reshape(2 * block_tok, group_size, head_dim)
    offsets = jnp.arange(block_tok, dtype=jnp.int32)
    doc_bounds = jnp.cumsum(doc_lengths)[:-1]
    page_count = block_tok // PAGE
    slot_count = 4 * page_count
    slot_range = jnp.arange(slot_count, dtype=jnp.int32)
    score_scale = head_dim ** (-0.5)

    def group_positions(owner_ids):
        block_starts = jnp.stack([owner_ids, 2 * axis_count - 1 - owner_ids], axis=1) * block_tok
        return (block_starts[:, :, None] + offsets[None, None, :]).reshape(-1)

    def doc_of(positions):
        return jnp.sum((positions[:, None] >= doc_bounds[None, :]).astype(jnp.int32), axis=1)

    q_pos = group_positions(my_index.reshape(1))
    q_doc = doc_of(q_pos)

    def attend_group(attn_state, key_rows, value_rows, allowed):
        running_max, weight_sum, accum = attn_state
        scores = (
            jnp.einsum("qhd,kd->qhk", query_rows, key_rows, preferred_element_type=jnp.float32)
            * score_scale
        )
        masked = jnp.where(allowed[:, None, :], scores, -1e30)
        new_max = jnp.maximum(running_max, jnp.max(masked, axis=2))
        weights = jnp.where(allowed[:, None, :], jnp.exp(masked - new_max[..., None]), 0.0)
        factor = jnp.exp(running_max - new_max)
        weight_sum = weight_sum * factor + jnp.sum(weights, axis=2)
        update = jnp.einsum(
            "qhk,kd->qhd",
            weights.astype(jnp.bfloat16),
            value_rows,
            preferred_element_type=jnp.float32,
        )
        accum = accum * factor[..., None] + update
        return (new_max, weight_sum, accum)

    def visit_group(attn_state, key_group, value_group, owner_ids):
        key_rows = key_group.reshape(-1, head_dim)
        value_rows = value_group.reshape(-1, head_dim)
        k_pos = group_positions(owner_ids)
        allowed = (k_pos[None, :] <= q_pos[:, None]) & (doc_of(k_pos)[None, :] == q_doc[:, None])
        return attend_group(attn_state, key_rows, value_rows, allowed)

    def place_pages(page_store, key_group, value_group, owner_ids):
        page_rows = jnp.concatenate([key_group, value_group], axis=-1).reshape(
            -1, PAGE * 2 * head_dim
        )
        slot_ids = jnp.take(page_slot, owner_ids, axis=0).reshape(-1) - my_index * slot_count
        selector = (slot_range[:, None] == slot_ids[None, :]).astype(jnp.bfloat16)
        return page_store + jnp.dot(selector, page_rows, preferred_element_type=jnp.float32)

    def fold_groups(step_fn, carried, kv_piece):
        key_piece, value_piece = kv_piece
        piece_len = key_piece.shape[0]
        width = 4
        owner_ids = jnp.arange(piece_len, dtype=jnp.int32).reshape(piece_len // width, width)
        key_groups = key_piece.reshape(piece_len // width, width, 2, block_tok, head_dim)
        value_groups = value_piece.reshape(piece_len // width, width, 2, block_tok, head_dim)

        def visit_one(inner_state, entry_tuple):
            key_group, value_group, owners = entry_tuple
            return (step_fn(inner_state, key_group, value_group, owners), None)

        return lax.scan(visit_one, carried, (key_groups, value_groups, owner_ids))[0]

    empty_store = jnp.zeros((slot_count, PAGE * 2 * head_dim), jnp.float32)
    start_state = (
        jnp.full((2 * block_tok, group_size), -1e30, jnp.float32),
        jnp.zeros((2 * block_tok, group_size), jnp.float32),
        jnp.zeros((2 * block_tok, group_size, head_dim), jnp.float32),
    )
    final_state = fold_groups(
        visit_group,
        start_state,
        (
            lax.all_gather(key_states, "blk", axis=0, tiled=True),
            lax.all_gather(value_states, "blk", axis=0, tiled=True),
        ),
    )
    page_store = fold_groups(
        place_pages,
        empty_store,
        (
            lax.all_gather(key_states, "blk", axis=0, tiled=True),
            lax.all_gather(value_states, "blk", axis=0, tiled=True),
        ),
    )
    running_max, weight_sum, accum = final_state
    attended = (
        (accum / weight_sum[..., None])
        .astype(jnp.bfloat16)
        .reshape(1, 2, block_tok, group_size * head_dim)
    )
    kv_cache = page_store.astype(jnp.bfloat16).reshape(slot_count, 1, PAGE, 2 * head_dim)
    return (attended, kv_cache)


def solution(mesh):
    return jax.shard_map(
        per_device if mesh.shape["blk"] <= 8 else per_device_long,
        mesh=mesh,
        in_specs=(
            P("blk", None, "head", None),
            P("blk", None, None, "head"),
            P("blk", None, None, "head"),
            P(),
            P(),
        ),
        out_specs=(P("blk", None, None, "head"), P("blk", "head", None, None)),
        check_vma=False,
    )
```

```python
import jax
import jax.numpy as jnp
from jax import lax
from jax.experimental import pallas as pl
from jax.experimental.pallas import tpu as pltpu
from jax.sharding import PartitionSpec as P

PAGE = 16
LOG2E = 1.4426950408889634


def attend_kernel(
    meta, doc_lengths, page_slot, q_all, near, far, attended, kv_cache, q_rows, kv_rows, inverse
):
    my_blk = meta[0]
    head_count, _, width = q_all.shape
    blk_count = 2 * near.shape[0]
    block_tok = near.shape[2]
    head_dim = near.shape[3] // 2
    sub_tok = block_tok // head_count
    group = width // head_dim
    pages_blk = block_tok // PAGE
    slot_count = kv_cache.shape[0]
    page_total = blk_count * 2 * pages_blk
    half_rows = blk_count * block_tok
    scale = head_dim**-0.5 * LOG2E

    for slot in range(slot_count):
        inverse[slot] = -1
    first_slot = my_blk * slot_count
    for page in range(page_total):
        local = page_slot[page] - first_slot
        mine = (local >= 0) & (local < slot_count)
        inverse[jnp.where(mine, local, slot_count)] = page

    for d in range(blk_count):
        owner = my_blk ^ d
        for half in range(2):
            block = owner if half == 0 else 2 * blk_count - 1 - owner
            kv_rows[pl.ds(pl.multiple_of(block * block_tok, block_tok), block_tok), :] = (
                near if d % 2 == 0 else far
            )[d // 2, half]
    for d in range(head_count):
        for half in range(2):
            for g in range(group):
                piece = q_all[d, half * sub_tok : (half + 1) * sub_tok, g * head_dim : (g + 1) * head_dim]
                q_rows[half, g, d * sub_tok : (d + 1) * sub_tok, :] = piece

    for slot in range(slot_count):
        page = inverse[slot]
        used = page >= 0
        page = jnp.maximum(page, 0)
        pair = page // (2 * pages_blk)
        rest = page - pair * (2 * pages_blk)
        second = rest >= pages_blk
        block = jnp.where(second, 2 * blk_count - 1 - pair, pair)
        start = block * block_tok + jnp.where(second, rest - pages_blk, rest) * PAGE
        rows = kv_rows[pl.ds(pl.multiple_of(start, PAGE), PAGE), :]
        kv_cache[slot, 0] = jnp.where(used, rows, jnp.zeros_like(rows))

    bounds = []
    total = 0
    for k in range(doc_lengths.shape[0] - 1):
        total = total + doc_lengths[k]
        bounds.append(total)

    for half in range(2):
        cols = half_rows * (half + 1)
        block = my_blk if half == 0 else 2 * blk_count - 1 - my_blk
        q_pos = block * block_tok + lax.broadcasted_iota(jnp.int32, (block_tok, 1), 0)
        first = jnp.zeros_like(q_pos)
        for bound in bounds:
            first = jnp.where(q_pos >= bound, bound, first)
        k_pos = lax.broadcasted_iota(jnp.int32, (block_tok, cols), 1)
        bias = jnp.where((k_pos <= q_pos) & (k_pos >= first), 0.0, -1e30)
        queries = q_rows[half].reshape(group * block_tok, head_dim)
        scores = lax.dot_general(
            queries,
            kv_rows[:cols, :head_dim],
            (((1,), (1,)), ((), ())),
            preferred_element_type=jnp.float32,
        )
        scores = scores.reshape(group, block_tok, cols) * scale + bias[None]
        top = jnp.max(scores, axis=2, keepdims=True)
        weights = jnp.exp2(scores - top)
        weight_sum = jnp.sum(weights, axis=2, keepdims=True)
        out = jnp.dot(
            weights.astype(jnp.bfloat16).reshape(group * block_tok, cols),
            kv_rows[:cols, head_dim:],
            preferred_element_type=jnp.float32,
        ).reshape(group, block_tok, head_dim)
        out = (out / weight_sum).astype(jnp.bfloat16)
        for g in range(group):
            attended[0, half, :, g * head_dim : (g + 1) * head_dim] = out[g]


def per_device(query_states, key_states, value_states, doc_lengths, page_slot):
    blk_count = lax.axis_size("blk")
    head_count = lax.axis_size("head")
    my_blk = lax.axis_index("blk")
    block_tok, head_dim = key_states.shape[2:]
    width = query_states.shape[3] // head_count
    group = width // head_dim
    slot_count = 4 * (block_tok // PAGE)
    meta = my_blk.reshape(1)

    pair = jnp.concatenate([key_states, value_states], axis=3)
    near = [
        lax.ppermute(pair, "blk", [(i, i ^ d) for i in range(blk_count)]) for d in range(2, blk_count, 2)
    ]
    tokens = query_states.shape[2]
    q_flat = query_states.reshape(2 * tokens, head_count * width)
    q_split = jnp.stack([q_flat[:, h * width : (h + 1) * width] for h in range(head_count)])
    q_all = lax.all_to_all(q_split, "head", split_axis=0, concat_axis=0, tiled=True)
    near, q_all = lax.optimization_barrier((near, q_all))
    near = jnp.concatenate([pair] + near, axis=0)
    far = lax.ppermute(near, "blk", [(i, i ^ 1) for i in range(blk_count)])

    smem = pl.BlockSpec(memory_space=pltpu.SMEM)
    vmem = pl.BlockSpec(memory_space=pltpu.VMEM)
    return pl.pallas_call(
        attend_kernel,
        out_shape=(
            jax.ShapeDtypeStruct((1, 2, block_tok, width), jnp.bfloat16),
            jax.ShapeDtypeStruct((slot_count, 1, PAGE, 2 * head_dim), jnp.bfloat16),
        ),
        in_specs=[smem] * 3 + [vmem] * 3,
        out_specs=(vmem, vmem),
        scratch_shapes=[
            pltpu.VMEM((2, group, block_tok, head_dim), jnp.bfloat16),
            pltpu.VMEM((2 * blk_count * block_tok, 2 * head_dim), jnp.bfloat16),
            pltpu.SMEM((slot_count + 1,), jnp.int32),
        ],
        compiler_params=pltpu.CompilerParams(vmem_limit_bytes=32 * 1024 * 1024),
    )(meta, doc_lengths, page_slot.reshape(-1), q_all, near, far)


def per_device_long(query_states, key_states, value_states, doc_lengths, page_slot):
    q_local = lax.all_to_all(query_states, "head", split_axis=3, concat_axis=2, tiled=True)
    axis_count = lax.axis_size("blk")
    my_index = lax.axis_index("blk")
    block_tok = q_local.shape[2]
    head_dim = key_states.shape[3]
    group_size = q_local.shape[3] // head_dim
    query_rows = q_local.reshape(2 * block_tok, group_size, head_dim)
    offsets = jnp.arange(block_tok, dtype=jnp.int32)
    doc_bounds = jnp.cumsum(doc_lengths)[:-1]
    page_count = block_tok // PAGE
    slot_count = 4 * page_count
    slot_range = jnp.arange(slot_count, dtype=jnp.int32)
    score_scale = head_dim ** (-0.5)

    def group_positions(owner_ids):
        block_starts = jnp.stack([owner_ids, 2 * axis_count - 1 - owner_ids], axis=1) * block_tok
        return (block_starts[:, :, None] + offsets[None, None, :]).reshape(-1)

    def doc_of(positions):
        return jnp.sum((positions[:, None] >= doc_bounds[None, :]).astype(jnp.int32), axis=1)

    q_pos = group_positions(my_index.reshape(1))
    q_doc = doc_of(q_pos)

    def attend_group(attn_state, key_rows, value_rows, allowed):
        running_max, weight_sum, accum = attn_state
        scores = (
            jnp.einsum("qhd,kd->qhk", query_rows, key_rows, preferred_element_type=jnp.float32)
            * score_scale
        )
        masked = jnp.where(allowed[:, None, :], scores, -1e30)
        new_max = jnp.maximum(running_max, jnp.max(masked, axis=2))
        weights = jnp.where(allowed[:, None, :], jnp.exp(masked - new_max[..., None]), 0.0)
        factor = jnp.exp(running_max - new_max)
        weight_sum = weight_sum * factor + jnp.sum(weights, axis=2)
        update = jnp.einsum(
            "qhk,kd->qhd",
            weights.astype(jnp.bfloat16),
            value_rows,
            preferred_element_type=jnp.float32,
        )
        accum = accum * factor[..., None] + update
        return (new_max, weight_sum, accum)

    def visit_group(attn_state, key_group, value_group, owner_ids):
        key_rows = key_group.reshape(-1, head_dim)
        value_rows = value_group.reshape(-1, head_dim)
        k_pos = group_positions(owner_ids)
        allowed = (k_pos[None, :] <= q_pos[:, None]) & (doc_of(k_pos)[None, :] == q_doc[:, None])
        return attend_group(attn_state, key_rows, value_rows, allowed)

    def place_pages(page_store, key_group, value_group, owner_ids):
        page_rows = jnp.concatenate([key_group, value_group], axis=-1).reshape(
            -1, PAGE * 2 * head_dim
        )
        slot_ids = jnp.take(page_slot, owner_ids, axis=0).reshape(-1) - my_index * slot_count
        selector = (slot_range[:, None] == slot_ids[None, :]).astype(jnp.bfloat16)
        return page_store + jnp.dot(selector, page_rows, preferred_element_type=jnp.float32)

    def fold_groups(step_fn, carried, kv_piece):
        key_piece, value_piece = kv_piece
        piece_len = key_piece.shape[0]
        width = 4
        owner_ids = jnp.arange(piece_len, dtype=jnp.int32).reshape(piece_len // width, width)
        key_groups = key_piece.reshape(piece_len // width, width, 2, block_tok, head_dim)
        value_groups = value_piece.reshape(piece_len // width, width, 2, block_tok, head_dim)

        def visit_one(inner_state, entry_tuple):
            key_group, value_group, owners = entry_tuple
            return (step_fn(inner_state, key_group, value_group, owners), None)

        return lax.scan(visit_one, carried, (key_groups, value_groups, owner_ids))[0]

    empty_store = jnp.zeros((slot_count, PAGE * 2 * head_dim), jnp.float32)
    start_state = (
        jnp.full((2 * block_tok, group_size), -1e30, jnp.float32),
        jnp.zeros((2 * block_tok, group_size), jnp.float32),
        jnp.zeros((2 * block_tok, group_size, head_dim), jnp.float32),
    )
    final_state = fold_groups(
        visit_group,
        start_state,
        (
            lax.all_gather(key_states, "blk", axis=0, tiled=True),
            lax.all_gather(value_states, "blk", axis=0, tiled=True),
        ),
    )
    page_store = fold_groups(
        place_pages,
        empty_store,
        (
            lax.all_gather(key_states, "blk", axis=0, tiled=True),
            lax.all_gather(value_states, "blk", axis=0, tiled=True),
        ),
    )
    running_max, weight_sum, accum = final_state
    attended = (
        (accum / weight_sum[..., None])
        .astype(jnp.bfloat16)
        .reshape(1, 2, block_tok, group_size * head_dim)
    )
    kv_cache = page_store.astype(jnp.bfloat16).reshape(slot_count, 1, PAGE, 2 * head_dim)
    return (attended, kv_cache)


def solution(mesh):
    return jax.shard_map(
        per_device if mesh.shape["blk"] <= 8 else per_device_long,
        mesh=mesh,
        in_specs=(
            P("blk", None, "head", None),
            P("blk", None, None, "head"),
            P("blk", None, None, "head"),
            P(),
            P(),
        ),
        out_specs=(P("blk", None, None, "head"), P("blk", "head", None, None)),
        check_vma=False,
    )
```

```python
import jax
import jax.numpy as jnp
from jax import lax
from jax.experimental import pallas as pl
from jax.experimental.pallas import tpu as pltpu
from jax.sharding import PartitionSpec as P

PAGE = 16
LOG2E = 1.4426950408889634
HEAD_DIM = 128


def spread_queries(q_all, half):
    senders, rows, width = q_all.shape
    sub_tok = rows // 2
    return jnp.concatenate(
        [
            q_all[d, half * sub_tok : (half + 1) * sub_tok, lane : lane + HEAD_DIM]
            for lane in range(0, width, HEAD_DIM)
            for d in range(senders)
        ],
        axis=0,
    )


def attend_part(meta, doc_lengths, q_all, pairs, half, core):
    chips, _, block_tok, _ = pairs.shape
    blk_count = 2 * chips
    my_blk = meta[0]
    queries = spread_queries(q_all, half)
    group = queries.shape[0] // block_tok
    sides = half + 1
    cols = chips * sides * block_tok
    rows = pairs[:, :sides].reshape(cols, 2 * HEAD_DIM)

    col = lax.broadcasted_iota(jnp.int32, (1, cols), 1)
    owner = (my_blk ^ core) ^ (2 * (col // (sides * block_tok)))
    block = owner
    if half == 1:
        block = jnp.where((col // block_tok) % 2 == 1, 2 * blk_count - 1 - owner, owner)
    k_pos = block * block_tok + col % block_tok
    my_block = my_blk if half == 0 else 2 * blk_count - 1 - my_blk
    q_pos = my_block * block_tok + lax.broadcasted_iota(jnp.int32, (block_tok, 1), 0)
    first = jnp.zeros_like(q_pos)
    bound = 0
    for k in range(doc_lengths.shape[0] - 1):
        bound = bound + doc_lengths[k]
        first = jnp.where(q_pos >= bound, bound, first)
    bias = jnp.where((k_pos <= q_pos) & (k_pos >= first), 0.0, -1e30)

    scores = lax.dot_general(
        queries, rows[:, :HEAD_DIM], (((1,), (1,)), ((), ())), preferred_element_type=jnp.float32
    )
    scores = scores.reshape(group, block_tok, cols) * (HEAD_DIM**-0.5 * LOG2E) + bias[None]
    scores = scores.reshape(group * block_tok, cols)
    top = jnp.max(scores, axis=1, keepdims=True)
    weights = jnp.exp2(scores - top)
    total = jnp.sum(weights, axis=1, keepdims=True)
    out = jnp.dot(weights.astype(jnp.bfloat16), rows[:, HEAD_DIM:], preferred_element_type=jnp.float32)
    return top, total, out


def near_kernel(meta, doc_lengths, q_all, near, top_ref, total_ref, out_ref):
    for half in range(2):
        top, total, out = attend_part(meta, doc_lengths, q_all, near, half, 0)
        top_ref[half] = top
        total_ref[half] = total
        out_ref[half] = out


def far_kernel(
    meta, doc_lengths, page_slot, q_all, near, far, top_ref, total_ref, out_ref, attended, kv_cache, inverse, pages, page_sem
):
    chips, _, block_tok, _ = near.shape
    pages_blk = block_tok // PAGE
    slot_count = kv_cache.shape[0]
    my_blk = meta[0]

    for slot in range(slot_count):
        inverse[slot] = -1
    first_slot = my_blk * slot_count
    for pair in range(2 * chips):
        for half in range(2):
            for n in range(pages_blk):
                local = page_slot[half, n, pair] - first_slot
                mine = (local >= 0) & (local < slot_count)
                inverse[jnp.where(mine, local, slot_count)] = (pair * 2 + half) * pages_blk + n
    for slot in range(slot_count):
        page = inverse[slot]
        used = page >= 0
        page = jnp.maximum(page, 0)
        pair = page // (2 * pages_blk)
        half = (page // pages_blk) % 2
        start = pl.multiple_of((page % pages_blk) * PAGE, PAGE)
        away = pair ^ my_blk
        rows = jnp.where(
            away % 2 == 1, far[away // 2, half, pl.ds(start, PAGE), :], near[away // 2, half, pl.ds(start, PAGE), :]
        )
        pages[slot, 0] = jnp.where(used, rows, jnp.zeros_like(rows))
    write = pltpu.make_async_copy(pages, kv_cache, page_sem)
    write.start()

    for half in range(2):
        top, total, out = attend_part(meta, doc_lengths, q_all, far, half, 1)
        best = jnp.maximum(top, top_ref[half])
        here = jnp.exp2(top - best)
        there = jnp.exp2(top_ref[half] - best)
        total = total * here + total_ref[half] * there
        out = ((out * here + out_ref[half] * there) / total).astype(jnp.bfloat16)
        for g in range(out.shape[0] // block_tok):
            attended[0, half, :, g * HEAD_DIM : (g + 1) * HEAD_DIM] = out[g * block_tok : (g + 1) * block_tok]
    write.wait()


def per_device(query_states, key_states, value_states, doc_lengths, page_slot):
    blk_count = lax.axis_size("blk")
    head_count = lax.axis_size("head")
    _, halves, tokens, q_width = query_states.shape
    block_tok = key_states.shape[2]
    width = q_width // head_count
    rows = width // HEAD_DIM * block_tok
    slot_count = 4 * (block_tok // PAGE)
    meta = lax.axis_index("blk").reshape(1).astype(jnp.int32)

    pair = jnp.concatenate([key_states, value_states], axis=3)
    pair, query_states = lax.optimization_barrier((pair, query_states))
    near = [
        lax.ppermute(pair, "blk", [(i, i ^ d) for i in range(blk_count)]) for d in range(2, blk_count, 2)
    ]
    q_flat = query_states.reshape(halves * tokens, q_width)
    q_split = jnp.stack([q_flat[:, h * width : (h + 1) * width] for h in range(head_count)])
    q_all = lax.all_to_all(q_split, "head", split_axis=0, concat_axis=0, tiled=True)
    near, q_all = lax.optimization_barrier((near, q_all))
    near = jnp.concatenate([pair] + near, axis=0)
    far = lax.ppermute(near, "blk", [(i, i ^ 1) for i in range(blk_count)])

    smem = pl.BlockSpec(memory_space=pltpu.SMEM)
    vmem = pl.BlockSpec(memory_space=pltpu.VMEM)
    params = pltpu.CompilerParams(vmem_limit_bytes=32 * 1024 * 1024)
    cost = pl.CostEstimate(flops=150_000_000, bytes_accessed=1_000_000, transcendentals=200_000)
    stats = pl.pallas_call(
        near_kernel,
        out_shape=(
            jax.ShapeDtypeStruct((2, rows, 1), jnp.float32),
            jax.ShapeDtypeStruct((2, rows, 1), jnp.float32),
            jax.ShapeDtypeStruct((2, rows, HEAD_DIM), jnp.float32),
        ),
        in_specs=[smem] * 2 + [vmem] * 2,
        out_specs=(vmem,) * 3,
        compiler_params=params,
        cost_estimate=cost,
    )(meta, doc_lengths, q_all, near)
    return pl.pallas_call(
        far_kernel,
        out_shape=(
            jax.ShapeDtypeStruct((1, 2, block_tok, width), jnp.bfloat16),
            jax.ShapeDtypeStruct((slot_count, 1, PAGE, 2 * HEAD_DIM), jnp.bfloat16),
        ),
        in_specs=[smem] * 3 + [vmem] * 6,
        out_specs=(vmem, pl.BlockSpec(memory_space=pl.ANY)),
        scratch_shapes=[
            pltpu.SMEM((slot_count + 1,), jnp.int32),
            pltpu.VMEM((slot_count, 1, PAGE, 2 * HEAD_DIM), jnp.bfloat16),
            pltpu.SemaphoreType.DMA,
        ],
        compiler_params=params,
        cost_estimate=cost,
    )(meta, doc_lengths, page_slot.transpose(1, 2, 0), q_all, near, far, *stats)


def per_device_long(query_states, key_states, value_states, doc_lengths, page_slot):
    q_local = lax.all_to_all(query_states, "head", split_axis=3, concat_axis=2, tiled=True)
    axis_count = lax.axis_size("blk")
    my_index = lax.axis_index("blk")
    block_tok = q_local.shape[2]
    head_dim = key_states.shape[3]
    group_size = q_local.shape[3] // head_dim
    query_rows = q_local.reshape(2 * block_tok, group_size, head_dim)
    offsets = jnp.arange(block_tok, dtype=jnp.int32)
    doc_bounds = jnp.cumsum(doc_lengths)[:-1]
    page_count = block_tok // PAGE
    slot_count = 4 * page_count
    slot_range = jnp.arange(slot_count, dtype=jnp.int32)
    score_scale = head_dim ** (-0.5)

    def group_positions(owner_ids):
        block_starts = jnp.stack([owner_ids, 2 * axis_count - 1 - owner_ids], axis=1) * block_tok
        return (block_starts[:, :, None] + offsets[None, None, :]).reshape(-1)

    def doc_of(positions):
        return jnp.sum((positions[:, None] >= doc_bounds[None, :]).astype(jnp.int32), axis=1)

    q_pos = group_positions(my_index.reshape(1))
    q_doc = doc_of(q_pos)

    def attend_group(attn_state, key_rows, value_rows, allowed):
        running_max, weight_sum, accum = attn_state
        scores = (
            jnp.einsum("qhd,kd->qhk", query_rows, key_rows, preferred_element_type=jnp.float32)
            * score_scale
        )
        masked = jnp.where(allowed[:, None, :], scores, -1e30)
        new_max = jnp.maximum(running_max, jnp.max(masked, axis=2))
        weights = jnp.where(allowed[:, None, :], jnp.exp(masked - new_max[..., None]), 0.0)
        factor = jnp.exp(running_max - new_max)
        weight_sum = weight_sum * factor + jnp.sum(weights, axis=2)
        update = jnp.einsum(
            "qhk,kd->qhd",
            weights.astype(jnp.bfloat16),
            value_rows,
            preferred_element_type=jnp.float32,
        )
        accum = accum * factor[..., None] + update
        return (new_max, weight_sum, accum)

    def visit_group(attn_state, key_group, value_group, owner_ids):
        key_rows = key_group.reshape(-1, head_dim)
        value_rows = value_group.reshape(-1, head_dim)
        k_pos = group_positions(owner_ids)
        allowed = (k_pos[None, :] <= q_pos[:, None]) & (doc_of(k_pos)[None, :] == q_doc[:, None])
        return attend_group(attn_state, key_rows, value_rows, allowed)

    def place_pages(page_store, key_group, value_group, owner_ids):
        page_rows = jnp.concatenate([key_group, value_group], axis=-1).reshape(
            -1, PAGE * 2 * head_dim
        )
        slot_ids = jnp.take(page_slot, owner_ids, axis=0).reshape(-1) - my_index * slot_count
        selector = (slot_range[:, None] == slot_ids[None, :]).astype(jnp.bfloat16)
        return page_store + jnp.dot(selector, page_rows, preferred_element_type=jnp.float32)

    def fold_groups(step_fn, carried, kv_piece):
        key_piece, value_piece = kv_piece
        piece_len = key_piece.shape[0]
        width = 4
        owner_ids = jnp.arange(piece_len, dtype=jnp.int32).reshape(piece_len // width, width)
        key_groups = key_piece.reshape(piece_len // width, width, 2, block_tok, head_dim)
        value_groups = value_piece.reshape(piece_len // width, width, 2, block_tok, head_dim)

        def visit_one(inner_state, entry_tuple):
            key_group, value_group, owners = entry_tuple
            return (step_fn(inner_state, key_group, value_group, owners), None)

        return lax.scan(visit_one, carried, (key_groups, value_groups, owner_ids))[0]

    empty_store = jnp.zeros((slot_count, PAGE * 2 * head_dim), jnp.float32)
    start_state = (
        jnp.full((2 * block_tok, group_size), -1e30, jnp.float32),
        jnp.zeros((2 * block_tok, group_size), jnp.float32),
        jnp.zeros((2 * block_tok, group_size, head_dim), jnp.float32),
    )
    final_state = fold_groups(
        visit_group,
        start_state,
        (
            lax.all_gather(key_states, "blk", axis=0, tiled=True),
            lax.all_gather(value_states, "blk", axis=0, tiled=True),
        ),
    )
    page_store = fold_groups(
        place_pages,
        empty_store,
        (
            lax.all_gather(key_states, "blk", axis=0, tiled=True),
            lax.all_gather(value_states, "blk", axis=0, tiled=True),
        ),
    )
    running_max, weight_sum, accum = final_state
    attended = (
        (accum / weight_sum[..., None])
        .astype(jnp.bfloat16)
        .reshape(1, 2, block_tok, group_size * head_dim)
    )
    kv_cache = page_store.astype(jnp.bfloat16).reshape(slot_count, 1, PAGE, 2 * head_dim)
    return (attended, kv_cache)


def solution(mesh):
    return jax.shard_map(
        per_device if mesh.shape["blk"] <= 8 else per_device_long,
        mesh=mesh,
        in_specs=(
            P("blk", None, "head", None),
            P("blk", None, None, "head"),
            P("blk", None, None, "head"),
            P(),
            P(),
        ),
        out_specs=(P("blk", None, None, "head"), P("blk", "head", None, None)),
        check_vma=False,
    )
```

```python
import jax
import jax.numpy as jnp
from jax import lax
from jax.experimental import pallas as pl
from jax.experimental.pallas import tpu as pltpu
from jax.sharding import PartitionSpec as P

PAGE = 16
LOG2E = 1.4426950408889634
HEAD_DIM = 128


def spread_queries(q_all, half):
    senders, rows, width = q_all.shape
    sub_tok = rows // 2
    return jnp.concatenate(
        [
            q_all[d, half * sub_tok : (half + 1) * sub_tok, lane : lane + HEAD_DIM]
            for lane in range(0, width, HEAD_DIM)
            for d in range(senders)
        ],
        axis=0,
    )


def key_bias(my_blk, doc_lengths, chips, block_tok, half, core):
    blk_count = 2 * chips
    sides = half + 1
    cols = chips * sides * block_tok
    col = lax.broadcasted_iota(jnp.int32, (1, cols), 1)
    owner = (my_blk ^ core) ^ (2 * (col // (sides * block_tok)))
    block = owner
    if half == 1:
        block = jnp.where((col // block_tok) % 2 == 1, 2 * blk_count - 1 - owner, owner)
    k_pos = block * block_tok + col % block_tok
    my_block = my_blk if half == 0 else 2 * blk_count - 1 - my_blk
    q_pos = my_block * block_tok + lax.broadcasted_iota(jnp.int32, (block_tok, 1), 0)
    first = jnp.zeros_like(q_pos)
    bound = 0
    for k in range(doc_lengths.shape[0] - 1):
        bound = bound + doc_lengths[k]
        first = jnp.where(q_pos >= bound, bound, first)
    return jnp.where((k_pos <= q_pos) & (k_pos >= first), 0.0, -1e30)


def page_targets(my_blk, page_slot, chips, block_tok, slot_count, core):
    pages_blk = block_tok // PAGE
    cols = chips * 2 * block_tok
    col = lax.broadcasted_iota(jnp.int32, (1, cols), 1)
    slots = jnp.zeros((1, cols), jnp.int32)
    for m in range(chips):
        owner = (my_blk ^ core) ^ (2 * m)
        for half in range(2):
            for n in range(pages_blk):
                slot = page_slot[half, n, owner]
                slots = jnp.where(col // PAGE == (m * 2 + half) * pages_blk + n, slot, slots)
    return (slots - my_blk * slot_count) * PAGE + col % PAGE


def place_pages(targets, pairs, slot_count):
    rows = pairs[...].reshape(-1, pairs.shape[-1])
    row = lax.broadcasted_iota(jnp.int32, (slot_count * PAGE, rows.shape[0]), 0)
    chosen = jnp.where(row == targets, 1.0, 0.0).astype(jnp.bfloat16)
    return jnp.dot(chosen, rows, preferred_element_type=jnp.float32)


def score_part(q_all, pairs, half):
    keys = pairs[:, : half + 1].reshape(-1, 2 * HEAD_DIM)[:, :HEAD_DIM]
    return lax.dot_general(
        spread_queries(q_all, half), keys, (((1,), (1,)), ((), ())), preferred_element_type=jnp.float32
    )


def weigh_part(scores, bias, pairs, half):
    values = pairs[:, : half + 1].reshape(-1, 2 * HEAD_DIM)[:, HEAD_DIM:]
    block_tok, cols = bias.shape
    scores = scores.reshape(-1, block_tok, cols) * (HEAD_DIM**-0.5 * LOG2E) + bias[None]
    scores = scores.reshape(-1, cols)
    top = jnp.max(scores, axis=1, keepdims=True)
    weights = jnp.exp2(scores - top)
    total = jnp.sum(weights, axis=1, keepdims=True)
    out = jnp.dot(weights.astype(jnp.bfloat16), values, preferred_element_type=jnp.float32)
    return top, total, out


def near_kernel(
    doc_hbm, slot_hbm, q_all, near, top_ref, total_ref, out_ref, pages_ref, far_bias_a, far_bias_b, far_targets,
    doc_lengths, page_slot, sems,
):
    chips, _, block_tok, _ = near.shape
    slot_count = pages_ref.shape[0] // PAGE
    my_blk = lax.axis_index("blk")
    fetch_doc = pltpu.make_async_copy(doc_hbm, doc_lengths, sems.at[0])
    fetch_slot = pltpu.make_async_copy(slot_hbm, page_slot, sems.at[1])
    fetch_doc.start()
    fetch_slot.start()
    scores = [score_part(q_all, near, half) for half in range(2)]
    fetch_doc.wait()
    fetch_slot.wait()
    for half in range(2):
        bias = key_bias(my_blk, doc_lengths, chips, block_tok, half, 0)
        top, total, out = weigh_part(scores[half], bias, near, half)
        top_ref[half] = top
        total_ref[half] = total
        out_ref[half] = out
    pages_ref[...] = place_pages(
        page_targets(my_blk, page_slot, chips, block_tok, slot_count, 0), near, slot_count
    ).astype(jnp.bfloat16)
    far_bias_a[...] = key_bias(my_blk, doc_lengths, chips, block_tok, 0, 1)
    far_bias_b[...] = key_bias(my_blk, doc_lengths, chips, block_tok, 1, 1)
    far_targets[...] = page_targets(my_blk, page_slot, chips, block_tok, slot_count, 1)


def far_kernel(
    q_all, far, top_ref, total_ref, out_ref, pages_ref, far_bias_a, far_bias_b, far_targets, attended, kv_cache,
    pages, result, sems,
):
    block_tok = far.shape[2]
    slot_count = kv_cache.shape[0]
    moved = place_pages(far_targets[...], far, slot_count) + pages_ref[...].astype(jnp.float32)
    pages[...] = moved.astype(jnp.bfloat16).reshape(pages.shape)
    writes = [pltpu.make_async_copy(pages, kv_cache, sems.at[2])]
    writes[0].start()
    for half in (1, 0):
        bias = (far_bias_a, far_bias_b)[half][...]
        top, total, out = weigh_part(score_part(q_all, far, half), bias, far, half)
        best = jnp.maximum(top, top_ref[half])
        here = jnp.exp2(top - best)
        there = jnp.exp2(top_ref[half] - best)
        total = total * here + total_ref[half] * there
        out = ((out * here + out_ref[half] * there) / total).astype(jnp.bfloat16)
        for g in range(out.shape[0] // block_tok):
            result[half, :, g * HEAD_DIM : (g + 1) * HEAD_DIM] = out[g * block_tok : (g + 1) * block_tok]
        writes.append(pltpu.make_async_copy(result.at[half], attended.at[0, half], sems.at[half]))
        writes[-1].start()
    for write in writes:
        write.wait()


def per_device(query_states, key_states, value_states, doc_lengths, page_slot):
    blk_count = lax.axis_size("blk")
    head_count = lax.axis_size("head")
    _, halves, tokens, q_width = query_states.shape
    block_tok = key_states.shape[2]
    width = q_width // head_count
    rows = width // HEAD_DIM * block_tok
    slot_count = 4 * (block_tok // PAGE)

    pair = jnp.concatenate([key_states, value_states], axis=3)
    near = [
        lax.ppermute(pair, "blk", [(i, i ^ d) for i in range(blk_count)]) for d in range(2, blk_count, 2)
    ]
    q_flat = query_states.reshape(halves * tokens, q_width)
    q_split = jnp.stack([q_flat[:, h * width : (h + 1) * width] for h in range(head_count)])
    near[0], q_split = lax.optimization_barrier((near[0], q_split))
    q_all = lax.all_to_all(q_split, "head", split_axis=0, concat_axis=0, tiled=True)
    near, q_all = lax.optimization_barrier((near, q_all))
    near = jnp.concatenate([pair] + near, axis=0)
    far = lax.ppermute(near, "blk", [(i, i ^ 1) for i in range(blk_count)])

    hbm = pl.BlockSpec(memory_space=pl.ANY)
    vmem = pl.BlockSpec(memory_space=pltpu.VMEM)
    params = pltpu.CompilerParams(vmem_limit_bytes=32 * 1024 * 1024)
    cost = pl.CostEstimate(flops=150_000_000, bytes_accessed=1_000_000, transcendentals=200_000)
    slots = page_slot.transpose(1, 2, 0)
    half_cols = blk_count // 2 * block_tok
    stats = pl.pallas_call(
        near_kernel,
        out_shape=(
            jax.ShapeDtypeStruct((2, rows, 1), jnp.float32),
            jax.ShapeDtypeStruct((2, rows, 1), jnp.float32),
            jax.ShapeDtypeStruct((2, rows, HEAD_DIM), jnp.float32),
            jax.ShapeDtypeStruct((slot_count * PAGE, 2 * HEAD_DIM), jnp.bfloat16),
            jax.ShapeDtypeStruct((block_tok, half_cols), jnp.float32),
            jax.ShapeDtypeStruct((block_tok, 2 * half_cols), jnp.float32),
            jax.ShapeDtypeStruct((1, 2 * half_cols), jnp.int32),
        ),
        in_specs=[hbm] * 2 + [vmem] * 2,
        out_specs=(vmem,) * 7,
        scratch_shapes=[
            pltpu.SMEM(doc_lengths.shape, jnp.int32),
            pltpu.SMEM(slots.shape, jnp.int32),
            pltpu.SemaphoreType.DMA((2,)),
        ],
        compiler_params=params,
        cost_estimate=cost,
    )(doc_lengths, slots, q_all, near)
    return pl.pallas_call(
        far_kernel,
        out_shape=(
            jax.ShapeDtypeStruct((1, 2, block_tok, width), jnp.bfloat16),
            jax.ShapeDtypeStruct((slot_count, 1, PAGE, 2 * HEAD_DIM), jnp.bfloat16),
        ),
        in_specs=[vmem] * 9,
        out_specs=(hbm, hbm),
        scratch_shapes=[
            pltpu.VMEM((slot_count, 1, PAGE, 2 * HEAD_DIM), jnp.bfloat16),
            pltpu.VMEM((2, block_tok, width), jnp.bfloat16),
            pltpu.SemaphoreType.DMA((3,)),
        ],
        compiler_params=params,
        cost_estimate=cost,
    )(q_all, far, *stats)


def per_device_long(query_states, key_states, value_states, doc_lengths, page_slot):
    q_local = lax.all_to_all(query_states, "head", split_axis=3, concat_axis=2, tiled=True)
    axis_count = lax.axis_size("blk")
    my_index = lax.axis_index("blk")
    block_tok = q_local.shape[2]
    head_dim = key_states.shape[3]
    group_size = q_local.shape[3] // head_dim
    query_rows = q_local.reshape(2 * block_tok, group_size, head_dim)
    offsets = jnp.arange(block_tok, dtype=jnp.int32)
    doc_bounds = jnp.cumsum(doc_lengths)[:-1]
    page_count = block_tok // PAGE
    slot_count = 4 * page_count
    slot_range = jnp.arange(slot_count, dtype=jnp.int32)
    score_scale = head_dim ** (-0.5)

    def group_positions(owner_ids):
        block_starts = jnp.stack([owner_ids, 2 * axis_count - 1 - owner_ids], axis=1) * block_tok
        return (block_starts[:, :, None] + offsets[None, None, :]).reshape(-1)

    def doc_of(positions):
        return jnp.sum((positions[:, None] >= doc_bounds[None, :]).astype(jnp.int32), axis=1)

    q_pos = group_positions(my_index.reshape(1))
    q_doc = doc_of(q_pos)

    def attend_group(attn_state, key_rows, value_rows, allowed):
        running_max, weight_sum, accum = attn_state
        scores = (
            jnp.einsum("qhd,kd->qhk", query_rows, key_rows, preferred_element_type=jnp.float32)
            * score_scale
        )
        masked = jnp.where(allowed[:, None, :], scores, -1e30)
        new_max = jnp.maximum(running_max, jnp.max(masked, axis=2))
        weights = jnp.where(allowed[:, None, :], jnp.exp(masked - new_max[..., None]), 0.0)
        factor = jnp.exp(running_max - new_max)
        weight_sum = weight_sum * factor + jnp.sum(weights, axis=2)
        update = jnp.einsum(
            "qhk,kd->qhd",
            weights.astype(jnp.bfloat16),
            value_rows,
            preferred_element_type=jnp.float32,
        )
        accum = accum * factor[..., None] + update
        return (new_max, weight_sum, accum)

    def visit_group(attn_state, key_group, value_group, owner_ids):
        key_rows = key_group.reshape(-1, head_dim)
        value_rows = value_group.reshape(-1, head_dim)
        k_pos = group_positions(owner_ids)
        allowed = (k_pos[None, :] <= q_pos[:, None]) & (doc_of(k_pos)[None, :] == q_doc[:, None])
        return attend_group(attn_state, key_rows, value_rows, allowed)

    def place_pages(page_store, key_group, value_group, owner_ids):
        page_rows = jnp.concatenate([key_group, value_group], axis=-1).reshape(
            -1, PAGE * 2 * head_dim
        )
        slot_ids = jnp.take(page_slot, owner_ids, axis=0).reshape(-1) - my_index * slot_count
        selector = (slot_range[:, None] == slot_ids[None, :]).astype(jnp.bfloat16)
        return page_store + jnp.dot(selector, page_rows, preferred_element_type=jnp.float32)

    def fold_groups(step_fn, carried, kv_piece):
        key_piece, value_piece = kv_piece
        piece_len = key_piece.shape[0]
        width = 4
        owner_ids = jnp.arange(piece_len, dtype=jnp.int32).reshape(piece_len // width, width)
        key_groups = key_piece.reshape(piece_len // width, width, 2, block_tok, head_dim)
        value_groups = value_piece.reshape(piece_len // width, width, 2, block_tok, head_dim)

        def visit_one(inner_state, entry_tuple):
            key_group, value_group, owners = entry_tuple
            return (step_fn(inner_state, key_group, value_group, owners), None)

        return lax.scan(visit_one, carried, (key_groups, value_groups, owner_ids))[0]

    empty_store = jnp.zeros((slot_count, PAGE * 2 * head_dim), jnp.float32)
    start_state = (
        jnp.full((2 * block_tok, group_size), -1e30, jnp.float32),
        jnp.zeros((2 * block_tok, group_size), jnp.float32),
        jnp.zeros((2 * block_tok, group_size, head_dim), jnp.float32),
    )
    final_state = fold_groups(
        visit_group,
        start_state,
        (
            lax.all_gather(key_states, "blk", axis=0, tiled=True),
            lax.all_gather(value_states, "blk", axis=0, tiled=True),
        ),
    )
    page_store = fold_groups(
        place_pages,
        empty_store,
        (
            lax.all_gather(key_states, "blk", axis=0, tiled=True),
            lax.all_gather(value_states, "blk", axis=0, tiled=True),
        ),
    )
    running_max, weight_sum, accum = final_state
    attended = (
        (accum / weight_sum[..., None])
        .astype(jnp.bfloat16)
        .reshape(1, 2, block_tok, group_size * head_dim)
    )
    kv_cache = page_store.astype(jnp.bfloat16).reshape(slot_count, 1, PAGE, 2 * head_dim)
    return (attended, kv_cache)


def solution(mesh):
    return jax.shard_map(
        per_device if mesh.shape["blk"] <= 8 else per_device_long,
        mesh=mesh,
        in_specs=(
            P("blk", None, "head", None),
            P("blk", None, None, "head"),
            P("blk", None, None, "head"),
            P(),
            P(),
        ),
        out_specs=(P("blk", None, None, "head"), P("blk", "head", None, None)),
        check_vma=False,
    )
```

```python
import jax
import jax.numpy as jnp
from jax import lax
from jax.experimental import pallas as pl
from jax.experimental.pallas import tpu as pltpu
from jax.sharding import PartitionSpec as P

PAGE = 16
LOG2E = 1.4426950408889634
HEAD_DIM = 128


def gather_queries(own, across, beside, q_rows):
    my_head = lax.axis_index("head")
    width = beside.shape[-1]
    sub_tok = own.shape[2]
    group = width // HEAD_DIM
    block_tok = q_rows.shape[1] // group
    for half in range(2):
        for g in range(group):
            lane = g * HEAD_DIM
            mine = pl.multiple_of(my_head * width + lane, HEAD_DIM)
            low = pl.multiple_of((my_head % 2) * width + lane, HEAD_DIM)
            parts = (
                own[0, half, :, pl.ds(mine, HEAD_DIM)],
                beside[0, half, :, lane : lane + HEAD_DIM],
                across[0, half, :, pl.ds(low, HEAD_DIM)],
                beside[1, half, :, lane : lane + HEAD_DIM],
            )
            for d, part in enumerate(parts):
                row = pl.multiple_of(g * block_tok + (my_head ^ d) * sub_tok, sub_tok)
                q_rows[half, pl.ds(row, sub_tok), :] = part


def key_bias(my_blk, doc_lengths, chips, block_tok, half, core):
    blk_count = 2 * chips
    sides = half + 1
    cols = chips * sides * block_tok
    col = lax.broadcasted_iota(jnp.int32, (1, cols), 1)
    owner = (my_blk ^ core) ^ (2 * (col // (sides * block_tok)))
    block = owner
    if half == 1:
        block = jnp.where((col // block_tok) % 2 == 1, 2 * blk_count - 1 - owner, owner)
    k_pos = block * block_tok + col % block_tok
    my_block = my_blk if half == 0 else 2 * blk_count - 1 - my_blk
    q_pos = my_block * block_tok + lax.broadcasted_iota(jnp.int32, (block_tok, 1), 0)
    first = jnp.zeros_like(q_pos)
    bound = 0
    for k in range(doc_lengths.shape[0] - 1):
        bound = bound + doc_lengths[k]
        first = jnp.where(q_pos >= bound, bound, first)
    return jnp.where((k_pos <= q_pos) & (k_pos >= first), 0.0, -1e30)


def page_targets(my_blk, page_slot, chips, block_tok, slot_count, core):
    pages_blk = block_tok // PAGE
    cols = chips * 2 * block_tok
    col = lax.broadcasted_iota(jnp.int32, (1, cols), 1)
    slots = jnp.zeros((1, cols), jnp.int32)
    for m in range(chips):
        owner = (my_blk ^ core) ^ (2 * m)
        for half in range(2):
            for n in range(pages_blk):
                slot = page_slot[half, n, owner]
                slots = jnp.where(col // PAGE == (m * 2 + half) * pages_blk + n, slot, slots)
    return (slots - my_blk * slot_count) * PAGE + col % PAGE


def place_pages(targets, pairs, slot_count):
    rows = pairs[...].reshape(-1, pairs.shape[-1])
    row = lax.broadcasted_iota(jnp.int32, (slot_count * PAGE, rows.shape[0]), 0)
    chosen = jnp.where(row == targets, 1.0, 0.0).astype(jnp.bfloat16)
    return jnp.dot(chosen, rows, preferred_element_type=jnp.float32)


def score_part(q_rows, pairs, half):
    keys = pairs[:, : half + 1].reshape(-1, 2 * HEAD_DIM)[:, :HEAD_DIM]
    return lax.dot_general(q_rows[half], keys, (((1,), (1,)), ((), ())), preferred_element_type=jnp.float32)


def weigh_part(scores, bias, pairs, half):
    values = pairs[:, : half + 1].reshape(-1, 2 * HEAD_DIM)[:, HEAD_DIM:]
    block_tok, cols = bias.shape
    scores = scores.reshape(-1, block_tok, cols) * (HEAD_DIM**-0.5 * LOG2E) + bias[None]
    scores = scores.reshape(-1, cols)
    top = jnp.max(scores, axis=1, keepdims=True)
    weights = jnp.exp2(scores - top)
    total = jnp.sum(weights, axis=1, keepdims=True)
    out = jnp.dot(weights.astype(jnp.bfloat16), values, preferred_element_type=jnp.float32)
    return top, total, out


def near_kernel(
    doc_hbm, slot_hbm, own, across, beside, near, q_rows, top_ref, total_ref, out_ref, pages_ref, far_bias_a,
    far_bias_b, far_targets, doc_lengths, page_slot, sems,
):
    chips, _, block_tok, _ = near.shape
    slot_count = pages_ref.shape[0] // PAGE
    my_blk = lax.axis_index("blk")
    fetch_doc = pltpu.make_async_copy(doc_hbm, doc_lengths, sems.at[0])
    fetch_slot = pltpu.make_async_copy(slot_hbm, page_slot, sems.at[1])
    fetch_doc.start()
    fetch_slot.start()
    gather_queries(own, across, beside, q_rows)
    scores = [score_part(q_rows, near, half) for half in range(2)]
    fetch_doc.wait()
    fetch_slot.wait()
    for half in range(2):
        bias = key_bias(my_blk, doc_lengths, chips, block_tok, half, 0)
        top, total, out = weigh_part(scores[half], bias, near, half)
        top_ref[half] = top
        total_ref[half] = total
        out_ref[half] = out
    pages_ref[...] = place_pages(
        page_targets(my_blk, page_slot, chips, block_tok, slot_count, 0), near, slot_count
    ).astype(jnp.bfloat16)
    far_bias_a[...] = key_bias(my_blk, doc_lengths, chips, block_tok, 0, 1)
    far_bias_b[...] = key_bias(my_blk, doc_lengths, chips, block_tok, 1, 1)
    far_targets[...] = page_targets(my_blk, page_slot, chips, block_tok, slot_count, 1)


def far_kernel(
    far, q_rows, top_ref, total_ref, out_ref, pages_ref, far_bias_a, far_bias_b, far_targets, attended, kv_cache,
    pages, result, sems,
):
    block_tok = far.shape[2]
    slot_count = kv_cache.shape[0]
    moved = place_pages(far_targets[...], far, slot_count) + pages_ref[...].astype(jnp.float32)
    pages[...] = moved.astype(jnp.bfloat16).reshape(pages.shape)
    writes = [pltpu.make_async_copy(pages, kv_cache, sems.at[2])]
    writes[0].start()
    for half in (1, 0):
        bias = (far_bias_a, far_bias_b)[half][...]
        top, total, out = weigh_part(score_part(q_rows, far, half), bias, far, half)
        best = jnp.maximum(top, top_ref[half])
        here = jnp.exp2(top - best)
        there = jnp.exp2(top_ref[half] - best)
        total = total * here + total_ref[half] * there
        out = ((out * here + out_ref[half] * there) / total).astype(jnp.bfloat16)
        for g in range(out.shape[0] // block_tok):
            result[half, :, g * HEAD_DIM : (g + 1) * HEAD_DIM] = out[g * block_tok : (g + 1) * block_tok]
        writes.append(pltpu.make_async_copy(result.at[half], attended.at[0, half], sems.at[half]))
        writes[-1].start()
    for write in writes:
        write.wait()


def per_device(query_states, key_states, value_states, doc_lengths, page_slot):
    blk_count = lax.axis_size("blk")
    head_count = lax.axis_size("head")
    q_width = query_states.shape[3]
    block_tok = key_states.shape[2]
    width = q_width // head_count
    rows = width // HEAD_DIM * block_tok
    slot_count = 4 * (block_tok // PAGE)

    pair = jnp.concatenate([key_states, value_states], axis=3)
    near = [
        lax.ppermute(pair, "blk", [(i, i ^ d) for i in range(blk_count)]) for d in range(2, blk_count, 2)
    ]
    my_head = lax.axis_index("head")
    part = lax.dynamic_slice_in_dim(query_states, ((my_head ^ 2) // 2) * 2 * width, 2 * width, axis=3)
    across = lax.ppermute(part, "head", [(i, i ^ 2) for i in range(head_count)])
    beside = jnp.concatenate(
        [
            lax.dynamic_slice_in_dim(query_states, (my_head ^ 1) * width, width, axis=3),
            lax.dynamic_slice_in_dim(across, (1 - my_head % 2) * width, width, axis=3),
        ],
        axis=0,
    )
    near, _ = lax.optimization_barrier((near, beside))
    beside = lax.ppermute(beside, "head", [(i, i ^ 1) for i in range(head_count)])
    near = jnp.concatenate([pair] + near, axis=0)
    far = lax.ppermute(near, "blk", [(i, i ^ 1) for i in range(blk_count)])

    hbm = pl.BlockSpec(memory_space=pl.ANY)
    vmem = pl.BlockSpec(memory_space=pltpu.VMEM)
    params = pltpu.CompilerParams(vmem_limit_bytes=32 * 1024 * 1024)
    cost = pl.CostEstimate(flops=4_000_000_000, bytes_accessed=1_000_000, transcendentals=200_000)
    slots = page_slot.transpose(1, 2, 0)
    half_cols = blk_count // 2 * block_tok
    stats = pl.pallas_call(
        near_kernel,
        out_shape=(
            jax.ShapeDtypeStruct((2, rows, HEAD_DIM), jnp.bfloat16),
            jax.ShapeDtypeStruct((2, rows, 1), jnp.float32),
            jax.ShapeDtypeStruct((2, rows, 1), jnp.float32),
            jax.ShapeDtypeStruct((2, rows, HEAD_DIM), jnp.float32),
            jax.ShapeDtypeStruct((slot_count * PAGE, 2 * HEAD_DIM), jnp.bfloat16),
            jax.ShapeDtypeStruct((block_tok, half_cols), jnp.float32),
            jax.ShapeDtypeStruct((block_tok, 2 * half_cols), jnp.float32),
            jax.ShapeDtypeStruct((1, 2 * half_cols), jnp.int32),
        ),
        in_specs=[hbm] * 2 + [vmem] * 4,
        out_specs=(vmem,) * 8,
        scratch_shapes=[
            pltpu.SMEM(doc_lengths.shape, jnp.int32),
            pltpu.SMEM(slots.shape, jnp.int32),
            pltpu.SemaphoreType.DMA((2,)),
        ],
        compiler_params=params,
        cost_estimate=cost,
    )(doc_lengths, slots, query_states, across, beside, near)
    return pl.pallas_call(
        far_kernel,
        out_shape=(
            jax.ShapeDtypeStruct((1, 2, block_tok, width), jnp.bfloat16),
            jax.ShapeDtypeStruct((slot_count, 1, PAGE, 2 * HEAD_DIM), jnp.bfloat16),
        ),
        in_specs=[vmem] * 9,
        out_specs=(hbm, hbm),
        scratch_shapes=[
            pltpu.VMEM((slot_count, 1, PAGE, 2 * HEAD_DIM), jnp.bfloat16),
            pltpu.VMEM((2, block_tok, width), jnp.bfloat16),
            pltpu.SemaphoreType.DMA((3,)),
        ],
        compiler_params=params,
        cost_estimate=cost,
    )(far, *stats)


def per_device_long(query_states, key_states, value_states, doc_lengths, page_slot):
    q_local = lax.all_to_all(query_states, "head", split_axis=3, concat_axis=2, tiled=True)
    axis_count = lax.axis_size("blk")
    my_index = lax.axis_index("blk")
    block_tok = q_local.shape[2]
    head_dim = key_states.shape[3]
    group_size = q_local.shape[3] // head_dim
    query_rows = q_local.reshape(2 * block_tok, group_size, head_dim)
    offsets = jnp.arange(block_tok, dtype=jnp.int32)
    doc_bounds = jnp.cumsum(doc_lengths)[:-1]
    page_count = block_tok // PAGE
    slot_count = 4 * page_count
    slot_range = jnp.arange(slot_count, dtype=jnp.int32)
    score_scale = head_dim ** (-0.5)

    def group_positions(owner_ids):
        block_starts = jnp.stack([owner_ids, 2 * axis_count - 1 - owner_ids], axis=1) * block_tok
        return (block_starts[:, :, None] + offsets[None, None, :]).reshape(-1)

    def doc_of(positions):
        return jnp.sum((positions[:, None] >= doc_bounds[None, :]).astype(jnp.int32), axis=1)

    q_pos = group_positions(my_index.reshape(1))
    q_doc = doc_of(q_pos)

    def attend_group(attn_state, key_rows, value_rows, allowed):
        running_max, weight_sum, accum = attn_state
        scores = (
            jnp.einsum("qhd,kd->qhk", query_rows, key_rows, preferred_element_type=jnp.float32)
            * score_scale
        )
        masked = jnp.where(allowed[:, None, :], scores, -1e30)
        new_max = jnp.maximum(running_max, jnp.max(masked, axis=2))
        weights = jnp.where(allowed[:, None, :], jnp.exp(masked - new_max[..., None]), 0.0)
        factor = jnp.exp(running_max - new_max)
        weight_sum = weight_sum * factor + jnp.sum(weights, axis=2)
        update = jnp.einsum(
            "qhk,kd->qhd",
            weights.astype(jnp.bfloat16),
            value_rows,
            preferred_element_type=jnp.float32,
        )
        accum = accum * factor[..., None] + update
        return (new_max, weight_sum, accum)

    def visit_group(attn_state, key_group, value_group, owner_ids):
        key_rows = key_group.reshape(-1, head_dim)
        value_rows = value_group.reshape(-1, head_dim)
        k_pos = group_positions(owner_ids)
        allowed = (k_pos[None, :] <= q_pos[:, None]) & (doc_of(k_pos)[None, :] == q_doc[:, None])
        return attend_group(attn_state, key_rows, value_rows, allowed)

    def place_pages(page_store, key_group, value_group, owner_ids):
        page_rows = jnp.concatenate([key_group, value_group], axis=-1).reshape(
            -1, PAGE * 2 * head_dim
        )
        slot_ids = jnp.take(page_slot, owner_ids, axis=0).reshape(-1) - my_index * slot_count
        selector = (slot_range[:, None] == slot_ids[None, :]).astype(jnp.bfloat16)
        return page_store + jnp.dot(selector, page_rows, preferred_element_type=jnp.float32)

    def fold_groups(step_fn, carried, kv_piece):
        key_piece, value_piece = kv_piece
        piece_len = key_piece.shape[0]
        width = 4
        owner_ids = jnp.arange(piece_len, dtype=jnp.int32).reshape(piece_len // width, width)
        key_groups = key_piece.reshape(piece_len // width, width, 2, block_tok, head_dim)
        value_groups = value_piece.reshape(piece_len // width, width, 2, block_tok, head_dim)

        def visit_one(inner_state, entry_tuple):
            key_group, value_group, owners = entry_tuple
            return (step_fn(inner_state, key_group, value_group, owners), None)

        return lax.scan(visit_one, carried, (key_groups, value_groups, owner_ids))[0]

    empty_store = jnp.zeros((slot_count, PAGE * 2 * head_dim), jnp.float32)
    start_state = (
        jnp.full((2 * block_tok, group_size), -1e30, jnp.float32),
        jnp.zeros((2 * block_tok, group_size), jnp.float32),
        jnp.zeros((2 * block_tok, group_size, head_dim), jnp.float32),
    )
    final_state = fold_groups(
        visit_group,
        start_state,
        (
            lax.all_gather(key_states, "blk", axis=0, tiled=True),
            lax.all_gather(value_states, "blk", axis=0, tiled=True),
        ),
    )
    page_store = fold_groups(
        place_pages,
        empty_store,
        (
            lax.all_gather(key_states, "blk", axis=0, tiled=True),
            lax.all_gather(value_states, "blk", axis=0, tiled=True),
        ),
    )
    running_max, weight_sum, accum = final_state
    attended = (
        (accum / weight_sum[..., None])
        .astype(jnp.bfloat16)
        .reshape(1, 2, block_tok, group_size * head_dim)
    )
    kv_cache = page_store.astype(jnp.bfloat16).reshape(slot_count, 1, PAGE, 2 * head_dim)
    return (attended, kv_cache)


def solution(mesh):
    return jax.shard_map(
        per_device if mesh.shape["blk"] <= 8 else per_device_long,
        mesh=mesh,
        in_specs=(
            P("blk", None, "head", None),
            P("blk", None, None, "head"),
            P("blk", None, None, "head"),
            P(),
            P(),
        ),
        out_specs=(P("blk", None, None, "head"), P("blk", "head", None, None)),
        check_vma=False,
    )
```

```python
import jax
import jax.numpy as jnp
from jax import lax
from jax.experimental import pallas as pl
from jax.experimental.pallas import tpu as pltpu
from jax.sharding import PartitionSpec as P

PAGE = 16
LOG2E = 1.4426950408889634
HEAD_DIM = 128


def gather_queries(own, across, beside, q_rows):
    my_head = lax.axis_index("head")
    width = beside.shape[-1]
    sub_tok = own.shape[2]
    group = width // HEAD_DIM
    block_tok = q_rows.shape[1] // group
    for half in range(2):
        for g in range(group):
            lane = g * HEAD_DIM
            mine = pl.multiple_of(my_head * width + lane, HEAD_DIM)
            low = pl.multiple_of((my_head % 2) * width + lane, HEAD_DIM)
            parts = (
                own[0, half, :, pl.ds(mine, HEAD_DIM)],
                beside[0, half, :, lane : lane + HEAD_DIM],
                across[0, half, :, pl.ds(low, HEAD_DIM)],
                beside[1, half, :, lane : lane + HEAD_DIM],
            )
            for d, part in enumerate(parts):
                row = pl.multiple_of(g * block_tok + (my_head ^ d) * sub_tok, sub_tok)
                q_rows[half, pl.ds(row, sub_tok), :] = part


def key_bias(my_blk, doc_lengths, chips, block_tok, half, core):
    blk_count = 2 * chips
    sides = half + 1
    cols = chips * sides * block_tok
    col = lax.broadcasted_iota(jnp.int32, (1, cols), 1)
    owner = (my_blk ^ core) ^ (2 * (col // (sides * block_tok)))
    block = owner
    if half == 1:
        block = jnp.where((col // block_tok) % 2 == 1, 2 * blk_count - 1 - owner, owner)
    k_pos = block * block_tok + col % block_tok
    my_block = my_blk if half == 0 else 2 * blk_count - 1 - my_blk
    q_pos = my_block * block_tok + lax.broadcasted_iota(jnp.int32, (block_tok, 1), 0)
    first = jnp.zeros_like(q_pos)
    bound = 0
    for k in range(doc_lengths.shape[0] - 1):
        bound = bound + doc_lengths[k]
        first = jnp.where(q_pos >= bound, bound, first)
    return jnp.where((k_pos <= q_pos) & (k_pos >= first), 0.0, -1e30)


def page_targets(my_blk, page_slot, chips, block_tok, slot_count, core):
    pages_blk = block_tok // PAGE
    cols = chips * 2 * block_tok
    col = lax.broadcasted_iota(jnp.int32, (1, cols), 1)
    slots = jnp.zeros((1, cols), jnp.int32)
    for m in range(chips):
        owner = (my_blk ^ core) ^ (2 * m)
        for half in range(2):
            for n in range(pages_blk):
                slot = page_slot[half, n, owner]
                slots = jnp.where(col // PAGE == (m * 2 + half) * pages_blk + n, slot, slots)
    return (slots - my_blk * slot_count) * PAGE + col % PAGE


def place_pages(targets, pairs, slot_count):
    rows = pairs[...].reshape(-1, pairs.shape[-1])
    row = lax.broadcasted_iota(jnp.int32, (slot_count * PAGE, rows.shape[0]), 0)
    chosen = jnp.where(row == targets, 1.0, 0.0).astype(jnp.bfloat16)
    return jnp.dot(chosen, rows, preferred_element_type=jnp.float32)


def score_part(q_rows, pairs, half):
    keys = pairs[:, : half + 1].reshape(-1, 2 * HEAD_DIM)[:, :HEAD_DIM]
    return lax.dot_general(q_rows[half], keys, (((1,), (1,)), ((), ())), preferred_element_type=jnp.float32)


def weigh_part(scores, bias, pairs, half):
    values = pairs[:, : half + 1].reshape(-1, 2 * HEAD_DIM)[:, HEAD_DIM:]
    block_tok, cols = bias.shape
    scores = scores.reshape(-1, block_tok, cols) * (HEAD_DIM**-0.5 * LOG2E) + bias[None]
    scores = scores.reshape(-1, cols)
    top = jnp.max(scores, axis=1, keepdims=True)
    weights = jnp.exp2(scores - top)
    total = jnp.sum(weights, axis=1, keepdims=True)
    out = jnp.dot(weights.astype(jnp.bfloat16), values, preferred_element_type=jnp.float32)
    return top, total, out


def near_kernel(
    doc_hbm, slot_hbm, own, across, beside, near, q_rows, top_ref, total_ref, out_ref, pages_ref, far_bias_a,
    far_bias_b, far_targets, doc_lengths, page_slot, sems,
):
    chips, _, block_tok, _ = near.shape
    slot_count = pages_ref.shape[0] // PAGE
    my_blk = lax.axis_index("blk")
    fetch_doc = pltpu.make_async_copy(doc_hbm, doc_lengths, sems.at[0])
    fetch_slot = pltpu.make_async_copy(slot_hbm, page_slot, sems.at[1])
    fetch_doc.start()
    fetch_slot.start()
    gather_queries(own, across, beside, q_rows)
    scores = [score_part(q_rows, near, half) for half in range(2)]
    fetch_doc.wait()
    fetch_slot.wait()
    for half in range(2):
        bias = key_bias(my_blk, doc_lengths, chips, block_tok, half, 0)
        top, total, out = weigh_part(scores[half], bias, near, half)
        top_ref[half] = top
        total_ref[half] = total
        out_ref[half] = out
    pages_ref[...] = place_pages(
        page_targets(my_blk, page_slot, chips, block_tok, slot_count, 0), near, slot_count
    ).astype(jnp.bfloat16)
    far_bias_a[...] = key_bias(my_blk, doc_lengths, chips, block_tok, 0, 1)
    far_bias_b[...] = key_bias(my_blk, doc_lengths, chips, block_tok, 1, 1)
    far_targets[...] = page_targets(my_blk, page_slot, chips, block_tok, slot_count, 1)


def far_kernel(
    far, q_rows, top_ref, total_ref, out_ref, pages_ref, far_bias_a, far_bias_b, far_targets, attended, kv_cache,
    pages, result, sems,
):
    block_tok = far.shape[2]
    slot_count = kv_cache.shape[0]
    moved = place_pages(far_targets[...], far, slot_count) + pages_ref[...].astype(jnp.float32)
    pages[...] = moved.astype(jnp.bfloat16).reshape(pages.shape)
    writes = [pltpu.make_async_copy(pages, kv_cache, sems.at[2])]
    writes[0].start()
    for half in (1, 0):
        bias = (far_bias_a, far_bias_b)[half][...]
        top, total, out = weigh_part(score_part(q_rows, far, half), bias, far, half)
        best = jnp.maximum(top, top_ref[half])
        here = jnp.exp2(top - best)
        there = jnp.exp2(top_ref[half] - best)
        total = total * here + total_ref[half] * there
        out = ((out * here + out_ref[half] * there) / total).astype(jnp.bfloat16)
        for g in range(out.shape[0] // block_tok):
            result[half, :, g * HEAD_DIM : (g + 1) * HEAD_DIM] = out[g * block_tok : (g + 1) * block_tok]
        writes.append(pltpu.make_async_copy(result.at[half], attended.at[0, half], sems.at[half]))
        writes[-1].start()
    for write in writes:
        write.wait()


def per_device(query_states, key_states, value_states, doc_lengths, page_slot):
    blk_count = lax.axis_size("blk")
    head_count = lax.axis_size("head")
    q_width = query_states.shape[3]
    block_tok = key_states.shape[2]
    width = q_width // head_count
    rows = width // HEAD_DIM * block_tok
    slot_count = 4 * (block_tok // PAGE)

    my_head = lax.axis_index("head")
    part = lax.dynamic_slice_in_dim(query_states, ((my_head ^ 2) // 2) * 2 * width, 2 * width, axis=3)
    across = lax.ppermute(part, "head", [(i, i ^ 2) for i in range(head_count)])
    pair = jnp.concatenate([key_states, value_states], axis=3)
    pair, _ = lax.optimization_barrier((pair, part))
    near = [
        lax.ppermute(pair, "blk", [(i, i ^ d) for i in range(blk_count)]) for d in range(2, blk_count, 2)
    ]
    beside = jnp.concatenate(
        [
            lax.dynamic_slice_in_dim(query_states, (my_head ^ 1) * width, width, axis=3),
            lax.dynamic_slice_in_dim(across, (1 - my_head % 2) * width, width, axis=3),
        ],
        axis=0,
    )
    near = lax.optimization_barrier((near[::-1], beside))[0][::-1]
    beside = lax.ppermute(beside, "head", [(i, i ^ 1) for i in range(head_count)])
    near = jnp.concatenate([pair] + near, axis=0)
    far = lax.ppermute(near, "blk", [(i, i ^ 1) for i in range(blk_count)])

    hbm = pl.BlockSpec(memory_space=pl.ANY)
    vmem = pl.BlockSpec(memory_space=pltpu.VMEM)
    params = pltpu.CompilerParams(vmem_limit_bytes=32 * 1024 * 1024)
    cost = pl.CostEstimate(flops=4_000_000_000, bytes_accessed=1_000_000, transcendentals=200_000)
    slots = page_slot.transpose(1, 2, 0)
    half_cols = blk_count // 2 * block_tok
    stats = pl.pallas_call(
        near_kernel,
        out_shape=(
            jax.ShapeDtypeStruct((2, rows, HEAD_DIM), jnp.bfloat16),
            jax.ShapeDtypeStruct((2, rows, 1), jnp.float32),
            jax.ShapeDtypeStruct((2, rows, 1), jnp.float32),
            jax.ShapeDtypeStruct((2, rows, HEAD_DIM), jnp.float32),
            jax.ShapeDtypeStruct((slot_count * PAGE, 2 * HEAD_DIM), jnp.bfloat16),
            jax.ShapeDtypeStruct((block_tok, half_cols), jnp.float32),
            jax.ShapeDtypeStruct((block_tok, 2 * half_cols), jnp.float32),
            jax.ShapeDtypeStruct((1, 2 * half_cols), jnp.int32),
        ),
        in_specs=[hbm] * 2 + [vmem] * 4,
        out_specs=(vmem,) * 8,
        scratch_shapes=[
            pltpu.SMEM(doc_lengths.shape, jnp.int32),
            pltpu.SMEM(slots.shape, jnp.int32),
            pltpu.SemaphoreType.DMA((2,)),
        ],
        compiler_params=params,
        cost_estimate=cost,
    )(doc_lengths, slots, query_states, across, beside, near)
    return pl.pallas_call(
        far_kernel,
        out_shape=(
            jax.ShapeDtypeStruct((1, 2, block_tok, width), jnp.bfloat16),
            jax.ShapeDtypeStruct((slot_count, 1, PAGE, 2 * HEAD_DIM), jnp.bfloat16),
        ),
        in_specs=[vmem] * 9,
        out_specs=(hbm, hbm),
        scratch_shapes=[
            pltpu.VMEM((slot_count, 1, PAGE, 2 * HEAD_DIM), jnp.bfloat16),
            pltpu.VMEM((2, block_tok, width), jnp.bfloat16),
            pltpu.SemaphoreType.DMA((3,)),
        ],
        compiler_params=params,
        cost_estimate=cost,
    )(far, *stats)


def per_device_long(query_states, key_states, value_states, doc_lengths, page_slot):
    q_local = lax.all_to_all(query_states, "head", split_axis=3, concat_axis=2, tiled=True)
    axis_count = lax.axis_size("blk")
    my_index = lax.axis_index("blk")
    block_tok = q_local.shape[2]
    head_dim = key_states.shape[3]
    group_size = q_local.shape[3] // head_dim
    query_rows = q_local.reshape(2 * block_tok, group_size, head_dim)
    offsets = jnp.arange(block_tok, dtype=jnp.int32)
    doc_bounds = jnp.cumsum(doc_lengths)[:-1]
    page_count = block_tok // PAGE
    slot_count = 4 * page_count
    slot_range = jnp.arange(slot_count, dtype=jnp.int32)
    score_scale = head_dim ** (-0.5)

    def group_positions(owner_ids):
        block_starts = jnp.stack([owner_ids, 2 * axis_count - 1 - owner_ids], axis=1) * block_tok
        return (block_starts[:, :, None] + offsets[None, None, :]).reshape(-1)

    def doc_of(positions):
        return jnp.sum((positions[:, None] >= doc_bounds[None, :]).astype(jnp.int32), axis=1)

    q_pos = group_positions(my_index.reshape(1))
    q_doc = doc_of(q_pos)

    def attend_group(attn_state, key_rows, value_rows, allowed):
        running_max, weight_sum, accum = attn_state
        scores = (
            jnp.einsum("qhd,kd->qhk", query_rows, key_rows, preferred_element_type=jnp.float32)
            * score_scale
        )
        masked = jnp.where(allowed[:, None, :], scores, -1e30)
        new_max = jnp.maximum(running_max, jnp.max(masked, axis=2))
        weights = jnp.where(allowed[:, None, :], jnp.exp(masked - new_max[..., None]), 0.0)
        factor = jnp.exp(running_max - new_max)
        weight_sum = weight_sum * factor + jnp.sum(weights, axis=2)
        update = jnp.einsum(
            "qhk,kd->qhd",
            weights.astype(jnp.bfloat16),
            value_rows,
            preferred_element_type=jnp.float32,
        )
        accum = accum * factor[..., None] + update
        return (new_max, weight_sum, accum)

    def visit_group(attn_state, key_group, value_group, owner_ids):
        key_rows = key_group.reshape(-1, head_dim)
        value_rows = value_group.reshape(-1, head_dim)
        k_pos = group_positions(owner_ids)
        allowed = (k_pos[None, :] <= q_pos[:, None]) & (doc_of(k_pos)[None, :] == q_doc[:, None])
        return attend_group(attn_state, key_rows, value_rows, allowed)

    def place_pages(page_store, key_group, value_group, owner_ids):
        page_rows = jnp.concatenate([key_group, value_group], axis=-1).reshape(
            -1, PAGE * 2 * head_dim
        )
        slot_ids = jnp.take(page_slot, owner_ids, axis=0).reshape(-1) - my_index * slot_count
        selector = (slot_range[:, None] == slot_ids[None, :]).astype(jnp.bfloat16)
        return page_store + jnp.dot(selector, page_rows, preferred_element_type=jnp.float32)

    def fold_groups(step_fn, carried, kv_piece):
        key_piece, value_piece = kv_piece
        piece_len = key_piece.shape[0]
        width = 4
        owner_ids = jnp.arange(piece_len, dtype=jnp.int32).reshape(piece_len // width, width)
        key_groups = key_piece.reshape(piece_len // width, width, 2, block_tok, head_dim)
        value_groups = value_piece.reshape(piece_len // width, width, 2, block_tok, head_dim)

        def visit_one(inner_state, entry_tuple):
            key_group, value_group, owners = entry_tuple
            return (step_fn(inner_state, key_group, value_group, owners), None)

        return lax.scan(visit_one, carried, (key_groups, value_groups, owner_ids))[0]

    empty_store = jnp.zeros((slot_count, PAGE * 2 * head_dim), jnp.float32)
    start_state = (
        jnp.full((2 * block_tok, group_size), -1e30, jnp.float32),
        jnp.zeros((2 * block_tok, group_size), jnp.float32),
        jnp.zeros((2 * block_tok, group_size, head_dim), jnp.float32),
    )
    final_state = fold_groups(
        visit_group,
        start_state,
        (
            lax.all_gather(key_states, "blk", axis=0, tiled=True),
            lax.all_gather(value_states, "blk", axis=0, tiled=True),
        ),
    )
    page_store = fold_groups(
        place_pages,
        empty_store,
        (
            lax.all_gather(key_states, "blk", axis=0, tiled=True),
            lax.all_gather(value_states, "blk", axis=0, tiled=True),
        ),
    )
    running_max, weight_sum, accum = final_state
    attended = (
        (accum / weight_sum[..., None])
        .astype(jnp.bfloat16)
        .reshape(1, 2, block_tok, group_size * head_dim)
    )
    kv_cache = page_store.astype(jnp.bfloat16).reshape(slot_count, 1, PAGE, 2 * head_dim)
    return (attended, kv_cache)


def solution(mesh):
    return jax.shard_map(
        per_device if mesh.shape["blk"] <= 8 else per_device_long,
        mesh=mesh,
        in_specs=(
            P("blk", None, "head", None),
            P("blk", None, None, "head"),
            P("blk", None, None, "head"),
            P(),
            P(),
        ),
        out_specs=(P("blk", None, None, "head"), P("blk", "head", None, None)),
        check_vma=False,
    )
```

```python
import jax
import jax.numpy as jnp
from jax import lax
from jax.experimental import pallas as pl
from jax.experimental.pallas import tpu as pltpu
from jax.sharding import PartitionSpec as P

PAGE = 16
LOG2E = 1.4426950408889634
HEAD_DIM = 128
LANES = 128


def gather_queries(own, across, beside, q_rows):
    my_head = lax.axis_index("head")
    width = beside.shape[-1]
    sub_tok = own.shape[2]
    group = width // HEAD_DIM
    block_tok = q_rows.shape[1] // group
    for half in range(2):
        for g in range(group):
            lane = g * HEAD_DIM
            mine = pl.multiple_of(my_head * width + lane, HEAD_DIM)
            low = pl.multiple_of((my_head % 2) * width + lane, HEAD_DIM)
            parts = (
                own[0, half, :, pl.ds(mine, HEAD_DIM)],
                beside[0, half, :, lane : lane + HEAD_DIM],
                across[0, half, :, pl.ds(low, HEAD_DIM)],
                beside[1, half, :, lane : lane + HEAD_DIM],
            )
            for d, part in enumerate(parts):
                row = pl.multiple_of(g * block_tok + (my_head ^ d) * sub_tok, sub_tok)
                q_rows[half, pl.ds(row, sub_tok), :] = part


def key_bias(my_blk, doc_lengths, chips, block_tok, half, core):
    blk_count = 2 * chips
    shape = (block_tok, LANES)
    my_block = my_blk if half == 0 else 2 * blk_count - 1 - my_blk
    q_pos = my_block * block_tok + lax.broadcasted_iota(jnp.int32, (1, LANES), 1) % block_tok
    first = jnp.zeros_like(q_pos)
    bound = 0
    for k in range(doc_lengths.shape[0] - 1):
        bound = bound + doc_lengths[k]
        first = jnp.where(q_pos >= bound, bound, first)
    row = lax.broadcasted_iota(jnp.int32, shape, 0)
    parts = []
    for m in range(chips):
        owner = (my_blk ^ core) ^ (2 * m)
        for side in range(half + 1):
            start = (owner if side == 0 else 2 * blk_count - 1 - owner) * block_tok
            parts.append(jnp.where((row <= q_pos - start) & (row >= first - start), 0.0, -1e30))
    return jnp.concatenate(parts, axis=0)


def page_targets(my_blk, page_slot, chips, block_tok, slot_count, core):
    pages_blk = block_tok // PAGE
    col = lax.broadcasted_iota(jnp.int32, (1, 2 * block_tok), 1)
    parts = []
    for m in range(chips):
        owner = (my_blk ^ core) ^ (2 * m)
        slots = jnp.zeros_like(col)
        for half in range(2):
            for n in range(pages_blk):
                slots = jnp.where(col // PAGE == half * pages_blk + n, page_slot[half, n, owner], slots)
        parts.append((slots - my_blk * slot_count) * PAGE + col % PAGE)
    return jnp.concatenate(parts, axis=1)


def place_pages(targets, pairs, slot_count):
    rows = pairs[...].reshape(-1, pairs.shape[-1])
    row = lax.broadcasted_iota(jnp.int32, (slot_count * PAGE, rows.shape[0]), 0)
    chosen = jnp.where(row == targets, 1.0, 0.0).astype(jnp.bfloat16)
    return jnp.dot(chosen, rows, preferred_element_type=jnp.float32)


def score_part(q_rows, pairs, half):
    keys = pairs[:, : half + 1].reshape(-1, 2 * HEAD_DIM)[:, :HEAD_DIM]
    return lax.dot_general(keys, q_rows[half], (((1,), (1,)), ((), ())), preferred_element_type=jnp.float32)


def weigh_part(scores, bias, pairs, half):
    values = pairs[:, : half + 1].reshape(-1, 2 * HEAD_DIM)[:, HEAD_DIM:]
    bias = jnp.concatenate([bias] * (scores.shape[1] // LANES), axis=1)
    scores = scores * (HEAD_DIM**-0.5 * LOG2E) + bias
    top = jnp.max(scores, axis=0, keepdims=True)
    weights = jnp.exp2(scores - top)
    total = jnp.sum(weights, axis=0, keepdims=True)
    out = lax.dot_general(
        values, weights.astype(jnp.bfloat16), (((0,), (0,)), ((), ())), preferred_element_type=jnp.float32
    )
    return top, total, out


def near_kernel(
    doc_hbm, slot_hbm, own, across, beside, near, q_rows, top_ref, total_ref, out_ref, pages_ref, far_bias_a,
    far_bias_b, far_targets, doc_lengths, page_slot, sems,
):
    chips, _, block_tok, _ = near.shape
    slot_count = pages_ref.shape[0] // PAGE
    my_blk = lax.axis_index("blk")
    fetch_doc = pltpu.make_async_copy(doc_hbm, doc_lengths, sems.at[0])
    fetch_slot = pltpu.make_async_copy(slot_hbm, page_slot, sems.at[1])
    fetch_doc.start()
    fetch_slot.start()
    gather_queries(own, across, beside, q_rows)
    scores = [score_part(q_rows, near, half) for half in range(2)]
    fetch_doc.wait()
    fetch_slot.wait()
    for half in range(2):
        bias = key_bias(my_blk, doc_lengths, chips, block_tok, half, 0)
        top, total, out = weigh_part(scores[half], bias, near, half)
        top_ref[half] = top
        total_ref[half] = total
        out_ref[half] = out
    pages_ref[...] = place_pages(
        page_targets(my_blk, page_slot, chips, block_tok, slot_count, 0), near, slot_count
    ).astype(jnp.bfloat16)
    far_bias_a[...] = key_bias(my_blk, doc_lengths, chips, block_tok, 0, 1)
    far_bias_b[...] = key_bias(my_blk, doc_lengths, chips, block_tok, 1, 1)
    far_targets[...] = page_targets(my_blk, page_slot, chips, block_tok, slot_count, 1)


def far_kernel(
    far, q_rows, top_ref, total_ref, out_ref, pages_ref, far_bias_a, far_bias_b, far_targets, attended, kv_cache,
    pages, result, sems,
):
    block_tok = far.shape[2]
    slot_count = kv_cache.shape[0]
    moved = place_pages(far_targets[...], far, slot_count) + pages_ref[...].astype(jnp.float32)
    pages[...] = moved.astype(jnp.bfloat16).reshape(pages.shape)
    writes = [pltpu.make_async_copy(pages, kv_cache, sems.at[2])]
    writes[0].start()
    for half in (1, 0):
        bias = (far_bias_a, far_bias_b)[half][...]
        top, total, out = weigh_part(score_part(q_rows, far, half), bias, far, half)
        best = jnp.maximum(top, top_ref[half])
        here = jnp.exp2(top - best)
        there = jnp.exp2(top_ref[half] - best)
        inverse = 1.0 / (total * here + total_ref[half] * there)
        out = (out * (here * inverse) + out_ref[half] * (there * inverse)).T.astype(jnp.bfloat16)
        for g in range(out.shape[0] // block_tok):
            result[half, :, g * HEAD_DIM : (g + 1) * HEAD_DIM] = out[g * block_tok : (g + 1) * block_tok]
        writes.append(pltpu.make_async_copy(result.at[half], attended.at[0, half], sems.at[half]))
        writes[-1].start()
    for write in writes:
        write.wait()


def per_device(query_states, key_states, value_states, doc_lengths, page_slot):
    blk_count = lax.axis_size("blk")
    head_count = lax.axis_size("head")
    q_width = query_states.shape[3]
    block_tok = key_states.shape[2]
    width = q_width // head_count
    rows = width // HEAD_DIM * block_tok
    slot_count = 4 * (block_tok // PAGE)

    my_head = lax.axis_index("head")
    part = lax.dynamic_slice_in_dim(query_states, ((my_head ^ 2) // 2) * 2 * width, 2 * width, axis=3)
    across = lax.ppermute(part, "head", [(i, i ^ 2) for i in range(head_count)])
    pair = jnp.concatenate([key_states, value_states], axis=3)
    pair, _ = lax.optimization_barrier((pair, part))
    near = [
        lax.ppermute(pair, "blk", [(i, i ^ d) for i in range(blk_count)]) for d in range(2, blk_count, 2)
    ]
    beside = jnp.concatenate(
        [
            lax.dynamic_slice_in_dim(query_states, (my_head ^ 1) * width, width, axis=3),
            lax.dynamic_slice_in_dim(across, (1 - my_head % 2) * width, width, axis=3),
        ],
        axis=0,
    )
    near = lax.optimization_barrier((near[::-1], beside))[0][::-1]
    beside = lax.ppermute(beside, "head", [(i, i ^ 1) for i in range(head_count)])
    near = jnp.concatenate([pair] + near, axis=0)
    far = lax.ppermute(near, "blk", [(i, i ^ 1) for i in range(blk_count)])

    hbm = pl.BlockSpec(memory_space=pl.ANY)
    vmem = pl.BlockSpec(memory_space=pltpu.VMEM)
    params = pltpu.CompilerParams(vmem_limit_bytes=32 * 1024 * 1024)
    cost = pl.CostEstimate(flops=4_000_000_000, bytes_accessed=1_000_000, transcendentals=200_000)
    slots = page_slot.transpose(1, 2, 0)
    half_cols = blk_count // 2 * block_tok
    stats = pl.pallas_call(
        near_kernel,
        out_shape=(
            jax.ShapeDtypeStruct((2, rows, HEAD_DIM), jnp.bfloat16),
            jax.ShapeDtypeStruct((2, 1, rows), jnp.float32),
            jax.ShapeDtypeStruct((2, 1, rows), jnp.float32),
            jax.ShapeDtypeStruct((2, HEAD_DIM, rows), jnp.float32),
            jax.ShapeDtypeStruct((slot_count * PAGE, 2 * HEAD_DIM), jnp.bfloat16),
            jax.ShapeDtypeStruct((half_cols, LANES), jnp.float32),
            jax.ShapeDtypeStruct((2 * half_cols, LANES), jnp.float32),
            jax.ShapeDtypeStruct((1, 2 * half_cols), jnp.int32),
        ),
        in_specs=[hbm] * 2 + [vmem] * 4,
        out_specs=(vmem,) * 8,
        scratch_shapes=[
            pltpu.SMEM(doc_lengths.shape, jnp.int32),
            pltpu.SMEM(slots.shape, jnp.int32),
            pltpu.SemaphoreType.DMA((2,)),
        ],
        compiler_params=params,
        cost_estimate=cost,
    )(doc_lengths, slots, query_states, across, beside, near)
    return pl.pallas_call(
        far_kernel,
        out_shape=(
            jax.ShapeDtypeStruct((1, 2, block_tok, width), jnp.bfloat16),
            jax.ShapeDtypeStruct((slot_count, 1, PAGE, 2 * HEAD_DIM), jnp.bfloat16),
        ),
        in_specs=[vmem] * 9,
        out_specs=(hbm, hbm),
        scratch_shapes=[
            pltpu.VMEM((slot_count, 1, PAGE, 2 * HEAD_DIM), jnp.bfloat16),
            pltpu.VMEM((2, block_tok, width), jnp.bfloat16),
            pltpu.SemaphoreType.DMA((3,)),
        ],
        compiler_params=params,
        cost_estimate=cost,
    )(far, *stats)


def per_device_long(query_states, key_states, value_states, doc_lengths, page_slot):
    q_local = lax.all_to_all(query_states, "head", split_axis=3, concat_axis=2, tiled=True)
    axis_count = lax.axis_size("blk")
    my_index = lax.axis_index("blk")
    block_tok = q_local.shape[2]
    head_dim = key_states.shape[3]
    group_size = q_local.shape[3] // head_dim
    query_rows = q_local.reshape(2 * block_tok, group_size, head_dim)
    offsets = jnp.arange(block_tok, dtype=jnp.int32)
    doc_bounds = jnp.cumsum(doc_lengths)[:-1]
    page_count = block_tok // PAGE
    slot_count = 4 * page_count
    slot_range = jnp.arange(slot_count, dtype=jnp.int32)
    score_scale = head_dim ** (-0.5)

    def group_positions(owner_ids):
        block_starts = jnp.stack([owner_ids, 2 * axis_count - 1 - owner_ids], axis=1) * block_tok
        return (block_starts[:, :, None] + offsets[None, None, :]).reshape(-1)

    def doc_of(positions):
        return jnp.sum((positions[:, None] >= doc_bounds[None, :]).astype(jnp.int32), axis=1)

    q_pos = group_positions(my_index.reshape(1))
    q_doc = doc_of(q_pos)

    def attend_group(attn_state, key_rows, value_rows, allowed):
        running_max, weight_sum, accum = attn_state
        scores = (
            jnp.einsum("qhd,kd->qhk", query_rows, key_rows, preferred_element_type=jnp.float32)
            * score_scale
        )
        masked = jnp.where(allowed[:, None, :], scores, -1e30)
        new_max = jnp.maximum(running_max, jnp.max(masked, axis=2))
        weights = jnp.where(allowed[:, None, :], jnp.exp(masked - new_max[..., None]), 0.0)
        factor = jnp.exp(running_max - new_max)
        weight_sum = weight_sum * factor + jnp.sum(weights, axis=2)
        update = jnp.einsum(
            "qhk,kd->qhd",
            weights.astype(jnp.bfloat16),
            value_rows,
            preferred_element_type=jnp.float32,
        )
        accum = accum * factor[..., None] + update
        return (new_max, weight_sum, accum)

    def visit_group(attn_state, key_group, value_group, owner_ids):
        key_rows = key_group.reshape(-1, head_dim)
        value_rows = value_group.reshape(-1, head_dim)
        k_pos = group_positions(owner_ids)
        allowed = (k_pos[None, :] <= q_pos[:, None]) & (doc_of(k_pos)[None, :] == q_doc[:, None])
        return attend_group(attn_state, key_rows, value_rows, allowed)

    def place_pages(page_store, key_group, value_group, owner_ids):
        page_rows = jnp.concatenate([key_group, value_group], axis=-1).reshape(
            -1, PAGE * 2 * head_dim
        )
        slot_ids = jnp.take(page_slot, owner_ids, axis=0).reshape(-1) - my_index * slot_count
        selector = (slot_range[:, None] == slot_ids[None, :]).astype(jnp.bfloat16)
        return page_store + jnp.dot(selector, page_rows, preferred_element_type=jnp.float32)

    def fold_groups(step_fn, carried, kv_piece):
        key_piece, value_piece = kv_piece
        piece_len = key_piece.shape[0]
        width = 4
        owner_ids = jnp.arange(piece_len, dtype=jnp.int32).reshape(piece_len // width, width)
        key_groups = key_piece.reshape(piece_len // width, width, 2, block_tok, head_dim)
        value_groups = value_piece.reshape(piece_len // width, width, 2, block_tok, head_dim)

        def visit_one(inner_state, entry_tuple):
            key_group, value_group, owners = entry_tuple
            return (step_fn(inner_state, key_group, value_group, owners), None)

        return lax.scan(visit_one, carried, (key_groups, value_groups, owner_ids))[0]

    empty_store = jnp.zeros((slot_count, PAGE * 2 * head_dim), jnp.float32)
    start_state = (
        jnp.full((2 * block_tok, group_size), -1e30, jnp.float32),
        jnp.zeros((2 * block_tok, group_size), jnp.float32),
        jnp.zeros((2 * block_tok, group_size, head_dim), jnp.float32),
    )
    final_state = fold_groups(
        visit_group,
        start_state,
        (
            lax.all_gather(key_states, "blk", axis=0, tiled=True),
            lax.all_gather(value_states, "blk", axis=0, tiled=True),
        ),
    )
    page_store = fold_groups(
        place_pages,
        empty_store,
        (
            lax.all_gather(key_states, "blk", axis=0, tiled=True),
            lax.all_gather(value_states, "blk", axis=0, tiled=True),
        ),
    )
    running_max, weight_sum, accum = final_state
    attended = (
        (accum / weight_sum[..., None])
        .astype(jnp.bfloat16)
        .reshape(1, 2, block_tok, group_size * head_dim)
    )
    kv_cache = page_store.astype(jnp.bfloat16).reshape(slot_count, 1, PAGE, 2 * head_dim)
    return (attended, kv_cache)


def solution(mesh):
    return jax.shard_map(
        per_device if mesh.shape["blk"] <= 8 else per_device_long,
        mesh=mesh,
        in_specs=(
            P("blk", None, "head", None),
            P("blk", None, None, "head"),
            P("blk", None, None, "head"),
            P(),
            P(),
        ),
        out_specs=(P("blk", None, None, "head"), P("blk", "head", None, None)),
        check_vma=False,
    )
```

```python
import jax
import jax.numpy as jnp
from jax import lax
from jax.experimental import pallas as pl
from jax.experimental.pallas import tpu as pltpu
from jax.sharding import PartitionSpec as P

PAGE = 16
LOG2E = 1.4426950408889634
HEAD_DIM = 128
LANES = 128


def gather_queries(own, across, beside, q_rows):
    my_head = lax.axis_index("head")
    width = beside.shape[-1]
    sub_tok = own.shape[2]
    group = width // HEAD_DIM
    block_tok = q_rows.shape[1] // group
    for half in range(2):
        for g in range(group):
            lane = g * HEAD_DIM
            mine = pl.multiple_of(my_head * width + lane, HEAD_DIM)
            low = pl.multiple_of((my_head % 2) * width + lane, HEAD_DIM)
            parts = (
                own[0, half, :, pl.ds(mine, HEAD_DIM)],
                beside[0, half, :, lane : lane + HEAD_DIM],
                across[0, half, :, pl.ds(low, HEAD_DIM)],
                beside[1, half, :, lane : lane + HEAD_DIM],
            )
            for d, part in enumerate(parts):
                row = pl.multiple_of(g * block_tok + (my_head ^ d) * sub_tok, sub_tok)
                q_rows[half, pl.ds(row, sub_tok), :] = part


def key_bias(my_blk, doc_lengths, chips, block_tok, half, core):
    blk_count = 2 * chips
    shape = (block_tok, LANES)
    my_block = my_blk if half == 0 else 2 * blk_count - 1 - my_blk
    q_pos = my_block * block_tok + lax.broadcasted_iota(jnp.int32, (1, LANES), 1) % block_tok
    first = jnp.zeros_like(q_pos)
    bound = 0
    for k in range(doc_lengths.shape[0] - 1):
        bound = bound + doc_lengths[k]
        first = jnp.where(q_pos >= bound, bound, first)
    row = lax.broadcasted_iota(jnp.int32, shape, 0)
    parts = []
    for m in range(chips):
        owner = (my_blk ^ core) ^ (2 * m)
        for side in range(half + 1):
            start = (owner if side == 0 else 2 * blk_count - 1 - owner) * block_tok
            parts.append(jnp.where((row <= q_pos - start) & (row >= first - start), 0.0, -1e30))
    return jnp.concatenate(parts, axis=0)


def page_targets(my_blk, page_slot, chips, block_tok, slot_count, core):
    pages_blk = block_tok // PAGE
    col = lax.broadcasted_iota(jnp.int32, (1, 2 * block_tok), 1)
    parts = []
    for m in range(chips):
        owner = (my_blk ^ core) ^ (2 * m)
        slots = jnp.zeros_like(col)
        for half in range(2):
            for n in range(pages_blk):
                slots = jnp.where(col // PAGE == half * pages_blk + n, page_slot[half, n, owner], slots)
        parts.append((slots - my_blk * slot_count) * PAGE + col % PAGE)
    return jnp.concatenate(parts, axis=1)


def place_pages(targets, pairs, slot_count):
    rows = pairs[...].reshape(-1, pairs.shape[-1])
    row = lax.broadcasted_iota(jnp.int32, (slot_count * PAGE, rows.shape[0]), 0)
    chosen = jnp.where(row == targets, 1.0, 0.0).astype(jnp.bfloat16)
    return jnp.dot(chosen, rows, preferred_element_type=jnp.float32)


def score_part(q_rows, pairs, half):
    keys = pairs[:, : half + 1].reshape(-1, 2 * HEAD_DIM)[:, :HEAD_DIM]
    return lax.dot_general(keys, q_rows[half], (((1,), (1,)), ((), ())), preferred_element_type=jnp.float32)


def weigh_part(scores, bias, pairs, half):
    values = pairs[:, : half + 1].reshape(-1, 2 * HEAD_DIM)[:, HEAD_DIM:]
    bias = jnp.concatenate([bias] * (scores.shape[1] // LANES), axis=1)
    scores = scores * (HEAD_DIM**-0.5 * LOG2E) + bias
    top = jnp.max(scores, axis=0, keepdims=True)
    weights = jnp.exp2(scores - top)
    total = jnp.sum(weights, axis=0, keepdims=True)
    out = lax.dot_general(
        values, weights.astype(jnp.bfloat16), (((0,), (0,)), ((), ())), preferred_element_type=jnp.float32
    )
    return top, total, out


def plan_kernel(
    doc_hbm, slot_hbm, bias_a, bias_b, targets, far_bias_a, far_bias_b, far_targets, doc_lengths, page_slot, sems
):
    fetch_doc = pltpu.make_async_copy(doc_hbm, doc_lengths, sems.at[0])
    fetch_slot = pltpu.make_async_copy(slot_hbm, page_slot, sems.at[1])
    fetch_doc.start()
    fetch_slot.start()
    fetch_doc.wait()
    fetch_slot.wait()
    my_blk = lax.axis_index("blk")
    chips = page_slot.shape[2] // 2
    block_tok = bias_a.shape[0] // chips
    slot_count = 4 * page_slot.shape[1]
    for core, refs in enumerate(((bias_a, bias_b, targets), (far_bias_a, far_bias_b, far_targets))):
        for half in range(2):
            refs[half][...] = key_bias(my_blk, doc_lengths, chips, block_tok, half, core)
        refs[2][...] = page_targets(my_blk, page_slot, chips, block_tok, slot_count, core)


def near_kernel(
    own, across, beside, near, bias_a, bias_b, targets, q_rows, top_ref, total_ref, out_ref, pages_ref
):
    slot_count = pages_ref.shape[0] // PAGE
    gather_queries(own, across, beside, q_rows)
    for half in (1, 0):
        bias = (bias_a, bias_b)[half][...]
        top, total, out = weigh_part(score_part(q_rows, near, half), bias, near, half)
        top_ref[half] = top
        total_ref[half] = total
        out_ref[half] = out
    pages_ref[...] = place_pages(targets[...], near, slot_count).astype(jnp.bfloat16)


def far_kernel(
    far, q_rows, top_ref, total_ref, out_ref, pages_ref, far_bias_a, far_bias_b, far_targets, attended, kv_cache,
    pages, result, sems,
):
    block_tok = far.shape[2]
    slot_count = kv_cache.shape[0]
    moved = place_pages(far_targets[...], far, slot_count) + pages_ref[...].astype(jnp.float32)
    pages[...] = moved.astype(jnp.bfloat16).reshape(pages.shape)
    writes = [pltpu.make_async_copy(pages, kv_cache, sems.at[2])]
    writes[0].start()
    for half in (1, 0):
        bias = (far_bias_a, far_bias_b)[half][...]
        top, total, out = weigh_part(score_part(q_rows, far, half), bias, far, half)
        best = jnp.maximum(top, top_ref[half])
        here = jnp.exp2(top - best)
        there = jnp.exp2(top_ref[half] - best)
        inverse = 1.0 / (total * here + total_ref[half] * there)
        out = (out * (here * inverse) + out_ref[half] * (there * inverse)).T.astype(jnp.bfloat16)
        for g in range(out.shape[0] // block_tok):
            result[half, :, g * HEAD_DIM : (g + 1) * HEAD_DIM] = out[g * block_tok : (g + 1) * block_tok]
        writes.append(pltpu.make_async_copy(result.at[half], attended.at[0, half], sems.at[half]))
        writes[-1].start()
    for write in writes:
        write.wait()


def per_device(query_states, key_states, value_states, doc_lengths, page_slot):
    blk_count = lax.axis_size("blk")
    head_count = lax.axis_size("head")
    q_width = query_states.shape[3]
    block_tok = key_states.shape[2]
    width = q_width // head_count
    rows = width // HEAD_DIM * block_tok
    slot_count = 4 * (block_tok // PAGE)
    hbm = pl.BlockSpec(memory_space=pl.ANY)
    vmem = pl.BlockSpec(memory_space=pltpu.VMEM)
    params = pltpu.CompilerParams(vmem_limit_bytes=32 * 1024 * 1024)
    cost = pl.CostEstimate(flops=4_000_000_000, bytes_accessed=1_000_000, transcendentals=200_000)

    my_head = lax.axis_index("head")
    part = lax.dynamic_slice_in_dim(query_states, ((my_head ^ 2) // 2) * 2 * width, 2 * width, axis=3)
    across = lax.ppermute(part, "head", [(i, i ^ 2) for i in range(head_count)])
    pair = jnp.concatenate([key_states, value_states], axis=3)
    pair, _ = lax.optimization_barrier((pair, part))
    near = [
        lax.ppermute(pair, "blk", [(i, i ^ d) for i in range(blk_count)]) for d in range(2, blk_count, 2)
    ]
    beside = jnp.concatenate(
        [
            lax.dynamic_slice_in_dim(query_states, (my_head ^ 1) * width, width, axis=3),
            lax.dynamic_slice_in_dim(across, (1 - my_head % 2) * width, width, axis=3),
        ],
        axis=0,
    )
    slots = page_slot.transpose(1, 2, 0)
    doc_lengths, slots, _ = lax.optimization_barrier((doc_lengths, slots, across))
    half_cols = blk_count // 2 * block_tok
    plan = pl.pallas_call(
        plan_kernel,
        out_shape=(
            jax.ShapeDtypeStruct((half_cols, LANES), jnp.float32),
            jax.ShapeDtypeStruct((2 * half_cols, LANES), jnp.float32),
            jax.ShapeDtypeStruct((1, 2 * half_cols), jnp.int32),
        )
        * 2,
        in_specs=[hbm] * 2,
        out_specs=(vmem,) * 6,
        scratch_shapes=[
            pltpu.SMEM(doc_lengths.shape, jnp.int32),
            pltpu.SMEM(slots.shape, jnp.int32),
            pltpu.SemaphoreType.DMA((2,)),
        ],
        compiler_params=params,
        cost_estimate=pl.CostEstimate(flops=1000, bytes_accessed=1000, transcendentals=0),
    )(doc_lengths, slots)
    near, _ = lax.optimization_barrier((near[::-1], beside))
    near = near[::-1]
    beside = lax.ppermute(beside, "head", [(i, i ^ 1) for i in range(head_count)])
    near = jnp.concatenate([pair] + near, axis=0)
    far = lax.ppermute(near, "blk", [(i, i ^ 1) for i in range(blk_count)])

    stats = pl.pallas_call(
        near_kernel,
        out_shape=(
            jax.ShapeDtypeStruct((2, rows, HEAD_DIM), jnp.bfloat16),
            jax.ShapeDtypeStruct((2, 1, rows), jnp.float32),
            jax.ShapeDtypeStruct((2, 1, rows), jnp.float32),
            jax.ShapeDtypeStruct((2, HEAD_DIM, rows), jnp.float32),
            jax.ShapeDtypeStruct((slot_count * PAGE, 2 * HEAD_DIM), jnp.bfloat16),
        ),
        in_specs=[vmem] * 7,
        out_specs=(vmem,) * 5,
        compiler_params=params,
        cost_estimate=cost,
    )(query_states, across, beside, near, *plan[:3])
    return pl.pallas_call(
        far_kernel,
        out_shape=(
            jax.ShapeDtypeStruct((1, 2, block_tok, width), jnp.bfloat16),
            jax.ShapeDtypeStruct((slot_count, 1, PAGE, 2 * HEAD_DIM), jnp.bfloat16),
        ),
        in_specs=[vmem] * 9,
        out_specs=(hbm, hbm),
        scratch_shapes=[
            pltpu.VMEM((slot_count, 1, PAGE, 2 * HEAD_DIM), jnp.bfloat16),
            pltpu.VMEM((2, block_tok, width), jnp.bfloat16),
            pltpu.SemaphoreType.DMA((3,)),
        ],
        compiler_params=params,
        cost_estimate=cost,
    )(far, *stats, *plan[3:])


def per_device_long(query_states, key_states, value_states, doc_lengths, page_slot):
    q_local = lax.all_to_all(query_states, "head", split_axis=3, concat_axis=2, tiled=True)
    axis_count = lax.axis_size("blk")
    my_index = lax.axis_index("blk")
    block_tok = q_local.shape[2]
    head_dim = key_states.shape[3]
    group_size = q_local.shape[3] // head_dim
    query_rows = q_local.reshape(2 * block_tok, group_size, head_dim)
    offsets = jnp.arange(block_tok, dtype=jnp.int32)
    doc_bounds = jnp.cumsum(doc_lengths)[:-1]
    page_count = block_tok // PAGE
    slot_count = 4 * page_count
    slot_range = jnp.arange(slot_count, dtype=jnp.int32)
    score_scale = head_dim ** (-0.5)

    def group_positions(owner_ids):
        block_starts = jnp.stack([owner_ids, 2 * axis_count - 1 - owner_ids], axis=1) * block_tok
        return (block_starts[:, :, None] + offsets[None, None, :]).reshape(-1)

    def doc_of(positions):
        return jnp.sum((positions[:, None] >= doc_bounds[None, :]).astype(jnp.int32), axis=1)

    q_pos = group_positions(my_index.reshape(1))
    q_doc = doc_of(q_pos)

    def attend_group(attn_state, key_rows, value_rows, allowed):
        running_max, weight_sum, accum = attn_state
        scores = (
            jnp.einsum("qhd,kd->qhk", query_rows, key_rows, preferred_element_type=jnp.float32)
            * score_scale
        )
        masked = jnp.where(allowed[:, None, :], scores, -1e30)
        new_max = jnp.maximum(running_max, jnp.max(masked, axis=2))
        weights = jnp.where(allowed[:, None, :], jnp.exp(masked - new_max[..., None]), 0.0)
        factor = jnp.exp(running_max - new_max)
        weight_sum = weight_sum * factor + jnp.sum(weights, axis=2)
        update = jnp.einsum(
            "qhk,kd->qhd",
            weights.astype(jnp.bfloat16),
            value_rows,
            preferred_element_type=jnp.float32,
        )
        accum = accum * factor[..., None] + update
        return (new_max, weight_sum, accum)

    def visit_group(attn_state, key_group, value_group, owner_ids):
        key_rows = key_group.reshape(-1, head_dim)
        value_rows = value_group.reshape(-1, head_dim)
        k_pos = group_positions(owner_ids)
        allowed = (k_pos[None, :] <= q_pos[:, None]) & (doc_of(k_pos)[None, :] == q_doc[:, None])
        return attend_group(attn_state, key_rows, value_rows, allowed)

    def place_pages(page_store, key_group, value_group, owner_ids):
        page_rows = jnp.concatenate([key_group, value_group], axis=-1).reshape(
            -1, PAGE * 2 * head_dim
        )
        slot_ids = jnp.take(page_slot, owner_ids, axis=0).reshape(-1) - my_index * slot_count
        selector = (slot_range[:, None] == slot_ids[None, :]).astype(jnp.bfloat16)
        return page_store + jnp.dot(selector, page_rows, preferred_element_type=jnp.float32)

    def fold_groups(step_fn, carried, kv_piece):
        key_piece, value_piece = kv_piece
        piece_len = key_piece.shape[0]
        width = 4
        owner_ids = jnp.arange(piece_len, dtype=jnp.int32).reshape(piece_len // width, width)
        key_groups = key_piece.reshape(piece_len // width, width, 2, block_tok, head_dim)
        value_groups = value_piece.reshape(piece_len // width, width, 2, block_tok, head_dim)

        def visit_one(inner_state, entry_tuple):
            key_group, value_group, owners = entry_tuple
            return (step_fn(inner_state, key_group, value_group, owners), None)

        return lax.scan(visit_one, carried, (key_groups, value_groups, owner_ids))[0]

    empty_store = jnp.zeros((slot_count, PAGE * 2 * head_dim), jnp.float32)
    start_state = (
        jnp.full((2 * block_tok, group_size), -1e30, jnp.float32),
        jnp.zeros((2 * block_tok, group_size), jnp.float32),
        jnp.zeros((2 * block_tok, group_size, head_dim), jnp.float32),
    )
    final_state = fold_groups(
        visit_group,
        start_state,
        (
            lax.all_gather(key_states, "blk", axis=0, tiled=True),
            lax.all_gather(value_states, "blk", axis=0, tiled=True),
        ),
    )
    page_store = fold_groups(
        place_pages,
        empty_store,
        (
            lax.all_gather(key_states, "blk", axis=0, tiled=True),
            lax.all_gather(value_states, "blk", axis=0, tiled=True),
        ),
    )
    running_max, weight_sum, accum = final_state
    attended = (
        (accum / weight_sum[..., None])
        .astype(jnp.bfloat16)
        .reshape(1, 2, block_tok, group_size * head_dim)
    )
    kv_cache = page_store.astype(jnp.bfloat16).reshape(slot_count, 1, PAGE, 2 * head_dim)
    return (attended, kv_cache)


def solution(mesh):
    return jax.shard_map(
        per_device if mesh.shape["blk"] <= 8 else per_device_long,
        mesh=mesh,
        in_specs=(
            P("blk", None, "head", None),
            P("blk", None, None, "head"),
            P("blk", None, None, "head"),
            P(),
            P(),
        ),
        out_specs=(P("blk", None, None, "head"), P("blk", "head", None, None)),
        check_vma=False,
    )
```

```python
import functools

import jax
import jax.numpy as jnp
from jax import lax
from jax.experimental import pallas as pl
from jax.experimental.pallas import tpu as pltpu
from jax.sharding import PartitionSpec as P

PAGE = 16
LOG2E = 1.4426950408889634
HEAD_DIM = 128
LANES = 128


def key_bias(my_blk, doc_lengths, chips, block_tok, sub_tok, half, core, odd):
    blk_count = 2 * chips
    shape = (block_tok, LANES)
    my_block = my_blk if half == 0 else 2 * blk_count - 1 - my_blk
    lane = lax.broadcasted_iota(jnp.int32, (1, LANES), 1)
    sender = (lax.axis_index("head") ^ odd) ^ (2 * (lane // sub_tok % 2))
    q_pos = my_block * block_tok + sender * sub_tok + lane % sub_tok
    first = jnp.zeros_like(q_pos)
    bound = 0
    for k in range(doc_lengths.shape[0] - 1):
        bound = bound + doc_lengths[k]
        first = jnp.where(q_pos >= bound, bound, first)
    row = lax.broadcasted_iota(jnp.int32, shape, 0)
    parts = []
    for m in range(chips):
        owner = (my_blk ^ core) ^ (2 * m)
        for side in range(half + 1):
            start = (owner if side == 0 else 2 * blk_count - 1 - owner) * block_tok
            parts.append(jnp.where((row <= q_pos - start) & (row >= first - start), 0.0, -1e30))
    return jnp.concatenate(parts, axis=0)


def page_targets(my_blk, page_slot, chips, block_tok, slot_count, core):
    pages_blk = block_tok // PAGE
    col = lax.broadcasted_iota(jnp.int32, (1, 2 * block_tok), 1)
    parts = []
    for m in range(chips):
        owner = (my_blk ^ core) ^ (2 * m)
        slots = jnp.zeros_like(col)
        for half in range(2):
            for n in range(pages_blk):
                slots = jnp.where(col // PAGE == half * pages_blk + n, page_slot[half, n, owner], slots)
        parts.append((slots - my_blk * slot_count) * PAGE + col % PAGE)
    return jnp.concatenate(parts, axis=1)


def place_pages(targets, pairs, slot_count):
    rows = pairs[...].reshape(-1, pairs.shape[-1])
    row = lax.broadcasted_iota(jnp.int32, (slot_count * PAGE, rows.shape[0]), 0)
    chosen = jnp.where(row == targets, 1.0, 0.0).astype(jnp.bfloat16)
    return jnp.dot(chosen, rows, preferred_element_type=jnp.float32)


def score_part(queries, pairs, half):
    keys = pairs[:, : half + 1].reshape(-1, 2 * HEAD_DIM)[:, :HEAD_DIM]
    return lax.dot_general(keys, queries, (((1,), (1,)), ((), ())), preferred_element_type=jnp.float32)


def weigh_part(scores, bias, pairs, half):
    values = pairs[:, : half + 1].reshape(-1, 2 * HEAD_DIM)[:, HEAD_DIM:]
    scores = scores * (HEAD_DIM**-0.5 * LOG2E) + bias
    top = jnp.max(scores, axis=0, keepdims=True)
    weights = jnp.exp2(scores - top)
    total = jnp.sum(weights, axis=0, keepdims=True)
    out = lax.dot_general(
        values, weights.astype(jnp.bfloat16), (((0,), (0,)), ((), ())), preferred_element_type=jnp.float32
    )
    return top, total, out


def first_kernel(
    doc_hbm, slot_hbm, own, across, near, q_ref, top_ref, total_ref, out_ref, bias_a, bias_b, far_bias_a, far_bias_b,
    far_targets, pages_ref, doc_lengths, page_slot, sems,
):
    chips, _, block_tok, _ = near.shape
    slot_count = pages_ref.shape[0] // PAGE
    width = across.shape[3] // 2
    sub_tok = own.shape[2]
    my_blk = lax.axis_index("blk")
    my_head = lax.axis_index("head")
    fetch_doc = pltpu.make_async_copy(doc_hbm, doc_lengths, sems.at[0])
    fetch_slot = pltpu.make_async_copy(slot_hbm, page_slot, sems.at[1])
    fetch_doc.start()
    fetch_slot.start()
    scores = []
    for half in range(2):
        parts = []
        for lane in range(0, width, HEAD_DIM):
            mine = pl.multiple_of(my_head * width + lane, HEAD_DIM)
            low = pl.multiple_of((my_head % 2) * width + lane, HEAD_DIM)
            parts.append(own[0, half, :, pl.ds(mine, HEAD_DIM)])
            parts.append(across[0, half, :, pl.ds(low, HEAD_DIM)])
        queries = jnp.concatenate(parts, axis=0)
        q_ref[half] = queries
        scores.append(score_part(queries, near, half))
    fetch_doc.wait()
    fetch_slot.wait()
    bias = functools.partial(key_bias, my_blk, doc_lengths, chips, block_tok, sub_tok)
    for half in (1, 0):
        top, total, out = weigh_part(scores[half], bias(half, 0, 0), near, half)
        top_ref[half] = top
        total_ref[half] = total
        out_ref[half] = out
        (bias_a, bias_b)[half][...] = bias(half, 0, 1)
        for odd in range(2):
            (far_bias_a, far_bias_b)[half][:, odd * LANES : (odd + 1) * LANES] = bias(half, 1, odd)
    targets = functools.partial(page_targets, my_blk, page_slot, chips, block_tok, slot_count)
    pages_ref[...] = place_pages(targets(0), near, slot_count).astype(jnp.bfloat16)
    far_targets[...] = targets(1)


def second_kernel(beside, near, bias_a, bias_b, q_ref, top_ref, total_ref, out_ref):
    width = beside.shape[3]
    for half in (1, 0):
        queries = jnp.concatenate(
            [beside[d, half, :, lane : lane + HEAD_DIM] for lane in range(0, width, HEAD_DIM) for d in range(2)], axis=0
        )
        q_ref[half] = queries
        bias = (bias_a, bias_b)[half][...]
        top, total, out = weigh_part(score_part(queries, near, half), bias, near, half)
        top_ref[half] = top
        total_ref[half] = total
        out_ref[half] = out


def far_kernel(
    far, far_bias_a, far_bias_b, far_targets, pages_ref, q_even, top_even, total_even, out_even, q_odd, top_odd,
    total_odd, out_odd, attended, kv_cache, pages, result, sems,
):
    slot_count = kv_cache.shape[0]
    my_head = lax.axis_index("head")
    moved = place_pages(far_targets[...], far, slot_count) + pages_ref[...].astype(jnp.float32)
    pages[...] = moved.astype(jnp.bfloat16).reshape(pages.shape)
    writes = [pltpu.make_async_copy(pages, kv_cache, sems.at[2])]
    writes[0].start()
    for half in (1, 0):
        queries = jnp.concatenate([q_even[half], q_odd[half]], axis=0)
        near_top = jnp.concatenate([top_even[half], top_odd[half]], axis=1)
        near_total = jnp.concatenate([total_even[half], total_odd[half]], axis=1)
        near_out = jnp.concatenate([out_even[half], out_odd[half]], axis=1)
        bias = (far_bias_a, far_bias_b)[half][...]
        top, total, out = weigh_part(score_part(queries, far, half), bias, far, half)
        best = jnp.maximum(top, near_top)
        here = jnp.exp2(top - best)
        there = jnp.exp2(near_top - best)
        inverse = 1.0 / (total * here + near_total * there)
        out = (out * (here * inverse) + near_out * (there * inverse)).T.astype(jnp.bfloat16)
        sub_tok = LANES * HEAD_DIM // (2 * result.shape[2])
        for odd in range(2):
            for g in range(result.shape[2] // HEAD_DIM):
                for p in range(2):
                    row = pl.multiple_of((my_head ^ (odd + 2 * p)) * sub_tok, sub_tok)
                    start = odd * LANES + (2 * g + p) * sub_tok
                    result[half, pl.ds(row, sub_tok), g * HEAD_DIM : (g + 1) * HEAD_DIM] = out[start : start + sub_tok]
        writes.append(pltpu.make_async_copy(result.at[half], attended.at[0, half], sems.at[half]))
        writes[-1].start()
    for write in writes:
        write.wait()


def per_device(query_states, key_states, value_states, doc_lengths, page_slot):
    blk_count = lax.axis_size("blk")
    head_count = lax.axis_size("head")
    q_width = query_states.shape[3]
    block_tok = key_states.shape[2]
    width = q_width // head_count
    slot_count = 4 * (block_tok // PAGE)

    my_head = lax.axis_index("head")
    part = lax.dynamic_slice_in_dim(query_states, ((my_head ^ 2) // 2) * 2 * width, 2 * width, axis=3)
    across = lax.ppermute(part, "head", [(i, i ^ 2) for i in range(head_count)])
    pair = jnp.concatenate([key_states, value_states], axis=3)
    pair, _ = lax.optimization_barrier((pair, part))
    near = [
        lax.ppermute(pair, "blk", [(i, i ^ d) for i in range(blk_count)]) for d in range(2, blk_count, 2)
    ]
    beside = jnp.concatenate(
        [
            lax.dynamic_slice_in_dim(query_states, (my_head ^ 1) * width, width, axis=3),
            lax.dynamic_slice_in_dim(across, (1 - my_head % 2) * width, width, axis=3),
        ],
        axis=0,
    )
    near = lax.optimization_barrier((near[::-1], beside))[0][::-1]
    beside = lax.ppermute(beside, "head", [(i, i ^ 1) for i in range(head_count)])
    near = jnp.concatenate([pair] + near, axis=0)
    far = lax.ppermute(near, "blk", [(i, i ^ 1) for i in range(blk_count)])

    hbm = pl.BlockSpec(memory_space=pl.ANY)
    vmem = pl.BlockSpec(memory_space=pltpu.VMEM)
    params = pltpu.CompilerParams(vmem_limit_bytes=32 * 1024 * 1024)
    cost = pl.CostEstimate(flops=4_000_000_000, bytes_accessed=1_000_000, transcendentals=200_000)
    slots = page_slot.transpose(1, 2, 0)
    half_cols = blk_count // 2 * block_tok
    stats = (
        jax.ShapeDtypeStruct((2, LANES, HEAD_DIM), jnp.bfloat16),
        jax.ShapeDtypeStruct((2, 1, LANES), jnp.float32),
        jax.ShapeDtypeStruct((2, 1, LANES), jnp.float32),
        jax.ShapeDtypeStruct((2, HEAD_DIM, LANES), jnp.float32),
    )
    *even, bias_a, bias_b, far_bias_a, far_bias_b, far_targets, pages = pl.pallas_call(
        first_kernel,
        out_shape=stats
        + (
            jax.ShapeDtypeStruct((half_cols, LANES), jnp.float32),
            jax.ShapeDtypeStruct((2 * half_cols, LANES), jnp.float32),
            jax.ShapeDtypeStruct((half_cols, 2 * LANES), jnp.float32),
            jax.ShapeDtypeStruct((2 * half_cols, 2 * LANES), jnp.float32),
            jax.ShapeDtypeStruct((1, 2 * half_cols), jnp.int32),
            jax.ShapeDtypeStruct((slot_count * PAGE, 2 * HEAD_DIM), jnp.bfloat16),
        ),
        in_specs=[hbm] * 2 + [vmem] * 3,
        out_specs=(vmem,) * 10,
        scratch_shapes=[
            pltpu.SMEM(doc_lengths.shape, jnp.int32),
            pltpu.SMEM(slots.shape, jnp.int32),
            pltpu.SemaphoreType.DMA((2,)),
        ],
        compiler_params=params,
        cost_estimate=cost,
    )(doc_lengths, slots, query_states, across, near)
    odd = pl.pallas_call(
        second_kernel,
        out_shape=stats,
        in_specs=[vmem] * 4,
        out_specs=(vmem,) * 4,
        compiler_params=params,
        cost_estimate=cost,
    )(beside, near, bias_a, bias_b)
    return pl.pallas_call(
        far_kernel,
        out_shape=(
            jax.ShapeDtypeStruct((1, 2, block_tok, width), jnp.bfloat16),
            jax.ShapeDtypeStruct((slot_count, 1, PAGE, 2 * HEAD_DIM), jnp.bfloat16),
        ),
        in_specs=[vmem] * 13,
        out_specs=(hbm, hbm),
        scratch_shapes=[
            pltpu.VMEM((slot_count, 1, PAGE, 2 * HEAD_DIM), jnp.bfloat16),
            pltpu.VMEM((2, block_tok, width), jnp.bfloat16),
            pltpu.SemaphoreType.DMA((3,)),
        ],
        compiler_params=params,
        cost_estimate=cost,
    )(far, far_bias_a, far_bias_b, far_targets, pages, *even, *odd)


def per_device_long(query_states, key_states, value_states, doc_lengths, page_slot):
    q_local = lax.all_to_all(query_states, "head", split_axis=3, concat_axis=2, tiled=True)
    axis_count = lax.axis_size("blk")
    my_index = lax.axis_index("blk")
    block_tok = q_local.shape[2]
    head_dim = key_states.shape[3]
    group_size = q_local.shape[3] // head_dim
    query_rows = q_local.reshape(2 * block_tok, group_size, head_dim)
    offsets = jnp.arange(block_tok, dtype=jnp.int32)
    doc_bounds = jnp.cumsum(doc_lengths)[:-1]
    page_count = block_tok // PAGE
    slot_count = 4 * page_count
    slot_range = jnp.arange(slot_count, dtype=jnp.int32)
    score_scale = head_dim ** (-0.5)

    def group_positions(owner_ids):
        block_starts = jnp.stack([owner_ids, 2 * axis_count - 1 - owner_ids], axis=1) * block_tok
        return (block_starts[:, :, None] + offsets[None, None, :]).reshape(-1)

    def doc_of(positions):
        return jnp.sum((positions[:, None] >= doc_bounds[None, :]).astype(jnp.int32), axis=1)

    q_pos = group_positions(my_index.reshape(1))
    q_doc = doc_of(q_pos)

    def attend_group(attn_state, key_rows, value_rows, allowed):
        running_max, weight_sum, accum = attn_state
        scores = (
            jnp.einsum("qhd,kd->qhk", query_rows, key_rows, preferred_element_type=jnp.float32)
            * score_scale
        )
        masked = jnp.where(allowed[:, None, :], scores, -1e30)
        new_max = jnp.maximum(running_max, jnp.max(masked, axis=2))
        weights = jnp.where(allowed[:, None, :], jnp.exp(masked - new_max[..., None]), 0.0)
        factor = jnp.exp(running_max - new_max)
        weight_sum = weight_sum * factor + jnp.sum(weights, axis=2)
        update = jnp.einsum(
            "qhk,kd->qhd",
            weights.astype(jnp.bfloat16),
            value_rows,
            preferred_element_type=jnp.float32,
        )
        accum = accum * factor[..., None] + update
        return (new_max, weight_sum, accum)

    def visit_group(attn_state, key_group, value_group, owner_ids):
        key_rows = key_group.reshape(-1, head_dim)
        value_rows = value_group.reshape(-1, head_dim)
        k_pos = group_positions(owner_ids)
        allowed = (k_pos[None, :] <= q_pos[:, None]) & (doc_of(k_pos)[None, :] == q_doc[:, None])
        return attend_group(attn_state, key_rows, value_rows, allowed)

    def place_pages(page_store, key_group, value_group, owner_ids):
        page_rows = jnp.concatenate([key_group, value_group], axis=-1).reshape(
            -1, PAGE * 2 * head_dim
        )
        slot_ids = jnp.take(page_slot, owner_ids, axis=0).reshape(-1) - my_index * slot_count
        selector = (slot_range[:, None] == slot_ids[None, :]).astype(jnp.bfloat16)
        return page_store + jnp.dot(selector, page_rows, preferred_element_type=jnp.float32)

    def fold_groups(step_fn, carried, kv_piece):
        key_piece, value_piece = kv_piece
        piece_len = key_piece.shape[0]
        width = 4
        owner_ids = jnp.arange(piece_len, dtype=jnp.int32).reshape(piece_len // width, width)
        key_groups = key_piece.reshape(piece_len // width, width, 2, block_tok, head_dim)
        value_groups = value_piece.reshape(piece_len // width, width, 2, block_tok, head_dim)

        def visit_one(inner_state, entry_tuple):
            key_group, value_group, owners = entry_tuple
            return (step_fn(inner_state, key_group, value_group, owners), None)

        return lax.scan(visit_one, carried, (key_groups, value_groups, owner_ids))[0]

    empty_store = jnp.zeros((slot_count, PAGE * 2 * head_dim), jnp.float32)
    start_state = (
        jnp.full((2 * block_tok, group_size), -1e30, jnp.float32),
        jnp.zeros((2 * block_tok, group_size), jnp.float32),
        jnp.zeros((2 * block_tok, group_size, head_dim), jnp.float32),
    )
    final_state = fold_groups(
        visit_group,
        start_state,
        (
            lax.all_gather(key_states, "blk", axis=0, tiled=True),
            lax.all_gather(value_states, "blk", axis=0, tiled=True),
        ),
    )
    page_store = fold_groups(
        place_pages,
        empty_store,
        (
            lax.all_gather(key_states, "blk", axis=0, tiled=True),
            lax.all_gather(value_states, "blk", axis=0, tiled=True),
        ),
    )
    running_max, weight_sum, accum = final_state
    attended = (
        (accum / weight_sum[..., None])
        .astype(jnp.bfloat16)
        .reshape(1, 2, block_tok, group_size * head_dim)
    )
    kv_cache = page_store.astype(jnp.bfloat16).reshape(slot_count, 1, PAGE, 2 * head_dim)
    return (attended, kv_cache)


def solution(mesh):
    return jax.shard_map(
        per_device if mesh.shape["blk"] <= 8 else per_device_long,
        mesh=mesh,
        in_specs=(
            P("blk", None, "head", None),
            P("blk", None, None, "head"),
            P("blk", None, None, "head"),
            P(),
            P(),
        ),
        out_specs=(P("blk", None, None, "head"), P("blk", "head", None, None)),
        check_vma=False,
    )
```

```python
import functools

import jax
import jax.numpy as jnp
from jax import lax
from jax.experimental import pallas as pl
from jax.experimental.pallas import tpu as pltpu
from jax.sharding import PartitionSpec as P

PAGE = 16
LOG2E = 1.4426950408889634
HEAD_DIM = 128
LANES = 128


def gather_queries(own, across, beside, half):
    my_head = lax.axis_index("head")
    width = beside.shape[-1]
    parts = []
    for lane in range(0, width, HEAD_DIM):
        mine = pl.multiple_of(my_head * width + lane, HEAD_DIM)
        low = pl.multiple_of((my_head % 2) * width + lane, HEAD_DIM)
        parts.append(own[0, half, :, pl.ds(mine, HEAD_DIM)])
        parts.append(beside[0, half, :, lane : lane + HEAD_DIM])
        parts.append(across[0, half, :, pl.ds(low, HEAD_DIM)])
        parts.append(beside[1, half, :, lane : lane + HEAD_DIM])
    return jnp.concatenate(parts, axis=0)


def key_bias(my_blk, lengths, chips, block_tok, sub_tok, half, core):
    blk_count = 2 * chips
    my_block = my_blk if half == 0 else 2 * blk_count - 1 - my_blk
    lane = lax.broadcasted_iota(jnp.int32, (1, LANES), 1)
    sender = lax.axis_index("head") ^ (lane % block_tok // sub_tok)
    q_pos = my_block * block_tok + sender * sub_tok + lane % sub_tok
    first = jnp.zeros_like(q_pos)
    bound = jnp.zeros_like(lengths[:, :1])
    for k in range(lengths.shape[1] - 1):
        bound = bound + lengths[:, k : k + 1]
        first = jnp.where(q_pos >= bound, bound, first)
    row = lax.broadcasted_iota(jnp.int32, (block_tok, LANES), 0)
    parts = []
    for m in range(chips):
        owner = (my_blk ^ core) ^ (2 * m)
        for side in range(half + 1):
            block = owner if side == 0 else 2 * blk_count - 1 - owner
            if core == 0 and m == 0 and side == half:
                allowed = (row <= q_pos - block * block_tok) & (row >= first - block * block_tok)
            else:
                allowed = row >= first - jnp.where(block < my_block, block * block_tok, -(2**28))
            parts.append(jnp.where(allowed, 0.0, -1e30))
    return jnp.concatenate(parts, axis=0)


def page_targets(my_blk, page_slot, chips, slot_count, core):
    _, pages_blk, blk_count = page_slot.shape
    chip = lax.broadcasted_iota(jnp.int32, (chips, blk_count), 0)
    owner = (my_blk ^ core) ^ (2 * chip)
    chosen = (owner == lax.broadcasted_iota(jnp.int32, (chips, blk_count), 1)).astype(jnp.float32).astype(jnp.bfloat16)
    cols = 2 * pages_blk * PAGE
    page = lax.broadcasted_iota(jnp.int32, (pages_blk, cols), 0)
    col = lax.broadcasted_iota(jnp.int32, (pages_blk, cols), 1)
    slots = 0.0
    for half in range(2):
        held = lax.dot_general(
            chosen,
            page_slot[half].astype(jnp.float32).astype(jnp.bfloat16),
            (((1,), (1,)), ((), ())),
            preferred_element_type=jnp.float32,
        )
        spread = (col // PAGE == page + half * pages_blk).astype(jnp.float32).astype(jnp.bfloat16)
        slots = slots + jnp.dot(held.astype(jnp.bfloat16), spread, preferred_element_type=jnp.float32)
    slots = slots.astype(jnp.int32) - my_blk * slot_count
    rows = slots * PAGE + lax.broadcasted_iota(jnp.int32, slots.shape, 1) % PAGE
    return jnp.concatenate([rows[m : m + 1] for m in range(chips)], axis=1)


def place_pages(targets, pairs, slot_count):
    rows = pairs[...].reshape(-1, pairs.shape[-1])
    row = lax.broadcasted_iota(jnp.int32, (slot_count * PAGE, rows.shape[0]), 0)
    chosen = jnp.where(row == targets, 1.0, 0.0).astype(jnp.bfloat16)
    return jnp.dot(chosen, rows, preferred_element_type=jnp.float32)


def score_part(queries, pairs, half):
    keys = pairs[:, : half + 1].reshape(-1, 2 * HEAD_DIM)[:, :HEAD_DIM]
    return lax.dot_general(keys, queries, (((1,), (1,)), ((), ())), preferred_element_type=jnp.float32)


def weigh_part(scores, bias, pairs, half):
    values = pairs[:, : half + 1].reshape(-1, 2 * HEAD_DIM)[:, HEAD_DIM:]
    bias = jnp.concatenate([bias] * (scores.shape[1] // LANES), axis=1)
    scores = scores * (HEAD_DIM**-0.5 * LOG2E) + bias
    top = jnp.max(scores, axis=0, keepdims=True)
    weights = jnp.exp2(scores - top)
    total = jnp.sum(weights, axis=0, keepdims=True)
    out = lax.dot_general(
        values, weights.astype(jnp.bfloat16), (((0,), (0,)), ((), ())), preferred_element_type=jnp.float32
    )
    return top, total, out


def near_kernel(
    lengths, page_slot, own, across, beside, near, q_rows, top_ref, total_ref, out_ref, pages_ref, far_bias_a,
    far_bias_b, far_targets,
):
    chips, _, block_tok, _ = near.shape
    slot_count = pages_ref.shape[0] // PAGE
    my_blk = lax.axis_index("blk")
    bias = functools.partial(key_bias, my_blk, lengths[...], chips, block_tok, own.shape[2])
    for half in (1, 0):
        queries = gather_queries(own, across, beside, half)
        q_rows[half] = queries
        top, total, out = weigh_part(score_part(queries, near, half), bias(half, 0), near, half)
        top_ref[half] = top
        total_ref[half] = total
        out_ref[half] = out
        (far_bias_a, far_bias_b)[half][...] = bias(half, 1)
    targets = functools.partial(page_targets, my_blk, page_slot, chips, slot_count)
    pages_ref[...] = place_pages(targets(0), near, slot_count).astype(jnp.bfloat16)
    far_targets[...] = targets(1)


def far_kernel(
    far, q_rows, top_ref, total_ref, out_ref, pages_ref, far_bias_a, far_bias_b, far_targets, attended, kv_cache,
    pages, result, sems,
):
    block_tok = far.shape[2]
    slot_count = kv_cache.shape[0]
    my_head = lax.axis_index("head")
    sub_tok = block_tok // lax.axis_size("head")
    moved = place_pages(far_targets[...], far, slot_count) + pages_ref[...].astype(jnp.float32)
    pages[...] = moved.astype(jnp.bfloat16).reshape(pages.shape)
    writes = [pltpu.make_async_copy(pages, kv_cache, sems.at[2])]
    writes[0].start()
    for half in (1, 0):
        bias = (far_bias_a, far_bias_b)[half][...]
        top, total, out = weigh_part(score_part(q_rows[half], far, half), bias, far, half)
        best = jnp.maximum(top, top_ref[half])
        here = jnp.exp2(top - best)
        there = jnp.exp2(top_ref[half] - best)
        inverse = 1.0 / (total * here + total_ref[half] * there)
        out = (out * (here * inverse) + out_ref[half] * (there * inverse)).T.astype(jnp.bfloat16)
        for g in range(out.shape[0] // block_tok):
            for d in range(block_tok // sub_tok):
                row = pl.multiple_of((my_head ^ d) * sub_tok, sub_tok)
                start = g * block_tok + d * sub_tok
                result[half, pl.ds(row, sub_tok), g * HEAD_DIM : (g + 1) * HEAD_DIM] = out[start : start + sub_tok]
        writes.append(pltpu.make_async_copy(result.at[half], attended.at[0, half], sems.at[half]))
        writes[-1].start()
    for write in writes:
        write.wait()


def per_device(query_states, key_states, value_states, doc_lengths, page_slot):
    blk_count = lax.axis_size("blk")
    head_count = lax.axis_size("head")
    q_width = query_states.shape[3]
    block_tok = key_states.shape[2]
    width = q_width // head_count
    rows = width // HEAD_DIM * block_tok
    slot_count = 4 * (block_tok // PAGE)

    my_head = lax.axis_index("head")
    part = lax.dynamic_slice_in_dim(query_states, ((my_head ^ 2) // 2) * 2 * width, 2 * width, axis=3)
    across = lax.ppermute(part, "head", [(i, i ^ 2) for i in range(head_count)])
    pair = jnp.concatenate([key_states, value_states], axis=3)
    pair, _ = lax.optimization_barrier((pair, part))
    near = [
        lax.ppermute(pair, "blk", [(i, i ^ d) for i in range(blk_count)]) for d in range(2, blk_count, 2)
    ]
    beside = jnp.concatenate(
        [
            lax.dynamic_slice_in_dim(query_states, (my_head ^ 1) * width, width, axis=3),
            lax.dynamic_slice_in_dim(across, (1 - my_head % 2) * width, width, axis=3),
        ],
        axis=0,
    )
    near = lax.optimization_barrier((near[::-1], beside))[0][::-1]
    beside = lax.ppermute(beside, "head", [(i, i ^ 1) for i in range(head_count)])
    near = jnp.concatenate([pair] + near, axis=0)
    far = lax.ppermute(near, "blk", [(i, i ^ 1) for i in range(blk_count)])

    hbm = pl.BlockSpec(memory_space=pl.ANY)
    vmem = pl.BlockSpec(memory_space=pltpu.VMEM)
    params = pltpu.CompilerParams(vmem_limit_bytes=32 * 1024 * 1024)
    cost = pl.CostEstimate(flops=4_000_000_000, bytes_accessed=1_000_000, transcendentals=200_000)
    half_cols = blk_count // 2 * block_tok
    stats = pl.pallas_call(
        near_kernel,
        out_shape=(
            jax.ShapeDtypeStruct((2, rows, HEAD_DIM), jnp.bfloat16),
            jax.ShapeDtypeStruct((2, 1, rows), jnp.float32),
            jax.ShapeDtypeStruct((2, 1, rows), jnp.float32),
            jax.ShapeDtypeStruct((2, HEAD_DIM, rows), jnp.float32),
            jax.ShapeDtypeStruct((slot_count * PAGE, 2 * HEAD_DIM), jnp.bfloat16),
            jax.ShapeDtypeStruct((half_cols, LANES), jnp.float32),
            jax.ShapeDtypeStruct((2 * half_cols, LANES), jnp.float32),
            jax.ShapeDtypeStruct((1, 2 * half_cols), jnp.int32),
        ),
        in_specs=[vmem] * 6,
        out_specs=(vmem,) * 8,
        compiler_params=params,
        cost_estimate=cost,
    )(doc_lengths.reshape(1, -1), page_slot.transpose(1, 2, 0), query_states, across, beside, near)
    return pl.pallas_call(
        far_kernel,
        out_shape=(
            jax.ShapeDtypeStruct((1, 2, block_tok, width), jnp.bfloat16),
            jax.ShapeDtypeStruct((slot_count, 1, PAGE, 2 * HEAD_DIM), jnp.bfloat16),
        ),
        in_specs=[vmem] * 9,
        out_specs=(hbm, hbm),
        scratch_shapes=[
            pltpu.VMEM((slot_count, 1, PAGE, 2 * HEAD_DIM), jnp.bfloat16),
            pltpu.VMEM((2, block_tok, width), jnp.bfloat16),
            pltpu.SemaphoreType.DMA((3,)),
        ],
        compiler_params=params,
        cost_estimate=cost,
    )(far, *stats)


def per_device_long(query_states, key_states, value_states, doc_lengths, page_slot):
    q_local = lax.all_to_all(query_states, "head", split_axis=3, concat_axis=2, tiled=True)
    axis_count = lax.axis_size("blk")
    my_index = lax.axis_index("blk")
    block_tok = q_local.shape[2]
    head_dim = key_states.shape[3]
    group_size = q_local.shape[3] // head_dim
    query_rows = q_local.reshape(2 * block_tok, group_size, head_dim)
    offsets = jnp.arange(block_tok, dtype=jnp.int32)
    doc_bounds = jnp.cumsum(doc_lengths)[:-1]
    page_count = block_tok // PAGE
    slot_count = 4 * page_count
    slot_range = jnp.arange(slot_count, dtype=jnp.int32)
    score_scale = head_dim ** (-0.5)

    def group_positions(owner_ids):
        block_starts = jnp.stack([owner_ids, 2 * axis_count - 1 - owner_ids], axis=1) * block_tok
        return (block_starts[:, :, None] + offsets[None, None, :]).reshape(-1)

    def doc_of(positions):
        return jnp.sum((positions[:, None] >= doc_bounds[None, :]).astype(jnp.int32), axis=1)

    q_pos = group_positions(my_index.reshape(1))
    q_doc = doc_of(q_pos)

    def attend_group(attn_state, key_rows, value_rows, allowed):
        running_max, weight_sum, accum = attn_state
        scores = (
            jnp.einsum("qhd,kd->qhk", query_rows, key_rows, preferred_element_type=jnp.float32)
            * score_scale
        )
        masked = jnp.where(allowed[:, None, :], scores, -1e30)
        new_max = jnp.maximum(running_max, jnp.max(masked, axis=2))
        weights = jnp.where(allowed[:, None, :], jnp.exp(masked - new_max[..., None]), 0.0)
        factor = jnp.exp(running_max - new_max)
        weight_sum = weight_sum * factor + jnp.sum(weights, axis=2)
        update = jnp.einsum(
            "qhk,kd->qhd",
            weights.astype(jnp.bfloat16),
            value_rows,
            preferred_element_type=jnp.float32,
        )
        accum = accum * factor[..., None] + update
        return (new_max, weight_sum, accum)

    def visit_group(attn_state, key_group, value_group, owner_ids):
        key_rows = key_group.reshape(-1, head_dim)
        value_rows = value_group.reshape(-1, head_dim)
        k_pos = group_positions(owner_ids)
        allowed = (k_pos[None, :] <= q_pos[:, None]) & (doc_of(k_pos)[None, :] == q_doc[:, None])
        return attend_group(attn_state, key_rows, value_rows, allowed)

    def place_pages(page_store, key_group, value_group, owner_ids):
        page_rows = jnp.concatenate([key_group, value_group], axis=-1).reshape(
            -1, PAGE * 2 * head_dim
        )
        slot_ids = jnp.take(page_slot, owner_ids, axis=0).reshape(-1) - my_index * slot_count
        selector = (slot_range[:, None] == slot_ids[None, :]).astype(jnp.bfloat16)
        return page_store + jnp.dot(selector, page_rows, preferred_element_type=jnp.float32)

    def fold_groups(step_fn, carried, kv_piece):
        key_piece, value_piece = kv_piece
        piece_len = key_piece.shape[0]
        width = 4
        owner_ids = jnp.arange(piece_len, dtype=jnp.int32).reshape(piece_len // width, width)
        key_groups = key_piece.reshape(piece_len // width, width, 2, block_tok, head_dim)
        value_groups = value_piece.reshape(piece_len // width, width, 2, block_tok, head_dim)

        def visit_one(inner_state, entry_tuple):
            key_group, value_group, owners = entry_tuple
            return (step_fn(inner_state, key_group, value_group, owners), None)

        return lax.scan(visit_one, carried, (key_groups, value_groups, owner_ids))[0]

    empty_store = jnp.zeros((slot_count, PAGE * 2 * head_dim), jnp.float32)
    start_state = (
        jnp.full((2 * block_tok, group_size), -1e30, jnp.float32),
        jnp.zeros((2 * block_tok, group_size), jnp.float32),
        jnp.zeros((2 * block_tok, group_size, head_dim), jnp.float32),
    )
    final_state = fold_groups(
        visit_group,
        start_state,
        (
            lax.all_gather(key_states, "blk", axis=0, tiled=True),
            lax.all_gather(value_states, "blk", axis=0, tiled=True),
        ),
    )
    page_store = fold_groups(
        place_pages,
        empty_store,
        (
            lax.all_gather(key_states, "blk", axis=0, tiled=True),
            lax.all_gather(value_states, "blk", axis=0, tiled=True),
        ),
    )
    running_max, weight_sum, accum = final_state
    attended = (
        (accum / weight_sum[..., None])
        .astype(jnp.bfloat16)
        .reshape(1, 2, block_tok, group_size * head_dim)
    )
    kv_cache = page_store.astype(jnp.bfloat16).reshape(slot_count, 1, PAGE, 2 * head_dim)
    return (attended, kv_cache)


def solution(mesh):
    return jax.shard_map(
        per_device if mesh.shape["blk"] <= 8 else per_device_long,
        mesh=mesh,
        in_specs=(
            P("blk", None, "head", None),
            P("blk", None, None, "head"),
            P("blk", None, None, "head"),
            P(),
            P(),
        ),
        out_specs=(P("blk", None, None, "head"), P("blk", "head", None, None)),
        check_vma=False,
    )
```

```python
import functools

import jax
import jax.numpy as jnp
from jax import lax
from jax.experimental import pallas as pl
from jax.experimental.pallas import tpu as pltpu
from jax.sharding import PartitionSpec as P

PAGE = 16
LOG2E = 1.4426950408889634
HEAD_DIM = 128
LANES = 128


def gather_queries(own, across, beside, half):
    my_head = lax.axis_index("head")
    width = beside.shape[-1]
    parts = []
    for lane in range(0, width, HEAD_DIM):
        mine = pl.multiple_of(my_head * width + lane, HEAD_DIM)
        low = pl.multiple_of((my_head & 1) * width + lane, HEAD_DIM)
        parts.append(own[0, half, :, pl.ds(mine, HEAD_DIM)])
        parts.append(beside[0, half, :, lane : lane + HEAD_DIM])
        parts.append(across[0, half, :, pl.ds(low, HEAD_DIM)])
        parts.append(beside[1, half, :, lane : lane + HEAD_DIM])
    return jnp.concatenate(parts, axis=0)


def key_bias(my_blk, lengths, chips, block_tok, sub_tok, half, core):
    blk_count = 2 * chips
    my_block = my_blk if half == 0 else 2 * blk_count - 1 - my_blk
    lane = lax.broadcasted_iota(jnp.int32, (1, LANES), 1)
    sender = lax.axis_index("head") ^ (lane % block_tok // sub_tok)
    q_pos = my_block * block_tok + sender * sub_tok + lane % sub_tok
    first = jnp.zeros_like(q_pos)
    bound = jnp.zeros_like(lengths[:, :1])
    for k in range(lengths.shape[1] - 1):
        bound = bound + lengths[:, k : k + 1]
        first = jnp.where(q_pos >= bound, bound, first)
    row = lax.broadcasted_iota(jnp.int32, (block_tok, LANES), 0)
    parts = []
    for m in range(chips):
        owner = (my_blk ^ core) ^ (2 * m)
        for side in range(half + 1):
            block = owner if side == 0 else 2 * blk_count - 1 - owner
            if core == 0 and m == 0 and side == half:
                allowed = (row <= q_pos - block * block_tok) & (row >= first - block * block_tok)
            else:
                allowed = row >= first - jnp.where(block < my_block, block * block_tok, -(2**28))
            parts.append(jnp.where(allowed, 0.0, -1e30))
    return jnp.concatenate(parts, axis=0)


def page_targets(my_blk, page_slot, chips, slot_count, core):
    _, pages_blk, blk_count = page_slot.shape
    chip = lax.broadcasted_iota(jnp.int32, (chips, blk_count), 0)
    owner = (my_blk ^ core) ^ (2 * chip)
    chosen = (owner == lax.broadcasted_iota(jnp.int32, (chips, blk_count), 1)).astype(jnp.float32).astype(jnp.bfloat16)
    cols = 2 * pages_blk * PAGE
    page = lax.broadcasted_iota(jnp.int32, (pages_blk, cols), 0)
    col = lax.broadcasted_iota(jnp.int32, (pages_blk, cols), 1)
    slots = 0.0
    for half in range(2):
        held = lax.dot_general(
            chosen,
            page_slot[half].astype(jnp.float32).astype(jnp.bfloat16),
            (((1,), (1,)), ((), ())),
            preferred_element_type=jnp.float32,
        )
        spread = (col // PAGE == page + half * pages_blk).astype(jnp.float32).astype(jnp.bfloat16)
        slots = slots + jnp.dot(held.astype(jnp.bfloat16), spread, preferred_element_type=jnp.float32)
    slots = slots.astype(jnp.int32) - my_blk * slot_count
    rows = slots * PAGE + lax.broadcasted_iota(jnp.int32, slots.shape, 1) % PAGE
    return jnp.concatenate([rows[m : m + 1] for m in range(chips)], axis=1)


def place_pages(targets, pairs, slot_count):
    rows = pairs[...].reshape(-1, pairs.shape[-1])
    row = lax.broadcasted_iota(jnp.int32, (slot_count * PAGE, rows.shape[0]), 0)
    chosen = jnp.where(row == targets, 1.0, 0.0).astype(jnp.bfloat16)
    return jnp.dot(chosen, rows, preferred_element_type=jnp.float32)


def score_part(queries, pairs, half):
    keys = pairs[:, : half + 1].reshape(-1, 2 * HEAD_DIM)[:, :HEAD_DIM]
    return lax.dot_general(keys, queries, (((1,), (1,)), ((), ())), preferred_element_type=jnp.float32)


def weigh_part(scores, bias, pairs, half):
    values = pairs[:, : half + 1].reshape(-1, 2 * HEAD_DIM)[:, HEAD_DIM:]
    bias = jnp.concatenate([bias] * (scores.shape[1] // LANES), axis=1)
    scores = scores * (HEAD_DIM**-0.5 * LOG2E) + bias
    top = jnp.max(scores, axis=0, keepdims=True)
    weights = jnp.exp2(scores - top)
    total = jnp.sum(weights, axis=0, keepdims=True)
    out = lax.dot_general(
        values, weights.astype(jnp.bfloat16), (((0,), (0,)), ((), ())), preferred_element_type=jnp.float32
    )
    return top, total, out


def near_kernel(
    lengths, page_slot, own, across, beside, near, q_rows, top_ref, total_ref, out_ref, pages_ref, far_bias_a,
    far_bias_b, far_targets,
):
    chips, _, block_tok, _ = near.shape
    slot_count = pages_ref.shape[0] // PAGE
    my_blk = lax.axis_index("blk")
    bias = functools.partial(key_bias, my_blk, lengths[...] - lax.axis_index("head"), chips, block_tok, own.shape[2])
    for half in (1, 0):
        queries = gather_queries(own, across, beside, half)
        q_rows[half] = queries
        top, total, out = weigh_part(score_part(queries, near, half), bias(half, 0), near, half)
        top_ref[half] = top
        total_ref[half] = total
        out_ref[half] = out
        (far_bias_a, far_bias_b)[half][...] = bias(half, 1)
    targets = functools.partial(page_targets, my_blk, page_slot, chips, slot_count)
    pages_ref[...] = place_pages(targets(0), near, slot_count).astype(jnp.bfloat16)
    far_targets[...] = targets(1)


def far_kernel(
    far, q_rows, top_ref, total_ref, out_ref, pages_ref, far_bias_a, far_bias_b, far_targets, attended, kv_cache,
    pages, result, sems,
):
    block_tok = far.shape[2]
    slot_count = kv_cache.shape[0]
    my_head = lax.axis_index("head")
    sub_tok = block_tok // lax.axis_size("head")
    moved = place_pages(far_targets[...], far, slot_count) + pages_ref[...].astype(jnp.float32)
    pages[...] = moved.astype(jnp.bfloat16).reshape(pages.shape)
    writes = [pltpu.make_async_copy(pages, kv_cache, sems.at[2])]
    writes[0].start()
    for half in (1, 0):
        bias = (far_bias_a, far_bias_b)[half][...]
        top, total, out = weigh_part(score_part(q_rows[half], far, half), bias, far, half)
        best = jnp.maximum(top, top_ref[half])
        here = jnp.exp2(top - best)
        there = jnp.exp2(top_ref[half] - best)
        inverse = 1.0 / (total * here + total_ref[half] * there)
        out = (out * (here * inverse) + out_ref[half] * (there * inverse)).T.astype(jnp.bfloat16)
        for g in range(out.shape[0] // block_tok):
            for d in range(block_tok // sub_tok):
                row = pl.multiple_of((my_head ^ d) * sub_tok, sub_tok)
                start = g * block_tok + d * sub_tok
                result[half, pl.ds(row, sub_tok), g * HEAD_DIM : (g + 1) * HEAD_DIM] = out[start : start + sub_tok]
        writes.append(pltpu.make_async_copy(result.at[half], attended.at[0, half], sems.at[half]))
        writes[-1].start()
    for write in writes:
        write.wait()


def per_device(query_states, key_states, value_states, doc_lengths, page_slot):
    blk_count = lax.axis_size("blk")
    head_count = lax.axis_size("head")
    q_width = query_states.shape[3]
    block_tok = key_states.shape[2]
    width = q_width // head_count
    rows = width // HEAD_DIM * block_tok
    slot_count = 4 * (block_tok // PAGE)

    my_head = lax.axis_index("head")
    part = lax.dynamic_slice_in_dim(query_states, ((my_head & 2) ^ 2) * width, 2 * width, axis=3)
    across = lax.ppermute(part, "head", [(i, i ^ 2) for i in range(head_count)])
    pair = jnp.concatenate([key_states, value_states], axis=3)
    lengths = doc_lengths + my_head
    pair, lengths, _ = lax.optimization_barrier((pair, lengths, part))
    near = [
        lax.ppermute(pair, "blk", [(i, i ^ d) for i in range(blk_count)]) for d in range(2, blk_count, 2)
    ]
    beside = jnp.concatenate(
        [
            lax.dynamic_slice_in_dim(query_states, (my_head ^ 1) * width, width, axis=3),
            lax.dynamic_slice_in_dim(across, ((my_head & 1) ^ 1) * width, width, axis=3),
        ],
        axis=0,
    )
    near = lax.optimization_barrier((near[::-1], beside))[0][::-1]
    beside = lax.ppermute(beside, "head", [(i, i ^ 1) for i in range(head_count)])
    near = jnp.concatenate([pair] + near, axis=0)
    far = lax.ppermute(near, "blk", [(i, i ^ 1) for i in range(blk_count)])

    hbm = pl.BlockSpec(memory_space=pl.ANY)
    vmem = pl.BlockSpec(memory_space=pltpu.VMEM)
    params = pltpu.CompilerParams(vmem_limit_bytes=32 * 1024 * 1024)
    cost = pl.CostEstimate(flops=4_000_000_000, bytes_accessed=1_000_000, transcendentals=200_000)
    half_cols = blk_count // 2 * block_tok
    stats = pl.pallas_call(
        near_kernel,
        out_shape=(
            jax.ShapeDtypeStruct((2, rows, HEAD_DIM), jnp.bfloat16),
            jax.ShapeDtypeStruct((2, 1, rows), jnp.float32),
            jax.ShapeDtypeStruct((2, 1, rows), jnp.float32),
            jax.ShapeDtypeStruct((2, HEAD_DIM, rows), jnp.float32),
            jax.ShapeDtypeStruct((slot_count * PAGE, 2 * HEAD_DIM), jnp.bfloat16),
            jax.ShapeDtypeStruct((half_cols, LANES), jnp.float32),
            jax.ShapeDtypeStruct((2 * half_cols, LANES), jnp.float32),
            jax.ShapeDtypeStruct((1, 2 * half_cols), jnp.int32),
        ),
        in_specs=[vmem] * 6,
        out_specs=(vmem,) * 8,
        compiler_params=params,
        cost_estimate=cost,
    )(lengths.reshape(1, -1), page_slot.transpose(1, 2, 0), query_states, across, beside, near)
    return pl.pallas_call(
        far_kernel,
        out_shape=(
            jax.ShapeDtypeStruct((1, 2, block_tok, width), jnp.bfloat16),
            jax.ShapeDtypeStruct((slot_count, 1, PAGE, 2 * HEAD_DIM), jnp.bfloat16),
        ),
        in_specs=[vmem] * 9,
        out_specs=(hbm, hbm),
        scratch_shapes=[
            pltpu.VMEM((slot_count, 1, PAGE, 2 * HEAD_DIM), jnp.bfloat16),
            pltpu.VMEM((2, block_tok, width), jnp.bfloat16),
            pltpu.SemaphoreType.DMA((3,)),
        ],
        compiler_params=params,
        cost_estimate=cost,
    )(far, *stats)


def per_device_long(query_states, key_states, value_states, doc_lengths, page_slot):
    q_local = lax.all_to_all(query_states, "head", split_axis=3, concat_axis=2, tiled=True)
    axis_count = lax.axis_size("blk")
    my_index = lax.axis_index("blk")
    block_tok = q_local.shape[2]
    head_dim = key_states.shape[3]
    group_size = q_local.shape[3] // head_dim
    query_rows = q_local.reshape(2 * block_tok, group_size, head_dim)
    offsets = jnp.arange(block_tok, dtype=jnp.int32)
    doc_bounds = jnp.cumsum(doc_lengths)[:-1]
    page_count = block_tok // PAGE
    slot_count = 4 * page_count
    slot_range = jnp.arange(slot_count, dtype=jnp.int32)
    score_scale = head_dim ** (-0.5)

    def group_positions(owner_ids):
        block_starts = jnp.stack([owner_ids, 2 * axis_count - 1 - owner_ids], axis=1) * block_tok
        return (block_starts[:, :, None] + offsets[None, None, :]).reshape(-1)

    def doc_of(positions):
        return jnp.sum((positions[:, None] >= doc_bounds[None, :]).astype(jnp.int32), axis=1)

    q_pos = group_positions(my_index.reshape(1))
    q_doc = doc_of(q_pos)

    def attend_group(attn_state, key_rows, value_rows, allowed):
        running_max, weight_sum, accum = attn_state
        scores = (
            jnp.einsum("qhd,kd->qhk", query_rows, key_rows, preferred_element_type=jnp.float32)
            * score_scale
        )
        masked = jnp.where(allowed[:, None, :], scores, -1e30)
        new_max = jnp.maximum(running_max, jnp.max(masked, axis=2))
        weights = jnp.where(allowed[:, None, :], jnp.exp(masked - new_max[..., None]), 0.0)
        factor = jnp.exp(running_max - new_max)
        weight_sum = weight_sum * factor + jnp.sum(weights, axis=2)
        update = jnp.einsum(
            "qhk,kd->qhd",
            weights.astype(jnp.bfloat16),
            value_rows,
            preferred_element_type=jnp.float32,
        )
        accum = accum * factor[..., None] + update
        return (new_max, weight_sum, accum)

    def visit_group(attn_state, key_group, value_group, owner_ids):
        key_rows = key_group.reshape(-1, head_dim)
        value_rows = value_group.reshape(-1, head_dim)
        k_pos = group_positions(owner_ids)
        allowed = (k_pos[None, :] <= q_pos[:, None]) & (doc_of(k_pos)[None, :] == q_doc[:, None])
        return attend_group(attn_state, key_rows, value_rows, allowed)

    def place_pages(page_store, key_group, value_group, owner_ids):
        page_rows = jnp.concatenate([key_group, value_group], axis=-1).reshape(
            -1, PAGE * 2 * head_dim
        )
        slot_ids = jnp.take(page_slot, owner_ids, axis=0).reshape(-1) - my_index * slot_count
        selector = (slot_range[:, None] == slot_ids[None, :]).astype(jnp.bfloat16)
        return page_store + jnp.dot(selector, page_rows, preferred_element_type=jnp.float32)

    def fold_groups(step_fn, carried, kv_piece):
        key_piece, value_piece = kv_piece
        piece_len = key_piece.shape[0]
        width = 4
        owner_ids = jnp.arange(piece_len, dtype=jnp.int32).reshape(piece_len // width, width)
        key_groups = key_piece.reshape(piece_len // width, width, 2, block_tok, head_dim)
        value_groups = value_piece.reshape(piece_len // width, width, 2, block_tok, head_dim)

        def visit_one(inner_state, entry_tuple):
            key_group, value_group, owners = entry_tuple
            return (step_fn(inner_state, key_group, value_group, owners), None)

        return lax.scan(visit_one, carried, (key_groups, value_groups, owner_ids))[0]

    empty_store = jnp.zeros((slot_count, PAGE * 2 * head_dim), jnp.float32)
    start_state = (
        jnp.full((2 * block_tok, group_size), -1e30, jnp.float32),
        jnp.zeros((2 * block_tok, group_size), jnp.float32),
        jnp.zeros((2 * block_tok, group_size, head_dim), jnp.float32),
    )
    final_state = fold_groups(
        visit_group,
        start_state,
        (
            lax.all_gather(key_states, "blk", axis=0, tiled=True),
            lax.all_gather(value_states, "blk", axis=0, tiled=True),
        ),
    )
    page_store = fold_groups(
        place_pages,
        empty_store,
        (
            lax.all_gather(key_states, "blk", axis=0, tiled=True),
            lax.all_gather(value_states, "blk", axis=0, tiled=True),
        ),
    )
    running_max, weight_sum, accum = final_state
    attended = (
        (accum / weight_sum[..., None])
        .astype(jnp.bfloat16)
        .reshape(1, 2, block_tok, group_size * head_dim)
    )
    kv_cache = page_store.astype(jnp.bfloat16).reshape(slot_count, 1, PAGE, 2 * head_dim)
    return (attended, kv_cache)


def solution(mesh):
    return jax.shard_map(
        per_device if mesh.shape["blk"] <= 8 else per_device_long,
        mesh=mesh,
        in_specs=(
            P("blk", None, "head", None),
            P("blk", None, None, "head"),
            P("blk", None, None, "head"),
            P(),
            P(),
        ),
        out_specs=(P("blk", None, None, "head"), P("blk", "head", None, None)),
        check_vma=False,
    )
```

```python
import functools

import jax
import jax.numpy as jnp
from jax import lax
from jax.experimental import pallas as pl
from jax.experimental.pallas import tpu as pltpu
from jax.sharding import PartitionSpec as P

PAGE = 16
LOG2E = 1.4426950408889634
HEAD_DIM = 128
LANES = 128


def gather_queries(own, across, beside, half):
    my_head = lax.axis_index("head")
    width = beside.shape[-1]
    parts = []
    for lane in range(0, width, HEAD_DIM):
        mine = pl.multiple_of(my_head * width + lane, HEAD_DIM)
        low = pl.multiple_of((my_head & 1) * width + lane, HEAD_DIM)
        parts.append(own[0, half, :, pl.ds(mine, HEAD_DIM)])
        parts.append(beside[0, half, :, lane : lane + HEAD_DIM])
        parts.append(across[0, half, :, pl.ds(low, HEAD_DIM)])
        parts.append(beside[1, half, :, lane : lane + HEAD_DIM])
    return jnp.concatenate(parts, axis=0)


def owners_of(my_blk, far):
    side = 2 << (my_blk & 1)
    if far:
        return [my_blk ^ 7 ^ side, my_blk ^ 6 ^ side, my_blk ^ 7]
    return [my_blk, my_blk ^ 1, my_blk ^ side, my_blk ^ 1 ^ side, my_blk ^ 6]


def key_bias(my_blk, lengths, blk_count, block_tok, sub_tok, half, far):
    my_block = my_blk if half == 0 else 2 * blk_count - 1 - my_blk
    lane = lax.broadcasted_iota(jnp.int32, (1, LANES), 1)
    sender = lax.axis_index("head") ^ (lane % block_tok // sub_tok)
    q_pos = my_block * block_tok + sender * sub_tok + lane % sub_tok
    first = jnp.zeros_like(q_pos)
    bound = jnp.zeros_like(lengths[:, :1])
    for k in range(lengths.shape[1] - 1):
        bound = bound + lengths[:, k : k + 1]
        first = jnp.where(q_pos >= bound, bound, first)
    row = lax.broadcasted_iota(jnp.int32, (block_tok, LANES), 0)
    parts = []
    for m, owner in enumerate(owners_of(my_blk, far)):
        for side in range(half + 1):
            block = owner if side == 0 else 2 * blk_count - 1 - owner
            if not far and m == 0 and side == half:
                allowed = (row <= q_pos - block * block_tok) & (row >= first - block * block_tok)
            else:
                allowed = row >= first - jnp.where(block < my_block, block * block_tok, -(2**28))
            parts.append(jnp.where(allowed, 0.0, -1e30))
    return jnp.concatenate(parts, axis=0)


def page_targets(my_blk, page_slot, slot_count, far):
    _, pages_blk, blk_count = page_slot.shape
    owners = owners_of(my_blk, far)
    shape = (len(owners), blk_count)
    piece = lax.broadcasted_iota(jnp.int32, shape, 0)
    owner = jnp.zeros(shape, jnp.int32)
    for m, held in enumerate(owners):
        owner = jnp.where(piece == m, held, owner)
    chosen = (owner == lax.broadcasted_iota(jnp.int32, shape, 1)).astype(jnp.float32).astype(jnp.bfloat16)
    cols = 2 * pages_blk * PAGE
    page = lax.broadcasted_iota(jnp.int32, (pages_blk, cols), 0)
    col = lax.broadcasted_iota(jnp.int32, (pages_blk, cols), 1)
    slots = 0.0
    for half in range(2):
        held = lax.dot_general(
            chosen,
            page_slot[half].astype(jnp.float32).astype(jnp.bfloat16),
            (((1,), (1,)), ((), ())),
            preferred_element_type=jnp.float32,
        )
        spread = (col // PAGE == page + half * pages_blk).astype(jnp.float32).astype(jnp.bfloat16)
        slots = slots + jnp.dot(held.astype(jnp.bfloat16), spread, preferred_element_type=jnp.float32)
    slots = slots.astype(jnp.int32) - my_blk * slot_count
    rows = slots * PAGE + lax.broadcasted_iota(jnp.int32, slots.shape, 1) % PAGE
    return jnp.concatenate([rows[m : m + 1] for m in range(len(owners))], axis=1)


def rows_of(pairs, halves, lane):
    return jnp.concatenate(
        [p[:, :halves, :, lane : lane + HEAD_DIM].reshape(-1, HEAD_DIM) for p in pairs], axis=0
    )


def place_pages(targets, pairs, slot_count):
    rows = jnp.concatenate([p[...].reshape(-1, p.shape[-1]) for p in pairs], axis=0)
    row = lax.broadcasted_iota(jnp.int32, (slot_count * PAGE, rows.shape[0]), 0)
    chosen = jnp.where(row == targets, 1.0, 0.0).astype(jnp.bfloat16)
    return jnp.dot(chosen, rows, preferred_element_type=jnp.float32)


def attend_part(queries, bias, pairs, half):
    scores = lax.dot_general(
        rows_of(pairs, half + 1, 0), queries, (((1,), (1,)), ((), ())), preferred_element_type=jnp.float32
    )
    bias = jnp.concatenate([bias] * (scores.shape[1] // LANES), axis=1)
    scores = scores * (HEAD_DIM**-0.5 * LOG2E) + bias
    top = jnp.max(scores, axis=0, keepdims=True)
    weights = jnp.exp2(scores - top)
    total = jnp.sum(weights, axis=0, keepdims=True)
    out = lax.dot_general(
        rows_of(pairs, half + 1, HEAD_DIM),
        weights.astype(jnp.bfloat16),
        (((0,), (0,)), ((), ())),
        preferred_element_type=jnp.float32,
    )
    return top, total, out


def near_kernel(
    lengths, page_slot, own, across, beside, chip, away, q_rows, top_ref, total_ref, out_ref, pages_ref, far_bias_a,
    far_bias_b, far_targets,
):
    blk_count = page_slot.shape[2]
    block_tok = chip.shape[2]
    slot_count = pages_ref.shape[0] // PAGE
    my_blk = lax.axis_index("blk")
    lengths = lengths[...] - lax.axis_index("head")
    bias = functools.partial(key_bias, my_blk, lengths, blk_count, block_tok, own.shape[2])
    for half in (1, 0):
        queries = gather_queries(own, across, beside, half)
        q_rows[half] = queries
        top, total, out = attend_part(queries, bias(half, False), (chip, away), half)
        top_ref[half] = top
        total_ref[half] = total
        out_ref[half] = out
        (far_bias_a, far_bias_b)[half][...] = bias(half, True)
    targets = functools.partial(page_targets, my_blk, page_slot, slot_count)
    pages_ref[...] = place_pages(targets(False), (chip, away), slot_count).astype(jnp.bfloat16)
    far_targets[...] = targets(True)


def far_kernel(
    far, q_rows, top_ref, total_ref, out_ref, pages_ref, far_bias_a, far_bias_b, far_targets, attended, kv_cache,
    pages, result, sems,
):
    block_tok = far.shape[2]
    slot_count = kv_cache.shape[0]
    my_head = lax.axis_index("head")
    sub_tok = block_tok // lax.axis_size("head")
    moved = place_pages(far_targets[...], (far,), slot_count) + pages_ref[...].astype(jnp.float32)
    pages[...] = moved.astype(jnp.bfloat16).reshape(pages.shape)
    writes = [pltpu.make_async_copy(pages, kv_cache, sems.at[2])]
    writes[0].start()
    for half in (1, 0):
        bias = (far_bias_a, far_bias_b)[half][...]
        top, total, out = attend_part(q_rows[half], bias, (far,), half)
        best = jnp.maximum(top, top_ref[half])
        here = jnp.exp2(top - best)
        there = jnp.exp2(top_ref[half] - best)
        inverse = 1.0 / (total * here + total_ref[half] * there)
        out = (out * (here * inverse) + out_ref[half] * (there * inverse)).T.astype(jnp.bfloat16)
        for g in range(out.shape[0] // block_tok):
            for d in range(block_tok // sub_tok):
                row = pl.multiple_of((my_head ^ d) * sub_tok, sub_tok)
                start = g * block_tok + d * sub_tok
                result[half, pl.ds(row, sub_tok), g * HEAD_DIM : (g + 1) * HEAD_DIM] = out[start : start + sub_tok]
        writes.append(pltpu.make_async_copy(result.at[half], attended.at[0, half], sems.at[half]))
        writes[-1].start()
    for write in writes:
        write.wait()


def per_device(query_states, key_states, value_states, doc_lengths, page_slot):
    blk_count = lax.axis_size("blk")
    head_count = lax.axis_size("head")
    q_width = query_states.shape[3]
    block_tok = key_states.shape[2]
    width = q_width // head_count
    rows = width // HEAD_DIM * block_tok
    slot_count = 4 * (block_tok // PAGE)

    my_head = lax.axis_index("head")
    part = lax.dynamic_slice_in_dim(query_states, ((my_head & 2) ^ 2) * width, 2 * width, axis=3)
    across = lax.ppermute(part, "head", [(i, i ^ 2) for i in range(head_count)])
    pair = jnp.concatenate([key_states, value_states], axis=3)
    lengths = doc_lengths + my_head
    pair, lengths, _ = lax.optimization_barrier((pair, lengths, part))
    mate = lax.ppermute(pair, "blk", [(i, i ^ 1) for i in range(blk_count)])
    across_chip = lax.ppermute(pair, "blk", [(i, i ^ 6) for i in range(blk_count)])
    chip = jnp.concatenate([pair, mate], axis=0)
    next_chip = lax.ppermute(chip, "blk", [(i, i ^ (2 << (i & 1))) for i in range(blk_count)])
    beside = jnp.concatenate(
        [
            lax.dynamic_slice_in_dim(query_states, (my_head ^ 1) * width, width, axis=3),
            lax.dynamic_slice_in_dim(across, ((my_head & 1) ^ 1) * width, width, axis=3),
        ],
        axis=0,
    )
    across_chip, next_chip, _ = lax.optimization_barrier((across_chip, next_chip, beside))
    beside = lax.ppermute(beside, "head", [(i, i ^ 1) for i in range(head_count)])
    away = jnp.concatenate([next_chip, across_chip], axis=0)
    far = lax.ppermute(away, "blk", [(i, i ^ 1) for i in range(blk_count)])

    hbm = pl.BlockSpec(memory_space=pl.ANY)
    vmem = pl.BlockSpec(memory_space=pltpu.VMEM)
    params = pltpu.CompilerParams(vmem_limit_bytes=32 * 1024 * 1024)
    cost = pl.CostEstimate(flops=4_000_000_000, bytes_accessed=1_000_000, transcendentals=200_000)
    far_cols = far.shape[0] * block_tok
    stats = pl.pallas_call(
        near_kernel,
        out_shape=(
            jax.ShapeDtypeStruct((2, rows, HEAD_DIM), jnp.bfloat16),
            jax.ShapeDtypeStruct((2, 1, rows), jnp.float32),
            jax.ShapeDtypeStruct((2, 1, rows), jnp.float32),
            jax.ShapeDtypeStruct((2, HEAD_DIM, rows), jnp.float32),
            jax.ShapeDtypeStruct((slot_count * PAGE, 2 * HEAD_DIM), jnp.bfloat16),
            jax.ShapeDtypeStruct((far_cols, LANES), jnp.float32),
            jax.ShapeDtypeStruct((2 * far_cols, LANES), jnp.float32),
            jax.ShapeDtypeStruct((1, 2 * far_cols), jnp.int32),
        ),
        in_specs=[vmem] * 7,
        out_specs=(vmem,) * 8,
        compiler_params=params,
        cost_estimate=cost,
    )(lengths.reshape(1, -1), page_slot.transpose(1, 2, 0), query_states, across, beside, chip, away)
    return pl.pallas_call(
        far_kernel,
        out_shape=(
            jax.ShapeDtypeStruct((1, 2, block_tok, width), jnp.bfloat16),
            jax.ShapeDtypeStruct((slot_count, 1, PAGE, 2 * HEAD_DIM), jnp.bfloat16),
        ),
        in_specs=[vmem] * 9,
        out_specs=(hbm, hbm),
        scratch_shapes=[
            pltpu.VMEM((slot_count, 1, PAGE, 2 * HEAD_DIM), jnp.bfloat16),
            pltpu.VMEM((2, block_tok, width), jnp.bfloat16),
            pltpu.SemaphoreType.DMA((3,)),
        ],
        compiler_params=params,
        cost_estimate=cost,
    )(far, *stats)


def per_device_long(query_states, key_states, value_states, doc_lengths, page_slot):
    q_local = lax.all_to_all(query_states, "head", split_axis=3, concat_axis=2, tiled=True)
    axis_count = lax.axis_size("blk")
    my_index = lax.axis_index("blk")
    block_tok = q_local.shape[2]
    head_dim = key_states.shape[3]
    group_size = q_local.shape[3] // head_dim
    query_rows = q_local.reshape(2 * block_tok, group_size, head_dim)
    offsets = jnp.arange(block_tok, dtype=jnp.int32)
    doc_bounds = jnp.cumsum(doc_lengths)[:-1]
    page_count = block_tok // PAGE
    slot_count = 4 * page_count
    slot_range = jnp.arange(slot_count, dtype=jnp.int32)
    score_scale = head_dim ** (-0.5)

    def group_positions(owner_ids):
        block_starts = jnp.stack([owner_ids, 2 * axis_count - 1 - owner_ids], axis=1) * block_tok
        return (block_starts[:, :, None] + offsets[None, None, :]).reshape(-1)

    def doc_of(positions):
        return jnp.sum((positions[:, None] >= doc_bounds[None, :]).astype(jnp.int32), axis=1)

    q_pos = group_positions(my_index.reshape(1))
    q_doc = doc_of(q_pos)

    def attend_group(attn_state, key_rows, value_rows, allowed):
        running_max, weight_sum, accum = attn_state
        scores = (
            jnp.einsum("qhd,kd->qhk", query_rows, key_rows, preferred_element_type=jnp.float32)
            * score_scale
        )
        masked = jnp.where(allowed[:, None, :], scores, -1e30)
        new_max = jnp.maximum(running_max, jnp.max(masked, axis=2))
        weights = jnp.where(allowed[:, None, :], jnp.exp(masked - new_max[..., None]), 0.0)
        factor = jnp.exp(running_max - new_max)
        weight_sum = weight_sum * factor + jnp.sum(weights, axis=2)
        update = jnp.einsum(
            "qhk,kd->qhd",
            weights.astype(jnp.bfloat16),
            value_rows,
            preferred_element_type=jnp.float32,
        )
        accum = accum * factor[..., None] + update
        return (new_max, weight_sum, accum)

    def visit_group(attn_state, key_group, value_group, owner_ids):
        key_rows = key_group.reshape(-1, head_dim)
        value_rows = value_group.reshape(-1, head_dim)
        k_pos = group_positions(owner_ids)
        allowed = (k_pos[None, :] <= q_pos[:, None]) & (doc_of(k_pos)[None, :] == q_doc[:, None])
        return attend_group(attn_state, key_rows, value_rows, allowed)

    def place_pages(page_store, key_group, value_group, owner_ids):
        page_rows = jnp.concatenate([key_group, value_group], axis=-1).reshape(
            -1, PAGE * 2 * head_dim
        )
        slot_ids = jnp.take(page_slot, owner_ids, axis=0).reshape(-1) - my_index * slot_count
        selector = (slot_range[:, None] == slot_ids[None, :]).astype(jnp.bfloat16)
        return page_store + jnp.dot(selector, page_rows, preferred_element_type=jnp.float32)

    def fold_groups(step_fn, carried, kv_piece):
        key_piece, value_piece = kv_piece
        piece_len = key_piece.shape[0]
        width = 4
        owner_ids = jnp.arange(piece_len, dtype=jnp.int32).reshape(piece_len // width, width)
        key_groups = key_piece.reshape(piece_len // width, width, 2, block_tok, head_dim)
        value_groups = value_piece.reshape(piece_len // width, width, 2, block_tok, head_dim)

        def visit_one(inner_state, entry_tuple):
            key_group, value_group, owners = entry_tuple
            return (step_fn(inner_state, key_group, value_group, owners), None)

        return lax.scan(visit_one, carried, (key_groups, value_groups, owner_ids))[0]

    empty_store = jnp.zeros((slot_count, PAGE * 2 * head_dim), jnp.float32)
    start_state = (
        jnp.full((2 * block_tok, group_size), -1e30, jnp.float32),
        jnp.zeros((2 * block_tok, group_size), jnp.float32),
        jnp.zeros((2 * block_tok, group_size, head_dim), jnp.float32),
    )
    final_state = fold_groups(
        visit_group,
        start_state,
        (
            lax.all_gather(key_states, "blk", axis=0, tiled=True),
            lax.all_gather(value_states, "blk", axis=0, tiled=True),
        ),
    )
    page_store = fold_groups(
        place_pages,
        empty_store,
        (
            lax.all_gather(key_states, "blk", axis=0, tiled=True),
            lax.all_gather(value_states, "blk", axis=0, tiled=True),
        ),
    )
    running_max, weight_sum, accum = final_state
    attended = (
        (accum / weight_sum[..., None])
        .astype(jnp.bfloat16)
        .reshape(1, 2, block_tok, group_size * head_dim)
    )
    kv_cache = page_store.astype(jnp.bfloat16).reshape(slot_count, 1, PAGE, 2 * head_dim)
    return (attended, kv_cache)


def solution(mesh):
    return jax.shard_map(
        per_device if (mesh.shape["blk"], mesh.shape["head"]) == (8, 4) else per_device_long,
        mesh=mesh,
        in_specs=(
            P("blk", None, "head", None),
            P("blk", None, None, "head"),
            P("blk", None, None, "head"),
            P(),
            P(),
        ),
        out_specs=(P("blk", None, None, "head"), P("blk", "head", None, None)),
        check_vma=False,
    )
```

```python
import functools

import jax
import jax.numpy as jnp
from jax import lax
from jax.experimental import pallas as pl
from jax.experimental.pallas import tpu as pltpu
from jax.sharding import PartitionSpec as P

PAGE = 16
LOG2E = 1.4426950408889634
HEAD_DIM = 128
LANES = 128


def gather_queries(own, across, beside, half):
    my_head = lax.axis_index("head")
    width = beside.shape[-1]
    parts = []
    for lane in range(0, width, HEAD_DIM):
        mine = pl.multiple_of(my_head * width + lane, HEAD_DIM)
        low = pl.multiple_of((my_head & 1) * width + lane, HEAD_DIM)
        parts.append(own[0, half, :, pl.ds(mine, HEAD_DIM)])
        parts.append(beside[0, half, :, lane : lane + HEAD_DIM])
        parts.append(across[0, half, :, pl.ds(low, HEAD_DIM)])
        parts.append(beside[1, half, :, lane : lane + HEAD_DIM])
    return jnp.concatenate(parts, axis=0)


def key_bias(my_blk, lengths, chips, block_tok, sub_tok, half, core):
    blk_count = 2 * chips
    my_block = my_blk if half == 0 else 2 * blk_count - 1 - my_blk
    lane = lax.broadcasted_iota(jnp.int32, (1, LANES), 1)
    sender = lax.axis_index("head") ^ (lane % block_tok // sub_tok)
    q_pos = my_block * block_tok + sender * sub_tok + lane % sub_tok
    first = jnp.zeros_like(q_pos)
    bound = jnp.zeros_like(lengths[:, :1])
    for k in range(lengths.shape[1] - 1):
        bound = bound + lengths[:, k : k + 1]
        first = jnp.where(q_pos >= bound, bound, first)
    row = lax.broadcasted_iota(jnp.int32, (block_tok, LANES), 0)
    parts = []
    for m in range(chips):
        owner = (my_blk ^ core) ^ (2 * m)
        for side in range(half + 1):
            block = owner if side == 0 else 2 * blk_count - 1 - owner
            if core == 0 and m == 0 and side == half:
                allowed = (row <= q_pos - block * block_tok) & (row >= first - block * block_tok)
            else:
                allowed = row >= first - jnp.where(block < my_block, block * block_tok, -(2**28))
            parts.append(jnp.where(allowed, 0.0, -1e30))
    return jnp.concatenate(parts, axis=0)


def page_targets(my_blk, page_slot, chips, slot_count, core):
    _, pages_blk, blk_count = page_slot.shape
    chip = lax.broadcasted_iota(jnp.int32, (chips, blk_count), 0)
    owner = (my_blk ^ core) ^ (2 * chip)
    chosen = (owner == lax.broadcasted_iota(jnp.int32, (chips, blk_count), 1)).astype(jnp.float32).astype(jnp.bfloat16)
    cols = 2 * pages_blk * PAGE
    page = lax.broadcasted_iota(jnp.int32, (pages_blk, cols), 0)
    col = lax.broadcasted_iota(jnp.int32, (pages_blk, cols), 1)
    slots = 0.0
    for half in range(2):
        held = lax.dot_general(
            chosen,
            page_slot[half].astype(jnp.float32).astype(jnp.bfloat16),
            (((1,), (1,)), ((), ())),
            preferred_element_type=jnp.float32,
        )
        spread = (col // PAGE == page + half * pages_blk).astype(jnp.float32).astype(jnp.bfloat16)
        slots = slots + jnp.dot(held.astype(jnp.bfloat16), spread, preferred_element_type=jnp.float32)
    slots = slots.astype(jnp.int32) - my_blk * slot_count
    rows = slots * PAGE + lax.broadcasted_iota(jnp.int32, slots.shape, 1) % PAGE
    return jnp.concatenate([rows[m : m + 1] for m in range(chips)], axis=1)


def place_pages(targets, pairs, slot_count):
    rows = pairs[...].reshape(-1, pairs.shape[-1])
    row = lax.broadcasted_iota(jnp.int32, (slot_count * PAGE, rows.shape[0]), 0)
    chosen = jnp.where(row == targets, 1.0, 0.0).astype(jnp.bfloat16)
    return jnp.dot(chosen, rows, preferred_element_type=jnp.float32)


def score_part(queries, pairs, half):
    keys = pairs[:, : half + 1].reshape(-1, 2 * HEAD_DIM)[:, :HEAD_DIM]
    return lax.dot_general(keys, queries, (((1,), (1,)), ((), ())), preferred_element_type=jnp.float32)


def soften(scores, bias):
    bias = jnp.concatenate([bias] * (scores.shape[1] // LANES), axis=1)
    scores = scores * (HEAD_DIM**-0.5 * LOG2E) + bias
    top = jnp.max(scores, axis=0, keepdims=True)
    weights = jnp.exp2(scores - top)
    return top, jnp.sum(weights, axis=0, keepdims=True), weights.astype(jnp.bfloat16)


def weigh_part(weights, pairs, half):
    values = pairs[:, : half + 1].reshape(-1, 2 * HEAD_DIM)[:, HEAD_DIM:]
    return lax.dot_general(values, weights, (((0,), (0,)), ((), ())), preferred_element_type=jnp.float32)


def near_kernel(
    lengths, page_slot, own, across, beside, near, q_rows, top_ref, total_ref, out_ref, pages_ref, far_bias_a,
    far_bias_b, far_targets,
):
    chips, _, block_tok, _ = near.shape
    slot_count = pages_ref.shape[0] // PAGE
    my_blk = lax.axis_index("blk")
    bias = functools.partial(key_bias, my_blk, lengths[...] - lax.axis_index("head"), chips, block_tok, own.shape[2])
    targets = functools.partial(page_targets, my_blk, page_slot, chips, slot_count)
    scores = {}
    for half in (1, 0):
        queries = gather_queries(own, across, beside, half)
        q_rows[half] = queries
        scores[half] = score_part(queries, near, half)
    for half in (1, 0):
        top_ref[half], total_ref[half], weights = soften(scores[half], bias(half, 0))
        out_ref[half] = weigh_part(weights, near, half)
    pages_ref[...] = place_pages(targets(0), near, slot_count).astype(jnp.bfloat16)
    for half in (1, 0):
        (far_bias_a, far_bias_b)[half][...] = bias(half, 1)
    far_targets[...] = targets(1)


def far_kernel(
    far, q_rows, top_ref, total_ref, out_ref, pages_ref, bias_a, bias_b, far_targets, attended, kv_cache,
    pages, result, sems,
):
    block_tok = far.shape[2]
    slot_count = kv_cache.shape[0]
    my_head = lax.axis_index("head")
    sub_tok = block_tok // lax.axis_size("head")
    scores = {half: score_part(q_rows[half], far, half) for half in (1, 0)}
    moved = place_pages(far_targets[...], far, slot_count) + pages_ref[...].astype(jnp.float32)
    pages[...] = moved.astype(jnp.bfloat16).reshape(pages.shape)
    writes = [pltpu.make_async_copy(pages, kv_cache, sems.at[2])]
    writes[0].start()
    parts = {}
    for half in (1, 0):
        top, total, weights = soften(scores[half], (bias_a, bias_b)[half][...])
        parts[half] = (top, total, weigh_part(weights, far, half))
    for half in (1, 0):
        top, total, out = parts[half]
        best = jnp.maximum(top, top_ref[half])
        here = jnp.exp2(top - best)
        there = jnp.exp2(top_ref[half] - best)
        inverse = 1.0 / (total * here + total_ref[half] * there)
        out = (out * (here * inverse) + out_ref[half] * (there * inverse)).T.astype(jnp.bfloat16)
        for g in range(out.shape[0] // block_tok):
            for d in range(block_tok // sub_tok):
                row = pl.multiple_of((my_head ^ d) * sub_tok, sub_tok)
                start = g * block_tok + d * sub_tok
                result[half, pl.ds(row, sub_tok), g * HEAD_DIM : (g + 1) * HEAD_DIM] = out[start : start + sub_tok]
        writes.append(pltpu.make_async_copy(result.at[half], attended.at[0, half], sems.at[half]))
        writes[-1].start()
    for write in writes:
        write.wait()


def per_device(query_states, key_states, value_states, doc_lengths, page_slot):
    blk_count = lax.axis_size("blk")
    head_count = lax.axis_size("head")
    q_width = query_states.shape[3]
    block_tok = key_states.shape[2]
    width = q_width // head_count
    rows = width // HEAD_DIM * block_tok
    slot_count = 4 * (block_tok // PAGE)

    my_head = lax.axis_index("head")
    part = lax.dynamic_slice_in_dim(query_states, ((my_head & 2) ^ 2) * width, 2 * width, axis=3)
    across = lax.ppermute(part, "head", [(i, i ^ 2) for i in range(head_count)])
    pair = jnp.concatenate([key_states, value_states], axis=3)
    lengths = doc_lengths + my_head
    pair, lengths, _ = lax.optimization_barrier((pair, lengths, part))
    near = [
        lax.ppermute(pair, "blk", [(i, i ^ d) for i in range(blk_count)]) for d in range(2, blk_count, 2)
    ]
    beside = jnp.concatenate(
        [
            lax.dynamic_slice_in_dim(query_states, (my_head ^ 1) * width, width, axis=3),
            lax.dynamic_slice_in_dim(across, ((my_head & 1) ^ 1) * width, width, axis=3),
        ],
        axis=0,
    )
    near = lax.optimization_barrier((near[::-1], beside))[0][::-1]
    beside = lax.ppermute(beside, "head", [(i, i ^ 1) for i in range(head_count)])
    near = jnp.concatenate([pair] + near, axis=0)
    far = lax.ppermute(near, "blk", [(i, i ^ 1) for i in range(blk_count)])

    hbm = pl.BlockSpec(memory_space=pl.ANY)
    vmem = pl.BlockSpec(memory_space=pltpu.VMEM)
    params = pltpu.CompilerParams(vmem_limit_bytes=32 * 1024 * 1024)
    cost = pl.CostEstimate(flops=4_000_000_000, bytes_accessed=1_000_000, transcendentals=200_000)
    half_cols = blk_count // 2 * block_tok
    stats = pl.pallas_call(
        near_kernel,
        out_shape=(
            jax.ShapeDtypeStruct((2, rows, HEAD_DIM), jnp.bfloat16),
            jax.ShapeDtypeStruct((2, 1, rows), jnp.float32),
            jax.ShapeDtypeStruct((2, 1, rows), jnp.float32),
            jax.ShapeDtypeStruct((2, HEAD_DIM, rows), jnp.float32),
            jax.ShapeDtypeStruct((slot_count * PAGE, 2 * HEAD_DIM), jnp.bfloat16),
            jax.ShapeDtypeStruct((half_cols, LANES), jnp.float32),
            jax.ShapeDtypeStruct((2 * half_cols, LANES), jnp.float32),
            jax.ShapeDtypeStruct((1, 2 * half_cols), jnp.int32),
        ),
        in_specs=[vmem] * 6,
        out_specs=(vmem,) * 8,
        compiler_params=params,
        cost_estimate=cost,
    )(lengths.reshape(1, -1), page_slot.transpose(1, 2, 0), query_states, across, beside, near)
    return pl.pallas_call(
        far_kernel,
        out_shape=(
            jax.ShapeDtypeStruct((1, 2, block_tok, width), jnp.bfloat16),
            jax.ShapeDtypeStruct((slot_count, 1, PAGE, 2 * HEAD_DIM), jnp.bfloat16),
        ),
        in_specs=[vmem] * 9,
        out_specs=(hbm, hbm),
        scratch_shapes=[
            pltpu.VMEM((slot_count, 1, PAGE, 2 * HEAD_DIM), jnp.bfloat16),
            pltpu.VMEM((2, block_tok, width), jnp.bfloat16),
            pltpu.SemaphoreType.DMA((3,)),
        ],
        compiler_params=params,
        cost_estimate=cost,
    )(far, *stats)


def per_device_long(query_states, key_states, value_states, doc_lengths, page_slot):
    q_local = lax.all_to_all(query_states, "head", split_axis=3, concat_axis=2, tiled=True)
    axis_count = lax.axis_size("blk")
    my_index = lax.axis_index("blk")
    block_tok = q_local.shape[2]
    head_dim = key_states.shape[3]
    group_size = q_local.shape[3] // head_dim
    query_rows = q_local.reshape(2 * block_tok, group_size, head_dim)
    offsets = jnp.arange(block_tok, dtype=jnp.int32)
    doc_bounds = jnp.cumsum(doc_lengths)[:-1]
    page_count = block_tok // PAGE
    slot_count = 4 * page_count
    slot_range = jnp.arange(slot_count, dtype=jnp.int32)
    score_scale = head_dim ** (-0.5)

    def group_positions(owner_ids):
        block_starts = jnp.stack([owner_ids, 2 * axis_count - 1 - owner_ids], axis=1) * block_tok
        return (block_starts[:, :, None] + offsets[None, None, :]).reshape(-1)

    def doc_of(positions):
        return jnp.sum((positions[:, None] >= doc_bounds[None, :]).astype(jnp.int32), axis=1)

    q_pos = group_positions(my_index.reshape(1))
    q_doc = doc_of(q_pos)

    def attend_group(attn_state, key_rows, value_rows, allowed):
        running_max, weight_sum, accum = attn_state
        scores = (
            jnp.einsum("qhd,kd->qhk", query_rows, key_rows, preferred_element_type=jnp.float32)
            * score_scale
        )
        masked = jnp.where(allowed[:, None, :], scores, -1e30)
        new_max = jnp.maximum(running_max, jnp.max(masked, axis=2))
        weights = jnp.where(allowed[:, None, :], jnp.exp(masked - new_max[..., None]), 0.0)
        factor = jnp.exp(running_max - new_max)
        weight_sum = weight_sum * factor + jnp.sum(weights, axis=2)
        update = jnp.einsum(
            "qhk,kd->qhd",
            weights.astype(jnp.bfloat16),
            value_rows,
            preferred_element_type=jnp.float32,
        )
        accum = accum * factor[..., None] + update
        return (new_max, weight_sum, accum)

    def visit_group(attn_state, key_group, value_group, owner_ids):
        key_rows = key_group.reshape(-1, head_dim)
        value_rows = value_group.reshape(-1, head_dim)
        k_pos = group_positions(owner_ids)
        allowed = (k_pos[None, :] <= q_pos[:, None]) & (doc_of(k_pos)[None, :] == q_doc[:, None])
        return attend_group(attn_state, key_rows, value_rows, allowed)

    def place_pages(page_store, key_group, value_group, owner_ids):
        page_rows = jnp.concatenate([key_group, value_group], axis=-1).reshape(
            -1, PAGE * 2 * head_dim
        )
        slot_ids = jnp.take(page_slot, owner_ids, axis=0).reshape(-1) - my_index * slot_count
        selector = (slot_range[:, None] == slot_ids[None, :]).astype(jnp.bfloat16)
        return page_store + jnp.dot(selector, page_rows, preferred_element_type=jnp.float32)

    def fold_groups(step_fn, carried, kv_piece):
        key_piece, value_piece = kv_piece
        piece_len = key_piece.shape[0]
        width = 4
        owner_ids = jnp.arange(piece_len, dtype=jnp.int32).reshape(piece_len // width, width)
        key_groups = key_piece.reshape(piece_len // width, width, 2, block_tok, head_dim)
        value_groups = value_piece.reshape(piece_len // width, width, 2, block_tok, head_dim)

        def visit_one(inner_state, entry_tuple):
            key_group, value_group, owners = entry_tuple
            return (step_fn(inner_state, key_group, value_group, owners), None)

        return lax.scan(visit_one, carried, (key_groups, value_groups, owner_ids))[0]

    empty_store = jnp.zeros((slot_count, PAGE * 2 * head_dim), jnp.float32)
    start_state = (
        jnp.full((2 * block_tok, group_size), -1e30, jnp.float32),
        jnp.zeros((2 * block_tok, group_size), jnp.float32),
        jnp.zeros((2 * block_tok, group_size, head_dim), jnp.float32),
    )
    final_state = fold_groups(
        visit_group,
        start_state,
        (
            lax.all_gather(key_states, "blk", axis=0, tiled=True),
            lax.all_gather(value_states, "blk", axis=0, tiled=True),
        ),
    )
    page_store = fold_groups(
        place_pages,
        empty_store,
        (
            lax.all_gather(key_states, "blk", axis=0, tiled=True),
            lax.all_gather(value_states, "blk", axis=0, tiled=True),
        ),
    )
    running_max, weight_sum, accum = final_state
    attended = (
        (accum / weight_sum[..., None])
        .astype(jnp.bfloat16)
        .reshape(1, 2, block_tok, group_size * head_dim)
    )
    kv_cache = page_store.astype(jnp.bfloat16).reshape(slot_count, 1, PAGE, 2 * head_dim)
    return (attended, kv_cache)


def solution(mesh):
    return jax.shard_map(
        per_device if mesh.shape["blk"] <= 8 else per_device_long,
        mesh=mesh,
        in_specs=(
            P("blk", None, "head", None),
            P("blk", None, None, "head"),
            P("blk", None, None, "head"),
            P(),
            P(),
        ),
        out_specs=(P("blk", None, None, "head"), P("blk", "head", None, None)),
        check_vma=False,
    )
```

```python
import functools

import jax
import jax.numpy as jnp
from jax import lax
from jax.experimental import pallas as pl
from jax.experimental.pallas import tpu as pltpu
from jax.sharding import PartitionSpec as P

PAGE = 16
LOG2E = 1.4426950408889634
HEAD_DIM = 128
LANES = 128


def gather_queries(q_all, half):
    senders, rows, width = q_all.shape
    sub_tok = rows // 2
    return jnp.concatenate(
        [
            q_all[d, half * sub_tok : (half + 1) * sub_tok, lane : lane + HEAD_DIM]
            for lane in range(0, width, HEAD_DIM)
            for d in range(senders)
        ],
        axis=0,
    )


def owners_of(my_blk, far):
    side = 2 << (my_blk & 1)
    if far:
        return [my_blk ^ 7 ^ side, my_blk ^ 6 ^ side, my_blk ^ 7]
    return [my_blk, my_blk ^ 1, my_blk ^ side, my_blk ^ 1 ^ side, my_blk ^ 6]


def key_bias(my_blk, lengths, blk_count, block_tok, half, far):
    my_block = my_blk if half == 0 else 2 * blk_count - 1 - my_blk
    q_pos = my_block * block_tok + lax.broadcasted_iota(jnp.int32, (1, LANES), 1) % block_tok
    first = jnp.zeros_like(q_pos)
    bound = jnp.zeros_like(lengths[:, :1])
    for k in range(lengths.shape[1] - 1):
        bound = bound + lengths[:, k : k + 1]
        first = jnp.where(q_pos >= bound, bound, first)
    row = lax.broadcasted_iota(jnp.int32, (block_tok, LANES), 0)
    parts = []
    for m, owner in enumerate(owners_of(my_blk, far)):
        for side in range(half + 1):
            block = owner if side == 0 else 2 * blk_count - 1 - owner
            if not far and m == 0 and side == half:
                allowed = (row <= q_pos - block * block_tok) & (row >= first - block * block_tok)
            else:
                allowed = row >= first - jnp.where(block < my_block, block * block_tok, -(2**28))
            parts.append(jnp.where(allowed, 0.0, -1e30))
    return jnp.concatenate(parts, axis=0)


def page_targets(my_blk, page_slot, slot_count, far):
    _, pages_blk, blk_count = page_slot.shape
    owners = owners_of(my_blk, far)
    shape = (len(owners), blk_count)
    piece = lax.broadcasted_iota(jnp.int32, shape, 0)
    owner = jnp.zeros(shape, jnp.int32)
    for m, held in enumerate(owners):
        owner = jnp.where(piece == m, held, owner)
    chosen = (owner == lax.broadcasted_iota(jnp.int32, shape, 1)).astype(jnp.float32).astype(jnp.bfloat16)
    cols = 2 * pages_blk * PAGE
    page = lax.broadcasted_iota(jnp.int32, (pages_blk, cols), 0)
    col = lax.broadcasted_iota(jnp.int32, (pages_blk, cols), 1)
    slots = 0.0
    for half in range(2):
        held = lax.dot_general(
            chosen,
            page_slot[half].astype(jnp.float32).astype(jnp.bfloat16),
            (((1,), (1,)), ((), ())),
            preferred_element_type=jnp.float32,
        )
        spread = (col // PAGE == page + half * pages_blk).astype(jnp.float32).astype(jnp.bfloat16)
        slots = slots + jnp.dot(held.astype(jnp.bfloat16), spread, preferred_element_type=jnp.float32)
    slots = slots.astype(jnp.int32) - my_blk * slot_count
    rows = slots * PAGE + lax.broadcasted_iota(jnp.int32, slots.shape, 1) % PAGE
    return jnp.concatenate([rows[m : m + 1] for m in range(len(owners))], axis=1)


def rows_of(pairs, halves, lane):
    return jnp.concatenate(
        [p[:, :halves, :, lane : lane + HEAD_DIM].reshape(-1, HEAD_DIM) for p in pairs], axis=0
    )


def place_pages(targets, pairs, slot_count):
    rows = jnp.concatenate([p[...].reshape(-1, p.shape[-1]) for p in pairs], axis=0)
    row = lax.broadcasted_iota(jnp.int32, (slot_count * PAGE, rows.shape[0]), 0)
    chosen = jnp.where(row == targets, 1.0, 0.0).astype(jnp.bfloat16)
    return jnp.dot(chosen, rows, preferred_element_type=jnp.float32)


def attend_part(queries, bias, pairs, half):
    scores = lax.dot_general(
        rows_of(pairs, half + 1, 0), queries, (((1,), (1,)), ((), ())), preferred_element_type=jnp.float32
    )
    bias = jnp.concatenate([bias] * (scores.shape[1] // LANES), axis=1)
    scores = scores * (HEAD_DIM**-0.5 * LOG2E) + bias
    top = jnp.max(scores, axis=0, keepdims=True)
    weights = jnp.exp2(scores - top)
    total = jnp.sum(weights, axis=0, keepdims=True)
    out = lax.dot_general(
        rows_of(pairs, half + 1, HEAD_DIM),
        weights.astype(jnp.bfloat16),
        (((0,), (0,)), ((), ())),
        preferred_element_type=jnp.float32,
    )
    return top, total, out


def near_kernel(
    lengths, page_slot, q_all, chip, away, q_rows, top_ref, total_ref, out_ref, pages_ref, far_bias_a, far_bias_b,
    far_targets,
):
    blk_count = page_slot.shape[2]
    block_tok = chip.shape[2]
    slot_count = pages_ref.shape[0] // PAGE
    my_blk = lax.axis_index("blk")
    bias = functools.partial(key_bias, my_blk, lengths[...], blk_count, block_tok)
    for half in (1, 0):
        queries = gather_queries(q_all, half)
        q_rows[half] = queries
        top, total, out = attend_part(queries, bias(half, False), (chip, away), half)
        top_ref[half] = top
        total_ref[half] = total
        out_ref[half] = out
        (far_bias_a, far_bias_b)[half][...] = bias(half, True)
    targets = functools.partial(page_targets, my_blk, page_slot, slot_count)
    pages_ref[...] = place_pages(targets(False), (chip, away), slot_count).astype(jnp.bfloat16)
    far_targets[...] = targets(True)


def far_kernel(
    far, q_rows, top_ref, total_ref, out_ref, pages_ref, far_bias_a, far_bias_b, far_targets, attended, kv_cache,
    pages, result, sems,
):
    block_tok = far.shape[2]
    slot_count = kv_cache.shape[0]
    moved = place_pages(far_targets[...], (far,), slot_count) + pages_ref[...].astype(jnp.float32)
    pages[...] = moved.astype(jnp.bfloat16).reshape(pages.shape)
    writes = [pltpu.make_async_copy(pages, kv_cache, sems.at[2])]
    writes[0].start()
    for half in (1, 0):
        bias = (far_bias_a, far_bias_b)[half][...]
        top, total, out = attend_part(q_rows[half], bias, (far,), half)
        best = jnp.maximum(top, top_ref[half])
        here = jnp.exp2(top - best)
        there = jnp.exp2(top_ref[half] - best)
        inverse = 1.0 / (total * here + total_ref[half] * there)
        out = (out * (here * inverse) + out_ref[half] * (there * inverse)).T.astype(jnp.bfloat16)
        for g in range(out.shape[0] // block_tok):
            result[half, :, g * HEAD_DIM : (g + 1) * HEAD_DIM] = out[g * block_tok : (g + 1) * block_tok]
        writes.append(pltpu.make_async_copy(result.at[half], attended.at[0, half], sems.at[half]))
        writes[-1].start()
    for write in writes:
        write.wait()


def per_device(query_states, key_states, value_states, doc_lengths, page_slot):
    blk_count = lax.axis_size("blk")
    head_count = lax.axis_size("head")
    q_width = query_states.shape[3]
    block_tok = key_states.shape[2]
    width = q_width // head_count
    rows = width // HEAD_DIM * block_tok
    slot_count = 4 * (block_tok // PAGE)

    my_head = lax.axis_index("head")
    pair = jnp.concatenate([key_states, value_states], axis=3)
    mate = lax.ppermute(pair, "blk", [(i, i ^ 1) for i in range(blk_count)])
    across_chip = lax.ppermute(pair, "blk", [(i, i ^ 6) for i in range(blk_count)])
    chip = jnp.concatenate([pair, mate], axis=0)
    next_chip = lax.ppermute(chip, "blk", [(i, i ^ (2 << (i & 1))) for i in range(blk_count)])
    query_states, chip = lax.optimization_barrier((query_states, chip))
    q_flat = query_states.reshape(-1, query_states.shape[3])
    q_split = jnp.stack([q_flat[:, h * width : (h + 1) * width] for h in range(head_count)])
    q_all = lax.cond(
        my_head < head_count,
        lambda q: lax.all_to_all(q, "head", split_axis=0, concat_axis=0, tiled=True),
        lambda q: q,
        q_split,
    )
    across_chip, next_chip, q_all = lax.optimization_barrier((across_chip, next_chip, q_all))
    away = jnp.concatenate([next_chip, across_chip], axis=0)
    far = lax.ppermute(away, "blk", [(i, i ^ 1) for i in range(blk_count)])

    hbm = pl.BlockSpec(memory_space=pl.ANY)
    vmem = pl.BlockSpec(memory_space=pltpu.VMEM)
    params = pltpu.CompilerParams(vmem_limit_bytes=32 * 1024 * 1024)
    cost = pl.CostEstimate(flops=4_000_000_000, bytes_accessed=1_000_000, transcendentals=200_000)
    far_cols = far.shape[0] * block_tok
    stats = pl.pallas_call(
        near_kernel,
        out_shape=(
            jax.ShapeDtypeStruct((2, rows, HEAD_DIM), jnp.bfloat16),
            jax.ShapeDtypeStruct((2, 1, rows), jnp.float32),
            jax.ShapeDtypeStruct((2, 1, rows), jnp.float32),
            jax.ShapeDtypeStruct((2, HEAD_DIM, rows), jnp.float32),
            jax.ShapeDtypeStruct((slot_count * PAGE, 2 * HEAD_DIM), jnp.bfloat16),
            jax.ShapeDtypeStruct((far_cols, LANES), jnp.float32),
            jax.ShapeDtypeStruct((2 * far_cols, LANES), jnp.float32),
            jax.ShapeDtypeStruct((1, 2 * far_cols), jnp.int32),
        ),
        in_specs=[vmem] * 5,
        out_specs=(vmem,) * 8,
        compiler_params=params,
        cost_estimate=cost,
    )(doc_lengths.reshape(1, -1), page_slot.transpose(1, 2, 0), q_all, chip, away)
    return pl.pallas_call(
        far_kernel,
        out_shape=(
            jax.ShapeDtypeStruct((1, 2, block_tok, width), jnp.bfloat16),
            jax.ShapeDtypeStruct((slot_count, 1, PAGE, 2 * HEAD_DIM), jnp.bfloat16),
        ),
        in_specs=[vmem] * 9,
        out_specs=(hbm, hbm),
        scratch_shapes=[
            pltpu.VMEM((slot_count, 1, PAGE, 2 * HEAD_DIM), jnp.bfloat16),
            pltpu.VMEM((2, block_tok, width), jnp.bfloat16),
            pltpu.SemaphoreType.DMA((3,)),
        ],
        compiler_params=params,
        cost_estimate=cost,
    )(far, *stats)


def per_device_long(query_states, key_states, value_states, doc_lengths, page_slot):
    q_local = lax.all_to_all(query_states, "head", split_axis=3, concat_axis=2, tiled=True)
    axis_count = lax.axis_size("blk")
    my_index = lax.axis_index("blk")
    block_tok = q_local.shape[2]
    head_dim = key_states.shape[3]
    group_size = q_local.shape[3] // head_dim
    query_rows = q_local.reshape(2 * block_tok, group_size, head_dim)
    offsets = jnp.arange(block_tok, dtype=jnp.int32)
    doc_bounds = jnp.cumsum(doc_lengths)[:-1]
    page_count = block_tok // PAGE
    slot_count = 4 * page_count
    slot_range = jnp.arange(slot_count, dtype=jnp.int32)
    score_scale = head_dim ** (-0.5)

    def group_positions(owner_ids):
        block_starts = jnp.stack([owner_ids, 2 * axis_count - 1 - owner_ids], axis=1) * block_tok
        return (block_starts[:, :, None] + offsets[None, None, :]).reshape(-1)

    def doc_of(positions):
        return jnp.sum((positions[:, None] >= doc_bounds[None, :]).astype(jnp.int32), axis=1)

    q_pos = group_positions(my_index.reshape(1))
    q_doc = doc_of(q_pos)

    def attend_group(attn_state, key_rows, value_rows, allowed):
        running_max, weight_sum, accum = attn_state
        scores = (
            jnp.einsum("qhd,kd->qhk", query_rows, key_rows, preferred_element_type=jnp.float32)
            * score_scale
        )
        masked = jnp.where(allowed[:, None, :], scores, -1e30)
        new_max = jnp.maximum(running_max, jnp.max(masked, axis=2))
        weights = jnp.where(allowed[:, None, :], jnp.exp(masked - new_max[..., None]), 0.0)
        factor = jnp.exp(running_max - new_max)
        weight_sum = weight_sum * factor + jnp.sum(weights, axis=2)
        update = jnp.einsum(
            "qhk,kd->qhd",
            weights.astype(jnp.bfloat16),
            value_rows,
            preferred_element_type=jnp.float32,
        )
        accum = accum * factor[..., None] + update
        return (new_max, weight_sum, accum)

    def visit_group(attn_state, key_group, value_group, owner_ids):
        key_rows = key_group.reshape(-1, head_dim)
        value_rows = value_group.reshape(-1, head_dim)
        k_pos = group_positions(owner_ids)
        allowed = (k_pos[None, :] <= q_pos[:, None]) & (doc_of(k_pos)[None, :] == q_doc[:, None])
        return attend_group(attn_state, key_rows, value_rows, allowed)

    def place_pages(page_store, key_group, value_group, owner_ids):
        page_rows = jnp.concatenate([key_group, value_group], axis=-1).reshape(
            -1, PAGE * 2 * head_dim
        )
        slot_ids = jnp.take(page_slot, owner_ids, axis=0).reshape(-1) - my_index * slot_count
        selector = (slot_range[:, None] == slot_ids[None, :]).astype(jnp.bfloat16)
        return page_store + jnp.dot(selector, page_rows, preferred_element_type=jnp.float32)

    def fold_groups(step_fn, carried, kv_piece):
        key_piece, value_piece = kv_piece
        piece_len = key_piece.shape[0]
        width = 4
        owner_ids = jnp.arange(piece_len, dtype=jnp.int32).reshape(piece_len // width, width)
        key_groups = key_piece.reshape(piece_len // width, width, 2, block_tok, head_dim)
        value_groups = value_piece.reshape(piece_len // width, width, 2, block_tok, head_dim)

        def visit_one(inner_state, entry_tuple):
            key_group, value_group, owners = entry_tuple
            return (step_fn(inner_state, key_group, value_group, owners), None)

        return lax.scan(visit_one, carried, (key_groups, value_groups, owner_ids))[0]

    empty_store = jnp.zeros((slot_count, PAGE * 2 * head_dim), jnp.float32)
    start_state = (
        jnp.full((2 * block_tok, group_size), -1e30, jnp.float32),
        jnp.zeros((2 * block_tok, group_size), jnp.float32),
        jnp.zeros((2 * block_tok, group_size, head_dim), jnp.float32),
    )
    final_state = fold_groups(
        visit_group,
        start_state,
        (
            lax.all_gather(key_states, "blk", axis=0, tiled=True),
            lax.all_gather(value_states, "blk", axis=0, tiled=True),
        ),
    )
    page_store = fold_groups(
        place_pages,
        empty_store,
        (
            lax.all_gather(key_states, "blk", axis=0, tiled=True),
            lax.all_gather(value_states, "blk", axis=0, tiled=True),
        ),
    )
    running_max, weight_sum, accum = final_state
    attended = (
        (accum / weight_sum[..., None])
        .astype(jnp.bfloat16)
        .reshape(1, 2, block_tok, group_size * head_dim)
    )
    kv_cache = page_store.astype(jnp.bfloat16).reshape(slot_count, 1, PAGE, 2 * head_dim)
    return (attended, kv_cache)


def solution(mesh):
    return jax.shard_map(
        per_device if (mesh.shape["blk"], mesh.shape["head"]) == (8, 4) else per_device_long,
        mesh=mesh,
        in_specs=(
            P("blk", None, "head", None),
            P("blk", None, None, "head"),
            P("blk", None, None, "head"),
            P(),
            P(),
        ),
        out_specs=(P("blk", None, None, "head"), P("blk", "head", None, None)),
        check_vma=False,
    )
```

```python
import functools

import jax
import jax.numpy as jnp
from jax import lax
from jax.experimental import pallas as pl
from jax.experimental.pallas import tpu as pltpu
from jax.sharding import PartitionSpec as P

PAGE = 16
LOG2E = 1.4426950408889634
HEAD_DIM = 128
LANES = 128


def gather_queries(own, across, beside, half):
    my_head = lax.axis_index("head")
    width = beside.shape[-1]
    parts = []
    for lane in range(0, width, HEAD_DIM):
        mine = pl.multiple_of(my_head * width + lane, HEAD_DIM)
        low = pl.multiple_of((my_head & 1) * width + lane, HEAD_DIM)
        parts.append(own[0, half, :, pl.ds(mine, HEAD_DIM)])
        parts.append(beside[0, half, :, lane : lane + HEAD_DIM])
        parts.append(across[0, half, :, pl.ds(low, HEAD_DIM)])
        parts.append(beside[1, half, :, lane : lane + HEAD_DIM])
    return jnp.concatenate(parts, axis=0)


def key_bias(my_blk, lengths, chips, block_tok, sub_tok, half, core):
    blk_count = 2 * chips
    my_block = my_blk if half == 0 else 2 * blk_count - 1 - my_blk
    lane = lax.broadcasted_iota(jnp.int32, (1, LANES), 1)
    sender = lax.axis_index("head") ^ (lane % block_tok // sub_tok)
    q_pos = my_block * block_tok + sender * sub_tok + lane % sub_tok
    first = jnp.zeros_like(q_pos)
    bound = jnp.zeros_like(lengths[:, :1])
    for k in range(lengths.shape[1] - 1):
        bound = bound + lengths[:, k : k + 1]
        first = jnp.where(q_pos >= bound, bound, first)
    row = lax.broadcasted_iota(jnp.int32, (block_tok, LANES), 0)
    parts = []
    for m in range(chips):
        owner = (my_blk ^ core) ^ (2 * m)
        for side in range(half + 1):
            block = owner if side == 0 else 2 * blk_count - 1 - owner
            if core == 0 and m == 0 and side == half:
                allowed = (row <= q_pos - block * block_tok) & (row >= first - block * block_tok)
            else:
                allowed = row >= first - jnp.where(block < my_block, block * block_tok, -(2**28))
            parts.append(jnp.where(allowed, 0.0, -1e30))
    return jnp.concatenate(parts, axis=0)


def page_targets(my_blk, page_slot, chips, slot_count, core):
    _, pages_blk, blk_count = page_slot.shape
    chip = lax.broadcasted_iota(jnp.int32, (chips, blk_count), 0)
    owner = (my_blk ^ core) ^ (2 * chip)
    chosen = (owner == lax.broadcasted_iota(jnp.int32, (chips, blk_count), 1)).astype(jnp.float32).astype(jnp.bfloat16)
    cols = 2 * pages_blk * PAGE
    page = lax.broadcasted_iota(jnp.int32, (pages_blk, cols), 0)
    col = lax.broadcasted_iota(jnp.int32, (pages_blk, cols), 1)
    slots = 0.0
    for half in range(2):
        held = lax.dot_general(
            chosen,
            page_slot[half].astype(jnp.float32).astype(jnp.bfloat16),
            (((1,), (1,)), ((), ())),
            preferred_element_type=jnp.float32,
        )
        spread = (col // PAGE == page + half * pages_blk).astype(jnp.float32).astype(jnp.bfloat16)
        slots = slots + jnp.dot(held.astype(jnp.bfloat16), spread, preferred_element_type=jnp.float32)
    slots = slots.astype(jnp.int32) - my_blk * slot_count
    rows = slots * PAGE + lax.broadcasted_iota(jnp.int32, slots.shape, 1) % PAGE
    return jnp.concatenate([rows[m : m + 1] for m in range(chips)], axis=1)


def place_pages(targets, pairs, slot_count):
    rows = pairs[...].reshape(-1, pairs.shape[-1])
    row = lax.broadcasted_iota(jnp.int32, (slot_count * PAGE, rows.shape[0]), 0)
    chosen = jnp.where(row == targets, 1.0, 0.0).astype(jnp.bfloat16)
    return jnp.dot(chosen, rows, preferred_element_type=jnp.float32)


def score_part(queries, pairs, half):
    keys = pairs[:, : half + 1].reshape(-1, 2 * HEAD_DIM)[:, :HEAD_DIM]
    return lax.dot_general(keys, queries, (((1,), (1,)), ((), ())), preferred_element_type=jnp.float32)


def soften(scores, bias):
    bias = jnp.concatenate([bias] * (scores.shape[1] // LANES), axis=1)
    scores = scores * (HEAD_DIM**-0.5 * LOG2E) + bias
    top = jnp.max(scores, axis=0, keepdims=True)
    weights = jnp.exp2(scores - top)
    return top, jnp.sum(weights, axis=0, keepdims=True), weights.astype(jnp.bfloat16)


def weigh_part(weights, pairs, half):
    values = pairs[:, : half + 1].reshape(-1, 2 * HEAD_DIM)[:, HEAD_DIM:]
    return lax.dot_general(values, weights, (((0,), (0,)), ((), ())), preferred_element_type=jnp.float32)


def part_kernel(queries, part):
    width = part.shape[3]
    start = pl.multiple_of(((lax.axis_index("head") & 2) ^ 2) * (width // 2), width)
    part[...] = queries[:, :, :, pl.ds(start, width)]


def near_kernel(
    lengths, page_slot, own, across, beside, near, q_rows, top_ref, total_ref, out_ref, pages_ref, far_bias_a,
    far_bias_b, far_targets,
):
    chips, _, block_tok, _ = near.shape
    slot_count = pages_ref.shape[0] // PAGE
    my_blk = lax.axis_index("blk")
    bias = functools.partial(key_bias, my_blk, lengths[...] - lax.axis_index("head"), chips, block_tok, own.shape[2])
    targets = functools.partial(page_targets, my_blk, page_slot, chips, slot_count)
    scores = {}
    for half in (1, 0):
        queries = gather_queries(own, across, beside, half)
        q_rows[half] = queries
        scores[half] = score_part(queries, near, half)
    for half in (1, 0):
        top_ref[half], total_ref[half], weights = soften(scores[half], bias(half, 0))
        out_ref[half] = weigh_part(weights, near, half)
    pages_ref[...] = place_pages(targets(0), near, slot_count).astype(jnp.bfloat16)
    for half in (1, 0):
        (far_bias_a, far_bias_b)[half][...] = bias(half, 1)
    far_targets[...] = targets(1)


def far_kernel(
    far, q_rows, top_ref, total_ref, out_ref, pages_ref, bias_a, bias_b, far_targets, attended, kv_cache,
    pages, result, sems,
):
    block_tok = far.shape[2]
    slot_count = kv_cache.shape[0]
    my_head = lax.axis_index("head")
    sub_tok = block_tok // lax.axis_size("head")
    scores = {half: score_part(q_rows[half], far, half) for half in (1, 0)}
    moved = place_pages(far_targets[...], far, slot_count) + pages_ref[...].astype(jnp.float32)
    pages[...] = moved.astype(jnp.bfloat16).reshape(pages.shape)
    writes = [pltpu.make_async_copy(pages, kv_cache, sems.at[2])]
    writes[0].start()
    parts = {}
    for half in (1, 0):
        top, total, weights = soften(scores[half], (bias_a, bias_b)[half][...])
        parts[half] = (top, total, weigh_part(weights, far, half))
    for half in (1, 0):
        top, total, out = parts[half]
        best = jnp.maximum(top, top_ref[half])
        here = jnp.exp2(top - best)
        there = jnp.exp2(top_ref[half] - best)
        inverse = 1.0 / (total * here + total_ref[half] * there)
        out = (out * (here * inverse) + out_ref[half] * (there * inverse)).T.astype(jnp.bfloat16)
        for g in range(out.shape[0] // block_tok):
            for d in range(block_tok // sub_tok):
                row = pl.multiple_of((my_head ^ d) * sub_tok, sub_tok)
                start = g * block_tok + d * sub_tok
                result[half, pl.ds(row, sub_tok), g * HEAD_DIM : (g + 1) * HEAD_DIM] = out[start : start + sub_tok]
        writes.append(pltpu.make_async_copy(result.at[half], attended.at[0, half], sems.at[half]))
        writes[-1].start()
    for write in writes:
        write.wait()


def per_device(query_states, key_states, value_states, doc_lengths, page_slot):
    blk_count = lax.axis_size("blk")
    head_count = lax.axis_size("head")
    q_width = query_states.shape[3]
    block_tok = key_states.shape[2]
    width = q_width // head_count
    rows = width // HEAD_DIM * block_tok
    slot_count = 4 * (block_tok // PAGE)

    my_head = lax.axis_index("head")
    vmem = pl.BlockSpec(memory_space=pltpu.VMEM)
    part = pl.pallas_call(
        part_kernel,
        out_shape=jax.ShapeDtypeStruct((*query_states.shape[:3], 2 * width), query_states.dtype),
        in_specs=[vmem],
        out_specs=vmem,
        compiler_params=pltpu.CompilerParams(vmem_limit_bytes=4 * 1024 * 1024),
        cost_estimate=pl.CostEstimate(flops=0, bytes_accessed=200_000, transcendentals=0),
    )(query_states)
    across = lax.ppermute(part, "head", [(i, i ^ 2) for i in range(head_count)])
    pair = jnp.concatenate([key_states, value_states], axis=3)
    lengths = doc_lengths + my_head
    pair, lengths, _ = lax.optimization_barrier((pair, lengths, part))
    near = [
        lax.ppermute(pair, "blk", [(i, i ^ d) for i in range(blk_count)]) for d in range(2, blk_count, 2)
    ]
    beside = jnp.concatenate(
        [
            lax.dynamic_slice_in_dim(query_states, (my_head ^ 1) * width, width, axis=3),
            lax.dynamic_slice_in_dim(across, ((my_head & 1) ^ 1) * width, width, axis=3),
        ],
        axis=0,
    )
    near = lax.optimization_barrier((near[::-1], beside))[0][::-1]
    beside = lax.ppermute(beside, "head", [(i, i ^ 1) for i in range(head_count)])
    near = jnp.concatenate([pair] + near, axis=0)
    far = lax.ppermute(near, "blk", [(i, i ^ 1) for i in range(blk_count)])

    hbm = pl.BlockSpec(memory_space=pl.ANY)
    params = pltpu.CompilerParams(vmem_limit_bytes=32 * 1024 * 1024)
    cost = pl.CostEstimate(flops=4_000_000_000, bytes_accessed=1_000_000, transcendentals=200_000)
    half_cols = blk_count // 2 * block_tok
    stats = pl.pallas_call(
        near_kernel,
        out_shape=(
            jax.ShapeDtypeStruct((2, rows, HEAD_DIM), jnp.bfloat16),
            jax.ShapeDtypeStruct((2, 1, rows), jnp.float32),
            jax.ShapeDtypeStruct((2, 1, rows), jnp.float32),
            jax.ShapeDtypeStruct((2, HEAD_DIM, rows), jnp.float32),
            jax.ShapeDtypeStruct((slot_count * PAGE, 2 * HEAD_DIM), jnp.bfloat16),
            jax.ShapeDtypeStruct((half_cols, LANES), jnp.float32),
            jax.ShapeDtypeStruct((2 * half_cols, LANES), jnp.float32),
            jax.ShapeDtypeStruct((1, 2 * half_cols), jnp.int32),
        ),
        in_specs=[vmem] * 6,
        out_specs=(vmem,) * 8,
        compiler_params=params,
        cost_estimate=cost,
    )(lengths.reshape(1, -1), page_slot.transpose(1, 2, 0), query_states, across, beside, near)
    return pl.pallas_call(
        far_kernel,
        out_shape=(
            jax.ShapeDtypeStruct((1, 2, block_tok, width), jnp.bfloat16),
            jax.ShapeDtypeStruct((slot_count, 1, PAGE, 2 * HEAD_DIM), jnp.bfloat16),
        ),
        in_specs=[vmem] * 9,
        out_specs=(hbm, hbm),
        scratch_shapes=[
            pltpu.VMEM((slot_count, 1, PAGE, 2 * HEAD_DIM), jnp.bfloat16),
            pltpu.VMEM((2, block_tok, width), jnp.bfloat16),
            pltpu.SemaphoreType.DMA((3,)),
        ],
        compiler_params=params,
        cost_estimate=cost,
    )(far, *stats)


def per_device_long(query_states, key_states, value_states, doc_lengths, page_slot):
    q_local = lax.all_to_all(query_states, "head", split_axis=3, concat_axis=2, tiled=True)
    axis_count = lax.axis_size("blk")
    my_index = lax.axis_index("blk")
    block_tok = q_local.shape[2]
    head_dim = key_states.shape[3]
    group_size = q_local.shape[3] // head_dim
    query_rows = q_local.reshape(2 * block_tok, group_size, head_dim)
    offsets = jnp.arange(block_tok, dtype=jnp.int32)
    doc_bounds = jnp.cumsum(doc_lengths)[:-1]
    page_count = block_tok // PAGE
    slot_count = 4 * page_count
    slot_range = jnp.arange(slot_count, dtype=jnp.int32)
    score_scale = head_dim ** (-0.5)

    def group_positions(owner_ids):
        block_starts = jnp.stack([owner_ids, 2 * axis_count - 1 - owner_ids], axis=1) * block_tok
        return (block_starts[:, :, None] + offsets[None, None, :]).reshape(-1)

    def doc_of(positions):
        return jnp.sum((positions[:, None] >= doc_bounds[None, :]).astype(jnp.int32), axis=1)

    q_pos = group_positions(my_index.reshape(1))
    q_doc = doc_of(q_pos)

    def attend_group(attn_state, key_rows, value_rows, allowed):
        running_max, weight_sum, accum = attn_state
        scores = (
            jnp.einsum("qhd,kd->qhk", query_rows, key_rows, preferred_element_type=jnp.float32)
            * score_scale
        )
        masked = jnp.where(allowed[:, None, :], scores, -1e30)
        new_max = jnp.maximum(running_max, jnp.max(masked, axis=2))
        weights = jnp.where(allowed[:, None, :], jnp.exp(masked - new_max[..., None]), 0.0)
        factor = jnp.exp(running_max - new_max)
        weight_sum = weight_sum * factor + jnp.sum(weights, axis=2)
        update = jnp.einsum(
            "qhk,kd->qhd",
            weights.astype(jnp.bfloat16),
            value_rows,
            preferred_element_type=jnp.float32,
        )
        accum = accum * factor[..., None] + update
        return (new_max, weight_sum, accum)

    def visit_group(attn_state, key_group, value_group, owner_ids):
        key_rows = key_group.reshape(-1, head_dim)
        value_rows = value_group.reshape(-1, head_dim)
        k_pos = group_positions(owner_ids)
        allowed = (k_pos[None, :] <= q_pos[:, None]) & (doc_of(k_pos)[None, :] == q_doc[:, None])
        return attend_group(attn_state, key_rows, value_rows, allowed)

    def place_pages(page_store, key_group, value_group, owner_ids):
        page_rows = jnp.concatenate([key_group, value_group], axis=-1).reshape(
            -1, PAGE * 2 * head_dim
        )
        slot_ids = jnp.take(page_slot, owner_ids, axis=0).reshape(-1) - my_index * slot_count
        selector = (slot_range[:, None] == slot_ids[None, :]).astype(jnp.bfloat16)
        return page_store + jnp.dot(selector, page_rows, preferred_element_type=jnp.float32)

    def fold_groups(step_fn, carried, kv_piece):
        key_piece, value_piece = kv_piece
        piece_len = key_piece.shape[0]
        width = 4
        owner_ids = jnp.arange(piece_len, dtype=jnp.int32).reshape(piece_len // width, width)
        key_groups = key_piece.reshape(piece_len // width, width, 2, block_tok, head_dim)
        value_groups = value_piece.reshape(piece_len // width, width, 2, block_tok, head_dim)

        def visit_one(inner_state, entry_tuple):
            key_group, value_group, owners = entry_tuple
            return (step_fn(inner_state, key_group, value_group, owners), None)

        return lax.scan(visit_one, carried, (key_groups, value_groups, owner_ids))[0]

    empty_store = jnp.zeros((slot_count, PAGE * 2 * head_dim), jnp.float32)
    start_state = (
        jnp.full((2 * block_tok, group_size), -1e30, jnp.float32),
        jnp.zeros((2 * block_tok, group_size), jnp.float32),
        jnp.zeros((2 * block_tok, group_size, head_dim), jnp.float32),
    )
    final_state = fold_groups(
        visit_group,
        start_state,
        (
            lax.all_gather(key_states, "blk", axis=0, tiled=True),
            lax.all_gather(value_states, "blk", axis=0, tiled=True),
        ),
    )
    page_store = fold_groups(
        place_pages,
        empty_store,
        (
            lax.all_gather(key_states, "blk", axis=0, tiled=True),
            lax.all_gather(value_states, "blk", axis=0, tiled=True),
        ),
    )
    running_max, weight_sum, accum = final_state
    attended = (
        (accum / weight_sum[..., None])
        .astype(jnp.bfloat16)
        .reshape(1, 2, block_tok, group_size * head_dim)
    )
    kv_cache = page_store.astype(jnp.bfloat16).reshape(slot_count, 1, PAGE, 2 * head_dim)
    return (attended, kv_cache)


def solution(mesh):
    return jax.shard_map(
        per_device if mesh.shape["blk"] <= 8 else per_device_long,
        mesh=mesh,
        in_specs=(
            P("blk", None, "head", None),
            P("blk", None, None, "head"),
            P("blk", None, None, "head"),
            P(),
            P(),
        ),
        out_specs=(P("blk", None, None, "head"), P("blk", "head", None, None)),
        check_vma=False,
    )
```

```python
import functools

import jax
import jax.numpy as jnp
from jax import lax
from jax.experimental import pallas as pl
from jax.experimental.pallas import tpu as pltpu
from jax.sharding import PartitionSpec as P

PAGE = 16
LOG2E = 1.4426950408889634
HEAD_DIM = 128
LANES = 128


def gather_queries(own, across, beside, half):
    my_head = lax.axis_index("head")
    width = beside.shape[-1]
    parts = []
    for lane in range(0, width, HEAD_DIM):
        mine = pl.multiple_of(my_head * width + lane, HEAD_DIM)
        low = pl.multiple_of((my_head & 1) * width + lane, HEAD_DIM)
        parts.append(own[0, half, :, pl.ds(mine, HEAD_DIM)])
        parts.append(beside[0, half, :, lane : lane + HEAD_DIM])
        parts.append(across[0, half, :, pl.ds(low, HEAD_DIM)])
        parts.append(beside[1, half, :, lane : lane + HEAD_DIM])
    return jnp.concatenate(parts, axis=0)


def key_bias(my_blk, lengths, chips, block_tok, sub_tok, half, core):
    blk_count = 2 * chips
    my_block = my_blk if half == 0 else 2 * blk_count - 1 - my_blk
    lane = lax.broadcasted_iota(jnp.int32, (1, LANES), 1)
    sender = lax.axis_index("head") ^ (lane % block_tok // sub_tok)
    q_pos = my_block * block_tok + sender * sub_tok + lane % sub_tok
    first = jnp.zeros_like(q_pos)
    bound = jnp.zeros_like(lengths[:, :1])
    for k in range(lengths.shape[1] - 1):
        bound = bound + lengths[:, k : k + 1]
        first = jnp.where(q_pos >= bound, bound, first)
    row = lax.broadcasted_iota(jnp.int32, (block_tok, LANES), 0)
    parts = []
    for m in range(chips):
        owner = (my_blk ^ core) ^ (2 * m)
        for side in range(half + 1):
            block = owner if side == 0 else 2 * blk_count - 1 - owner
            if core == 0 and m == 0 and side == half:
                allowed = (row <= q_pos - block * block_tok) & (row >= first - block * block_tok)
            else:
                allowed = row >= first - jnp.where(block < my_block, block * block_tok, -(2**28))
            parts.append(jnp.where(allowed, 0.0, -1e30))
    return jnp.concatenate(parts, axis=0)


def move_pages(my_blk, page_slot, keys, values, slot_count, core, pages):
    chips, halves, block_tok, _ = keys.shape
    for m in range(chips):
        owner = (my_blk ^ core) ^ (2 * m)
        for half in range(halves):
            for n in range(block_tok // PAGE):
                slot = page_slot[half, n, owner] - my_blk * slot_count
                slot = jnp.where((slot >= 0) & (slot < slot_count), slot, slot_count)
                rows = pl.ds(pl.multiple_of(slot * PAGE, PAGE), PAGE)
                pages[rows, :HEAD_DIM] = keys[m, half, n * PAGE : (n + 1) * PAGE, :]
                pages[rows, HEAD_DIM:] = values[m, half, n * PAGE : (n + 1) * PAGE, :]


def score_part(queries, keys, half):
    keys = keys[:, : half + 1].reshape(-1, HEAD_DIM)
    return lax.dot_general(keys, queries, (((1,), (1,)), ((), ())), preferred_element_type=jnp.float32)


def soften(scores, bias):
    bias = jnp.concatenate([bias] * (scores.shape[1] // LANES), axis=1)
    scores = scores * (HEAD_DIM**-0.5 * LOG2E) + bias
    top = jnp.max(scores, axis=0, keepdims=True)
    weights = jnp.exp2(scores - top)
    return top, jnp.sum(weights, axis=0, keepdims=True), weights.astype(jnp.bfloat16)


def weigh_part(weights, values, half):
    values = values[:, : half + 1].reshape(-1, HEAD_DIM)
    return lax.dot_general(values, weights, (((0,), (0,)), ((), ())), preferred_element_type=jnp.float32)


def near_kernel(
    lengths, page_slot, own, across, beside, near_k, near_v, q_rows, top_ref, total_ref, out_ref, pages_ref, far_bias_a,
    far_bias_b, slots, sem,
):
    chips, _, block_tok, _ = near_k.shape
    slot_count = pages_ref.shape[0] // PAGE - 1
    fetch = pltpu.make_async_copy(page_slot, slots, sem)
    fetch.start()
    my_blk = lax.axis_index("blk")
    bias = functools.partial(key_bias, my_blk, lengths[...] - lax.axis_index("head"), chips, block_tok, own.shape[2])
    scores = {}
    for half in (1, 0):
        queries = gather_queries(own, across, beside, half)
        q_rows[half] = queries
        scores[half] = score_part(queries, near_k, half)
    for half in (1, 0):
        top_ref[half], total_ref[half], weights = soften(scores[half], bias(half, 0))
        out_ref[half] = weigh_part(weights, near_v, half)
    for half in (1, 0):
        (far_bias_a, far_bias_b)[half][...] = bias(half, 1)
    pages_ref[...] = jnp.zeros_like(pages_ref)
    fetch.wait()
    move_pages(my_blk, slots, near_k, near_v, slot_count, 0, pages_ref)


def far_kernel(
    page_slot, far_k, far_v, q_rows, top_ref, total_ref, out_ref, pages_ref, bias_a, bias_b, attended, kv_cache,
    pages, result, slots, sems,
):
    block_tok = far_k.shape[2]
    slot_count = kv_cache.shape[0] // PAGE
    my_head = lax.axis_index("head")
    sub_tok = block_tok // lax.axis_size("head")
    my_blk = lax.axis_index("blk")
    fetch = pltpu.make_async_copy(page_slot, slots, sems.at[3])
    fetch.start()
    scores = {half: score_part(q_rows[half], far_k, half) for half in (1, 0)}
    parts = {}
    for half in (1, 0):
        top, total, weights = soften(scores[half], (bias_a, bias_b)[half][...])
        parts[half] = (top, total, weigh_part(weights, far_v, half))
    pages[...] = pages_ref[...]
    fetch.wait()
    move_pages(my_blk, slots, far_k, far_v, slot_count, 1, pages)
    writes = [pltpu.make_async_copy(pages.at[: slot_count * PAGE], kv_cache, sems.at[2])]
    writes[0].start()
    for half in (1, 0):
        top, total, out = parts[half]
        best = jnp.maximum(top, top_ref[half])
        here = jnp.exp2(top - best)
        there = jnp.exp2(top_ref[half] - best)
        inverse = 1.0 / (total * here + total_ref[half] * there)
        out = (out * (here * inverse) + out_ref[half] * (there * inverse)).T.astype(jnp.bfloat16)
        for g in range(out.shape[0] // block_tok):
            for d in range(block_tok // sub_tok):
                row = pl.multiple_of((my_head ^ d) * sub_tok, sub_tok)
                start = g * block_tok + d * sub_tok
                result[half, pl.ds(row, sub_tok), g * HEAD_DIM : (g + 1) * HEAD_DIM] = out[start : start + sub_tok]
        writes.append(pltpu.make_async_copy(result.at[half], attended.at[0, half], sems.at[half]))
        writes[-1].start()
    for write in writes:
        write.wait()


def per_device(query_states, key_states, value_states, doc_lengths, page_slot):
    blk_count = lax.axis_size("blk")
    head_count = lax.axis_size("head")
    q_width = query_states.shape[3]
    block_tok = key_states.shape[2]
    width = q_width // head_count
    rows = width // HEAD_DIM * block_tok
    slot_count = 4 * (block_tok // PAGE)

    my_head = lax.axis_index("head")
    part = lax.dynamic_slice_in_dim(query_states, ((my_head & 2) ^ 2) * width, 2 * width, axis=3)
    across = lax.ppermute(part, "head", [(i, i ^ 2) for i in range(head_count)])
    pair = jnp.concatenate([key_states, value_states], axis=3)
    lengths = doc_lengths + my_head
    pair, lengths, _ = lax.optimization_barrier((pair, lengths, part))
    near = [
        lax.ppermute(pair, "blk", [(i, i ^ d) for i in range(blk_count)]) for d in range(2, blk_count, 2)
    ]
    beside = jnp.concatenate(
        [
            lax.dynamic_slice_in_dim(query_states, (my_head ^ 1) * width, width, axis=3),
            lax.dynamic_slice_in_dim(across, ((my_head & 1) ^ 1) * width, width, axis=3),
        ],
        axis=0,
    )
    near = lax.optimization_barrier((near[::-1], beside))[0][::-1]
    beside = lax.ppermute(beside, "head", [(i, i ^ 1) for i in range(head_count)])
    near = [pair] + near
    near_k = jnp.concatenate([p[..., :HEAD_DIM] for p in near], axis=0)
    near_v = jnp.concatenate([p[..., HEAD_DIM:] for p in near], axis=0)
    far_k, far_v = (lax.ppermute(x, "blk", [(i, i ^ 1) for i in range(blk_count)]) for x in (near_k, near_v))

    hbm = pl.BlockSpec(memory_space=pl.ANY)
    vmem = pl.BlockSpec(memory_space=pltpu.VMEM)
    params = pltpu.CompilerParams(vmem_limit_bytes=32 * 1024 * 1024)
    cost = pl.CostEstimate(flops=4_000_000_000, bytes_accessed=1_000_000, transcendentals=200_000)
    half_cols = blk_count // 2 * block_tok
    slots = page_slot.transpose(1, 2, 0)
    stats = pl.pallas_call(
        near_kernel,
        out_shape=(
            jax.ShapeDtypeStruct((2, rows, HEAD_DIM), jnp.bfloat16),
            jax.ShapeDtypeStruct((2, 1, rows), jnp.float32),
            jax.ShapeDtypeStruct((2, 1, rows), jnp.float32),
            jax.ShapeDtypeStruct((2, HEAD_DIM, rows), jnp.float32),
            jax.ShapeDtypeStruct(((slot_count + 1) * PAGE, 2 * HEAD_DIM), jnp.bfloat16),
            jax.ShapeDtypeStruct((half_cols, LANES), jnp.float32),
            jax.ShapeDtypeStruct((2 * half_cols, LANES), jnp.float32),
        ),
        in_specs=[vmem, hbm] + [vmem] * 5,
        out_specs=(vmem,) * 7,
        scratch_shapes=[pltpu.SMEM(slots.shape, jnp.int32), pltpu.SemaphoreType.DMA],
        compiler_params=params,
        cost_estimate=cost,
    )(lengths.reshape(1, -1), slots, query_states, across, beside, near_k, near_v)
    attended, kv_cache = pl.pallas_call(
        far_kernel,
        out_shape=(
            jax.ShapeDtypeStruct((1, 2, block_tok, width), jnp.bfloat16),
            jax.ShapeDtypeStruct((slot_count * PAGE, 2 * HEAD_DIM), jnp.bfloat16),
        ),
        in_specs=[hbm] + [vmem] * 9,
        out_specs=(hbm, hbm),
        scratch_shapes=[
            pltpu.VMEM(((slot_count + 1) * PAGE, 2 * HEAD_DIM), jnp.bfloat16),
            pltpu.VMEM((2, block_tok, width), jnp.bfloat16),
            pltpu.SMEM(slots.shape, jnp.int32),
            pltpu.SemaphoreType.DMA((4,)),
        ],
        compiler_params=params,
        cost_estimate=cost,
    )(slots, far_k, far_v, *stats)
    return attended, kv_cache.reshape(slot_count, 1, PAGE, 2 * HEAD_DIM)


def per_device_long(query_states, key_states, value_states, doc_lengths, page_slot):
    q_local = lax.all_to_all(query_states, "head", split_axis=3, concat_axis=2, tiled=True)
    axis_count = lax.axis_size("blk")
    my_index = lax.axis_index("blk")
    block_tok = q_local.shape[2]
    head_dim = key_states.shape[3]
    group_size = q_local.shape[3] // head_dim
    query_rows = q_local.reshape(2 * block_tok, group_size, head_dim)
    offsets = jnp.arange(block_tok, dtype=jnp.int32)
    doc_bounds = jnp.cumsum(doc_lengths)[:-1]
    page_count = block_tok // PAGE
    slot_count = 4 * page_count
    slot_range = jnp.arange(slot_count, dtype=jnp.int32)
    score_scale = head_dim ** (-0.5)

    def group_positions(owner_ids):
        block_starts = jnp.stack([owner_ids, 2 * axis_count - 1 - owner_ids], axis=1) * block_tok
        return (block_starts[:, :, None] + offsets[None, None, :]).reshape(-1)

    def doc_of(positions):
        return jnp.sum((positions[:, None] >= doc_bounds[None, :]).astype(jnp.int32), axis=1)

    q_pos = group_positions(my_index.reshape(1))
    q_doc = doc_of(q_pos)

    def attend_group(attn_state, key_rows, value_rows, allowed):
        running_max, weight_sum, accum = attn_state
        scores = (
            jnp.einsum("qhd,kd->qhk", query_rows, key_rows, preferred_element_type=jnp.float32)
            * score_scale
        )
        masked = jnp.where(allowed[:, None, :], scores, -1e30)
        new_max = jnp.maximum(running_max, jnp.max(masked, axis=2))
        weights = jnp.where(allowed[:, None, :], jnp.exp(masked - new_max[..., None]), 0.0)
        factor = jnp.exp(running_max - new_max)
        weight_sum = weight_sum * factor + jnp.sum(weights, axis=2)
        update = jnp.einsum(
            "qhk,kd->qhd",
            weights.astype(jnp.bfloat16),
            value_rows,
            preferred_element_type=jnp.float32,
        )
        accum = accum * factor[..., None] + update
        return (new_max, weight_sum, accum)

    def visit_group(attn_state, key_group, value_group, owner_ids):
        key_rows = key_group.reshape(-1, head_dim)
        value_rows = value_group.reshape(-1, head_dim)
        k_pos = group_positions(owner_ids)
        allowed = (k_pos[None, :] <= q_pos[:, None]) & (doc_of(k_pos)[None, :] == q_doc[:, None])
        return attend_group(attn_state, key_rows, value_rows, allowed)

    def place_pages(page_store, key_group, value_group, owner_ids):
        page_rows = jnp.concatenate([key_group, value_group], axis=-1).reshape(
            -1, PAGE * 2 * head_dim
        )
        slot_ids = jnp.take(page_slot, owner_ids, axis=0).reshape(-1) - my_index * slot_count
        selector = (slot_range[:, None] == slot_ids[None, :]).astype(jnp.bfloat16)
        return page_store + jnp.dot(selector, page_rows, preferred_element_type=jnp.float32)

    def fold_groups(step_fn, carried, kv_piece):
        key_piece, value_piece = kv_piece
        piece_len = key_piece.shape[0]
        width = 4
        owner_ids = jnp.arange(piece_len, dtype=jnp.int32).reshape(piece_len // width, width)
        key_groups = key_piece.reshape(piece_len // width, width, 2, block_tok, head_dim)
        value_groups = value_piece.reshape(piece_len // width, width, 2, block_tok, head_dim)

        def visit_one(inner_state, entry_tuple):
            key_group, value_group, owners = entry_tuple
            return (step_fn(inner_state, key_group, value_group, owners), None)

        return lax.scan(visit_one, carried, (key_groups, value_groups, owner_ids))[0]

    empty_store = jnp.zeros((slot_count, PAGE * 2 * head_dim), jnp.float32)
    start_state = (
        jnp.full((2 * block_tok, group_size), -1e30, jnp.float32),
        jnp.zeros((2 * block_tok, group_size), jnp.float32),
        jnp.zeros((2 * block_tok, group_size, head_dim), jnp.float32),
    )
    final_state = fold_groups(
        visit_group,
        start_state,
        (
            lax.all_gather(key_states, "blk", axis=0, tiled=True),
            lax.all_gather(value_states, "blk", axis=0, tiled=True),
        ),
    )
    page_store = fold_groups(
        place_pages,
        empty_store,
        (
            lax.all_gather(key_states, "blk", axis=0, tiled=True),
            lax.all_gather(value_states, "blk", axis=0, tiled=True),
        ),
    )
    running_max, weight_sum, accum = final_state
    attended = (
        (accum / weight_sum[..., None])
        .astype(jnp.bfloat16)
        .reshape(1, 2, block_tok, group_size * head_dim)
    )
    kv_cache = page_store.astype(jnp.bfloat16).reshape(slot_count, 1, PAGE, 2 * head_dim)
    return (attended, kv_cache)


def solution(mesh):
    return jax.shard_map(
        per_device if mesh.shape["blk"] <= 8 else per_device_long,
        mesh=mesh,
        in_specs=(
            P("blk", None, "head", None),
            P("blk", None, None, "head"),
            P("blk", None, None, "head"),
            P(),
            P(),
        ),
        out_specs=(P("blk", None, None, "head"), P("blk", "head", None, None)),
        check_vma=False,
    )
```

```python
import functools

import jax
import jax.numpy as jnp
from jax import lax
from jax.experimental import pallas as pl
from jax.experimental.pallas import tpu as pltpu
from jax.sharding import PartitionSpec as P

PAGE = 16
LOG2E = 1.4426950408889634
HEAD_DIM = 128
LANES = 128


def gather_queries(own, across, beside, half):
    my_head = lax.axis_index("head")
    width = beside.shape[-1]
    parts = []
    for lane in range(0, width, HEAD_DIM):
        mine = pl.multiple_of(my_head * width + lane, HEAD_DIM)
        low = pl.multiple_of((my_head & 1) * width + lane, HEAD_DIM)
        parts.append(own[0, half, :, pl.ds(mine, HEAD_DIM)])
        parts.append(beside[0, half, :, lane : lane + HEAD_DIM])
        parts.append(across[0, half, :, pl.ds(low, HEAD_DIM)])
        parts.append(beside[1, half, :, lane : lane + HEAD_DIM])
    return jnp.concatenate(parts, axis=0)


def key_bias(my_blk, lengths, chips, block_tok, sub_tok, half, core):
    blk_count = 2 * chips
    my_block = my_blk if half == 0 else 2 * blk_count - 1 - my_blk
    lane = lax.broadcasted_iota(jnp.int32, (1, LANES), 1)
    sender = lax.axis_index("head") ^ (lane % block_tok // sub_tok)
    q_pos = my_block * block_tok + sender * sub_tok + lane % sub_tok
    first = jnp.zeros_like(q_pos)
    bound = jnp.zeros_like(lengths[:, :1])
    for k in range(lengths.shape[1] - 1):
        bound = bound + lengths[:, k : k + 1]
        first = jnp.where(q_pos >= bound, bound, first)
    row = lax.broadcasted_iota(jnp.int32, (block_tok, LANES), 0)
    parts = []
    for m in range(chips):
        owner = (my_blk ^ core) ^ (2 * m)
        for side in range(half + 1):
            block = owner if side == 0 else 2 * blk_count - 1 - owner
            if core == 0 and m == 0 and side == half:
                allowed = (row <= q_pos - block * block_tok) & (row >= first - block * block_tok)
            else:
                allowed = row >= first - jnp.where(block < my_block, block * block_tok, -(2**28))
            parts.append(jnp.where(allowed, 0.0, -1e30))
    return jnp.concatenate(parts, axis=0)


def page_targets(my_blk, page_slot, chips, slot_count, core):
    _, pages_blk, blk_count = page_slot.shape
    chip = lax.broadcasted_iota(jnp.int32, (chips, blk_count), 0)
    owner = (my_blk ^ core) ^ (2 * chip)
    chosen = (owner == lax.broadcasted_iota(jnp.int32, (chips, blk_count), 1)).astype(jnp.float32).astype(jnp.bfloat16)
    cols = 2 * pages_blk * PAGE
    page = lax.broadcasted_iota(jnp.int32, (pages_blk, cols), 0)
    col = lax.broadcasted_iota(jnp.int32, (pages_blk, cols), 1)
    slots = 0.0
    for half in range(2):
        held = lax.dot_general(
            chosen,
            page_slot[half].astype(jnp.float32).astype(jnp.bfloat16),
            (((1,), (1,)), ((), ())),
            preferred_element_type=jnp.float32,
        )
        spread = (col // PAGE == page + half * pages_blk).astype(jnp.float32).astype(jnp.bfloat16)
        slots = slots + jnp.dot(held.astype(jnp.bfloat16), spread, preferred_element_type=jnp.float32)
    slots = slots.astype(jnp.int32) - my_blk * slot_count
    rows = slots * PAGE + lax.broadcasted_iota(jnp.int32, slots.shape, 1) % PAGE
    return jnp.concatenate([rows[m : m + 1] for m in range(chips)], axis=1)


def place_pages(targets, keys, values, slot_count):
    rows = jnp.concatenate([keys[...].reshape(-1, HEAD_DIM), values[...].reshape(-1, HEAD_DIM)], axis=1)
    row = lax.broadcasted_iota(jnp.int32, (slot_count * PAGE, rows.shape[0]), 0)
    chosen = jnp.where(row == targets, 1.0, 0.0).astype(jnp.bfloat16)
    return jnp.dot(chosen, rows, preferred_element_type=jnp.float32)


def score_part(queries, keys, half):
    keys = keys[:, : half + 1].reshape(-1, HEAD_DIM)
    return lax.dot_general(keys, queries, (((1,), (1,)), ((), ())), preferred_element_type=jnp.float32)


def soften(scores, bias):
    bias = jnp.concatenate([bias] * (scores.shape[1] // LANES), axis=1)
    scores = scores * (HEAD_DIM**-0.5 * LOG2E) + bias
    top = jnp.max(scores, axis=0, keepdims=True)
    weights = jnp.exp2(scores - top)
    return top, jnp.sum(weights, axis=0, keepdims=True), weights.astype(jnp.bfloat16)


def weigh_part(weights, values, half):
    values = values[:, : half + 1].reshape(-1, HEAD_DIM)
    return lax.dot_general(values, weights, (((0,), (0,)), ((), ())), preferred_element_type=jnp.float32)


def near_kernel(
    lengths, page_slot, own, across, beside, near_k, near_v, q_rows, top_ref, total_ref, out_ref, pages_ref, far_bias_a,
    far_bias_b, far_targets,
):
    chips, _, block_tok, _ = near_k.shape
    slot_count = pages_ref.shape[0] // PAGE
    my_blk = lax.axis_index("blk")
    bias = functools.partial(key_bias, my_blk, lengths[...] - lax.axis_index("head"), chips, block_tok, own.shape[2])
    targets = functools.partial(page_targets, my_blk, page_slot, chips, slot_count)
    scores = {}
    for half in (1, 0):
        queries = gather_queries(own, across, beside, half)
        q_rows[half] = queries
        scores[half] = score_part(queries, near_k, half)
    for half in (1, 0):
        top_ref[half], total_ref[half], weights = soften(scores[half], bias(half, 0))
        out_ref[half] = weigh_part(weights, near_v, half)
    pages_ref[...] = place_pages(targets(0), near_k, near_v, slot_count).astype(jnp.bfloat16)
    for half in (1, 0):
        (far_bias_a, far_bias_b)[half][...] = bias(half, 1)
    far_targets[...] = targets(1)


def far_kernel(
    far_k, far_v, q_rows, top_ref, total_ref, out_ref, pages_ref, bias_a, bias_b, far_targets, attended, kv_cache,
    pages, result, sems,
):
    block_tok = far_k.shape[2]
    slot_count = kv_cache.shape[0]
    my_head = lax.axis_index("head")
    sub_tok = block_tok // lax.axis_size("head")
    scores = {half: score_part(q_rows[half], far_k, half) for half in (1, 0)}
    moved = place_pages(far_targets[...], far_k, far_v, slot_count) + pages_ref[...].astype(jnp.float32)
    pages[...] = moved.astype(jnp.bfloat16).reshape(pages.shape)
    writes = []

    def write(source, target):
        writes.append(pltpu.make_async_copy(source, target, sems.at[len(writes)]))
        writes[-1].start()

    for slot in range(0, slot_count, 4):
        write(pages.at[slot : slot + 4], kv_cache.at[slot : slot + 4])
    parts = {}
    for half in (1, 0):
        top, total, weights = soften(scores[half], (bias_a, bias_b)[half][...])
        parts[half] = (top, total, weigh_part(weights, far_v, half))
    for half in (1, 0):
        top, total, out = parts[half]
        best = jnp.maximum(top, top_ref[half])
        here = jnp.exp2(top - best)
        there = jnp.exp2(top_ref[half] - best)
        inverse = 1.0 / (total * here + total_ref[half] * there)
        out = (out * (here * inverse) + out_ref[half] * (there * inverse)).T.astype(jnp.bfloat16)
        for g in range(out.shape[0] // block_tok):
            for d in range(block_tok // sub_tok):
                row = pl.multiple_of((my_head ^ d) * sub_tok, sub_tok)
                start = g * block_tok + d * sub_tok
                result[half, pl.ds(row, sub_tok), g * HEAD_DIM : (g + 1) * HEAD_DIM] = out[start : start + sub_tok]
        for row in range(0, block_tok, 32):
            write(result.at[half, row : row + 32], attended.at[0, half, row : row + 32])
    for copy in writes:
        copy.wait()


def per_device(query_states, key_states, value_states, doc_lengths, page_slot):
    blk_count = lax.axis_size("blk")
    head_count = lax.axis_size("head")
    q_width = query_states.shape[3]
    block_tok = key_states.shape[2]
    width = q_width // head_count
    rows = width // HEAD_DIM * block_tok
    slot_count = 4 * (block_tok // PAGE)

    my_head = lax.axis_index("head")
    part = lax.dynamic_slice_in_dim(query_states, ((my_head & 2) ^ 2) * width, 2 * width, axis=3)
    across = lax.ppermute(part, "head", [(i, i ^ 2) for i in range(head_count)])
    pair = jnp.concatenate([key_states, value_states], axis=3)
    lengths = doc_lengths + my_head
    pair, lengths, _ = lax.optimization_barrier((pair, lengths, part))
    near = [
        lax.ppermute(pair, "blk", [(i, i ^ d) for i in range(blk_count)]) for d in range(2, blk_count, 2)
    ]
    beside = jnp.concatenate(
        [
            lax.dynamic_slice_in_dim(query_states, (my_head ^ 1) * width, width, axis=3),
            lax.dynamic_slice_in_dim(across, ((my_head & 1) ^ 1) * width, width, axis=3),
        ],
        axis=0,
    )
    near = lax.optimization_barrier((near[::-1], beside))[0][::-1]
    beside = lax.ppermute(beside, "head", [(i, i ^ 1) for i in range(head_count)])
    near = [pair] + near
    near_k = jnp.concatenate([p[..., :HEAD_DIM] for p in near], axis=0)
    near_v = jnp.concatenate([p[..., HEAD_DIM:] for p in near], axis=0)
    far_k, far_v = (lax.ppermute(x, "blk", [(i, i ^ 1) for i in range(blk_count)]) for x in (near_k, near_v))

    hbm = pl.BlockSpec(memory_space=pl.ANY)
    vmem = pl.BlockSpec(memory_space=pltpu.VMEM)
    params = pltpu.CompilerParams(vmem_limit_bytes=32 * 1024 * 1024)
    cost = pl.CostEstimate(flops=4_000_000_000, bytes_accessed=1_000_000, transcendentals=200_000)
    half_cols = blk_count // 2 * block_tok
    stats = pl.pallas_call(
        near_kernel,
        out_shape=(
            jax.ShapeDtypeStruct((2, rows, HEAD_DIM), jnp.bfloat16),
            jax.ShapeDtypeStruct((2, 1, rows), jnp.float32),
            jax.ShapeDtypeStruct((2, 1, rows), jnp.float32),
            jax.ShapeDtypeStruct((2, HEAD_DIM, rows), jnp.float32),
            jax.ShapeDtypeStruct((slot_count * PAGE, 2 * HEAD_DIM), jnp.bfloat16),
            jax.ShapeDtypeStruct((half_cols, LANES), jnp.float32),
            jax.ShapeDtypeStruct((2 * half_cols, LANES), jnp.float32),
            jax.ShapeDtypeStruct((1, 2 * half_cols), jnp.int32),
        ),
        in_specs=[vmem] * 7,
        out_specs=(vmem,) * 8,
        compiler_params=params,
        cost_estimate=cost,
    )(lengths.reshape(1, -1), page_slot.transpose(1, 2, 0), query_states, across, beside, near_k, near_v)
    return pl.pallas_call(
        far_kernel,
        out_shape=(
            jax.ShapeDtypeStruct((1, 2, block_tok, width), jnp.bfloat16),
            jax.ShapeDtypeStruct((slot_count, 1, PAGE, 2 * HEAD_DIM), jnp.bfloat16),
        ),
        in_specs=[vmem] * 10,
        out_specs=(hbm, hbm),
        scratch_shapes=[
            pltpu.VMEM((slot_count, 1, PAGE, 2 * HEAD_DIM), jnp.bfloat16),
            pltpu.VMEM((2, block_tok, width), jnp.bfloat16),
            pltpu.SemaphoreType.DMA((slot_count // 4 + 2 * (block_tok // 32),)),
        ],
        compiler_params=params,
        cost_estimate=cost,
    )(far_k, far_v, *stats)


def per_device_long(query_states, key_states, value_states, doc_lengths, page_slot):
    q_local = lax.all_to_all(query_states, "head", split_axis=3, concat_axis=2, tiled=True)
    axis_count = lax.axis_size("blk")
    my_index = lax.axis_index("blk")
    block_tok = q_local.shape[2]
    head_dim = key_states.shape[3]
    group_size = q_local.shape[3] // head_dim
    query_rows = q_local.reshape(2 * block_tok, group_size, head_dim)
    offsets = jnp.arange(block_tok, dtype=jnp.int32)
    doc_bounds = jnp.cumsum(doc_lengths)[:-1]
    page_count = block_tok // PAGE
    slot_count = 4 * page_count
    slot_range = jnp.arange(slot_count, dtype=jnp.int32)
    score_scale = head_dim ** (-0.5)

    def group_positions(owner_ids):
        block_starts = jnp.stack([owner_ids, 2 * axis_count - 1 - owner_ids], axis=1) * block_tok
        return (block_starts[:, :, None] + offsets[None, None, :]).reshape(-1)

    def doc_of(positions):
        return jnp.sum((positions[:, None] >= doc_bounds[None, :]).astype(jnp.int32), axis=1)

    q_pos = group_positions(my_index.reshape(1))
    q_doc = doc_of(q_pos)

    def attend_group(attn_state, key_rows, value_rows, allowed):
        running_max, weight_sum, accum = attn_state
        scores = (
            jnp.einsum("qhd,kd->qhk", query_rows, key_rows, preferred_element_type=jnp.float32)
            * score_scale
        )
        masked = jnp.where(allowed[:, None, :], scores, -1e30)
        new_max = jnp.maximum(running_max, jnp.max(masked, axis=2))
        weights = jnp.where(allowed[:, None, :], jnp.exp(masked - new_max[..., None]), 0.0)
        factor = jnp.exp(running_max - new_max)
        weight_sum = weight_sum * factor + jnp.sum(weights, axis=2)
        update = jnp.einsum(
            "qhk,kd->qhd",
            weights.astype(jnp.bfloat16),
            value_rows,
            preferred_element_type=jnp.float32,
        )
        accum = accum * factor[..., None] + update
        return (new_max, weight_sum, accum)

    def visit_group(attn_state, key_group, value_group, owner_ids):
        key_rows = key_group.reshape(-1, head_dim)
        value_rows = value_group.reshape(-1, head_dim)
        k_pos = group_positions(owner_ids)
        allowed = (k_pos[None, :] <= q_pos[:, None]) & (doc_of(k_pos)[None, :] == q_doc[:, None])
        return attend_group(attn_state, key_rows, value_rows, allowed)

    def place_pages(page_store, key_group, value_group, owner_ids):
        page_rows = jnp.concatenate([key_group, value_group], axis=-1).reshape(
            -1, PAGE * 2 * head_dim
        )
        slot_ids = jnp.take(page_slot, owner_ids, axis=0).reshape(-1) - my_index * slot_count
        selector = (slot_range[:, None] == slot_ids[None, :]).astype(jnp.bfloat16)
        return page_store + jnp.dot(selector, page_rows, preferred_element_type=jnp.float32)

    def fold_groups(step_fn, carried, kv_piece):
        key_piece, value_piece = kv_piece
        piece_len = key_piece.shape[0]
        width = 4
        owner_ids = jnp.arange(piece_len, dtype=jnp.int32).reshape(piece_len // width, width)
        key_groups = key_piece.reshape(piece_len // width, width, 2, block_tok, head_dim)
        value_groups = value_piece.reshape(piece_len // width, width, 2, block_tok, head_dim)

        def visit_one(inner_state, entry_tuple):
            key_group, value_group, owners = entry_tuple
            return (step_fn(inner_state, key_group, value_group, owners), None)

        return lax.scan(visit_one, carried, (key_groups, value_groups, owner_ids))[0]

    empty_store = jnp.zeros((slot_count, PAGE * 2 * head_dim), jnp.float32)
    start_state = (
        jnp.full((2 * block_tok, group_size), -1e30, jnp.float32),
        jnp.zeros((2 * block_tok, group_size), jnp.float32),
        jnp.zeros((2 * block_tok, group_size, head_dim), jnp.float32),
    )
    final_state = fold_groups(
        visit_group,
        start_state,
        (
            lax.all_gather(key_states, "blk", axis=0, tiled=True),
            lax.all_gather(value_states, "blk", axis=0, tiled=True),
        ),
    )
    page_store = fold_groups(
        place_pages,
        empty_store,
        (
            lax.all_gather(key_states, "blk", axis=0, tiled=True),
            lax.all_gather(value_states, "blk", axis=0, tiled=True),
        ),
    )
    running_max, weight_sum, accum = final_state
    attended = (
        (accum / weight_sum[..., None])
        .astype(jnp.bfloat16)
        .reshape(1, 2, block_tok, group_size * head_dim)
    )
    kv_cache = page_store.astype(jnp.bfloat16).reshape(slot_count, 1, PAGE, 2 * head_dim)
    return (attended, kv_cache)


def solution(mesh):
    return jax.shard_map(
        per_device if mesh.shape["blk"] <= 8 else per_device_long,
        mesh=mesh,
        in_specs=(
            P("blk", None, "head", None),
            P("blk", None, None, "head"),
            P("blk", None, None, "head"),
            P(),
            P(),
        ),
        out_specs=(P("blk", None, None, "head"), P("blk", "head", None, None)),
        check_vma=False,
    )
```

```python
import functools

import jax
import jax.numpy as jnp
from jax import lax
from jax.experimental import pallas as pl
from jax.experimental.pallas import tpu as pltpu
from jax.sharding import PartitionSpec as P

PAGE = 16
LOG2E = 1.4426950408889634
HEAD_DIM = 128
LANES = 128


def gather_queries(own, across, beside, half):
    my_head = lax.axis_index("head")
    width = beside.shape[-1]
    parts = []
    for lane in range(0, width, HEAD_DIM):
        mine = pl.multiple_of(my_head * width + lane, HEAD_DIM)
        low = pl.multiple_of((my_head & 1) * width + lane, HEAD_DIM)
        parts.append(own[0, half, :, pl.ds(mine, HEAD_DIM)])
        parts.append(beside[0, half, :, lane : lane + HEAD_DIM])
        parts.append(across[0, half, :, pl.ds(low, HEAD_DIM)])
        parts.append(beside[1, half, :, lane : lane + HEAD_DIM])
    return jnp.concatenate(parts, axis=0)


def key_bias(my_blk, lengths, chips, block_tok, sub_tok, half, core):
    blk_count = 2 * chips
    my_block = my_blk if half == 0 else 2 * blk_count - 1 - my_blk
    lane = lax.broadcasted_iota(jnp.int32, (1, LANES), 1)
    sender = lax.axis_index("head") ^ (lane % block_tok // sub_tok)
    q_pos = my_block * block_tok + sender * sub_tok + lane % sub_tok
    first = jnp.zeros_like(q_pos)
    bound = jnp.zeros_like(lengths[:, :1])
    for k in range(lengths.shape[1] - 1):
        bound = bound + lengths[:, k : k + 1]
        first = jnp.where(q_pos >= bound, bound, first)
    row = lax.broadcasted_iota(jnp.int32, (block_tok, LANES), 0)
    parts = []
    for m in range(chips):
        owner = (my_blk ^ core) ^ (2 * m)
        for side in range(half + 1):
            block = owner if side == 0 else 2 * blk_count - 1 - owner
            if core == 0 and m == 0 and side == half:
                allowed = (row <= q_pos - block * block_tok) & (row >= first - block * block_tok)
            else:
                allowed = row >= first - jnp.where(block < my_block, block * block_tok, -(2**28))
            parts.append(jnp.where(allowed, 0.0, -1e30))
    return jnp.concatenate(parts, axis=0)


def page_targets(my_blk, page_slot, chips, slot_count, core):
    _, pages_blk, blk_count = page_slot.shape
    chip = lax.broadcasted_iota(jnp.int32, (chips, blk_count), 0)
    owner = (my_blk ^ core) ^ (2 * chip)
    chosen = (owner == lax.broadcasted_iota(jnp.int32, (chips, blk_count), 1)).astype(jnp.float32).astype(jnp.bfloat16)
    cols = 2 * pages_blk * PAGE
    page = lax.broadcasted_iota(jnp.int32, (pages_blk, cols), 0)
    col = lax.broadcasted_iota(jnp.int32, (pages_blk, cols), 1)
    slots = 0.0
    for half in range(2):
        held = lax.dot_general(
            chosen,
            page_slot[half].astype(jnp.float32).astype(jnp.bfloat16),
            (((1,), (1,)), ((), ())),
            preferred_element_type=jnp.float32,
        )
        spread = (col // PAGE == page + half * pages_blk).astype(jnp.float32).astype(jnp.bfloat16)
        slots = slots + jnp.dot(held.astype(jnp.bfloat16), spread, preferred_element_type=jnp.float32)
    slots = slots.astype(jnp.int32) - my_blk * slot_count
    rows = slots * PAGE + lax.broadcasted_iota(jnp.int32, slots.shape, 1) % PAGE
    return jnp.concatenate([rows[m : m + 1] for m in range(chips)], axis=1)


def place_pages(targets, keys, values, slot_count):
    rows = jnp.concatenate([keys[...].reshape(-1, HEAD_DIM), values[...].reshape(-1, HEAD_DIM)], axis=1)
    row = lax.broadcasted_iota(jnp.int32, (slot_count * PAGE, rows.shape[0]), 0)
    chosen = jnp.where(row == targets, 1.0, 0.0).astype(jnp.bfloat16)
    return jnp.dot(chosen, rows, preferred_element_type=jnp.float32)


def score_part(queries, keys, half):
    keys = keys[:, : half + 1].reshape(-1, HEAD_DIM)
    return lax.dot_general(keys, queries, (((1,), (1,)), ((), ())), preferred_element_type=jnp.float32)


def soften(scores, bias):
    bias = jnp.concatenate([bias] * (scores.shape[1] // LANES), axis=1)
    scores = scores * (HEAD_DIM**-0.5 * LOG2E) + bias
    top = jnp.max(scores, axis=0, keepdims=True)
    weights = jnp.exp2(scores - top)
    return top, jnp.sum(weights, axis=0, keepdims=True), weights.astype(jnp.bfloat16)


def weigh_part(weights, values, half):
    values = values[:, : half + 1].reshape(-1, HEAD_DIM)
    return lax.dot_general(values, weights, (((0,), (0,)), ((), ())), preferred_element_type=jnp.float32)


def fetch_kernel(queries, lengths, page_slot, part, lengths_out, slots_out, sems):
    _, halves, _, width = part.shape
    start = ((lax.axis_index("head") & 2) ^ 2) * (width // 2)
    pairs = [(lengths, lengths_out), (page_slot, slots_out)]
    for half in range(halves):
        for lane in range(0, width, width // 2):
            lanes = pl.ds(pl.multiple_of(start + lane, width // 2), width // 2)
            pairs.append((queries.at[0, half, :, lanes], part.at[0, half, :, lane : lane + width // 2]))
    copies = [pltpu.make_async_copy(a, b, sems.at[k]) for k, (a, b) in enumerate(pairs)]
    for copy in copies:
        copy.start()
    for copy in copies:
        copy.wait()


def plan_kernel(
    lengths, page_slot, near_k, near_v, bias_a, bias_b, far_bias_a, far_bias_b, far_targets, pages_ref
):
    chips, _, block_tok, _ = near_k.shape
    slot_count = pages_ref.shape[0] // PAGE
    sub_tok = block_tok // lax.axis_size("head")
    my_blk = lax.axis_index("blk")
    targets = functools.partial(page_targets, my_blk, page_slot, chips, slot_count)
    pages_ref[...] = place_pages(targets(0), near_k, near_v, slot_count).astype(jnp.bfloat16)
    far_targets[...] = targets(1)
    bias = functools.partial(key_bias, my_blk, lengths[...], chips, block_tok, sub_tok)
    for half in range(2):
        (bias_a, bias_b)[half][...] = bias(half, 0)
        (far_bias_a, far_bias_b)[half][...] = bias(half, 1)


def near_kernel(own, across, beside, near_k, near_v, bias_a, bias_b, q_rows, top_ref, total_ref, out_ref):
    scores = {}
    for half in (1, 0):
        queries = gather_queries(own, across, beside, half)
        q_rows[half] = queries
        scores[half] = score_part(queries, near_k, half)
    for half in (1, 0):
        top_ref[half], total_ref[half], weights = soften(scores[half], (bias_a, bias_b)[half][...])
        out_ref[half] = weigh_part(weights, near_v, half)


def far_kernel(
    far_k, far_v, bias_a, bias_b, far_targets, pages_ref, q_rows, top_ref, total_ref, out_ref, attended, kv_cache,
    pages, result, sems,
):
    block_tok = far_k.shape[2]
    slot_count = kv_cache.shape[0]
    my_head = lax.axis_index("head")
    sub_tok = block_tok // lax.axis_size("head")
    scores = {half: score_part(q_rows[half], far_k, half) for half in (1, 0)}
    moved = place_pages(far_targets[...], far_k, far_v, slot_count) + pages_ref[...].astype(jnp.float32)
    pages[...] = moved.astype(jnp.bfloat16).reshape(pages.shape)
    writes = [pltpu.make_async_copy(pages, kv_cache, sems.at[2])]
    writes[0].start()
    parts = {}
    for half in (1, 0):
        top, total, weights = soften(scores[half], (bias_a, bias_b)[half][...])
        parts[half] = (top, total, weigh_part(weights, far_v, half))
    for half in (1, 0):
        top, total, out = parts[half]
        best = jnp.maximum(top, top_ref[half])
        here = jnp.exp2(top - best)
        there = jnp.exp2(top_ref[half] - best)
        inverse = 1.0 / (total * here + total_ref[half] * there)
        out = (out * (here * inverse) + out_ref[half] * (there * inverse)).T.astype(jnp.bfloat16)
        for g in range(out.shape[0] // block_tok):
            for d in range(block_tok // sub_tok):
                row = pl.multiple_of((my_head ^ d) * sub_tok, sub_tok)
                start = g * block_tok + d * sub_tok
                result[half, pl.ds(row, sub_tok), g * HEAD_DIM : (g + 1) * HEAD_DIM] = out[start : start + sub_tok]
        writes.append(pltpu.make_async_copy(result.at[half], attended.at[0, half], sems.at[half]))
        writes[-1].start()
    for write in writes:
        write.wait()


def per_device(query_states, key_states, value_states, doc_lengths, page_slot):
    blk_count = lax.axis_size("blk")
    head_count = lax.axis_size("head")
    q_width = query_states.shape[3]
    block_tok = key_states.shape[2]
    width = q_width // head_count
    rows = width // HEAD_DIM * block_tok
    slot_count = 4 * (block_tok // PAGE)

    my_head = lax.axis_index("head")
    hbm = pl.BlockSpec(memory_space=pl.ANY)
    vmem = pl.BlockSpec(memory_space=pltpu.VMEM)
    fetched = [query_states, doc_lengths.reshape(1, -1), page_slot.transpose(1, 2, 0)]
    part, lengths, slots = pl.pallas_call(
        fetch_kernel,
        out_shape=(
            jax.ShapeDtypeStruct((*query_states.shape[:3], 2 * width), query_states.dtype),
            *(jax.ShapeDtypeStruct(x.shape, x.dtype) for x in fetched[1:]),
        ),
        in_specs=[hbm] * 3,
        out_specs=(vmem,) * 3,
        scratch_shapes=[pltpu.SemaphoreType.DMA((6,))],
        compiler_params=pltpu.CompilerParams(vmem_limit_bytes=4 * 1024 * 1024),
        cost_estimate=pl.CostEstimate(flops=0, bytes_accessed=200_000, transcendentals=0),
    )(*(pltpu.with_memory_space_constraint(x, pltpu.HBM) for x in fetched))
    across = lax.ppermute(part, "head", [(i, i ^ 2) for i in range(head_count)])
    pair = jnp.concatenate([key_states, value_states], axis=3)
    pair, _ = lax.optimization_barrier((pair, part))
    near = [
        lax.ppermute(pair, "blk", [(i, i ^ d) for i in range(blk_count)]) for d in range(2, blk_count, 2)
    ]
    beside = jnp.concatenate(
        [
            lax.dynamic_slice_in_dim(query_states, (my_head ^ 1) * width, width, axis=3),
            lax.dynamic_slice_in_dim(across, ((my_head & 1) ^ 1) * width, width, axis=3),
        ],
        axis=0,
    )
    near = lax.optimization_barrier((near[::-1], beside))[0][::-1]
    beside = lax.ppermute(beside, "head", [(i, i ^ 1) for i in range(head_count)])
    near = [pair] + near
    near_k = jnp.concatenate([p[..., :HEAD_DIM] for p in near], axis=0)
    near_v = jnp.concatenate([p[..., HEAD_DIM:] for p in near], axis=0)
    far_k, far_v = (lax.ppermute(x, "blk", [(i, i ^ 1) for i in range(blk_count)]) for x in (near_k, near_v))

    params = pltpu.CompilerParams(vmem_limit_bytes=32 * 1024 * 1024)
    cost = pl.CostEstimate(flops=4_000_000_000, bytes_accessed=1_000_000, transcendentals=200_000)
    half_cols = blk_count // 2 * block_tok
    *bias, far_bias_a, far_bias_b, far_targets, pages = pl.pallas_call(
        plan_kernel,
        out_shape=(
            jax.ShapeDtypeStruct((half_cols, LANES), jnp.float32),
            jax.ShapeDtypeStruct((2 * half_cols, LANES), jnp.float32),
        )
        * 2
        + (
            jax.ShapeDtypeStruct((1, 2 * half_cols), jnp.int32),
            jax.ShapeDtypeStruct((slot_count * PAGE, 2 * HEAD_DIM), jnp.bfloat16),
        ),
        in_specs=[vmem] * 4,
        out_specs=(vmem,) * 6,
        compiler_params=params,
        cost_estimate=cost,
    )(lengths, slots, near_k, near_v)
    stats = pl.pallas_call(
        near_kernel,
        out_shape=(
            jax.ShapeDtypeStruct((2, rows, HEAD_DIM), jnp.bfloat16),
            jax.ShapeDtypeStruct((2, 1, rows), jnp.float32),
            jax.ShapeDtypeStruct((2, 1, rows), jnp.float32),
            jax.ShapeDtypeStruct((2, HEAD_DIM, rows), jnp.float32),
        ),
        in_specs=[vmem] * 7,
        out_specs=(vmem,) * 4,
        compiler_params=params,
        cost_estimate=cost,
    )(query_states, across, beside, near_k, near_v, *bias)
    return pl.pallas_call(
        far_kernel,
        out_shape=(
            jax.ShapeDtypeStruct((1, 2, block_tok, width), jnp.bfloat16),
            jax.ShapeDtypeStruct((slot_count, 1, PAGE, 2 * HEAD_DIM), jnp.bfloat16),
        ),
        in_specs=[vmem] * 10,
        out_specs=(hbm, hbm),
        scratch_shapes=[
            pltpu.VMEM((slot_count, 1, PAGE, 2 * HEAD_DIM), jnp.bfloat16),
            pltpu.VMEM((2, block_tok, width), jnp.bfloat16),
            pltpu.SemaphoreType.DMA((3,)),
        ],
        compiler_params=params,
        cost_estimate=cost,
    )(far_k, far_v, far_bias_a, far_bias_b, far_targets, pages, *stats)


def per_device_long(query_states, key_states, value_states, doc_lengths, page_slot):
    q_local = lax.all_to_all(query_states, "head", split_axis=3, concat_axis=2, tiled=True)
    axis_count = lax.axis_size("blk")
    my_index = lax.axis_index("blk")
    block_tok = q_local.shape[2]
    head_dim = key_states.shape[3]
    group_size = q_local.shape[3] // head_dim
    query_rows = q_local.reshape(2 * block_tok, group_size, head_dim)
    offsets = jnp.arange(block_tok, dtype=jnp.int32)
    doc_bounds = jnp.cumsum(doc_lengths)[:-1]
    page_count = block_tok // PAGE
    slot_count = 4 * page_count
    slot_range = jnp.arange(slot_count, dtype=jnp.int32)
    score_scale = head_dim ** (-0.5)

    def group_positions(owner_ids):
        block_starts = jnp.stack([owner_ids, 2 * axis_count - 1 - owner_ids], axis=1) * block_tok
        return (block_starts[:, :, None] + offsets[None, None, :]).reshape(-1)

    def doc_of(positions):
        return jnp.sum((positions[:, None] >= doc_bounds[None, :]).astype(jnp.int32), axis=1)

    q_pos = group_positions(my_index.reshape(1))
    q_doc = doc_of(q_pos)

    def attend_group(attn_state, key_rows, value_rows, allowed):
        running_max, weight_sum, accum = attn_state
        scores = (
            jnp.einsum("qhd,kd->qhk", query_rows, key_rows, preferred_element_type=jnp.float32)
            * score_scale
        )
        masked = jnp.where(allowed[:, None, :], scores, -1e30)
        new_max = jnp.maximum(running_max, jnp.max(masked, axis=2))
        weights = jnp.where(allowed[:, None, :], jnp.exp(masked - new_max[..., None]), 0.0)
        factor = jnp.exp(running_max - new_max)
        weight_sum = weight_sum * factor + jnp.sum(weights, axis=2)
        update = jnp.einsum(
            "qhk,kd->qhd",
            weights.astype(jnp.bfloat16),
            value_rows,
            preferred_element_type=jnp.float32,
        )
        accum = accum * factor[..., None] + update
        return (new_max, weight_sum, accum)

    def visit_group(attn_state, key_group, value_group, owner_ids):
        key_rows = key_group.reshape(-1, head_dim)
        value_rows = value_group.reshape(-1, head_dim)
        k_pos = group_positions(owner_ids)
        allowed = (k_pos[None, :] <= q_pos[:, None]) & (doc_of(k_pos)[None, :] == q_doc[:, None])
        return attend_group(attn_state, key_rows, value_rows, allowed)

    def place_pages(page_store, key_group, value_group, owner_ids):
        page_rows = jnp.concatenate([key_group, value_group], axis=-1).reshape(
            -1, PAGE * 2 * head_dim
        )
        slot_ids = jnp.take(page_slot, owner_ids, axis=0).reshape(-1) - my_index * slot_count
        selector = (slot_range[:, None] == slot_ids[None, :]).astype(jnp.bfloat16)
        return page_store + jnp.dot(selector, page_rows, preferred_element_type=jnp.float32)

    def fold_groups(step_fn, carried, kv_piece):
        key_piece, value_piece = kv_piece
        piece_len = key_piece.shape[0]
        width = 4
        owner_ids = jnp.arange(piece_len, dtype=jnp.int32).reshape(piece_len // width, width)
        key_groups = key_piece.reshape(piece_len // width, width, 2, block_tok, head_dim)
        value_groups = value_piece.reshape(piece_len // width, width, 2, block_tok, head_dim)

        def visit_one(inner_state, entry_tuple):
            key_group, value_group, owners = entry_tuple
            return (step_fn(inner_state, key_group, value_group, owners), None)

        return lax.scan(visit_one, carried, (key_groups, value_groups, owner_ids))[0]

    empty_store = jnp.zeros((slot_count, PAGE * 2 * head_dim), jnp.float32)
    start_state = (
        jnp.full((2 * block_tok, group_size), -1e30, jnp.float32),
        jnp.zeros((2 * block_tok, group_size), jnp.float32),
        jnp.zeros((2 * block_tok, group_size, head_dim), jnp.float32),
    )
    final_state = fold_groups(
        visit_group,
        start_state,
        (
            lax.all_gather(key_states, "blk", axis=0, tiled=True),
            lax.all_gather(value_states, "blk", axis=0, tiled=True),
        ),
    )
    page_store = fold_groups(
        place_pages,
        empty_store,
        (
            lax.all_gather(key_states, "blk", axis=0, tiled=True),
            lax.all_gather(value_states, "blk", axis=0, tiled=True),
        ),
    )
    running_max, weight_sum, accum = final_state
    attended = (
        (accum / weight_sum[..., None])
        .astype(jnp.bfloat16)
        .reshape(1, 2, block_tok, group_size * head_dim)
    )
    kv_cache = page_store.astype(jnp.bfloat16).reshape(slot_count, 1, PAGE, 2 * head_dim)
    return (attended, kv_cache)


def solution(mesh):
    return jax.shard_map(
        per_device if mesh.shape["blk"] <= 8 else per_device_long,
        mesh=mesh,
        in_specs=(
            P("blk", None, "head", None),
            P("blk", None, None, "head"),
            P("blk", None, None, "head"),
            P(),
            P(),
        ),
        out_specs=(P("blk", None, None, "head"), P("blk", "head", None, None)),
        check_vma=False,
    )
```

```python
import functools

import jax
import jax.numpy as jnp
from jax import lax
from jax.experimental import pallas as pl
from jax.experimental.pallas import tpu as pltpu
from jax.sharding import PartitionSpec as P

PAGE = 16
LOG2E = 1.4426950408889634
HEAD_DIM = 128
LANES = 128


def gather_queries(own, across, beside, half):
    my_head = lax.axis_index("head")
    width = beside.shape[-1]
    parts = []
    for lane in range(0, width, HEAD_DIM):
        mine = pl.multiple_of(my_head * width + lane, HEAD_DIM)
        low = pl.multiple_of((my_head & 1) * width + lane, HEAD_DIM)
        parts.append(own[0, half, :, pl.ds(mine, HEAD_DIM)])
        parts.append(beside[0, half, :, lane : lane + HEAD_DIM])
        parts.append(across[0, half, :, pl.ds(low, HEAD_DIM)])
        parts.append(beside[1, half, :, lane : lane + HEAD_DIM])
    return jnp.concatenate(parts, axis=0)


def key_bias(my_blk, lengths, chips, block_tok, sub_tok, half, core):
    blk_count = 2 * chips
    my_block = my_blk if half == 0 else 2 * blk_count - 1 - my_blk
    lane = lax.broadcasted_iota(jnp.int32, (1, LANES), 1)
    sender = lax.axis_index("head") ^ (lane % block_tok // sub_tok)
    q_pos = my_block * block_tok + sender * sub_tok + lane % sub_tok
    first = jnp.zeros_like(q_pos)
    bound = jnp.zeros_like(lengths[:, :1])
    for k in range(lengths.shape[1] - 1):
        bound = bound + lengths[:, k : k + 1]
        first = jnp.where(q_pos >= bound, bound, first)
    row = lax.broadcasted_iota(jnp.int32, (block_tok, LANES), 0)
    parts = []
    for m in range(chips):
        owner = (my_blk ^ core) ^ (2 * m)
        for side in range(half + 1):
            block = owner if side == 0 else 2 * blk_count - 1 - owner
            if core == 0 and m == 0 and side == half:
                allowed = (row <= q_pos - block * block_tok) & (row >= first - block * block_tok)
            else:
                allowed = row >= first - jnp.where(block < my_block, block * block_tok, -(2**28))
            parts.append(jnp.where(allowed, 0.0, -1e30))
    return jnp.concatenate(parts, axis=0)


def page_targets(my_blk, page_slot, chips, slot_count, core):
    _, pages_blk, blk_count = page_slot.shape
    chip = lax.broadcasted_iota(jnp.int32, (chips, blk_count), 0)
    owner = (my_blk ^ core) ^ (2 * chip)
    chosen = (owner == lax.broadcasted_iota(jnp.int32, (chips, blk_count), 1)).astype(jnp.float32).astype(jnp.bfloat16)
    cols = 2 * pages_blk * PAGE
    page = lax.broadcasted_iota(jnp.int32, (pages_blk, cols), 0)
    col = lax.broadcasted_iota(jnp.int32, (pages_blk, cols), 1)
    slots = 0.0
    for half in range(2):
        held = lax.dot_general(
            chosen,
            page_slot[half].astype(jnp.float32).astype(jnp.bfloat16),
            (((1,), (1,)), ((), ())),
            preferred_element_type=jnp.float32,
        )
        spread = (col // PAGE == page + half * pages_blk).astype(jnp.float32).astype(jnp.bfloat16)
        slots = slots + jnp.dot(held.astype(jnp.bfloat16), spread, preferred_element_type=jnp.float32)
    slots = slots.astype(jnp.int32) - my_blk * slot_count
    rows = slots * PAGE + lax.broadcasted_iota(jnp.int32, slots.shape, 1) % PAGE
    return jnp.concatenate([rows[m : m + 1] for m in range(chips)], axis=1)


def place_pages(targets, pairs, slot_count):
    rows = pairs[...].reshape(-1, pairs.shape[-1])
    row = lax.broadcasted_iota(jnp.int32, (slot_count * PAGE, rows.shape[0]), 0)
    chosen = jnp.where(row == targets, 1.0, 0.0).astype(jnp.bfloat16)
    return jnp.dot(chosen, rows, preferred_element_type=jnp.float32)


def score_part(queries, pairs, half):
    keys = pairs[:, : half + 1].reshape(-1, 2 * HEAD_DIM)[:, :HEAD_DIM]
    return lax.dot_general(keys, queries, (((1,), (1,)), ((), ())), preferred_element_type=jnp.float32)


def soften(scores, bias):
    bias = jnp.concatenate([bias] * (scores.shape[1] // LANES), axis=1)
    scores = scores * (HEAD_DIM**-0.5 * LOG2E) + bias
    top = jnp.max(scores, axis=0, keepdims=True)
    weights = jnp.exp2(scores - top)
    return top, jnp.sum(weights, axis=0, keepdims=True), weights.astype(jnp.bfloat16)


def weigh_part(weights, pairs, half):
    values = pairs[:, : half + 1].reshape(-1, 2 * HEAD_DIM)[:, HEAD_DIM:]
    return lax.dot_general(values, weights, (((0,), (0,)), ((), ())), preferred_element_type=jnp.float32)


def fetch_kernel(queries, lengths, page_slot, part, lengths_out, slots_out, sems):
    _, halves, _, width = part.shape
    start = ((lax.axis_index("head") & 2) ^ 2) * (width // 2)
    pairs = [(lengths, lengths_out), (page_slot, slots_out)]
    for half in range(halves):
        for lane in range(0, width, width // 2):
            lanes = pl.ds(pl.multiple_of(start + lane, width // 2), width // 2)
            pairs.append((queries.at[0, half, :, lanes], part.at[0, half, :, lane : lane + width // 2]))
    copies = [pltpu.make_async_copy(a, b, sems.at[k]) for k, (a, b) in enumerate(pairs)]
    for copy in copies:
        copy.start()
    for copy in copies:
        copy.wait()


def plan_kernel(
    lengths, page_slot, near, bias_a, bias_b, far_bias_a, far_bias_b, far_targets, pages_ref
):
    chips, _, block_tok, _ = near.shape
    slot_count = pages_ref.shape[0] // PAGE
    sub_tok = block_tok // lax.axis_size("head")
    my_blk = lax.axis_index("blk")
    targets = functools.partial(page_targets, my_blk, page_slot, chips, slot_count)
    pages_ref[...] = place_pages(targets(0), near, slot_count).astype(jnp.bfloat16)
    far_targets[...] = targets(1)
    bias = functools.partial(key_bias, my_blk, lengths[...], chips, block_tok, sub_tok)
    for half in range(2):
        (bias_a, bias_b)[half][...] = bias(half, 0)
        (far_bias_a, far_bias_b)[half][...] = bias(half, 1)


def near_kernel(own, across, beside, near, bias_a, bias_b, q_rows, top_ref, total_ref, out_ref):
    scores = {}
    for half in (1, 0):
        queries = gather_queries(own, across, beside, half)
        q_rows[half] = queries
        scores[half] = score_part(queries, near, half)
    for half in (1, 0):
        top_ref[half], total_ref[half], weights = soften(scores[half], (bias_a, bias_b)[half][...])
        out_ref[half] = weigh_part(weights, near, half)


def far_kernel(
    far, bias_a, bias_b, far_targets, pages_ref, q_rows, top_ref, total_ref, out_ref, attended, kv_cache,
    pages, result, sems,
):
    block_tok = far.shape[2]
    slot_count = kv_cache.shape[0]
    my_head = lax.axis_index("head")
    sub_tok = block_tok // lax.axis_size("head")
    scores = {half: score_part(q_rows[half], far, half) for half in (1, 0)}
    moved = place_pages(far_targets[...], far, slot_count) + pages_ref[...].astype(jnp.float32)
    pages[...] = moved.astype(jnp.bfloat16).reshape(pages.shape)
    writes = [pltpu.make_async_copy(pages, kv_cache, sems.at[2])]
    writes[0].start()
    parts = {}
    for half in (1, 0):
        top, total, weights = soften(scores[half], (bias_a, bias_b)[half][...])
        parts[half] = (top, total, weigh_part(weights, far, half))
    for half in (1, 0):
        top, total, out = parts[half]
        best = jnp.maximum(top, top_ref[half])
        here = jnp.exp2(top - best)
        there = jnp.exp2(top_ref[half] - best)
        inverse = 1.0 / (total * here + total_ref[half] * there)
        out = (out * (here * inverse) + out_ref[half] * (there * inverse)).T.astype(jnp.bfloat16)
        for g in range(out.shape[0] // block_tok):
            for d in range(block_tok // sub_tok):
                row = pl.multiple_of((my_head ^ d) * sub_tok, sub_tok)
                start = g * block_tok + d * sub_tok
                result[half, pl.ds(row, sub_tok), g * HEAD_DIM : (g + 1) * HEAD_DIM] = out[start : start + sub_tok]
        writes.append(pltpu.make_async_copy(result.at[half], attended.at[0, half], sems.at[half]))
        writes[-1].start()
    for write in writes:
        write.wait()


def per_device(query_states, key_states, value_states, doc_lengths, page_slot):
    blk_count = lax.axis_size("blk")
    head_count = lax.axis_size("head")
    q_width = query_states.shape[3]
    block_tok = key_states.shape[2]
    width = q_width // head_count
    rows = width // HEAD_DIM * block_tok
    slot_count = 4 * (block_tok // PAGE)

    my_head = lax.axis_index("head")
    hbm = pl.BlockSpec(memory_space=pl.ANY)
    vmem = pl.BlockSpec(memory_space=pltpu.VMEM)
    fetched = [query_states, doc_lengths.reshape(1, -1), page_slot.transpose(1, 2, 0)]
    part, lengths, slots = pl.pallas_call(
        fetch_kernel,
        out_shape=(
            jax.ShapeDtypeStruct((*query_states.shape[:3], 2 * width), query_states.dtype),
            *(jax.ShapeDtypeStruct(x.shape, x.dtype) for x in fetched[1:]),
        ),
        in_specs=[hbm] * 3,
        out_specs=(vmem,) * 3,
        scratch_shapes=[pltpu.SemaphoreType.DMA((6,))],
        compiler_params=pltpu.CompilerParams(vmem_limit_bytes=4 * 1024 * 1024),
        cost_estimate=pl.CostEstimate(flops=0, bytes_accessed=200_000, transcendentals=0),
    )(*(pltpu.with_memory_space_constraint(x, pltpu.HBM) for x in fetched))
    across = lax.ppermute(part, "head", [(i, i ^ 2) for i in range(head_count)])
    pair = jnp.concatenate([key_states, value_states], axis=3)
    pair, _ = lax.optimization_barrier((pair, part))
    near = [
        lax.ppermute(pair, "blk", [(i, i ^ d) for i in range(blk_count)]) for d in range(2, blk_count, 2)
    ]
    beside = jnp.concatenate(
        [
            lax.dynamic_slice_in_dim(query_states, (my_head ^ 1) * width, width, axis=3),
            lax.dynamic_slice_in_dim(across, ((my_head & 1) ^ 1) * width, width, axis=3),
        ],
        axis=0,
    )
    near = lax.optimization_barrier((near[::-1], beside))[0][::-1]
    beside = lax.ppermute(beside, "head", [(i, i ^ 1) for i in range(head_count)])
    near = jnp.concatenate([pair] + near, axis=0)
    far = lax.ppermute(near, "blk", [(i, i ^ 1) for i in range(blk_count)])

    params = pltpu.CompilerParams(vmem_limit_bytes=32 * 1024 * 1024)
    cost = pl.CostEstimate(flops=4_000_000_000, bytes_accessed=1_000_000, transcendentals=200_000)
    half_cols = blk_count // 2 * block_tok
    *bias, far_bias_a, far_bias_b, far_targets, pages = pl.pallas_call(
        plan_kernel,
        out_shape=(
            jax.ShapeDtypeStruct((half_cols, LANES), jnp.float32),
            jax.ShapeDtypeStruct((2 * half_cols, LANES), jnp.float32),
        )
        * 2
        + (
            jax.ShapeDtypeStruct((1, 2 * half_cols), jnp.int32),
            jax.ShapeDtypeStruct((slot_count * PAGE, 2 * HEAD_DIM), jnp.bfloat16),
        ),
        in_specs=[vmem] * 3,
        out_specs=(vmem,) * 6,
        compiler_params=params,
        cost_estimate=cost,
    )(lengths, slots, near)
    stats = pl.pallas_call(
        near_kernel,
        out_shape=(
            jax.ShapeDtypeStruct((2, rows, HEAD_DIM), jnp.bfloat16),
            jax.ShapeDtypeStruct((2, 1, rows), jnp.float32),
            jax.ShapeDtypeStruct((2, 1, rows), jnp.float32),
            jax.ShapeDtypeStruct((2, HEAD_DIM, rows), jnp.float32),
        ),
        in_specs=[vmem] * 6,
        out_specs=(vmem,) * 4,
        compiler_params=params,
        cost_estimate=cost,
    )(query_states, across, beside, near, *bias)
    return pl.pallas_call(
        far_kernel,
        out_shape=(
            jax.ShapeDtypeStruct((1, 2, block_tok, width), jnp.bfloat16),
            jax.ShapeDtypeStruct((slot_count, 1, PAGE, 2 * HEAD_DIM), jnp.bfloat16),
        ),
        in_specs=[vmem] * 9,
        out_specs=(hbm, hbm),
        scratch_shapes=[
            pltpu.VMEM((slot_count, 1, PAGE, 2 * HEAD_DIM), jnp.bfloat16),
            pltpu.VMEM((2, block_tok, width), jnp.bfloat16),
            pltpu.SemaphoreType.DMA((3,)),
        ],
        compiler_params=params,
        cost_estimate=cost,
    )(far, far_bias_a, far_bias_b, far_targets, pages, *stats)


def per_device_long(query_states, key_states, value_states, doc_lengths, page_slot):
    q_local = lax.all_to_all(query_states, "head", split_axis=3, concat_axis=2, tiled=True)
    axis_count = lax.axis_size("blk")
    my_index = lax.axis_index("blk")
    block_tok = q_local.shape[2]
    head_dim = key_states.shape[3]
    group_size = q_local.shape[3] // head_dim
    query_rows = q_local.reshape(2 * block_tok, group_size, head_dim)
    offsets = jnp.arange(block_tok, dtype=jnp.int32)
    doc_bounds = jnp.cumsum(doc_lengths)[:-1]
    page_count = block_tok // PAGE
    slot_count = 4 * page_count
    slot_range = jnp.arange(slot_count, dtype=jnp.int32)
    score_scale = head_dim ** (-0.5)

    def group_positions(owner_ids):
        block_starts = jnp.stack([owner_ids, 2 * axis_count - 1 - owner_ids], axis=1) * block_tok
        return (block_starts[:, :, None] + offsets[None, None, :]).reshape(-1)

    def doc_of(positions):
        return jnp.sum((positions[:, None] >= doc_bounds[None, :]).astype(jnp.int32), axis=1)

    q_pos = group_positions(my_index.reshape(1))
    q_doc = doc_of(q_pos)

    def attend_group(attn_state, key_rows, value_rows, allowed):
        running_max, weight_sum, accum = attn_state
        scores = (
            jnp.einsum("qhd,kd->qhk", query_rows, key_rows, preferred_element_type=jnp.float32)
            * score_scale
        )
        masked = jnp.where(allowed[:, None, :], scores, -1e30)
        new_max = jnp.maximum(running_max, jnp.max(masked, axis=2))
        weights = jnp.where(allowed[:, None, :], jnp.exp(masked - new_max[..., None]), 0.0)
        factor = jnp.exp(running_max - new_max)
        weight_sum = weight_sum * factor + jnp.sum(weights, axis=2)
        update = jnp.einsum(
            "qhk,kd->qhd",
            weights.astype(jnp.bfloat16),
            value_rows,
            preferred_element_type=jnp.float32,
        )
        accum = accum * factor[..., None] + update
        return (new_max, weight_sum, accum)

    def visit_group(attn_state, key_group, value_group, owner_ids):
        key_rows = key_group.reshape(-1, head_dim)
        value_rows = value_group.reshape(-1, head_dim)
        k_pos = group_positions(owner_ids)
        allowed = (k_pos[None, :] <= q_pos[:, None]) & (doc_of(k_pos)[None, :] == q_doc[:, None])
        return attend_group(attn_state, key_rows, value_rows, allowed)

    def place_pages(page_store, key_group, value_group, owner_ids):
        page_rows = jnp.concatenate([key_group, value_group], axis=-1).reshape(
            -1, PAGE * 2 * head_dim
        )
        slot_ids = jnp.take(page_slot, owner_ids, axis=0).reshape(-1) - my_index * slot_count
        selector = (slot_range[:, None] == slot_ids[None, :]).astype(jnp.bfloat16)
        return page_store + jnp.dot(selector, page_rows, preferred_element_type=jnp.float32)

    def fold_groups(step_fn, carried, kv_piece):
        key_piece, value_piece = kv_piece
        piece_len = key_piece.shape[0]
        width = 4
        owner_ids = jnp.arange(piece_len, dtype=jnp.int32).reshape(piece_len // width, width)
        key_groups = key_piece.reshape(piece_len // width, width, 2, block_tok, head_dim)
        value_groups = value_piece.reshape(piece_len // width, width, 2, block_tok, head_dim)

        def visit_one(inner_state, entry_tuple):
            key_group, value_group, owners = entry_tuple
            return (step_fn(inner_state, key_group, value_group, owners), None)

        return lax.scan(visit_one, carried, (key_groups, value_groups, owner_ids))[0]

    empty_store = jnp.zeros((slot_count, PAGE * 2 * head_dim), jnp.float32)
    start_state = (
        jnp.full((2 * block_tok, group_size), -1e30, jnp.float32),
        jnp.zeros((2 * block_tok, group_size), jnp.float32),
        jnp.zeros((2 * block_tok, group_size, head_dim), jnp.float32),
    )
    final_state = fold_groups(
        visit_group,
        start_state,
        (
            lax.all_gather(key_states, "blk", axis=0, tiled=True),
            lax.all_gather(value_states, "blk", axis=0, tiled=True),
        ),
    )
    page_store = fold_groups(
        place_pages,
        empty_store,
        (
            lax.all_gather(key_states, "blk", axis=0, tiled=True),
            lax.all_gather(value_states, "blk", axis=0, tiled=True),
        ),
    )
    running_max, weight_sum, accum = final_state
    attended = (
        (accum / weight_sum[..., None])
        .astype(jnp.bfloat16)
        .reshape(1, 2, block_tok, group_size * head_dim)
    )
    kv_cache = page_store.astype(jnp.bfloat16).reshape(slot_count, 1, PAGE, 2 * head_dim)
    return (attended, kv_cache)


def solution(mesh):
    return jax.shard_map(
        per_device if mesh.shape["blk"] <= 8 else per_device_long,
        mesh=mesh,
        in_specs=(
            P("blk", None, "head", None),
            P("blk", None, None, "head"),
            P("blk", None, None, "head"),
            P(),
            P(),
        ),
        out_specs=(P("blk", None, None, "head"), P("blk", "head", None, None)),
        check_vma=False,
    )
```

```python
import functools

import jax
import jax.numpy as jnp
from jax import lax
from jax.experimental import pallas as pl
from jax.experimental.pallas import tpu as pltpu
from jax.sharding import PartitionSpec as P

PAGE = 16
LOG2E = 1.4426950408889634
HEAD_DIM = 128
LANES = 128


def gather_queries(own, across, beside, half):
    my_head = lax.axis_index("head")
    width = beside.shape[-1]
    parts = []
    for lane in range(0, width, HEAD_DIM):
        mine = pl.multiple_of(my_head * width + lane, HEAD_DIM)
        low = pl.multiple_of((my_head & 1) * width + lane, HEAD_DIM)
        parts.append(own[0, half, :, pl.ds(mine, HEAD_DIM)])
        parts.append(beside[0, half, :, lane : lane + HEAD_DIM])
        parts.append(across[0, half, :, pl.ds(low, HEAD_DIM)])
        parts.append(beside[1, half, :, lane : lane + HEAD_DIM])
    return jnp.concatenate(parts, axis=0)


def key_bias(my_blk, lengths, chips, block_tok, sub_tok, half, core):
    blk_count = 2 * chips
    my_block = my_blk if half == 0 else 2 * blk_count - 1 - my_blk
    lane = lax.broadcasted_iota(jnp.int32, (1, LANES), 1)
    sender = lax.axis_index("head") ^ (lane % block_tok // sub_tok)
    q_pos = my_block * block_tok + sender * sub_tok + lane % sub_tok
    first = jnp.zeros_like(q_pos)
    bound = jnp.zeros_like(lengths[:, :1])
    for k in range(lengths.shape[1] - 1):
        bound = bound + lengths[:, k : k + 1]
        first = jnp.where(q_pos >= bound, bound, first)
    row = lax.broadcasted_iota(jnp.int32, (block_tok, LANES), 0)
    parts = []
    for m in range(chips):
        owner = (my_blk ^ core) ^ (2 * m)
        for side in range(half + 1):
            block = owner if side == 0 else 2 * blk_count - 1 - owner
            if core == 0 and m == 0 and side == half:
                allowed = (row <= q_pos - block * block_tok) & (row >= first - block * block_tok)
            else:
                allowed = row >= first - jnp.where(block < my_block, block * block_tok, -(2**28))
            parts.append(jnp.where(allowed, 0.0, -1e30))
    return jnp.concatenate(parts, axis=0)


def page_targets(my_blk, page_slot, chips, slot_count, core):
    _, pages_blk, blk_count = page_slot.shape
    chip = lax.broadcasted_iota(jnp.int32, (chips, blk_count), 0)
    owner = (my_blk ^ core) ^ (2 * chip)
    chosen = (owner == lax.broadcasted_iota(jnp.int32, (chips, blk_count), 1)).astype(jnp.float32).astype(jnp.bfloat16)
    cols = 2 * pages_blk * PAGE
    page = lax.broadcasted_iota(jnp.int32, (pages_blk, cols), 0)
    col = lax.broadcasted_iota(jnp.int32, (pages_blk, cols), 1)
    slots = 0.0
    for half in range(2):
        held = lax.dot_general(
            chosen,
            page_slot[half].astype(jnp.float32).astype(jnp.bfloat16),
            (((1,), (1,)), ((), ())),
            preferred_element_type=jnp.float32,
        )
        spread = (col // PAGE == page + half * pages_blk).astype(jnp.float32).astype(jnp.bfloat16)
        slots = slots + jnp.dot(held.astype(jnp.bfloat16), spread, preferred_element_type=jnp.float32)
    slots = slots.astype(jnp.int32) - my_blk * slot_count
    rows = slots * PAGE + lax.broadcasted_iota(jnp.int32, slots.shape, 1) % PAGE
    return jnp.concatenate([rows[m : m + 1] for m in range(chips)], axis=1)


def choose_pages(targets, slot_count):
    row = lax.broadcasted_iota(jnp.int32, (slot_count * PAGE, targets.shape[1]), 0)
    return jnp.where(row == targets, 1.0, 0.0).astype(jnp.bfloat16)


def place_pages(chosen, pairs):
    return jnp.dot(chosen, pairs[...].reshape(-1, pairs.shape[-1]), preferred_element_type=jnp.float32)


def score_part(queries, pairs, half):
    keys = pairs[:, : half + 1].reshape(-1, 2 * HEAD_DIM)[:, :HEAD_DIM]
    return lax.dot_general(keys, queries, (((1,), (1,)), ((), ())), preferred_element_type=jnp.float32)


def soften(scores, bias):
    bias = jnp.concatenate([bias] * (scores.shape[1] // LANES), axis=1)
    scores = scores * (HEAD_DIM**-0.5 * LOG2E) + bias
    top = jnp.max(scores, axis=0, keepdims=True)
    weights = jnp.exp2(scores - top)
    return top, jnp.sum(weights, axis=0, keepdims=True), weights.astype(jnp.bfloat16)


def weigh_part(weights, pairs, half):
    values = pairs[:, : half + 1].reshape(-1, 2 * HEAD_DIM)[:, HEAD_DIM:]
    return lax.dot_general(values, weights, (((0,), (0,)), ((), ())), preferred_element_type=jnp.float32)


def fetch_kernel(queries, lengths, page_slot, part, lengths_out, slots_out, sems):
    _, halves, _, width = part.shape
    start = ((lax.axis_index("head") & 2) ^ 2) * (width // 2)
    pairs = [(lengths, lengths_out), (page_slot, slots_out)]
    for half in range(halves):
        for lane in range(0, width, width // 2):
            lanes = pl.ds(pl.multiple_of(start + lane, width // 2), width // 2)
            pairs.append((queries.at[0, half, :, lanes], part.at[0, half, :, lane : lane + width // 2]))
    copies = [pltpu.make_async_copy(a, b, sems.at[k]) for k, (a, b) in enumerate(pairs)]
    for copy in copies:
        copy.start()
    for copy in copies:
        copy.wait()


def plan_kernel(
    lengths, page_slot, near, bias_a, bias_b, far_bias_a, far_bias_b, far_chosen, pages_ref
):
    chips, _, block_tok, _ = near.shape
    slot_count = pages_ref.shape[0] // PAGE
    sub_tok = block_tok // lax.axis_size("head")
    my_blk = lax.axis_index("blk")
    targets = functools.partial(page_targets, my_blk, page_slot, chips, slot_count)
    pages_ref[...] = place_pages(choose_pages(targets(0), slot_count), near).astype(jnp.bfloat16)
    far_chosen[...] = choose_pages(targets(1), slot_count)
    bias = functools.partial(key_bias, my_blk, lengths[...], chips, block_tok, sub_tok)
    for half in range(2):
        (bias_a, bias_b)[half][...] = bias(half, 0)
        (far_bias_a, far_bias_b)[half][...] = bias(half, 1)


def near_kernel(own, across, beside, near, bias_a, bias_b, q_rows, top_ref, total_ref, out_ref):
    scores = {}
    for half in (1, 0):
        queries = gather_queries(own, across, beside, half)
        q_rows[half] = queries
        scores[half] = score_part(queries, near, half)
    for half in (1, 0):
        top_ref[half], total_ref[half], weights = soften(scores[half], (bias_a, bias_b)[half][...])
        out_ref[half] = weigh_part(weights, near, half)


def far_kernel(
    far, bias_a, bias_b, far_chosen, pages_ref, q_rows, top_ref, total_ref, out_ref, attended, kv_cache,
    pages, result, sems,
):
    block_tok = far.shape[2]
    slot_count = kv_cache.shape[0]
    my_head = lax.axis_index("head")
    sub_tok = block_tok // lax.axis_size("head")
    scores = {half: score_part(q_rows[half], far, half) for half in (1, 0)}
    moved = place_pages(far_chosen[...], far) + pages_ref[...].astype(jnp.float32)
    pages[...] = moved.astype(jnp.bfloat16).reshape(pages.shape)
    writes = [pltpu.make_async_copy(pages, kv_cache, sems.at[2])]
    writes[0].start()
    parts = {}
    for half in (1, 0):
        top, total, weights = soften(scores[half], (bias_a, bias_b)[half][...])
        parts[half] = (top, total, weigh_part(weights, far, half))
    for half in (1, 0):
        top, total, out = parts[half]
        best = jnp.maximum(top, top_ref[half])
        here = jnp.exp2(top - best)
        there = jnp.exp2(top_ref[half] - best)
        inverse = 1.0 / (total * here + total_ref[half] * there)
        out = (out * (here * inverse) + out_ref[half] * (there * inverse)).astype(jnp.bfloat16).T
        for g in range(out.shape[0] // block_tok):
            for d in range(block_tok // sub_tok):
                row = pl.multiple_of((my_head ^ d) * sub_tok, sub_tok)
                start = g * block_tok + d * sub_tok
                result[half, pl.ds(row, sub_tok), g * HEAD_DIM : (g + 1) * HEAD_DIM] = out[start : start + sub_tok]
        writes.append(pltpu.make_async_copy(result.at[half], attended.at[0, half], sems.at[half]))
        writes[-1].start()
    for write in writes:
        write.wait()


def per_device(query_states, key_states, value_states, doc_lengths, page_slot):
    blk_count = lax.axis_size("blk")
    head_count = lax.axis_size("head")
    q_width = query_states.shape[3]
    block_tok = key_states.shape[2]
    width = q_width // head_count
    rows = width // HEAD_DIM * block_tok
    slot_count = 4 * (block_tok // PAGE)

    my_head = lax.axis_index("head")
    hbm = pl.BlockSpec(memory_space=pl.ANY)
    vmem = pl.BlockSpec(memory_space=pltpu.VMEM)
    fetched = [query_states, doc_lengths.reshape(1, -1), page_slot.transpose(1, 2, 0)]
    part, lengths, slots = pl.pallas_call(
        fetch_kernel,
        out_shape=(
            jax.ShapeDtypeStruct((*query_states.shape[:3], 2 * width), query_states.dtype),
            *(jax.ShapeDtypeStruct(x.shape, x.dtype) for x in fetched[1:]),
        ),
        in_specs=[hbm] * 3,
        out_specs=(vmem,) * 3,
        scratch_shapes=[pltpu.SemaphoreType.DMA((6,))],
        compiler_params=pltpu.CompilerParams(vmem_limit_bytes=4 * 1024 * 1024),
        cost_estimate=pl.CostEstimate(flops=0, bytes_accessed=200_000, transcendentals=0),
    )(*(pltpu.with_memory_space_constraint(x, pltpu.HBM) for x in fetched))
    across = lax.ppermute(part, "head", [(i, i ^ 2) for i in range(head_count)])
    pair = jnp.concatenate([key_states, value_states], axis=3)
    pair, _ = lax.optimization_barrier((pair, part))
    near = [
        lax.ppermute(pair, "blk", [(i, i ^ d) for i in range(blk_count)]) for d in range(2, blk_count, 2)
    ]
    beside = jnp.concatenate(
        [
            lax.dynamic_slice_in_dim(query_states, (my_head ^ 1) * width, width, axis=3),
            lax.dynamic_slice_in_dim(across, ((my_head & 1) ^ 1) * width, width, axis=3),
        ],
        axis=0,
    )
    near = lax.optimization_barrier((near[::-1], beside))[0][::-1]
    beside = lax.ppermute(beside, "head", [(i, i ^ 1) for i in range(head_count)])
    near = jnp.concatenate([pair] + near, axis=0)
    far = lax.ppermute(near, "blk", [(i, i ^ 1) for i in range(blk_count)])

    params = pltpu.CompilerParams(vmem_limit_bytes=32 * 1024 * 1024)
    cost = pl.CostEstimate(flops=4_000_000_000, bytes_accessed=1_000_000, transcendentals=200_000)
    half_cols = blk_count // 2 * block_tok
    *bias, far_bias_a, far_bias_b, far_chosen, pages = pl.pallas_call(
        plan_kernel,
        out_shape=(
            jax.ShapeDtypeStruct((half_cols, LANES), jnp.float32),
            jax.ShapeDtypeStruct((2 * half_cols, LANES), jnp.float32),
        )
        * 2
        + (
            jax.ShapeDtypeStruct((slot_count * PAGE, 2 * half_cols), jnp.bfloat16),
            jax.ShapeDtypeStruct((slot_count * PAGE, 2 * HEAD_DIM), jnp.bfloat16),
        ),
        in_specs=[vmem] * 3,
        out_specs=(vmem,) * 6,
        compiler_params=params,
        cost_estimate=cost,
    )(lengths, slots, near)
    stats = pl.pallas_call(
        near_kernel,
        out_shape=(
            jax.ShapeDtypeStruct((2, rows, HEAD_DIM), jnp.bfloat16),
            jax.ShapeDtypeStruct((2, 1, rows), jnp.float32),
            jax.ShapeDtypeStruct((2, 1, rows), jnp.float32),
            jax.ShapeDtypeStruct((2, HEAD_DIM, rows), jnp.float32),
        ),
        in_specs=[vmem] * 6,
        out_specs=(vmem,) * 4,
        compiler_params=params,
        cost_estimate=cost,
    )(query_states, across, beside, near, *bias)
    return pl.pallas_call(
        far_kernel,
        out_shape=(
            jax.ShapeDtypeStruct((1, 2, block_tok, width), jnp.bfloat16),
            jax.ShapeDtypeStruct((slot_count, 1, PAGE, 2 * HEAD_DIM), jnp.bfloat16),
        ),
        in_specs=[vmem] * 9,
        out_specs=(hbm, hbm),
        scratch_shapes=[
            pltpu.VMEM((slot_count, 1, PAGE, 2 * HEAD_DIM), jnp.bfloat16),
            pltpu.VMEM((2, block_tok, width), jnp.bfloat16),
            pltpu.SemaphoreType.DMA((3,)),
        ],
        compiler_params=params,
        cost_estimate=cost,
    )(far, far_bias_a, far_bias_b, far_chosen, pages, *stats)


def per_device_long(query_states, key_states, value_states, doc_lengths, page_slot):
    q_local = lax.all_to_all(query_states, "head", split_axis=3, concat_axis=2, tiled=True)
    axis_count = lax.axis_size("blk")
    my_index = lax.axis_index("blk")
    block_tok = q_local.shape[2]
    head_dim = key_states.shape[3]
    group_size = q_local.shape[3] // head_dim
    query_rows = q_local.reshape(2 * block_tok, group_size, head_dim)
    offsets = jnp.arange(block_tok, dtype=jnp.int32)
    doc_bounds = jnp.cumsum(doc_lengths)[:-1]
    page_count = block_tok // PAGE
    slot_count = 4 * page_count
    slot_range = jnp.arange(slot_count, dtype=jnp.int32)
    score_scale = head_dim ** (-0.5)

    def group_positions(owner_ids):
        block_starts = jnp.stack([owner_ids, 2 * axis_count - 1 - owner_ids], axis=1) * block_tok
        return (block_starts[:, :, None] + offsets[None, None, :]).reshape(-1)

    def doc_of(positions):
        return jnp.sum((positions[:, None] >= doc_bounds[None, :]).astype(jnp.int32), axis=1)

    q_pos = group_positions(my_index.reshape(1))
    q_doc = doc_of(q_pos)

    def attend_group(attn_state, key_rows, value_rows, allowed):
        running_max, weight_sum, accum = attn_state
        scores = (
            jnp.einsum("qhd,kd->qhk", query_rows, key_rows, preferred_element_type=jnp.float32)
            * score_scale
        )
        masked = jnp.where(allowed[:, None, :], scores, -1e30)
        new_max = jnp.maximum(running_max, jnp.max(masked, axis=2))
        weights = jnp.where(allowed[:, None, :], jnp.exp(masked - new_max[..., None]), 0.0)
        factor = jnp.exp(running_max - new_max)
        weight_sum = weight_sum * factor + jnp.sum(weights, axis=2)
        update = jnp.einsum(
            "qhk,kd->qhd",
            weights.astype(jnp.bfloat16),
            value_rows,
            preferred_element_type=jnp.float32,
        )
        accum = accum * factor[..., None] + update
        return (new_max, weight_sum, accum)

    def visit_group(attn_state, key_group, value_group, owner_ids):
        key_rows = key_group.reshape(-1, head_dim)
        value_rows = value_group.reshape(-1, head_dim)
        k_pos = group_positions(owner_ids)
        allowed = (k_pos[None, :] <= q_pos[:, None]) & (doc_of(k_pos)[None, :] == q_doc[:, None])
        return attend_group(attn_state, key_rows, value_rows, allowed)

    def place_pages(page_store, key_group, value_group, owner_ids):
        page_rows = jnp.concatenate([key_group, value_group], axis=-1).reshape(
            -1, PAGE * 2 * head_dim
        )
        slot_ids = jnp.take(page_slot, owner_ids, axis=0).reshape(-1) - my_index * slot_count
        selector = (slot_range[:, None] == slot_ids[None, :]).astype(jnp.bfloat16)
        return page_store + jnp.dot(selector, page_rows, preferred_element_type=jnp.float32)

    def fold_groups(step_fn, carried, kv_piece):
        key_piece, value_piece = kv_piece
        piece_len = key_piece.shape[0]
        width = 4
        owner_ids = jnp.arange(piece_len, dtype=jnp.int32).reshape(piece_len // width, width)
        key_groups = key_piece.reshape(piece_len // width, width, 2, block_tok, head_dim)
        value_groups = value_piece.reshape(piece_len // width, width, 2, block_tok, head_dim)

        def visit_one(inner_state, entry_tuple):
            key_group, value_group, owners = entry_tuple
            return (step_fn(inner_state, key_group, value_group, owners), None)

        return lax.scan(visit_one, carried, (key_groups, value_groups, owner_ids))[0]

    empty_store = jnp.zeros((slot_count, PAGE * 2 * head_dim), jnp.float32)
    start_state = (
        jnp.full((2 * block_tok, group_size), -1e30, jnp.float32),
        jnp.zeros((2 * block_tok, group_size), jnp.float32),
        jnp.zeros((2 * block_tok, group_size, head_dim), jnp.float32),
    )
    final_state = fold_groups(
        visit_group,
        start_state,
        (
            lax.all_gather(key_states, "blk", axis=0, tiled=True),
            lax.all_gather(value_states, "blk", axis=0, tiled=True),
        ),
    )
    page_store = fold_groups(
        place_pages,
        empty_store,
        (
            lax.all_gather(key_states, "blk", axis=0, tiled=True),
            lax.all_gather(value_states, "blk", axis=0, tiled=True),
        ),
    )
    running_max, weight_sum, accum = final_state
    attended = (
        (accum / weight_sum[..., None])
        .astype(jnp.bfloat16)
        .reshape(1, 2, block_tok, group_size * head_dim)
    )
    kv_cache = page_store.astype(jnp.bfloat16).reshape(slot_count, 1, PAGE, 2 * head_dim)
    return (attended, kv_cache)


def solution(mesh):
    return jax.shard_map(
        per_device if mesh.shape["blk"] <= 8 else per_device_long,
        mesh=mesh,
        in_specs=(
            P("blk", None, "head", None),
            P("blk", None, None, "head"),
            P("blk", None, None, "head"),
            P(),
            P(),
        ),
        out_specs=(P("blk", None, None, "head"), P("blk", "head", None, None)),
        check_vma=False,
    )
```

```python
import functools

import jax
import jax.numpy as jnp
from jax import lax
from jax.experimental import pallas as pl
from jax.experimental.pallas import tpu as pltpu
from jax.sharding import PartitionSpec as P

PAGE = 16
LOG2E = 1.4426950408889634
HEAD_DIM = 128
LANES = 128


def gather_queries(own, across, beside, half):
    my_head = lax.axis_index("head")
    width = beside.shape[-1]
    parts = []
    for lane in range(0, width, HEAD_DIM):
        mine = pl.multiple_of(my_head * width + lane, HEAD_DIM)
        low = pl.multiple_of((my_head & 1) * width + lane, HEAD_DIM)
        parts.append(own[0, half, :, pl.ds(mine, HEAD_DIM)])
        parts.append(beside[0, half, :, lane : lane + HEAD_DIM])
        parts.append(across[0, half, :, pl.ds(low, HEAD_DIM)])
        parts.append(beside[1, half, :, lane : lane + HEAD_DIM])
    return jnp.concatenate(parts, axis=0)


def key_bias(my_blk, lengths, chips, block_tok, sub_tok, half, core):
    blk_count = 2 * chips
    my_block = my_blk if half == 0 else 2 * blk_count - 1 - my_blk
    lane = lax.broadcasted_iota(jnp.int32, (1, LANES), 1)
    sender = lax.axis_index("head") ^ (lane % block_tok // sub_tok)
    q_pos = my_block * block_tok + sender * sub_tok + lane % sub_tok
    first = jnp.zeros_like(q_pos)
    bound = jnp.zeros_like(lengths[:, :1])
    for k in range(lengths.shape[1] - 1):
        bound = bound + lengths[:, k : k + 1]
        first = jnp.where(q_pos >= bound, bound, first)
    row = lax.broadcasted_iota(jnp.int32, (block_tok, LANES), 0)
    parts = []
    for m in range(chips):
        owner = (my_blk ^ core) ^ (2 * m)
        for side in range(half + 1):
            block = owner if side == 0 else 2 * blk_count - 1 - owner
            if core == 0 and m == 0 and side == half:
                allowed = (row <= q_pos - block * block_tok) & (row >= first - block * block_tok)
            else:
                allowed = row >= first - jnp.where(block < my_block, block * block_tok, -(2**28))
            parts.append(jnp.where(allowed, 0.0, -1e30))
    return jnp.concatenate(parts, axis=0)


def page_targets(my_blk, page_slot, chips, slot_count, core):
    _, pages_blk, blk_count = page_slot.shape
    chip = lax.broadcasted_iota(jnp.int32, (chips, blk_count), 0)
    owner = (my_blk ^ core) ^ (2 * chip)
    chosen = (owner == lax.broadcasted_iota(jnp.int32, (chips, blk_count), 1)).astype(jnp.float32).astype(jnp.bfloat16)
    cols = 2 * pages_blk * PAGE
    page = lax.broadcasted_iota(jnp.int32, (pages_blk, cols), 0)
    col = lax.broadcasted_iota(jnp.int32, (pages_blk, cols), 1)
    slots = 0.0
    for half in range(2):
        held = lax.dot_general(
            chosen,
            page_slot[half].astype(jnp.float32).astype(jnp.bfloat16),
            (((1,), (1,)), ((), ())),
            preferred_element_type=jnp.float32,
        )
        spread = (col // PAGE == page + half * pages_blk).astype(jnp.float32).astype(jnp.bfloat16)
        slots = slots + jnp.dot(held.astype(jnp.bfloat16), spread, preferred_element_type=jnp.float32)
    slots = slots.astype(jnp.int32) - my_blk * slot_count
    rows = slots * PAGE + lax.broadcasted_iota(jnp.int32, slots.shape, 1) % PAGE
    return jnp.concatenate([rows[m : m + 1] for m in range(chips)], axis=1)


def choose_pages(targets, slot_count):
    row = lax.broadcasted_iota(jnp.int32, (slot_count * PAGE, targets.shape[1]), 0)
    return jnp.where(row == targets, 1.0, 0.0).astype(jnp.bfloat16)


def place_pages(chosen, pairs):
    return jnp.dot(chosen, pairs[...].reshape(-1, pairs.shape[-1]), preferred_element_type=jnp.float32)


def score_part(queries, pairs, half):
    keys = pairs[:, : half + 1].reshape(-1, 2 * HEAD_DIM)[:, :HEAD_DIM]
    return lax.dot_general(keys, queries, (((1,), (1,)), ((), ())), preferred_element_type=jnp.float32)


def soften(scores, bias):
    bias = jnp.concatenate([bias] * (scores.shape[1] // LANES), axis=1)
    scores = scores * (HEAD_DIM**-0.5 * LOG2E) + bias
    top = jnp.max(scores, axis=0, keepdims=True)
    weights = jnp.exp2(scores - top)
    return top, jnp.sum(weights, axis=0, keepdims=True), weights.astype(jnp.bfloat16)


def weigh_part(weights, pairs, half):
    values = pairs[:, : half + 1].reshape(-1, 2 * HEAD_DIM)[:, HEAD_DIM:]
    return lax.dot_general(values, weights, (((0,), (0,)), ((), ())), preferred_element_type=jnp.float32)


def fetch_kernel(queries, lengths, page_slot, part, lengths_out, slots_out, sems):
    _, halves, _, width = part.shape
    start = ((lax.axis_index("head") & 2) ^ 2) * (width // 2)
    pairs = [(lengths, lengths_out), (page_slot, slots_out)]
    for half in range(halves):
        for lane in range(0, width, width // 2):
            lanes = pl.ds(pl.multiple_of(start + lane, width // 2), width // 2)
            pairs.append((queries.at[0, half, :, lanes], part.at[0, half, :, lane : lane + width // 2]))
    copies = [pltpu.make_async_copy(a, b, sems.at[k]) for k, (a, b) in enumerate(pairs)]
    for copy in copies:
        copy.start()
    for copy in copies:
        copy.wait()


def plan_kernel(
    lengths, page_slot, near, bias_a, bias_b, far_bias_a, far_bias_b, far_chosen, pages_ref
):
    chips, _, block_tok, _ = near.shape
    slot_count = pages_ref.shape[0] // PAGE
    sub_tok = block_tok // lax.axis_size("head")
    my_blk = lax.axis_index("blk")
    targets = functools.partial(page_targets, my_blk, page_slot, chips, slot_count)
    pages_ref[...] = place_pages(choose_pages(targets(0), slot_count), near).astype(jnp.bfloat16)
    far_chosen[...] = choose_pages(targets(1), slot_count)
    bias = functools.partial(key_bias, my_blk, lengths[...], chips, block_tok, sub_tok)
    for half in range(2):
        (bias_a, bias_b)[half][...] = bias(half, 0)
        (far_bias_a, far_bias_b)[half][...] = bias(half, 1)


def near_kernel(own, across, beside, near, bias_a, bias_b, q_rows, top_ref, total_ref, out_ref):
    scores = {}
    for half in (1, 0):
        queries = gather_queries(own, across, beside, half)
        q_rows[half] = queries
        scores[half] = score_part(queries, near, half)
    for half in (1, 0):
        top_ref[half], total_ref[half], weights = soften(scores[half], (bias_a, bias_b)[half][...])
        out_ref[half] = weigh_part(weights, near, half)


def far_kernel(
    far, bias_a, bias_b, far_chosen, pages_ref, q_rows, top_ref, total_ref, out_ref, attended, kv_cache,
    pages, result, sems,
):
    block_tok = far.shape[2]
    slot_count = kv_cache.shape[0]
    my_head = lax.axis_index("head")
    sub_tok = block_tok // lax.axis_size("head")
    moved = place_pages(far_chosen[...], far) + pages_ref[...].astype(jnp.float32)
    pages[...] = moved.astype(jnp.bfloat16).reshape(pages.shape)
    writes = [pltpu.make_async_copy(pages, kv_cache, sems.at[2])]
    writes[0].start()
    scores = {half: score_part(q_rows[half], far, half) for half in (1, 0)}
    parts = {}
    for half in (1, 0):
        top, total, weights = soften(scores[half], (bias_a, bias_b)[half][...])
        parts[half] = (top, total, weigh_part(weights, far, half))
    for half in (1, 0):
        top, total, out = parts[half]
        best = jnp.maximum(top, top_ref[half])
        here = jnp.exp2(top - best)
        there = jnp.exp2(top_ref[half] - best)
        inverse = 1.0 / (total * here + total_ref[half] * there)
        out = (out * (here * inverse) + out_ref[half] * (there * inverse)).astype(jnp.bfloat16).T
        for g in range(out.shape[0] // block_tok):
            for d in range(block_tok // sub_tok):
                row = pl.multiple_of((my_head ^ d) * sub_tok, sub_tok)
                start = g * block_tok + d * sub_tok
                result[half, pl.ds(row, sub_tok), g * HEAD_DIM : (g + 1) * HEAD_DIM] = out[start : start + sub_tok]
        writes.append(pltpu.make_async_copy(result.at[half], attended.at[0, half], sems.at[half]))
        writes[-1].start()
    for write in writes:
        write.wait()


def per_device(query_states, key_states, value_states, doc_lengths, page_slot):
    blk_count = lax.axis_size("blk")
    head_count = lax.axis_size("head")
    q_width = query_states.shape[3]
    block_tok = key_states.shape[2]
    width = q_width // head_count
    rows = width // HEAD_DIM * block_tok
    slot_count = 4 * (block_tok // PAGE)

    my_head = lax.axis_index("head")
    hbm = pl.BlockSpec(memory_space=pl.ANY)
    vmem = pl.BlockSpec(memory_space=pltpu.VMEM)
    fetched = [query_states, doc_lengths.reshape(1, -1), page_slot.transpose(1, 2, 0)]
    part, lengths, slots = pl.pallas_call(
        fetch_kernel,
        out_shape=(
            jax.ShapeDtypeStruct((*query_states.shape[:3], 2 * width), query_states.dtype),
            *(jax.ShapeDtypeStruct(x.shape, x.dtype) for x in fetched[1:]),
        ),
        in_specs=[hbm] * 3,
        out_specs=(vmem,) * 3,
        scratch_shapes=[pltpu.SemaphoreType.DMA((6,))],
        compiler_params=pltpu.CompilerParams(vmem_limit_bytes=4 * 1024 * 1024),
        cost_estimate=pl.CostEstimate(flops=0, bytes_accessed=200_000, transcendentals=0),
    )(*(pltpu.with_memory_space_constraint(x, pltpu.HBM) for x in fetched))
    across = lax.ppermute(part, "head", [(i, i ^ 2) for i in range(head_count)])
    pair = jnp.concatenate([key_states, value_states], axis=3)
    pair, _ = lax.optimization_barrier((pair, part))
    near = [
        lax.ppermute(pair, "blk", [(i, i ^ d) for i in range(blk_count)]) for d in range(2, blk_count, 2)
    ]
    beside = jnp.concatenate(
        [
            lax.dynamic_slice_in_dim(query_states, (my_head ^ 1) * width, width, axis=3),
            lax.dynamic_slice_in_dim(across, ((my_head & 1) ^ 1) * width, width, axis=3),
        ],
        axis=0,
    )
    order = (2, 0, 1)
    sent = lax.optimization_barrier(([near[k] for k in order], beside))[0]
    near = [sent[order.index(k)] for k in range(len(near))]
    beside = lax.ppermute(beside, "head", [(i, i ^ 1) for i in range(head_count)])
    near = jnp.concatenate([pair] + near, axis=0)
    far = lax.ppermute(near, "blk", [(i, i ^ 1) for i in range(blk_count)])

    params = pltpu.CompilerParams(vmem_limit_bytes=32 * 1024 * 1024)
    cost = pl.CostEstimate(flops=4_000_000_000, bytes_accessed=1_000_000, transcendentals=200_000)
    half_cols = blk_count // 2 * block_tok
    *bias, far_bias_a, far_bias_b, far_chosen, pages = pl.pallas_call(
        plan_kernel,
        out_shape=(
            jax.ShapeDtypeStruct((half_cols, LANES), jnp.float32),
            jax.ShapeDtypeStruct((2 * half_cols, LANES), jnp.float32),
        )
        * 2
        + (
            jax.ShapeDtypeStruct((slot_count * PAGE, 2 * half_cols), jnp.bfloat16),
            jax.ShapeDtypeStruct((slot_count * PAGE, 2 * HEAD_DIM), jnp.bfloat16),
        ),
        in_specs=[vmem] * 3,
        out_specs=(vmem,) * 6,
        compiler_params=params,
        cost_estimate=cost,
    )(lengths, slots, near)
    stats = pl.pallas_call(
        near_kernel,
        out_shape=(
            jax.ShapeDtypeStruct((2, rows, HEAD_DIM), jnp.bfloat16),
            jax.ShapeDtypeStruct((2, 1, rows), jnp.float32),
            jax.ShapeDtypeStruct((2, 1, rows), jnp.float32),
            jax.ShapeDtypeStruct((2, HEAD_DIM, rows), jnp.float32),
        ),
        in_specs=[vmem] * 6,
        out_specs=(vmem,) * 4,
        compiler_params=params,
        cost_estimate=cost,
    )(query_states, across, beside, near, *bias)
    return pl.pallas_call(
        far_kernel,
        out_shape=(
            jax.ShapeDtypeStruct((1, 2, block_tok, width), jnp.bfloat16),
            jax.ShapeDtypeStruct((slot_count, 1, PAGE, 2 * HEAD_DIM), jnp.bfloat16),
        ),
        in_specs=[vmem] * 9,
        out_specs=(hbm, hbm),
        scratch_shapes=[
            pltpu.VMEM((slot_count, 1, PAGE, 2 * HEAD_DIM), jnp.bfloat16),
            pltpu.VMEM((2, block_tok, width), jnp.bfloat16),
            pltpu.SemaphoreType.DMA((3,)),
        ],
        compiler_params=params,
        cost_estimate=cost,
    )(far, far_bias_a, far_bias_b, far_chosen, pages, *stats)


def per_device_long(query_states, key_states, value_states, doc_lengths, page_slot):
    q_local = lax.all_to_all(query_states, "head", split_axis=3, concat_axis=2, tiled=True)
    axis_count = lax.axis_size("blk")
    my_index = lax.axis_index("blk")
    block_tok = q_local.shape[2]
    head_dim = key_states.shape[3]
    group_size = q_local.shape[3] // head_dim
    query_rows = q_local.reshape(2 * block_tok, group_size, head_dim)
    offsets = jnp.arange(block_tok, dtype=jnp.int32)
    doc_bounds = jnp.cumsum(doc_lengths)[:-1]
    page_count = block_tok // PAGE
    slot_count = 4 * page_count
    slot_range = jnp.arange(slot_count, dtype=jnp.int32)
    score_scale = head_dim ** (-0.5)

    def group_positions(owner_ids):
        block_starts = jnp.stack([owner_ids, 2 * axis_count - 1 - owner_ids], axis=1) * block_tok
        return (block_starts[:, :, None] + offsets[None, None, :]).reshape(-1)

    def doc_of(positions):
        return jnp.sum((positions[:, None] >= doc_bounds[None, :]).astype(jnp.int32), axis=1)

    q_pos = group_positions(my_index.reshape(1))
    q_doc = doc_of(q_pos)

    def attend_group(attn_state, key_rows, value_rows, allowed):
        running_max, weight_sum, accum = attn_state
        scores = (
            jnp.einsum("qhd,kd->qhk", query_rows, key_rows, preferred_element_type=jnp.float32)
            * score_scale
        )
        masked = jnp.where(allowed[:, None, :], scores, -1e30)
        new_max = jnp.maximum(running_max, jnp.max(masked, axis=2))
        weights = jnp.where(allowed[:, None, :], jnp.exp(masked - new_max[..., None]), 0.0)
        factor = jnp.exp(running_max - new_max)
        weight_sum = weight_sum * factor + jnp.sum(weights, axis=2)
        update = jnp.einsum(
            "qhk,kd->qhd",
            weights.astype(jnp.bfloat16),
            value_rows,
            preferred_element_type=jnp.float32,
        )
        accum = accum * factor[..., None] + update
        return (new_max, weight_sum, accum)

    def visit_group(attn_state, key_group, value_group, owner_ids):
        key_rows = key_group.reshape(-1, head_dim)
        value_rows = value_group.reshape(-1, head_dim)
        k_pos = group_positions(owner_ids)
        allowed = (k_pos[None, :] <= q_pos[:, None]) & (doc_of(k_pos)[None, :] == q_doc[:, None])
        return attend_group(attn_state, key_rows, value_rows, allowed)

    def place_pages(page_store, key_group, value_group, owner_ids):
        page_rows = jnp.concatenate([key_group, value_group], axis=-1).reshape(
            -1, PAGE * 2 * head_dim
        )
        slot_ids = jnp.take(page_slot, owner_ids, axis=0).reshape(-1) - my_index * slot_count
        selector = (slot_range[:, None] == slot_ids[None, :]).astype(jnp.bfloat16)
        return page_store + jnp.dot(selector, page_rows, preferred_element_type=jnp.float32)

    def fold_groups(step_fn, carried, kv_piece):
        key_piece, value_piece = kv_piece
        piece_len = key_piece.shape[0]
        width = 4
        owner_ids = jnp.arange(piece_len, dtype=jnp.int32).reshape(piece_len // width, width)
        key_groups = key_piece.reshape(piece_len // width, width, 2, block_tok, head_dim)
        value_groups = value_piece.reshape(piece_len // width, width, 2, block_tok, head_dim)

        def visit_one(inner_state, entry_tuple):
            key_group, value_group, owners = entry_tuple
            return (step_fn(inner_state, key_group, value_group, owners), None)

        return lax.scan(visit_one, carried, (key_groups, value_groups, owner_ids))[0]

    empty_store = jnp.zeros((slot_count, PAGE * 2 * head_dim), jnp.float32)
    start_state = (
        jnp.full((2 * block_tok, group_size), -1e30, jnp.float32),
        jnp.zeros((2 * block_tok, group_size), jnp.float32),
        jnp.zeros((2 * block_tok, group_size, head_dim), jnp.float32),
    )
    final_state = fold_groups(
        visit_group,
        start_state,
        (
            lax.all_gather(key_states, "blk", axis=0, tiled=True),
            lax.all_gather(value_states, "blk", axis=0, tiled=True),
        ),
    )
    page_store = fold_groups(
        place_pages,
        empty_store,
        (
            lax.all_gather(key_states, "blk", axis=0, tiled=True),
            lax.all_gather(value_states, "blk", axis=0, tiled=True),
        ),
    )
    running_max, weight_sum, accum = final_state
    attended = (
        (accum / weight_sum[..., None])
        .astype(jnp.bfloat16)
        .reshape(1, 2, block_tok, group_size * head_dim)
    )
    kv_cache = page_store.astype(jnp.bfloat16).reshape(slot_count, 1, PAGE, 2 * head_dim)
    return (attended, kv_cache)


def solution(mesh):
    return jax.shard_map(
        per_device if mesh.shape["blk"] <= 8 else per_device_long,
        mesh=mesh,
        in_specs=(
            P("blk", None, "head", None),
            P("blk", None, None, "head"),
            P("blk", None, None, "head"),
            P(),
            P(),
        ),
        out_specs=(P("blk", None, None, "head"), P("blk", "head", None, None)),
        check_vma=False,
    )
```

```python
import functools

import jax
import jax.numpy as jnp
from jax import lax
from jax.experimental import pallas as pl
from jax.experimental.pallas import tpu as pltpu
from jax.sharding import PartitionSpec as P

PAGE = 16
LOG2E = 1.4426950408889634
HEAD_DIM = 128
LANES = 128


def gather_queries(own, across, beside, half):
    my_head = lax.axis_index("head")
    width = beside.shape[-1]
    parts = []
    for lane in range(0, width, HEAD_DIM):
        mine = pl.multiple_of(my_head * width + lane, HEAD_DIM)
        low = pl.multiple_of((my_head & 1) * width + lane, HEAD_DIM)
        parts.append(own[0, half, :, pl.ds(mine, HEAD_DIM)])
        parts.append(beside[0, half, :, lane : lane + HEAD_DIM])
        parts.append(across[0, half, :, pl.ds(low, HEAD_DIM)])
        parts.append(beside[1, half, :, lane : lane + HEAD_DIM])
    return jnp.concatenate(parts, axis=0)


def key_bias(my_blk, lengths, chips, block_tok, sub_tok, half, core):
    blk_count = 2 * chips
    my_block = my_blk if half == 0 else 2 * blk_count - 1 - my_blk
    lane = lax.broadcasted_iota(jnp.int32, (1, LANES), 1)
    sender = lax.axis_index("head") ^ (lane % block_tok // sub_tok)
    q_pos = my_block * block_tok + sender * sub_tok + lane % sub_tok
    first = jnp.zeros_like(q_pos)
    bound = jnp.zeros_like(lengths[:, :1])
    for k in range(lengths.shape[1] - 1):
        bound = bound + lengths[:, k : k + 1]
        first = jnp.where(q_pos >= bound, bound, first)
    row = lax.broadcasted_iota(jnp.int32, (block_tok, LANES), 0)
    parts = []
    for m in range(chips):
        owner = (my_blk ^ core) ^ (2 * m)
        for side in range(half + 1):
            block = owner if side == 0 else 2 * blk_count - 1 - owner
            if core == 0 and m == 0 and side == half:
                allowed = (row <= q_pos - block * block_tok) & (row >= first - block * block_tok)
            else:
                allowed = row >= first - jnp.where(block < my_block, block * block_tok, -(2**28))
            parts.append(jnp.where(allowed, 0.0, -1e30))
    return jnp.concatenate(parts, axis=0)


def page_targets(my_blk, page_slot, chips, slot_count, core):
    _, pages_blk, blk_count = page_slot.shape
    chip = lax.broadcasted_iota(jnp.int32, (chips, blk_count), 0)
    owner = (my_blk ^ core) ^ (2 * chip)
    chosen = (owner == lax.broadcasted_iota(jnp.int32, (chips, blk_count), 1)).astype(jnp.float32).astype(jnp.bfloat16)
    cols = 2 * pages_blk * PAGE
    page = lax.broadcasted_iota(jnp.int32, (pages_blk, cols), 0)
    col = lax.broadcasted_iota(jnp.int32, (pages_blk, cols), 1)
    slots = 0.0
    for half in range(2):
        held = lax.dot_general(
            chosen,
            page_slot[half].astype(jnp.float32).astype(jnp.bfloat16),
            (((1,), (1,)), ((), ())),
            preferred_element_type=jnp.float32,
        )
        spread = (col // PAGE == page + half * pages_blk).astype(jnp.float32).astype(jnp.bfloat16)
        slots = slots + jnp.dot(held.astype(jnp.bfloat16), spread, preferred_element_type=jnp.float32)
    slots = slots.astype(jnp.int32) - my_blk * slot_count
    rows = slots * PAGE + lax.broadcasted_iota(jnp.int32, slots.shape, 1) % PAGE
    return jnp.concatenate([rows[m : m + 1] for m in range(chips)], axis=1)


def choose_pages(targets, slot_count):
    row = lax.broadcasted_iota(jnp.int32, (slot_count * PAGE, targets.shape[1]), 0)
    return jnp.where(row == targets, 1.0, 0.0).astype(jnp.bfloat16)


def place_pages(chosen, pairs):
    return jnp.dot(chosen, pairs[...].reshape(-1, pairs.shape[-1]), preferred_element_type=jnp.float32)


def score_part(queries, pairs, half):
    keys = pairs[:, : half + 1].reshape(-1, 2 * HEAD_DIM)[:, :HEAD_DIM]
    return lax.dot_general(keys, queries, (((1,), (1,)), ((), ())), preferred_element_type=jnp.float32)


def soften(scores, bias):
    bias = jnp.concatenate([bias] * (scores.shape[1] // LANES), axis=1)
    scores = scores * (HEAD_DIM**-0.5 * LOG2E) + bias
    top = jnp.max(scores, axis=0, keepdims=True)
    weights = jnp.exp2(scores - top)
    return top, jnp.sum(weights, axis=0, keepdims=True), weights.astype(jnp.bfloat16)


def weigh_part(weights, pairs, half):
    values = pairs[:, : half + 1].reshape(-1, 2 * HEAD_DIM)[:, HEAD_DIM:]
    return lax.dot_general(values, weights, (((0,), (0,)), ((), ())), preferred_element_type=jnp.float32)


def fetch_kernel(queries, lengths, page_slot, part, lengths_out, slots_out, sems):
    _, halves, _, width = part.shape
    start = ((lax.axis_index("head") & 2) ^ 2) * (width // 2)
    pairs = [(lengths, lengths_out), (page_slot, slots_out)]
    for half in range(halves):
        for lane in range(0, width, width // 2):
            lanes = pl.ds(pl.multiple_of(start + lane, width // 2), width // 2)
            pairs.append((queries.at[0, half, :, lanes], part.at[0, half, :, lane : lane + width // 2]))
    copies = [pltpu.make_async_copy(a, b, sems.at[k]) for k, (a, b) in enumerate(pairs)]
    for copy in copies:
        copy.start()
    for copy in copies:
        copy.wait()


def plan_kernel(
    lengths, page_slot, near, bias_a, bias_b, far_bias_a, far_bias_b, far_chosen, pages_ref
):
    chips, _, block_tok, _ = near.shape
    slot_count = pages_ref.shape[0] // PAGE
    sub_tok = block_tok // lax.axis_size("head")
    my_blk = lax.axis_index("blk")
    targets = functools.partial(page_targets, my_blk, page_slot, chips, slot_count)
    pages_ref[...] = place_pages(choose_pages(targets(0), slot_count), near).astype(jnp.bfloat16)
    far_chosen[...] = choose_pages(targets(1), slot_count)
    bias = functools.partial(key_bias, my_blk, lengths[...], chips, block_tok, sub_tok)
    for half in range(2):
        (bias_a, bias_b)[half][...] = bias(half, 0)
    first, second = bias(0, 1), bias(1, 1)
    for m in range(chips):
        rows = slice(m * block_tok, (m + 1) * block_tok)
        far_bias_a[rows] = second[2 * m * block_tok : (2 * m + 1) * block_tok]
        far_bias_b[rows] = jnp.where(
            (my_blk ^ 1 ^ (2 * m)) < my_blk, first[rows], second[(2 * m + 1) * block_tok : (2 * m + 2) * block_tok]
        )


def near_kernel(own, across, beside, near, bias_a, bias_b, q_rows, top_ref, total_ref, out_ref):
    scores = {}
    for half in (1, 0):
        queries = gather_queries(own, across, beside, half)
        q_rows[half] = queries
        scores[half] = score_part(queries, near, half)
    for half in (1, 0):
        top_ref[half], total_ref[half], weights = soften(scores[half], (bias_a, bias_b)[half][...])
        out_ref[half] = weigh_part(weights, near, half)


def far_kernel(
    far, bias_a, bias_b, far_chosen, pages_ref, q_rows, top_ref, total_ref, out_ref, attended, kv_cache,
    pages, result, sems,
):
    block_tok = far.shape[2]
    slot_count = kv_cache.shape[0]
    my_head = lax.axis_index("head")
    sub_tok = block_tok // lax.axis_size("head")
    scores = {half: score_part(q_rows[half], far, half) for half in (1, 0)}
    moved = place_pages(far_chosen[...], far) + pages_ref[...].astype(jnp.float32)
    pages[...] = moved.astype(jnp.bfloat16).reshape(pages.shape)
    writes = [pltpu.make_async_copy(pages, kv_cache, sems.at[2])]
    writes[0].start()
    my_blk = lax.axis_index("blk")
    chips = far.shape[0]
    early = [(my_blk ^ 1 ^ (2 * m)) < my_blk for m in range(chips)]
    scale = HEAD_DIM**-0.5 * LOG2E
    wide = scores[1].shape[1] // LANES

    def block(array, k):
        return array[k * block_tok : (k + 1) * block_tok]

    def masked(rows, bias):
        return rows * scale + jnp.concatenate([bias] * wide, axis=1)

    base = [masked(block(scores[1], 2 * m), bias_a[m * block_tok : (m + 1) * block_tok]) for m in range(chips)]
    pick = [
        masked(
            jnp.where(early[m], block(scores[0], m), block(scores[1], 2 * m + 1)),
            bias_b[m * block_tok : (m + 1) * block_tok],
        )
        for m in range(chips)
    ]
    peak = [jnp.max(x, axis=0, keepdims=True) for x in pick]
    none = jnp.full_like(peak[0], -1e30)
    tops = [none, functools.reduce(jnp.maximum, [jnp.max(x, axis=0, keepdims=True) for x in base])]
    for m in range(chips):
        tops[0] = jnp.maximum(tops[0], jnp.where(early[m], peak[m], none))
        tops[1] = jnp.maximum(tops[1], jnp.where(early[m], none, peak[m]))
    sums = [jnp.zeros_like(none), jnp.zeros_like(none)]
    weights = [[], []]
    for m in range(chips):
        low = jnp.exp2(base[m] - tops[1])
        one = jnp.exp2(pick[m] - jnp.where(early[m], tops[0], tops[1]))
        part = jnp.sum(one, axis=0, keepdims=True)
        sums[0] = sums[0] + jnp.where(early[m], part, 0.0)
        sums[1] = sums[1] + jnp.sum(low, axis=0, keepdims=True) + jnp.where(early[m], 0.0, part)
        one = one.astype(jnp.bfloat16)
        zero = jnp.zeros_like(one)
        weights[0].append(jnp.where(early[m], one, zero))
        weights[1] += [low.astype(jnp.bfloat16), jnp.where(early[m], zero, one)]
    parts = {
        half: (tops[half], sums[half], weigh_part(jnp.concatenate(weights[half], axis=0), far, half)) for half in (1, 0)
    }
    for half in (1, 0):
        top, total, out = parts[half]
        best = jnp.maximum(top, top_ref[half])
        here = jnp.exp2(top - best)
        there = jnp.exp2(top_ref[half] - best)
        inverse = 1.0 / (total * here + total_ref[half] * there)
        out = (out * (here * inverse) + out_ref[half] * (there * inverse)).astype(jnp.bfloat16).T
        for g in range(out.shape[0] // block_tok):
            for d in range(block_tok // sub_tok):
                row = pl.multiple_of((my_head ^ d) * sub_tok, sub_tok)
                start = g * block_tok + d * sub_tok
                result[half, pl.ds(row, sub_tok), g * HEAD_DIM : (g + 1) * HEAD_DIM] = out[start : start + sub_tok]
        writes.append(pltpu.make_async_copy(result.at[half], attended.at[0, half], sems.at[half]))
        writes[-1].start()
    for write in writes:
        write.wait()


def per_device(query_states, key_states, value_states, doc_lengths, page_slot):
    blk_count = lax.axis_size("blk")
    head_count = lax.axis_size("head")
    q_width = query_states.shape[3]
    block_tok = key_states.shape[2]
    width = q_width // head_count
    rows = width // HEAD_DIM * block_tok
    slot_count = 4 * (block_tok // PAGE)

    my_head = lax.axis_index("head")
    hbm = pl.BlockSpec(memory_space=pl.ANY)
    vmem = pl.BlockSpec(memory_space=pltpu.VMEM)
    fetched = [query_states, doc_lengths.reshape(1, -1), page_slot.transpose(1, 2, 0)]
    part, lengths, slots = pl.pallas_call(
        fetch_kernel,
        out_shape=(
            jax.ShapeDtypeStruct((*query_states.shape[:3], 2 * width), query_states.dtype),
            *(jax.ShapeDtypeStruct(x.shape, x.dtype) for x in fetched[1:]),
        ),
        in_specs=[hbm] * 3,
        out_specs=(vmem,) * 3,
        scratch_shapes=[pltpu.SemaphoreType.DMA((6,))],
        compiler_params=pltpu.CompilerParams(vmem_limit_bytes=4 * 1024 * 1024),
        cost_estimate=pl.CostEstimate(flops=0, bytes_accessed=200_000, transcendentals=0),
    )(*(pltpu.with_memory_space_constraint(x, pltpu.HBM) for x in fetched))
    across = lax.ppermute(part, "head", [(i, i ^ 2) for i in range(head_count)])
    pair = jnp.concatenate([key_states, value_states], axis=3)
    pair, _ = lax.optimization_barrier((pair, part))
    near = [
        lax.ppermute(pair, "blk", [(i, i ^ d) for i in range(blk_count)]) for d in range(2, blk_count, 2)
    ]
    beside = jnp.concatenate(
        [
            lax.dynamic_slice_in_dim(query_states, (my_head ^ 1) * width, width, axis=3),
            lax.dynamic_slice_in_dim(across, ((my_head & 1) ^ 1) * width, width, axis=3),
        ],
        axis=0,
    )
    near = lax.optimization_barrier((near[::-1], beside))[0][::-1]
    beside = lax.ppermute(beside, "head", [(i, i ^ 1) for i in range(head_count)])
    near = jnp.concatenate([pair] + near, axis=0)
    far = lax.ppermute(near, "blk", [(i, i ^ 1) for i in range(blk_count)])

    params = pltpu.CompilerParams(vmem_limit_bytes=32 * 1024 * 1024)
    cost = pl.CostEstimate(flops=4_000_000_000, bytes_accessed=1_000_000, transcendentals=200_000)
    half_cols = blk_count // 2 * block_tok
    *bias, far_bias_a, far_bias_b, far_chosen, pages = pl.pallas_call(
        plan_kernel,
        out_shape=(
            jax.ShapeDtypeStruct((half_cols, LANES), jnp.float32),
            jax.ShapeDtypeStruct((2 * half_cols, LANES), jnp.float32),
            jax.ShapeDtypeStruct((half_cols, LANES), jnp.float32),
            jax.ShapeDtypeStruct((half_cols, LANES), jnp.float32),
        )
        + (
            jax.ShapeDtypeStruct((slot_count * PAGE, 2 * half_cols), jnp.bfloat16),
            jax.ShapeDtypeStruct((slot_count * PAGE, 2 * HEAD_DIM), jnp.bfloat16),
        ),
        in_specs=[vmem] * 3,
        out_specs=(vmem,) * 6,
        compiler_params=params,
        cost_estimate=cost,
    )(lengths, slots, near)
    stats = pl.pallas_call(
        near_kernel,
        out_shape=(
            jax.ShapeDtypeStruct((2, rows, HEAD_DIM), jnp.bfloat16),
            jax.ShapeDtypeStruct((2, 1, rows), jnp.float32),
            jax.ShapeDtypeStruct((2, 1, rows), jnp.float32),
            jax.ShapeDtypeStruct((2, HEAD_DIM, rows), jnp.float32),
        ),
        in_specs=[vmem] * 6,
        out_specs=(vmem,) * 4,
        compiler_params=params,
        cost_estimate=cost,
    )(query_states, across, beside, near, *bias)
    return pl.pallas_call(
        far_kernel,
        out_shape=(
            jax.ShapeDtypeStruct((1, 2, block_tok, width), jnp.bfloat16),
            jax.ShapeDtypeStruct((slot_count, 1, PAGE, 2 * HEAD_DIM), jnp.bfloat16),
        ),
        in_specs=[vmem] * 9,
        out_specs=(hbm, hbm),
        scratch_shapes=[
            pltpu.VMEM((slot_count, 1, PAGE, 2 * HEAD_DIM), jnp.bfloat16),
            pltpu.VMEM((2, block_tok, width), jnp.bfloat16),
            pltpu.SemaphoreType.DMA((3,)),
        ],
        compiler_params=params,
        cost_estimate=cost,
    )(far, far_bias_a, far_bias_b, far_chosen, pages, *stats)


def per_device_long(query_states, key_states, value_states, doc_lengths, page_slot):
    q_local = lax.all_to_all(query_states, "head", split_axis=3, concat_axis=2, tiled=True)
    axis_count = lax.axis_size("blk")
    my_index = lax.axis_index("blk")
    block_tok = q_local.shape[2]
    head_dim = key_states.shape[3]
    group_size = q_local.shape[3] // head_dim
    query_rows = q_local.reshape(2 * block_tok, group_size, head_dim)
    offsets = jnp.arange(block_tok, dtype=jnp.int32)
    doc_bounds = jnp.cumsum(doc_lengths)[:-1]
    page_count = block_tok // PAGE
    slot_count = 4 * page_count
    slot_range = jnp.arange(slot_count, dtype=jnp.int32)
    score_scale = head_dim ** (-0.5)

    def group_positions(owner_ids):
        block_starts = jnp.stack([owner_ids, 2 * axis_count - 1 - owner_ids], axis=1) * block_tok
        return (block_starts[:, :, None] + offsets[None, None, :]).reshape(-1)

    def doc_of(positions):
        return jnp.sum((positions[:, None] >= doc_bounds[None, :]).astype(jnp.int32), axis=1)

    q_pos = group_positions(my_index.reshape(1))
    q_doc = doc_of(q_pos)

    def attend_group(attn_state, key_rows, value_rows, allowed):
        running_max, weight_sum, accum = attn_state
        scores = (
            jnp.einsum("qhd,kd->qhk", query_rows, key_rows, preferred_element_type=jnp.float32)
            * score_scale
        )
        masked = jnp.where(allowed[:, None, :], scores, -1e30)
        new_max = jnp.maximum(running_max, jnp.max(masked, axis=2))
        weights = jnp.where(allowed[:, None, :], jnp.exp(masked - new_max[..., None]), 0.0)
        factor = jnp.exp(running_max - new_max)
        weight_sum = weight_sum * factor + jnp.sum(weights, axis=2)
        update = jnp.einsum(
            "qhk,kd->qhd",
            weights.astype(jnp.bfloat16),
            value_rows,
            preferred_element_type=jnp.float32,
        )
        accum = accum * factor[..., None] + update
        return (new_max, weight_sum, accum)

    def visit_group(attn_state, key_group, value_group, owner_ids):
        key_rows = key_group.reshape(-1, head_dim)
        value_rows = value_group.reshape(-1, head_dim)
        k_pos = group_positions(owner_ids)
        allowed = (k_pos[None, :] <= q_pos[:, None]) & (doc_of(k_pos)[None, :] == q_doc[:, None])
        return attend_group(attn_state, key_rows, value_rows, allowed)

    def place_pages(page_store, key_group, value_group, owner_ids):
        page_rows = jnp.concatenate([key_group, value_group], axis=-1).reshape(
            -1, PAGE * 2 * head_dim
        )
        slot_ids = jnp.take(page_slot, owner_ids, axis=0).reshape(-1) - my_index * slot_count
        selector = (slot_range[:, None] == slot_ids[None, :]).astype(jnp.bfloat16)
        return page_store + jnp.dot(selector, page_rows, preferred_element_type=jnp.float32)

    def fold_groups(step_fn, carried, kv_piece):
        key_piece, value_piece = kv_piece
        piece_len = key_piece.shape[0]
        width = 4
        owner_ids = jnp.arange(piece_len, dtype=jnp.int32).reshape(piece_len // width, width)
        key_groups = key_piece.reshape(piece_len // width, width, 2, block_tok, head_dim)
        value_groups = value_piece.reshape(piece_len // width, width, 2, block_tok, head_dim)

        def visit_one(inner_state, entry_tuple):
            key_group, value_group, owners = entry_tuple
            return (step_fn(inner_state, key_group, value_group, owners), None)

        return lax.scan(visit_one, carried, (key_groups, value_groups, owner_ids))[0]

    empty_store = jnp.zeros((slot_count, PAGE * 2 * head_dim), jnp.float32)
    start_state = (
        jnp.full((2 * block_tok, group_size), -1e30, jnp.float32),
        jnp.zeros((2 * block_tok, group_size), jnp.float32),
        jnp.zeros((2 * block_tok, group_size, head_dim), jnp.float32),
    )
    final_state = fold_groups(
        visit_group,
        start_state,
        (
            lax.all_gather(key_states, "blk", axis=0, tiled=True),
            lax.all_gather(value_states, "blk", axis=0, tiled=True),
        ),
    )
    page_store = fold_groups(
        place_pages,
        empty_store,
        (
            lax.all_gather(key_states, "blk", axis=0, tiled=True),
            lax.all_gather(value_states, "blk", axis=0, tiled=True),
        ),
    )
    running_max, weight_sum, accum = final_state
    attended = (
        (accum / weight_sum[..., None])
        .astype(jnp.bfloat16)
        .reshape(1, 2, block_tok, group_size * head_dim)
    )
    kv_cache = page_store.astype(jnp.bfloat16).reshape(slot_count, 1, PAGE, 2 * head_dim)
    return (attended, kv_cache)


def solution(mesh):
    return jax.shard_map(
        per_device if mesh.shape["blk"] <= 8 else per_device_long,
        mesh=mesh,
        in_specs=(
            P("blk", None, "head", None),
            P("blk", None, None, "head"),
            P("blk", None, None, "head"),
            P(),
            P(),
        ),
        out_specs=(P("blk", None, None, "head"), P("blk", "head", None, None)),
        check_vma=False,
    )
```

```python
import functools

import jax
import jax.numpy as jnp
from jax import lax
from jax.experimental import pallas as pl
from jax.experimental.pallas import tpu as pltpu
from jax.sharding import PartitionSpec as P

PAGE = 16
LOG2E = 1.4426950408889634
HEAD_DIM = 128
LANES = 128


def gather_queries(own, across, beside, half):
    my_head = lax.axis_index("head")
    width = beside.shape[-1]
    parts = []
    for lane in range(0, width, HEAD_DIM):
        mine = pl.multiple_of(my_head * width + lane, HEAD_DIM)
        low = pl.multiple_of((my_head & 1) * width + lane, HEAD_DIM)
        parts.append(own[0, half, :, pl.ds(mine, HEAD_DIM)])
        parts.append(beside[0, half, :, lane : lane + HEAD_DIM])
        parts.append(across[0, half, :, pl.ds(low, HEAD_DIM)])
        parts.append(beside[1, half, :, lane : lane + HEAD_DIM])
    return jnp.concatenate(parts, axis=0)


def key_bias(my_blk, lengths, chips, block_tok, sub_tok, half, core):
    blk_count = 2 * chips
    my_block = my_blk if half == 0 else 2 * blk_count - 1 - my_blk
    lane = lax.broadcasted_iota(jnp.int32, (1, LANES), 1)
    sender = lax.axis_index("head") ^ (lane % block_tok // sub_tok)
    q_pos = my_block * block_tok + sender * sub_tok + lane % sub_tok
    first = jnp.zeros_like(q_pos)
    bound = jnp.zeros_like(lengths[:, :1])
    for k in range(lengths.shape[1] - 1):
        bound = bound + lengths[:, k : k + 1]
        first = jnp.where(q_pos >= bound, bound, first)
    row = lax.broadcasted_iota(jnp.int32, (block_tok, LANES), 0)
    parts = []
    for m in range(chips):
        owner = (my_blk ^ core) ^ (2 * m)
        for side in range(half + 1):
            block = owner if side == 0 else 2 * blk_count - 1 - owner
            if core == 0 and m == 0 and side == half:
                allowed = (row <= q_pos - block * block_tok) & (row >= first - block * block_tok)
            else:
                allowed = row >= first - jnp.where(block < my_block, block * block_tok, -(2**28))
            parts.append(jnp.where(allowed, 0.0, -1e30))
    return jnp.concatenate(parts, axis=0)


def page_targets(my_blk, page_slot, chips, slot_count, core):
    _, pages_blk, blk_count = page_slot.shape
    chip = lax.broadcasted_iota(jnp.int32, (chips, blk_count), 0)
    owner = (my_blk ^ core) ^ (2 * chip)
    chosen = (owner == lax.broadcasted_iota(jnp.int32, (chips, blk_count), 1)).astype(jnp.float32).astype(jnp.bfloat16)
    cols = 2 * pages_blk * PAGE
    page = lax.broadcasted_iota(jnp.int32, (pages_blk, cols), 0)
    col = lax.broadcasted_iota(jnp.int32, (pages_blk, cols), 1)
    slots = 0.0
    for half in range(2):
        held = lax.dot_general(
            chosen,
            page_slot[half].astype(jnp.float32).astype(jnp.bfloat16),
            (((1,), (1,)), ((), ())),
            preferred_element_type=jnp.float32,
        )
        spread = (col // PAGE == page + half * pages_blk).astype(jnp.float32).astype(jnp.bfloat16)
        slots = slots + jnp.dot(held.astype(jnp.bfloat16), spread, preferred_element_type=jnp.float32)
    slots = slots.astype(jnp.int32) - my_blk * slot_count
    rows = slots * PAGE + lax.broadcasted_iota(jnp.int32, slots.shape, 1) % PAGE
    return jnp.concatenate([rows[m : m + 1] for m in range(chips)], axis=1)


def choose_pages(targets, slot_count):
    row = lax.broadcasted_iota(jnp.int32, (slot_count * PAGE, targets.shape[1]), 0)
    return jnp.where(row == targets, 1.0, 0.0).astype(jnp.bfloat16)


def place_pages(chosen, pairs):
    return jnp.dot(chosen, pairs[...].reshape(-1, pairs.shape[-1]), preferred_element_type=jnp.float32)


def score_part(queries, pairs, half):
    keys = pairs[:, : half + 1].reshape(-1, 2 * HEAD_DIM)[:, :HEAD_DIM]
    return lax.dot_general(keys, queries, (((1,), (1,)), ((), ())), preferred_element_type=jnp.float32)


def soften(scores, bias):
    bias = jnp.concatenate([bias] * (scores.shape[1] // LANES), axis=1)
    scores = scores * (HEAD_DIM**-0.5 * LOG2E) + bias
    top = jnp.max(scores, axis=0, keepdims=True)
    weights = jnp.exp2(scores - top)
    return top, jnp.sum(weights, axis=0, keepdims=True), weights.astype(jnp.bfloat16)


def weigh_part(weights, pairs, half):
    values = pairs[:, : half + 1].reshape(-1, 2 * HEAD_DIM)[:, HEAD_DIM:]
    return lax.dot_general(values, weights, (((0,), (0,)), ((), ())), preferred_element_type=jnp.float32)


def fetch_kernel(queries, lengths, page_slot, part, lengths_out, slots_out, sems):
    _, halves, _, width = part.shape
    start = ((lax.axis_index("head") & 2) ^ 2) * (width // 2)
    pairs = []
    for half in range(halves):
        for lane in range(0, width, width // 2):
            lanes = pl.ds(pl.multiple_of(start + lane, width // 2), width // 2)
            pairs.append((queries.at[0, half, :, lanes], part.at[0, half, :, lane : lane + width // 2]))
    pairs += [(lengths, lengths_out), (page_slot, slots_out)]
    copies = [pltpu.make_async_copy(a, b, sems.at[k]) for k, (a, b) in enumerate(pairs)]
    for copy in copies:
        copy.start()
    for copy in copies:
        copy.wait()


def plan_kernel(
    lengths, page_slot, near, bias_a, bias_b, far_bias_a, far_bias_b, far_chosen, pages_ref
):
    chips, _, block_tok, _ = near.shape
    slot_count = pages_ref.shape[0] // PAGE
    sub_tok = block_tok // lax.axis_size("head")
    my_blk = lax.axis_index("blk")
    targets = functools.partial(page_targets, my_blk, page_slot, chips, slot_count)
    pages_ref[...] = place_pages(choose_pages(targets(0), slot_count), near).astype(jnp.bfloat16)
    far_chosen[...] = choose_pages(targets(1), slot_count)
    bias = functools.partial(key_bias, my_blk, lengths[...], chips, block_tok, sub_tok)
    for half in range(2):
        (bias_a, bias_b)[half][...] = bias(half, 0)
    first, second = bias(0, 1), bias(1, 1)
    for m in range(chips):
        rows = slice(m * block_tok, (m + 1) * block_tok)
        far_bias_a[rows] = second[2 * m * block_tok : (2 * m + 1) * block_tok]
        far_bias_b[rows] = jnp.where(
            (my_blk ^ 1 ^ (2 * m)) < my_blk, first[rows], second[(2 * m + 1) * block_tok : (2 * m + 2) * block_tok]
        )


def near_kernel(own, across, beside, near, bias_a, bias_b, q_rows, top_ref, total_ref, out_ref):
    scores = {}
    for half in (1, 0):
        queries = gather_queries(own, across, beside, half)
        q_rows[half] = queries
        scores[half] = score_part(queries, near, half)
    for half in (1, 0):
        top_ref[half], total_ref[half], weights = soften(scores[half], (bias_a, bias_b)[half][...])
        out_ref[half] = weigh_part(weights, near, half)


def far_kernel(
    far, bias_a, bias_b, far_chosen, pages_ref, q_rows, top_ref, total_ref, out_ref, attended, kv_cache,
    pages, result, sems,
):
    block_tok = far.shape[2]
    slot_count = kv_cache.shape[0]
    my_head = lax.axis_index("head")
    sub_tok = block_tok // lax.axis_size("head")
    scores = {half: score_part(q_rows[half], far, half) for half in (1, 0)}
    moved = place_pages(far_chosen[...], far) + pages_ref[...].astype(jnp.float32)
    pages[...] = moved.astype(jnp.bfloat16).reshape(pages.shape)
    writes = [pltpu.make_async_copy(pages, kv_cache, sems.at[2])]
    writes[0].start()
    my_blk = lax.axis_index("blk")
    chips = far.shape[0]
    early = [(my_blk ^ 1 ^ (2 * m)) < my_blk for m in range(chips)]
    scale = HEAD_DIM**-0.5 * LOG2E
    wide = scores[1].shape[1] // LANES

    def block(array, k):
        return array[k * block_tok : (k + 1) * block_tok]

    def masked(rows, bias):
        return rows * scale + jnp.concatenate([bias] * wide, axis=1)

    base = [masked(block(scores[1], 2 * m), bias_a[m * block_tok : (m + 1) * block_tok]) for m in range(chips)]
    pick = [
        masked(
            jnp.where(early[m], block(scores[0], m), block(scores[1], 2 * m + 1)),
            bias_b[m * block_tok : (m + 1) * block_tok],
        )
        for m in range(chips)
    ]
    peak = [jnp.max(x, axis=0, keepdims=True) for x in pick]
    none = jnp.full_like(peak[0], -1e30)
    tops = [none, functools.reduce(jnp.maximum, [jnp.max(x, axis=0, keepdims=True) for x in base])]
    for m in range(chips):
        tops[0] = jnp.maximum(tops[0], jnp.where(early[m], peak[m], none))
        tops[1] = jnp.maximum(tops[1], jnp.where(early[m], none, peak[m]))
    sums = [jnp.zeros_like(none), jnp.zeros_like(none)]
    weights = [[], []]
    for m in range(chips):
        low = jnp.exp2(base[m] - tops[1])
        one = jnp.exp2(pick[m] - jnp.where(early[m], tops[0], tops[1]))
        part = jnp.sum(one, axis=0, keepdims=True)
        sums[0] = sums[0] + jnp.where(early[m], part, 0.0)
        sums[1] = sums[1] + jnp.sum(low, axis=0, keepdims=True) + jnp.where(early[m], 0.0, part)
        one = one.astype(jnp.bfloat16)
        zero = jnp.zeros_like(one)
        weights[0].append(jnp.where(early[m], one, zero))
        weights[1] += [low.astype(jnp.bfloat16), jnp.where(early[m], zero, one)]
    parts = {
        half: (tops[half], sums[half], weigh_part(jnp.concatenate(weights[half], axis=0), far, half)) for half in range(2)
    }
    for half in range(2):
        top, total, out = parts[half]
        best = jnp.maximum(top, top_ref[half])
        here = jnp.exp2(top - best)
        there = jnp.exp2(top_ref[half] - best)
        inverse = 1.0 / (total * here + total_ref[half] * there)
        out = (out * (here * inverse) + out_ref[half] * (there * inverse)).astype(jnp.bfloat16).T
        for g in range(out.shape[0] // block_tok):
            for d in range(block_tok // sub_tok):
                row = pl.multiple_of((my_head ^ d) * sub_tok, sub_tok)
                start = g * block_tok + d * sub_tok
                result[half, pl.ds(row, sub_tok), g * HEAD_DIM : (g + 1) * HEAD_DIM] = out[start : start + sub_tok]
        writes.append(pltpu.make_async_copy(result.at[half], attended.at[0, half], sems.at[half]))
        writes[-1].start()
    for write in writes:
        write.wait()


def per_device(query_states, key_states, value_states, doc_lengths, page_slot):
    blk_count = lax.axis_size("blk")
    head_count = lax.axis_size("head")
    q_width = query_states.shape[3]
    block_tok = key_states.shape[2]
    width = q_width // head_count
    rows = width // HEAD_DIM * block_tok
    slot_count = 4 * (block_tok // PAGE)

    my_head = lax.axis_index("head")
    hbm = pl.BlockSpec(memory_space=pl.ANY)
    vmem = pl.BlockSpec(memory_space=pltpu.VMEM)
    fetched = [query_states, doc_lengths.reshape(1, -1), page_slot.transpose(1, 2, 0)]
    part, lengths, slots = pl.pallas_call(
        fetch_kernel,
        out_shape=(
            jax.ShapeDtypeStruct((*query_states.shape[:3], 2 * width), query_states.dtype),
            *(jax.ShapeDtypeStruct(x.shape, x.dtype) for x in fetched[1:]),
        ),
        in_specs=[hbm] * 3,
        out_specs=(vmem,) * 3,
        scratch_shapes=[pltpu.SemaphoreType.DMA((6,))],
        compiler_params=pltpu.CompilerParams(vmem_limit_bytes=4 * 1024 * 1024),
        cost_estimate=pl.CostEstimate(flops=0, bytes_accessed=200_000, transcendentals=0),
    )(*(pltpu.with_memory_space_constraint(x, pltpu.HBM) for x in fetched))
    across = lax.ppermute(part, "head", [(i, i ^ 2) for i in range(head_count)])
    pair = jnp.concatenate([key_states, value_states], axis=3)
    pair, _ = lax.optimization_barrier((pair, part))
    near = [
        lax.ppermute(pair, "blk", [(i, i ^ d) for i in range(blk_count)]) for d in range(2, blk_count, 2)
    ]
    beside = jnp.concatenate(
        [
            lax.dynamic_slice_in_dim(query_states, (my_head ^ 1) * width, width, axis=3),
            lax.dynamic_slice_in_dim(across, ((my_head & 1) ^ 1) * width, width, axis=3),
        ],
        axis=0,
    )
    near = lax.optimization_barrier((near[::-1], beside))[0][::-1]
    beside = lax.ppermute(beside, "head", [(i, i ^ 1) for i in range(head_count)])
    near = jnp.concatenate([pair] + near, axis=0)
    far = lax.ppermute(near, "blk", [(i, i ^ 1) for i in range(blk_count)])

    params = pltpu.CompilerParams(vmem_limit_bytes=32 * 1024 * 1024)
    cost = pl.CostEstimate(flops=4_000_000_000, bytes_accessed=1_000_000, transcendentals=200_000)
    half_cols = blk_count // 2 * block_tok
    *bias, far_bias_a, far_bias_b, far_chosen, pages = pl.pallas_call(
        plan_kernel,
        out_shape=(
            jax.ShapeDtypeStruct((half_cols, LANES), jnp.float32),
            jax.ShapeDtypeStruct((2 * half_cols, LANES), jnp.float32),
            jax.ShapeDtypeStruct((half_cols, LANES), jnp.float32),
            jax.ShapeDtypeStruct((half_cols, LANES), jnp.float32),
        )
        + (
            jax.ShapeDtypeStruct((slot_count * PAGE, 2 * half_cols), jnp.bfloat16),
            jax.ShapeDtypeStruct((slot_count * PAGE, 2 * HEAD_DIM), jnp.bfloat16),
        ),
        in_specs=[vmem] * 3,
        out_specs=(vmem,) * 6,
        compiler_params=params,
        cost_estimate=cost,
    )(lengths, slots, near)
    stats = pl.pallas_call(
        near_kernel,
        out_shape=(
            jax.ShapeDtypeStruct((2, rows, HEAD_DIM), jnp.bfloat16),
            jax.ShapeDtypeStruct((2, 1, rows), jnp.float32),
            jax.ShapeDtypeStruct((2, 1, rows), jnp.float32),
            jax.ShapeDtypeStruct((2, HEAD_DIM, rows), jnp.float32),
        ),
        in_specs=[vmem] * 6,
        out_specs=(vmem,) * 4,
        compiler_params=params,
        cost_estimate=cost,
    )(query_states, across, beside, near, *bias)
    return pl.pallas_call(
        far_kernel,
        out_shape=(
            jax.ShapeDtypeStruct((1, 2, block_tok, width), jnp.bfloat16),
            jax.ShapeDtypeStruct((slot_count, 1, PAGE, 2 * HEAD_DIM), jnp.bfloat16),
        ),
        in_specs=[vmem] * 9,
        out_specs=(hbm, hbm),
        scratch_shapes=[
            pltpu.VMEM((slot_count, 1, PAGE, 2 * HEAD_DIM), jnp.bfloat16),
            pltpu.VMEM((2, block_tok, width), jnp.bfloat16),
            pltpu.SemaphoreType.DMA((3,)),
        ],
        compiler_params=params,
        cost_estimate=cost,
    )(far, far_bias_a, far_bias_b, far_chosen, pages, *stats)


def per_device_long(query_states, key_states, value_states, doc_lengths, page_slot):
    q_local = lax.all_to_all(query_states, "head", split_axis=3, concat_axis=2, tiled=True)
    axis_count = lax.axis_size("blk")
    my_index = lax.axis_index("blk")
    block_tok = q_local.shape[2]
    head_dim = key_states.shape[3]
    group_size = q_local.shape[3] // head_dim
    query_rows = q_local.reshape(2 * block_tok, group_size, head_dim)
    offsets = jnp.arange(block_tok, dtype=jnp.int32)
    doc_bounds = jnp.cumsum(doc_lengths)[:-1]
    page_count = block_tok // PAGE
    slot_count = 4 * page_count
    slot_range = jnp.arange(slot_count, dtype=jnp.int32)
    score_scale = head_dim ** (-0.5)

    def group_positions(owner_ids):
        block_starts = jnp.stack([owner_ids, 2 * axis_count - 1 - owner_ids], axis=1) * block_tok
        return (block_starts[:, :, None] + offsets[None, None, :]).reshape(-1)

    def doc_of(positions):
        return jnp.sum((positions[:, None] >= doc_bounds[None, :]).astype(jnp.int32), axis=1)

    q_pos = group_positions(my_index.reshape(1))
    q_doc = doc_of(q_pos)

    def attend_group(attn_state, key_rows, value_rows, allowed):
        running_max, weight_sum, accum = attn_state
        scores = (
            jnp.einsum("qhd,kd->qhk", query_rows, key_rows, preferred_element_type=jnp.float32)
            * score_scale
        )
        masked = jnp.where(allowed[:, None, :], scores, -1e30)
        new_max = jnp.maximum(running_max, jnp.max(masked, axis=2))
        weights = jnp.where(allowed[:, None, :], jnp.exp(masked - new_max[..., None]), 0.0)
        factor = jnp.exp(running_max - new_max)
        weight_sum = weight_sum * factor + jnp.sum(weights, axis=2)
        update = jnp.einsum(
            "qhk,kd->qhd",
            weights.astype(jnp.bfloat16),
            value_rows,
            preferred_element_type=jnp.float32,
        )
        accum = accum * factor[..., None] + update
        return (new_max, weight_sum, accum)

    def visit_group(attn_state, key_group, value_group, owner_ids):
        key_rows = key_group.reshape(-1, head_dim)
        value_rows = value_group.reshape(-1, head_dim)
        k_pos = group_positions(owner_ids)
        allowed = (k_pos[None, :] <= q_pos[:, None]) & (doc_of(k_pos)[None, :] == q_doc[:, None])
        return attend_group(attn_state, key_rows, value_rows, allowed)

    def place_pages(page_store, key_group, value_group, owner_ids):
        page_rows = jnp.concatenate([key_group, value_group], axis=-1).reshape(
            -1, PAGE * 2 * head_dim
        )
        slot_ids = jnp.take(page_slot, owner_ids, axis=0).reshape(-1) - my_index * slot_count
        selector = (slot_range[:, None] == slot_ids[None, :]).astype(jnp.bfloat16)
        return page_store + jnp.dot(selector, page_rows, preferred_element_type=jnp.float32)

    def fold_groups(step_fn, carried, kv_piece):
        key_piece, value_piece = kv_piece
        piece_len = key_piece.shape[0]
        width = 4
        owner_ids = jnp.arange(piece_len, dtype=jnp.int32).reshape(piece_len // width, width)
        key_groups = key_piece.reshape(piece_len // width, width, 2, block_tok, head_dim)
        value_groups = value_piece.reshape(piece_len // width, width, 2, block_tok, head_dim)

        def visit_one(inner_state, entry_tuple):
            key_group, value_group, owners = entry_tuple
            return (step_fn(inner_state, key_group, value_group, owners), None)

        return lax.scan(visit_one, carried, (key_groups, value_groups, owner_ids))[0]

    empty_store = jnp.zeros((slot_count, PAGE * 2 * head_dim), jnp.float32)
    start_state = (
        jnp.full((2 * block_tok, group_size), -1e30, jnp.float32),
        jnp.zeros((2 * block_tok, group_size), jnp.float32),
        jnp.zeros((2 * block_tok, group_size, head_dim), jnp.float32),
    )
    final_state = fold_groups(
        visit_group,
        start_state,
        (
            lax.all_gather(key_states, "blk", axis=0, tiled=True),
            lax.all_gather(value_states, "blk", axis=0, tiled=True),
        ),
    )
    page_store = fold_groups(
        place_pages,
        empty_store,
        (
            lax.all_gather(key_states, "blk", axis=0, tiled=True),
            lax.all_gather(value_states, "blk", axis=0, tiled=True),
        ),
    )
    running_max, weight_sum, accum = final_state
    attended = (
        (accum / weight_sum[..., None])
        .astype(jnp.bfloat16)
        .reshape(1, 2, block_tok, group_size * head_dim)
    )
    kv_cache = page_store.astype(jnp.bfloat16).reshape(slot_count, 1, PAGE, 2 * head_dim)
    return (attended, kv_cache)


def solution(mesh):
    return jax.shard_map(
        per_device if mesh.shape["blk"] <= 8 else per_device_long,
        mesh=mesh,
        in_specs=(
            P("blk", None, "head", None),
            P("blk", None, None, "head"),
            P("blk", None, None, "head"),
            P(),
            P(),
        ),
        out_specs=(P("blk", None, None, "head"), P("blk", "head", None, None)),
        check_vma=False,
    )
```

```python
import functools

import jax
import jax.numpy as jnp
from jax import lax
from jax.experimental import pallas as pl
from jax.experimental.pallas import tpu as pltpu
from jax.sharding import PartitionSpec as P

PAGE = 16
LOG2E = 1.4426950408889634
HEAD_DIM = 128
LANES = 128


def gather_queries(own, across, beside, half):
    my_head = lax.axis_index("head")
    width = beside.shape[-1]
    parts = []
    for lane in range(0, width, HEAD_DIM):
        mine = pl.multiple_of(my_head * width + lane, HEAD_DIM)
        low = pl.multiple_of((my_head & 1) * width + lane, HEAD_DIM)
        parts.append(own[0, half, :, pl.ds(mine, HEAD_DIM)])
        parts.append(beside[0, half, :, lane : lane + HEAD_DIM])
        parts.append(across[0, half, :, pl.ds(low, HEAD_DIM)])
        parts.append(beside[1, half, :, lane : lane + HEAD_DIM])
    return jnp.concatenate(parts, axis=0)


def key_bias(my_blk, lengths, chips, block_tok, sub_tok, half, core):
    blk_count = 2 * chips
    my_block = my_blk if half == 0 else 2 * blk_count - 1 - my_blk
    lane = lax.broadcasted_iota(jnp.int32, (1, LANES), 1)
    sender = lax.axis_index("head") ^ (lane % block_tok // sub_tok)
    q_pos = my_block * block_tok + sender * sub_tok + lane % sub_tok
    first = jnp.zeros_like(q_pos)
    bound = jnp.zeros_like(lengths[:, :1])
    for k in range(lengths.shape[1] - 1):
        bound = bound + lengths[:, k : k + 1]
        first = jnp.where(q_pos >= bound, bound, first)
    row = lax.broadcasted_iota(jnp.int32, (block_tok, LANES), 0)
    parts = []
    for m in range(chips):
        owner = (my_blk ^ core) ^ (2 * m)
        for side in range(half + 1):
            block = owner if side == 0 else 2 * blk_count - 1 - owner
            if core == 0 and m == 0 and side == half:
                allowed = (row <= q_pos - block * block_tok) & (row >= first - block * block_tok)
            else:
                allowed = row >= first - jnp.where(block < my_block, block * block_tok, -(2**28))
            parts.append(jnp.where(allowed, 0.0, -1e30))
    return jnp.concatenate(parts, axis=0)


def page_targets(my_blk, page_slot, chips, slot_count, core):
    _, pages_blk, blk_count = page_slot.shape
    chip = lax.broadcasted_iota(jnp.int32, (chips, blk_count), 0)
    owner = (my_blk ^ core) ^ (2 * chip)
    chosen = (owner == lax.broadcasted_iota(jnp.int32, (chips, blk_count), 1)).astype(jnp.float32).astype(jnp.bfloat16)
    cols = 2 * pages_blk * PAGE
    page = lax.broadcasted_iota(jnp.int32, (pages_blk, cols), 0)
    col = lax.broadcasted_iota(jnp.int32, (pages_blk, cols), 1)
    slots = 0.0
    for half in range(2):
        held = lax.dot_general(
            chosen,
            page_slot[half].astype(jnp.float32).astype(jnp.bfloat16),
            (((1,), (1,)), ((), ())),
            preferred_element_type=jnp.float32,
        )
        spread = (col // PAGE == page + half * pages_blk).astype(jnp.float32).astype(jnp.bfloat16)
        slots = slots + jnp.dot(held.astype(jnp.bfloat16), spread, preferred_element_type=jnp.float32)
    slots = slots.astype(jnp.int32) - my_blk * slot_count
    rows = slots * PAGE + lax.broadcasted_iota(jnp.int32, slots.shape, 1) % PAGE
    return jnp.concatenate([rows[m : m + 1] for m in range(chips)], axis=1)


def choose_pages(targets, slot_count):
    row = lax.broadcasted_iota(jnp.int32, (slot_count * PAGE, targets.shape[1]), 0)
    return jnp.where(row == targets, 1.0, 0.0).astype(jnp.bfloat16)


def place_pages(chosen, pairs):
    return jnp.dot(chosen, pairs[...].reshape(-1, pairs.shape[-1]), preferred_element_type=jnp.float32)


def score_part(queries, pairs, half):
    keys = pairs[:, : half + 1].reshape(-1, 2 * HEAD_DIM)[:, :HEAD_DIM]
    return lax.dot_general(keys, queries, (((1,), (1,)), ((), ())), preferred_element_type=jnp.float32)


def soften(scores, bias):
    bias = jnp.concatenate([bias] * (scores.shape[1] // LANES), axis=1)
    scores = scores * (HEAD_DIM**-0.5 * LOG2E) + bias
    top = jnp.max(scores, axis=0, keepdims=True)
    weights = jnp.exp2(scores - top)
    return top, jnp.sum(weights, axis=0, keepdims=True), weights.astype(jnp.bfloat16)


def weigh_part(weights, pairs, half):
    values = pairs[:, : half + 1].reshape(-1, 2 * HEAD_DIM)[:, HEAD_DIM:]
    return lax.dot_general(values, weights, (((0,), (0,)), ((), ())), preferred_element_type=jnp.float32)


def fetch_kernel(queries, lengths, page_slot, part, lengths_out, slots_out, sems):
    _, halves, _, width = part.shape
    start = ((lax.axis_index("head") & 2) ^ 2) * (width // 2)
    pairs = []
    for half in range(halves):
        for lane in range(0, width, width // 2):
            lanes = pl.ds(pl.multiple_of(start + lane, width // 2), width // 2)
            pairs.append((queries.at[0, half, :, lanes], part.at[0, half, :, lane : lane + width // 2]))
    pairs += [(lengths, lengths_out), (page_slot, slots_out)]
    copies = [pltpu.make_async_copy(a, b, sems.at[k]) for k, (a, b) in enumerate(pairs)]
    for copy in copies:
        copy.start()
    for copy in copies:
        copy.wait()


def plan_kernel(
    lengths, page_slot, near, bias_a, bias_b, far_bias_a, far_bias_b, far_chosen, pages_ref
):
    chips, _, block_tok, _ = near.shape
    slot_count = pages_ref.shape[0] // PAGE
    sub_tok = block_tok // lax.axis_size("head")
    my_blk = lax.axis_index("blk")
    targets = functools.partial(page_targets, my_blk, page_slot, chips, slot_count)
    pages_ref[...] = place_pages(choose_pages(targets(0), slot_count), near).astype(jnp.bfloat16)
    far_chosen[...] = choose_pages(targets(1), slot_count)
    bias = functools.partial(key_bias, my_blk, lengths[...], chips, block_tok, sub_tok)
    for half in range(2):
        (bias_a, bias_b)[half][...] = bias(half, 0)
    first, second = bias(0, 1), bias(1, 1)
    for m in range(chips):
        rows = slice(m * block_tok, (m + 1) * block_tok)
        far_bias_a[rows] = second[2 * m * block_tok : (2 * m + 1) * block_tok]
        far_bias_b[rows] = jnp.where(
            (my_blk ^ 1 ^ (2 * m)) < my_blk, first[rows], second[(2 * m + 1) * block_tok : (2 * m + 2) * block_tok]
        )


def near_kernel(own, across, beside, near, bias_a, bias_b, q_rows, top_ref, total_ref, out_ref):
    scores = {}
    for half in (1, 0):
        queries = gather_queries(own, across, beside, half)
        q_rows[half] = queries
        scores[half] = score_part(queries, near, half)
    for half in (1, 0):
        top_ref[half], total_ref[half], weights = soften(scores[half], (bias_a, bias_b)[half][...])
        out_ref[half] = weigh_part(weights, near, half)


def far_kernel(
    far, bias_a, bias_b, far_chosen, pages_ref, q_rows, top_ref, total_ref, out_ref, attended, kv_cache,
    pages, result, sems,
):
    block_tok = far.shape[2]
    slot_count = kv_cache.shape[0]
    my_head = lax.axis_index("head")
    sub_tok = block_tok // lax.axis_size("head")
    scores = {half: score_part(q_rows[half], far, half) for half in (1, 0)}
    my_blk = lax.axis_index("blk")
    chips = far.shape[0]
    early = [(my_blk ^ 1 ^ (2 * m)) < my_blk for m in range(chips)]
    scale = HEAD_DIM**-0.5 * LOG2E
    wide = scores[1].shape[1] // LANES

    def block(array, k):
        return array[k * block_tok : (k + 1) * block_tok]

    def masked(rows, bias):
        return rows * scale + jnp.concatenate([bias] * wide, axis=1)

    base = [masked(block(scores[1], 2 * m), bias_a[m * block_tok : (m + 1) * block_tok]) for m in range(chips)]
    pick = [
        masked(
            jnp.where(early[m], block(scores[0], m), block(scores[1], 2 * m + 1)),
            bias_b[m * block_tok : (m + 1) * block_tok],
        )
        for m in range(chips)
    ]
    peak = [jnp.max(x, axis=0, keepdims=True) for x in pick]
    none = jnp.full_like(peak[0], -1e30)
    tops = [none, functools.reduce(jnp.maximum, [jnp.max(x, axis=0, keepdims=True) for x in base])]
    for m in range(chips):
        tops[0] = jnp.maximum(tops[0], jnp.where(early[m], peak[m], none))
        tops[1] = jnp.maximum(tops[1], jnp.where(early[m], none, peak[m]))
    sums = [jnp.zeros_like(none), jnp.zeros_like(none)]
    weights = [[], []]
    for m in range(chips):
        low = jnp.exp2(base[m] - tops[1])
        one = jnp.exp2(pick[m] - jnp.where(early[m], tops[0], tops[1]))
        part = jnp.sum(one, axis=0, keepdims=True)
        sums[0] = sums[0] + jnp.where(early[m], part, 0.0)
        sums[1] = sums[1] + jnp.sum(low, axis=0, keepdims=True) + jnp.where(early[m], 0.0, part)
        one = one.astype(jnp.bfloat16)
        zero = jnp.zeros_like(one)
        weights[0].append(jnp.where(early[m], one, zero))
        weights[1] += [low.astype(jnp.bfloat16), jnp.where(early[m], zero, one)]
    parts = {
        half: (tops[half], sums[half], weigh_part(jnp.concatenate(weights[half], axis=0), far, half)) for half in range(2)
    }
    moved = place_pages(far_chosen[...], far) + pages_ref[...].astype(jnp.float32)
    pages[...] = moved.astype(jnp.bfloat16).reshape(pages.shape)
    writes = []
    for k, slot in enumerate(range(0, slot_count, slot_count // 4)):
        some = pl.ds(slot, slot_count // 4)
        writes.append(pltpu.make_async_copy(pages.at[some], kv_cache.at[some], sems.at[2 + k]))
        writes[-1].start()
    for half in range(2):
        top, total, out = parts[half]
        best = jnp.maximum(top, top_ref[half])
        here = jnp.exp2(top - best)
        there = jnp.exp2(top_ref[half] - best)
        inverse = 1.0 / (total * here + total_ref[half] * there)
        out = (out * (here * inverse) + out_ref[half] * (there * inverse)).astype(jnp.bfloat16).T
        for g in range(out.shape[0] // block_tok):
            for d in range(block_tok // sub_tok):
                row = pl.multiple_of((my_head ^ d) * sub_tok, sub_tok)
                start = g * block_tok + d * sub_tok
                result[half, pl.ds(row, sub_tok), g * HEAD_DIM : (g + 1) * HEAD_DIM] = out[start : start + sub_tok]
        writes.append(pltpu.make_async_copy(result.at[half], attended.at[0, half], sems.at[half]))
        writes[-1].start()
    for write in writes:
        write.wait()


def per_device(query_states, key_states, value_states, doc_lengths, page_slot):
    blk_count = lax.axis_size("blk")
    head_count = lax.axis_size("head")
    q_width = query_states.shape[3]
    block_tok = key_states.shape[2]
    width = q_width // head_count
    rows = width // HEAD_DIM * block_tok
    slot_count = 4 * (block_tok // PAGE)

    my_head = lax.axis_index("head")
    hbm = pl.BlockSpec(memory_space=pl.ANY)
    vmem = pl.BlockSpec(memory_space=pltpu.VMEM)
    fetched = [query_states, doc_lengths.reshape(1, -1), page_slot.transpose(1, 2, 0)]
    part, lengths, slots = pl.pallas_call(
        fetch_kernel,
        out_shape=(
            jax.ShapeDtypeStruct((*query_states.shape[:3], 2 * width), query_states.dtype),
            *(jax.ShapeDtypeStruct(x.shape, x.dtype) for x in fetched[1:]),
        ),
        in_specs=[hbm] * 3,
        out_specs=(vmem,) * 3,
        scratch_shapes=[pltpu.SemaphoreType.DMA((6,))],
        compiler_params=pltpu.CompilerParams(vmem_limit_bytes=4 * 1024 * 1024),
        cost_estimate=pl.CostEstimate(flops=0, bytes_accessed=200_000, transcendentals=0),
    )(*(pltpu.with_memory_space_constraint(x, pltpu.HBM) for x in fetched))
    across = lax.ppermute(part, "head", [(i, i ^ 2) for i in range(head_count)])
    pair = jnp.concatenate([key_states, value_states], axis=3)
    pair, _ = lax.optimization_barrier((pair, part))
    near = [
        lax.ppermute(pair, "blk", [(i, i ^ d) for i in range(blk_count)]) for d in range(2, blk_count, 2)
    ]
    beside = jnp.concatenate(
        [
            lax.dynamic_slice_in_dim(query_states, (my_head ^ 1) * width, width, axis=3),
            lax.dynamic_slice_in_dim(across, ((my_head & 1) ^ 1) * width, width, axis=3),
        ],
        axis=0,
    )
    near = lax.optimization_barrier((near[::-1], beside))[0][::-1]
    beside = lax.ppermute(beside, "head", [(i, i ^ 1) for i in range(head_count)])
    near = jnp.concatenate([pair] + near, axis=0)
    far = lax.ppermute(near, "blk", [(i, i ^ 1) for i in range(blk_count)])

    params = pltpu.CompilerParams(vmem_limit_bytes=32 * 1024 * 1024)
    cost = pl.CostEstimate(flops=4_000_000_000, bytes_accessed=1_000_000, transcendentals=200_000)
    half_cols = blk_count // 2 * block_tok
    *bias, far_bias_a, far_bias_b, far_chosen, pages = pl.pallas_call(
        plan_kernel,
        out_shape=(
            jax.ShapeDtypeStruct((half_cols, LANES), jnp.float32),
            jax.ShapeDtypeStruct((2 * half_cols, LANES), jnp.float32),
            jax.ShapeDtypeStruct((half_cols, LANES), jnp.float32),
            jax.ShapeDtypeStruct((half_cols, LANES), jnp.float32),
        )
        + (
            jax.ShapeDtypeStruct((slot_count * PAGE, 2 * half_cols), jnp.bfloat16),
            jax.ShapeDtypeStruct((slot_count * PAGE, 2 * HEAD_DIM), jnp.bfloat16),
        ),
        in_specs=[vmem] * 3,
        out_specs=(vmem,) * 6,
        compiler_params=params,
        cost_estimate=cost,
    )(lengths, slots, near)
    stats = pl.pallas_call(
        near_kernel,
        out_shape=(
            jax.ShapeDtypeStruct((2, rows, HEAD_DIM), jnp.bfloat16),
            jax.ShapeDtypeStruct((2, 1, rows), jnp.float32),
            jax.ShapeDtypeStruct((2, 1, rows), jnp.float32),
            jax.ShapeDtypeStruct((2, HEAD_DIM, rows), jnp.float32),
        ),
        in_specs=[vmem] * 6,
        out_specs=(vmem,) * 4,
        compiler_params=params,
        cost_estimate=cost,
    )(query_states, across, beside, near, *bias)
    return pl.pallas_call(
        far_kernel,
        out_shape=(
            jax.ShapeDtypeStruct((1, 2, block_tok, width), jnp.bfloat16),
            jax.ShapeDtypeStruct((slot_count, 1, PAGE, 2 * HEAD_DIM), jnp.bfloat16),
        ),
        in_specs=[vmem] * 9,
        out_specs=(hbm, hbm),
        scratch_shapes=[
            pltpu.VMEM((slot_count, 1, PAGE, 2 * HEAD_DIM), jnp.bfloat16),
            pltpu.VMEM((2, block_tok, width), jnp.bfloat16),
            pltpu.SemaphoreType.DMA((6,)),
        ],
        compiler_params=params,
        cost_estimate=cost,
    )(far, far_bias_a, far_bias_b, far_chosen, pages, *stats)


def per_device_long(query_states, key_states, value_states, doc_lengths, page_slot):
    q_local = lax.all_to_all(query_states, "head", split_axis=3, concat_axis=2, tiled=True)
    axis_count = lax.axis_size("blk")
    my_index = lax.axis_index("blk")
    block_tok = q_local.shape[2]
    head_dim = key_states.shape[3]
    group_size = q_local.shape[3] // head_dim
    query_rows = q_local.reshape(2 * block_tok, group_size, head_dim)
    offsets = jnp.arange(block_tok, dtype=jnp.int32)
    doc_bounds = jnp.cumsum(doc_lengths)[:-1]
    page_count = block_tok // PAGE
    slot_count = 4 * page_count
    slot_range = jnp.arange(slot_count, dtype=jnp.int32)
    score_scale = head_dim ** (-0.5)

    def group_positions(owner_ids):
        block_starts = jnp.stack([owner_ids, 2 * axis_count - 1 - owner_ids], axis=1) * block_tok
        return (block_starts[:, :, None] + offsets[None, None, :]).reshape(-1)

    def doc_of(positions):
        return jnp.sum((positions[:, None] >= doc_bounds[None, :]).astype(jnp.int32), axis=1)

    q_pos = group_positions(my_index.reshape(1))
    q_doc = doc_of(q_pos)

    def attend_group(attn_state, key_rows, value_rows, allowed):
        running_max, weight_sum, accum = attn_state
        scores = (
            jnp.einsum("qhd,kd->qhk", query_rows, key_rows, preferred_element_type=jnp.float32)
            * score_scale
        )
        masked = jnp.where(allowed[:, None, :], scores, -1e30)
        new_max = jnp.maximum(running_max, jnp.max(masked, axis=2))
        weights = jnp.where(allowed[:, None, :], jnp.exp(masked - new_max[..., None]), 0.0)
        factor = jnp.exp(running_max - new_max)
        weight_sum = weight_sum * factor + jnp.sum(weights, axis=2)
        update = jnp.einsum(
            "qhk,kd->qhd",
            weights.astype(jnp.bfloat16),
            value_rows,
            preferred_element_type=jnp.float32,
        )
        accum = accum * factor[..., None] + update
        return (new_max, weight_sum, accum)

    def visit_group(attn_state, key_group, value_group, owner_ids):
        key_rows = key_group.reshape(-1, head_dim)
        value_rows = value_group.reshape(-1, head_dim)
        k_pos = group_positions(owner_ids)
        allowed = (k_pos[None, :] <= q_pos[:, None]) & (doc_of(k_pos)[None, :] == q_doc[:, None])
        return attend_group(attn_state, key_rows, value_rows, allowed)

    def place_pages(page_store, key_group, value_group, owner_ids):
        page_rows = jnp.concatenate([key_group, value_group], axis=-1).reshape(
            -1, PAGE * 2 * head_dim
        )
        slot_ids = jnp.take(page_slot, owner_ids, axis=0).reshape(-1) - my_index * slot_count
        selector = (slot_range[:, None] == slot_ids[None, :]).astype(jnp.bfloat16)
        return page_store + jnp.dot(selector, page_rows, preferred_element_type=jnp.float32)

    def fold_groups(step_fn, carried, kv_piece):
        key_piece, value_piece = kv_piece
        piece_len = key_piece.shape[0]
        width = 4
        owner_ids = jnp.arange(piece_len, dtype=jnp.int32).reshape(piece_len // width, width)
        key_groups = key_piece.reshape(piece_len // width, width, 2, block_tok, head_dim)
        value_groups = value_piece.reshape(piece_len // width, width, 2, block_tok, head_dim)

        def visit_one(inner_state, entry_tuple):
            key_group, value_group, owners = entry_tuple
            return (step_fn(inner_state, key_group, value_group, owners), None)

        return lax.scan(visit_one, carried, (key_groups, value_groups, owner_ids))[0]

    empty_store = jnp.zeros((slot_count, PAGE * 2 * head_dim), jnp.float32)
    start_state = (
        jnp.full((2 * block_tok, group_size), -1e30, jnp.float32),
        jnp.zeros((2 * block_tok, group_size), jnp.float32),
        jnp.zeros((2 * block_tok, group_size, head_dim), jnp.float32),
    )
    final_state = fold_groups(
        visit_group,
        start_state,
        (
            lax.all_gather(key_states, "blk", axis=0, tiled=True),
            lax.all_gather(value_states, "blk", axis=0, tiled=True),
        ),
    )
    page_store = fold_groups(
        place_pages,
        empty_store,
        (
            lax.all_gather(key_states, "blk", axis=0, tiled=True),
            lax.all_gather(value_states, "blk", axis=0, tiled=True),
        ),
    )
    running_max, weight_sum, accum = final_state
    attended = (
        (accum / weight_sum[..., None])
        .astype(jnp.bfloat16)
        .reshape(1, 2, block_tok, group_size * head_dim)
    )
    kv_cache = page_store.astype(jnp.bfloat16).reshape(slot_count, 1, PAGE, 2 * head_dim)
    return (attended, kv_cache)


def solution(mesh):
    return jax.shard_map(
        per_device if mesh.shape["blk"] <= 8 else per_device_long,
        mesh=mesh,
        in_specs=(
            P("blk", None, "head", None),
            P("blk", None, None, "head"),
            P("blk", None, None, "head"),
            P(),
            P(),
        ),
        out_specs=(P("blk", None, None, "head"), P("blk", "head", None, None)),
        check_vma=False,
    )
```

```python
import functools

import jax
import jax.numpy as jnp
from jax import lax
from jax.experimental import pallas as pl
from jax.experimental.pallas import tpu as pltpu
from jax.sharding import PartitionSpec as P

PAGE = 16
LOG2E = 1.4426950408889634
HEAD_DIM = 128
LANES = 128


def gather_queries(own, across, beside, half):
    my_head = lax.axis_index("head")
    width = beside.shape[-1]
    parts = []
    for lane in range(0, width, HEAD_DIM):
        mine = pl.multiple_of(my_head * width + lane, HEAD_DIM)
        low = pl.multiple_of((my_head & 1) * width + lane, HEAD_DIM)
        parts.append(own[0, half, :, pl.ds(mine, HEAD_DIM)])
        parts.append(beside[0, half, :, lane : lane + HEAD_DIM])
        parts.append(across[0, half, :, pl.ds(low, HEAD_DIM)])
        parts.append(beside[1, half, :, lane : lane + HEAD_DIM])
    return jnp.concatenate(parts, axis=0)


def key_bias(my_blk, lengths, chips, block_tok, sub_tok, half, core):
    blk_count = 2 * chips
    my_block = my_blk if half == 0 else 2 * blk_count - 1 - my_blk
    lane = lax.broadcasted_iota(jnp.int32, (1, LANES), 1)
    sender = lax.axis_index("head") ^ (lane % block_tok // sub_tok)
    q_pos = my_block * block_tok + sender * sub_tok + lane % sub_tok
    first = jnp.zeros_like(q_pos)
    bound = jnp.zeros_like(lengths[:, :1])
    for k in range(lengths.shape[1] - 1):
        bound = bound + lengths[:, k : k + 1]
        first = jnp.where(q_pos >= bound, bound, first)
    row = lax.broadcasted_iota(jnp.int32, (block_tok, LANES), 0)
    parts = []
    for m in range(chips):
        owner = (my_blk ^ core) ^ (2 * m)
        for side in range(half + 1):
            block = owner if side == 0 else 2 * blk_count - 1 - owner
            if core == 0 and m == 0 and side == half:
                allowed = (row <= q_pos - block * block_tok) & (row >= first - block * block_tok)
            else:
                allowed = row >= first - jnp.where(block < my_block, block * block_tok, -(2**28))
            parts.append(jnp.where(allowed, 0.0, -1e30))
    return jnp.concatenate(parts, axis=0)


def page_targets(my_blk, page_slot, chips, slot_count, core):
    _, pages_blk, blk_count = page_slot.shape
    chip = lax.broadcasted_iota(jnp.int32, (chips, blk_count), 0)
    owner = (my_blk ^ core) ^ (2 * chip)
    chosen = (owner == lax.broadcasted_iota(jnp.int32, (chips, blk_count), 1)).astype(jnp.float32).astype(jnp.bfloat16)
    cols = 2 * pages_blk * PAGE
    page = lax.broadcasted_iota(jnp.int32, (pages_blk, cols), 0)
    col = lax.broadcasted_iota(jnp.int32, (pages_blk, cols), 1)
    slots = 0.0
    for half in range(2):
        held = lax.dot_general(
            chosen,
            page_slot[half].astype(jnp.float32).astype(jnp.bfloat16),
            (((1,), (1,)), ((), ())),
            preferred_element_type=jnp.float32,
        )
        spread = (col // PAGE == page + half * pages_blk).astype(jnp.float32).astype(jnp.bfloat16)
        slots = slots + jnp.dot(held.astype(jnp.bfloat16), spread, preferred_element_type=jnp.float32)
    slots = slots.astype(jnp.int32) - my_blk * slot_count
    rows = slots * PAGE + lax.broadcasted_iota(jnp.int32, slots.shape, 1) % PAGE
    return jnp.concatenate([rows[m : m + 1] for m in range(chips)], axis=1)


def choose_pages(targets, slot_count):
    row = lax.broadcasted_iota(jnp.int32, (slot_count * PAGE, targets.shape[1]), 0)
    return jnp.where(row == targets, 1.0, 0.0).astype(jnp.bfloat16)


def place_pages(chosen, pairs):
    return jnp.dot(chosen, pairs[...].reshape(-1, pairs.shape[-1]), preferred_element_type=jnp.float32)


def score_part(queries, pairs, half):
    keys = pairs[:, : half + 1].reshape(-1, 2 * HEAD_DIM)[:, :HEAD_DIM]
    return lax.dot_general(keys, queries, (((1,), (1,)), ((), ())), preferred_element_type=jnp.float32)


def soften(scores, bias):
    bias = jnp.concatenate([bias] * (scores.shape[1] // LANES), axis=1)
    scores = scores * (HEAD_DIM**-0.5 * LOG2E) + bias
    top = jnp.max(scores, axis=0, keepdims=True)
    weights = jnp.exp2(scores - top)
    return top, jnp.sum(weights, axis=0, keepdims=True), weights.astype(jnp.bfloat16)


def weigh_part(weights, pairs, half):
    values = pairs[:, : half + 1].reshape(-1, 2 * HEAD_DIM)[:, HEAD_DIM:]
    return lax.dot_general(values, weights, (((0,), (0,)), ((), ())), preferred_element_type=jnp.float32)


def fetch_kernel(queries, lengths, page_slot, part, lengths_out, slots_out, sems):
    _, halves, _, width = part.shape
    start = ((lax.axis_index("head") & 2) ^ 2) * (width // 2)
    pairs = []
    for half in range(halves):
        for lane in range(0, width, width // 2):
            lanes = pl.ds(pl.multiple_of(start + lane, width // 2), width // 2)
            pairs.append((queries.at[0, half, :, lanes], part.at[0, half, :, lane : lane + width // 2]))
    pairs += [(lengths, lengths_out), (page_slot, slots_out)]
    copies = [pltpu.make_async_copy(a, b, sems.at[k]) for k, (a, b) in enumerate(pairs)]
    for copy in copies:
        copy.start()
    for copy in copies:
        copy.wait()


def plan_kernel(
    lengths, page_slot, near, bias_a, bias_b, far_bias_a, far_bias_b, far_chosen, pages_ref
):
    chips, _, block_tok, _ = near.shape
    slot_count = pages_ref.shape[0] // PAGE
    sub_tok = block_tok // lax.axis_size("head")
    my_blk = lax.axis_index("blk")
    targets = functools.partial(page_targets, my_blk, page_slot, chips, slot_count)
    pages_ref[...] = place_pages(choose_pages(targets(0), slot_count), near).astype(jnp.bfloat16)
    far_chosen[...] = choose_pages(targets(1), slot_count)
    bias = functools.partial(key_bias, my_blk, lengths[...], chips, block_tok, sub_tok)
    for half in range(2):
        (bias_a, bias_b)[half][...] = bias(half, 0)
        (far_bias_a, far_bias_b)[half][...] = bias(half, 1)


def near_kernel(own, across, beside, near, bias_a, bias_b, q_rows, top_ref, total_ref, out_ref):
    scores = {}
    for half in (1, 0):
        queries = gather_queries(own, across, beside, half)
        q_rows[half] = queries
        scores[half] = score_part(queries, near, half)
    for half in (1, 0):
        top_ref[half], total_ref[half], weights = soften(scores[half], (bias_a, bias_b)[half][...])
        out_ref[half] = weigh_part(weights, near, half)


def far_kernel(
    far, bias_a, bias_b, far_chosen, pages_ref, q_rows, top_ref, total_ref, out_ref, attended, kv_cache,
    pages, result, sems,
):
    block_tok = far.shape[2]
    slot_count = kv_cache.shape[0]
    my_head = lax.axis_index("head")
    sub_tok = block_tok // lax.axis_size("head")
    scores = {half: score_part(q_rows[half], far, half) for half in (1, 0)}
    moved = place_pages(far_chosen[...], far) + pages_ref[...].astype(jnp.float32)
    pages[...] = moved.astype(jnp.bfloat16).reshape(pages.shape)
    writes = [pltpu.make_async_copy(pages, kv_cache, sems.at[2])]
    writes[0].start()
    parts = {}
    for half in (1, 0):
        top, total, weights = soften(scores[half], (bias_a, bias_b)[half][...])
        parts[half] = (top, total, weigh_part(weights, far, half))
    for half in (1, 0):
        top, total, out = parts[half]
        best = jnp.maximum(top, top_ref[half])
        here = jnp.exp2(top - best)
        there = jnp.exp2(top_ref[half] - best)
        inverse = 1.0 / (total * here + total_ref[half] * there)
        out = (out * (here * inverse) + out_ref[half] * (there * inverse)).astype(jnp.bfloat16).T
        for g in range(out.shape[0] // block_tok):
            for d in range(block_tok // sub_tok):
                row = pl.multiple_of((my_head ^ d) * sub_tok, sub_tok)
                start = g * block_tok + d * sub_tok
                result[half, pl.ds(row, sub_tok), g * HEAD_DIM : (g + 1) * HEAD_DIM] = out[start : start + sub_tok]
        writes.append(pltpu.make_async_copy(result.at[half], attended.at[0, half], sems.at[half]))
        writes[-1].start()
    for write in writes:
        write.wait()


def per_device(query_states, key_states, value_states, doc_lengths, page_slot):
    blk_count = lax.axis_size("blk")
    head_count = lax.axis_size("head")
    q_width = query_states.shape[3]
    block_tok = key_states.shape[2]
    width = q_width // head_count
    rows = width // HEAD_DIM * block_tok
    slot_count = 4 * (block_tok // PAGE)

    my_head = lax.axis_index("head")
    hbm = pl.BlockSpec(memory_space=pl.ANY)
    vmem = pl.BlockSpec(memory_space=pltpu.VMEM)
    fetched = [query_states, doc_lengths.reshape(1, -1), page_slot.transpose(1, 2, 0)]
    part, lengths, slots = pl.pallas_call(
        fetch_kernel,
        out_shape=(
            jax.ShapeDtypeStruct((*query_states.shape[:3], 2 * width), query_states.dtype),
            *(jax.ShapeDtypeStruct(x.shape, x.dtype) for x in fetched[1:]),
        ),
        in_specs=[hbm] * 3,
        out_specs=(vmem,) * 3,
        scratch_shapes=[pltpu.SemaphoreType.DMA((6,))],
        compiler_params=pltpu.CompilerParams(vmem_limit_bytes=4 * 1024 * 1024),
        cost_estimate=pl.CostEstimate(flops=0, bytes_accessed=200_000, transcendentals=0),
    )(*(pltpu.with_memory_space_constraint(x, pltpu.HBM) for x in fetched))
    across = lax.ppermute(part, "head", [(i, i ^ 2) for i in range(head_count)])
    pair = jnp.concatenate([key_states, value_states], axis=3)
    pair, _ = lax.optimization_barrier((pair, part))
    near = [
        lax.ppermute(pair, "blk", [(i, i ^ d) for i in range(blk_count)]) for d in range(2, blk_count, 2)
    ]
    beside = jnp.concatenate(
        [
            lax.dynamic_slice_in_dim(query_states, (my_head ^ 1) * width, width, axis=3),
            lax.dynamic_slice_in_dim(across, ((my_head & 1) ^ 1) * width, width, axis=3),
        ],
        axis=0,
    )
    near = lax.optimization_barrier((near[::-1], beside))[0][::-1]
    beside = lax.ppermute(beside, "head", [(i, i ^ 1) for i in range(head_count)])
    near = jnp.concatenate([pair] + near, axis=0)
    far = lax.ppermute(near, "blk", [(i, i ^ 1) for i in range(blk_count)])

    params = pltpu.CompilerParams(vmem_limit_bytes=32 * 1024 * 1024)
    cost = pl.CostEstimate(flops=4_000_000_000, bytes_accessed=1_000_000, transcendentals=200_000)
    half_cols = blk_count // 2 * block_tok
    *bias, far_bias_a, far_bias_b, far_chosen, pages = pl.pallas_call(
        plan_kernel,
        out_shape=(
            jax.ShapeDtypeStruct((half_cols, LANES), jnp.float32),
            jax.ShapeDtypeStruct((2 * half_cols, LANES), jnp.float32),
        )
        * 2
        + (
            jax.ShapeDtypeStruct((slot_count * PAGE, 2 * half_cols), jnp.bfloat16),
            jax.ShapeDtypeStruct((slot_count * PAGE, 2 * HEAD_DIM), jnp.bfloat16),
        ),
        in_specs=[vmem] * 3,
        out_specs=(vmem,) * 6,
        compiler_params=params,
        cost_estimate=cost,
    )(lengths, slots, near)
    stats = pl.pallas_call(
        near_kernel,
        out_shape=(
            jax.ShapeDtypeStruct((2, rows, HEAD_DIM), jnp.bfloat16),
            jax.ShapeDtypeStruct((2, 1, rows), jnp.float32),
            jax.ShapeDtypeStruct((2, 1, rows), jnp.float32),
            jax.ShapeDtypeStruct((2, HEAD_DIM, rows), jnp.float32),
        ),
        in_specs=[vmem] * 6,
        out_specs=(vmem,) * 4,
        compiler_params=params,
        cost_estimate=cost,
    )(query_states, across, beside, near, *bias)
    return pl.pallas_call(
        far_kernel,
        out_shape=(
            jax.ShapeDtypeStruct((1, 2, block_tok, width), jnp.bfloat16),
            jax.ShapeDtypeStruct((slot_count, 1, PAGE, 2 * HEAD_DIM), jnp.bfloat16),
        ),
        in_specs=[vmem] * 9,
        out_specs=(hbm, hbm),
        scratch_shapes=[
            pltpu.VMEM((slot_count, 1, PAGE, 2 * HEAD_DIM), jnp.bfloat16),
            pltpu.VMEM((2, block_tok, width), jnp.bfloat16),
            pltpu.SemaphoreType.DMA((3,)),
        ],
        compiler_params=params,
        cost_estimate=cost,
    )(far, far_bias_a, far_bias_b, far_chosen, pages, *stats)


def per_device_long(query_states, key_states, value_states, doc_lengths, page_slot):
    q_local = lax.all_to_all(query_states, "head", split_axis=3, concat_axis=2, tiled=True)
    axis_count = lax.axis_size("blk")
    my_index = lax.axis_index("blk")
    block_tok = q_local.shape[2]
    head_dim = key_states.shape[3]
    group_size = q_local.shape[3] // head_dim
    query_rows = q_local.reshape(2 * block_tok, group_size, head_dim)
    offsets = jnp.arange(block_tok, dtype=jnp.int32)
    doc_bounds = jnp.cumsum(doc_lengths)[:-1]
    page_count = block_tok // PAGE
    slot_count = 4 * page_count
    slot_range = jnp.arange(slot_count, dtype=jnp.int32)
    score_scale = head_dim ** (-0.5)

    def group_positions(owner_ids):
        block_starts = jnp.stack([owner_ids, 2 * axis_count - 1 - owner_ids], axis=1) * block_tok
        return (block_starts[:, :, None] + offsets[None, None, :]).reshape(-1)

    def doc_of(positions):
        return jnp.sum((positions[:, None] >= doc_bounds[None, :]).astype(jnp.int32), axis=1)

    q_pos = group_positions(my_index.reshape(1))
    q_doc = doc_of(q_pos)

    def attend_group(attn_state, key_rows, value_rows, allowed):
        running_max, weight_sum, accum = attn_state
        scores = (
            jnp.einsum("qhd,kd->qhk", query_rows, key_rows, preferred_element_type=jnp.float32)
            * score_scale
        )
        masked = jnp.where(allowed[:, None, :], scores, -1e30)
        new_max = jnp.maximum(running_max, jnp.max(masked, axis=2))
        weights = jnp.where(allowed[:, None, :], jnp.exp(masked - new_max[..., None]), 0.0)
        factor = jnp.exp(running_max - new_max)
        weight_sum = weight_sum * factor + jnp.sum(weights, axis=2)
        update = jnp.einsum(
            "qhk,kd->qhd",
            weights.astype(jnp.bfloat16),
            value_rows,
            preferred_element_type=jnp.float32,
        )
        accum = accum * factor[..., None] + update
        return (new_max, weight_sum, accum)

    def visit_group(attn_state, key_group, value_group, owner_ids):
        key_rows = key_group.reshape(-1, head_dim)
        value_rows = value_group.reshape(-1, head_dim)
        k_pos = group_positions(owner_ids)
        allowed = (k_pos[None, :] <= q_pos[:, None]) & (doc_of(k_pos)[None, :] == q_doc[:, None])
        return attend_group(attn_state, key_rows, value_rows, allowed)

    def place_pages(page_store, key_group, value_group, owner_ids):
        page_rows = jnp.concatenate([key_group, value_group], axis=-1).reshape(
            -1, PAGE * 2 * head_dim
        )
        slot_ids = jnp.take(page_slot, owner_ids, axis=0).reshape(-1) - my_index * slot_count
        selector = (slot_range[:, None] == slot_ids[None, :]).astype(jnp.bfloat16)
        return page_store + jnp.dot(selector, page_rows, preferred_element_type=jnp.float32)

    def fold_groups(step_fn, carried, kv_piece):
        key_piece, value_piece = kv_piece
        piece_len = key_piece.shape[0]
        width = 4
        owner_ids = jnp.arange(piece_len, dtype=jnp.int32).reshape(piece_len // width, width)
        key_groups = key_piece.reshape(piece_len // width, width, 2, block_tok, head_dim)
        value_groups = value_piece.reshape(piece_len // width, width, 2, block_tok, head_dim)

        def visit_one(inner_state, entry_tuple):
            key_group, value_group, owners = entry_tuple
            return (step_fn(inner_state, key_group, value_group, owners), None)

        return lax.scan(visit_one, carried, (key_groups, value_groups, owner_ids))[0]

    empty_store = jnp.zeros((slot_count, PAGE * 2 * head_dim), jnp.float32)
    start_state = (
        jnp.full((2 * block_tok, group_size), -1e30, jnp.float32),
        jnp.zeros((2 * block_tok, group_size), jnp.float32),
        jnp.zeros((2 * block_tok, group_size, head_dim), jnp.float32),
    )
    final_state = fold_groups(
        visit_group,
        start_state,
        (
            lax.all_gather(key_states, "blk", axis=0, tiled=True),
            lax.all_gather(value_states, "blk", axis=0, tiled=True),
        ),
    )
    page_store = fold_groups(
        place_pages,
        empty_store,
        (
            lax.all_gather(key_states, "blk", axis=0, tiled=True),
            lax.all_gather(value_states, "blk", axis=0, tiled=True),
        ),
    )
    running_max, weight_sum, accum = final_state
    attended = (
        (accum / weight_sum[..., None])
        .astype(jnp.bfloat16)
        .reshape(1, 2, block_tok, group_size * head_dim)
    )
    kv_cache = page_store.astype(jnp.bfloat16).reshape(slot_count, 1, PAGE, 2 * head_dim)
    return (attended, kv_cache)


def solution(mesh):
    return jax.shard_map(
        per_device if mesh.shape["blk"] <= 8 else per_device_long,
        mesh=mesh,
        in_specs=(
            P("blk", None, "head", None),
            P("blk", None, None, "head"),
            P("blk", None, None, "head"),
            P(),
            P(),
        ),
        out_specs=(P("blk", None, None, "head"), P("blk", "head", None, None)),
        check_vma=False,
    )
```
